32 devices in a mesh: batch: 8 (over z, y), seq: 4 (over x, core).
Axes of the slice: x: 2, y: 2, z: 4, core: 2. Of those that a mesh axis runs over, the one named last changes fastest.
Arguments:
- tokens: bfloat16 [4, 8, 1024, 512], P(None, 'batch', 'seq'), may hold values from -6 to 6
- first_length: int32 [4, 8], P(None, 'batch'), may hold values from 512 to 1024, as said below
- cotangent: bfloat16 [4, 8, 1024, 512], P(None, 'batch', 'seq'), may hold values from -6 to 6
- positions: bfloat16 [1024, 512], P(None, ('batch', 'seq')), may hold values from -3 to 3
- inward: bfloat16 [512, 1536], P(('batch', 'seq')), may hold values from -0.25 to 0.25
- intake: bfloat16 [1024], P(('batch', 'seq')), may hold values from -3 to 3
- outward: bfloat16 [512, 512], P(('batch', 'seq')), may hold values from -2 to 2
- outlet: bfloat16 [512], P(('batch', 'seq')), may hold values from -2 to 2
- steady: bfloat16 [512], P(('batch', 'seq')), may hold values from 0.5 to 1.5
- offset: bfloat16 [512], P(('batch', 'seq')), may hold values from -2 to 2
- expand: bfloat16 [512, 2048], P(('batch', 'seq')), may hold values from -0.25 to 0.25
- spread: bfloat16 [2048], P(('batch', 'seq')), may hold values from -2 to 2
- contract: bfloat16 [2048, 512], P(('batch', 'seq')), may hold values from -0.125 to 0.125
- settle: bfloat16 [512], P(('batch', 'seq')), may hold values from -2 to 2
- temper: bfloat16 [512], P(('batch', 'seq')), may hold values from 0.5 to 1.5
- anchor: bfloat16 [512], P(('batch', 'seq')), may hold values from -2 to 2
Outputs:
- layer_output: bfloat16 [4, 8, 1024, 512], P(None, 'batch', 'seq')
- tokens_grad: bfloat16 [4, 8, 1024, 512], P(None, 'batch', 'seq')
- positions_grad: float32 [1024, 512], P(None, ('batch', 'seq'))
- inward_grad: float32 [512, 1536], P(('batch', 'seq'))
- intake_grad: float32 [1024], P(('batch', 'seq'))
- outward_grad: float32 [512, 512], P(('batch', 'seq'))
- outlet_grad: float32 [512], P(('batch', 'seq'))
- steady_grad: float32 [512], P(('batch', 'seq'))
- offset_grad: float32 [512], P(('batch', 'seq'))
- expand_grad: float32 [512, 2048], P(('batch', 'seq'))
- spread_grad: float32 [2048], P(('batch', 'seq'))
- contract_grad: float32 [2048, 512], P(('batch', 'seq'))
- settle_grad: float32 [512], P(('batch', 'seq'))
- temper_grad: float32 [512], P(('batch', 'seq'))
- anchor_grad: float32 [512], P(('batch', 'seq'))
The draws below stay inside these ranges and needn't reach their ends.
Inputs may be any that keep to these rules, and one draw needn't show every extreme that they name: `first_length`: each entry is 1024 // 2 (a pack of two documents of equal length) or 1024 (a pack of one document); among the packs of one index of batch over all micro-batches, both kinds occur.
All inputs are finite; a program needn't handle non-finite values.
Results may differ from the reference program's by a relative error of at most 0.015.
The reference program's roundings to bfloat16 on the way count: a program that leaves them out, or rounds other values in their place, can miss the bound.
Values may be sent and summed in bfloat16 or wider, within the bound.
No kernel may reach another device: no remote copies, remote signals or barrier semaphores. Data moves between devices by JAX's collectives and lax.ppermute only.
A program may use at most 128 MiB of HBM per device.

```python
import math
import jax
import jax.numpy as jnp
from jax import lax

D = 512
HEADS = 8
FF = 2048
HEAD_DIM = 64
SEQ_LEN = 1024
MICRO = 4
PACK_DEV = 1
PACKS = 8


def draw_first_length(key, part):
    key = jax.random.fold_in(key, 7)
    groups = PACKS // PACK_DEV
    count = MICRO * PACK_DEV
    flag_key, whole_key, shift_key = jax.random.split(key, 3)
    flags = jax.random.randint(flag_key, (groups, count), 0, 2)
    whole_at = jax.random.randint(whole_key, (groups, 1), 0, count)
    split_at = (whole_at + 1 + jax.random.randint(shift_key, (groups, 1), 0, count - 1)) % count
    places = jnp.arange(count, dtype=jnp.int32)[None, :]
    flags = jnp.where(places == whole_at, 1, jnp.where(places == split_at, 0, flags))
    lengths = jnp.where(flags == 1, SEQ_LEN, SEQ_LEN // 2).astype(jnp.int32)
    lengths = lengths.reshape(groups, MICRO, PACK_DEV).transpose(1, 0, 2).reshape(MICRO, PACKS)
    return lengths


def block_levels(key, dims, pieces, smallest, largest):
    def one(axis_at, blocks):
        heights = jax.random.uniform(jax.random.fold_in(jax.random.fold_in(key, 6), axis_at), (blocks,), jnp.float32, smallest / len(pieces), largest / len(pieces))
        return jnp.repeat(jnp.exp(heights), dims[axis_at] // blocks).reshape((-1,) + (1,) * (len(dims) - axis_at - 1))

    loudness = one(*pieces[0])
    for cut in pieces[1:]:
        loudness = loudness * one(*cut)
    return loudness


def noise(own_key, extent, scale, bound, pieces=(), kind=jnp.bfloat16):
    loudness = block_levels(own_key, extent, pieces, -0.22, 0.18) if pieces else 1.0
    values = jax.random.normal(own_key, extent, jnp.float32) * scale * loudness
    return jnp.minimum(jnp.maximum(values, -bound), bound).astype(kind)


def setup_inputs(seed: int = 0) -> dict:
    seeds = jax.random.split(jax.random.key(seed), 17)
    tokens = noise(seeds[0], (MICRO, PACKS, SEQ_LEN, D), 1.0, 6.0, ((1, 8), (2, 4)))
    first_length = draw_first_length(jax.random.fold_in(seeds[16], 71), 0)
    cotangent = noise(seeds[2], (MICRO, PACKS, SEQ_LEN, D), 1.0, 6.0, ((1, 8), (2, 4)))
    positions = noise(seeds[3], (SEQ_LEN, D), 0.5, 3.0, ((1, 32),))
    inward = noise(seeds[4], (D, 3 * D), D ** -0.5, 0.25, ((0, 32),))
    intake = noise(seeds[5], (2 * D,), 0.5, 3.0, ((0, 32),))
    outward = noise(seeds[6], (D, D), (D * 16 // SEQ_LEN) ** -0.5, 2.0, ((0, 32),))
    outlet = noise(seeds[7], (D,), 0.3, 2.0, ((0, 32),))
    steady = jnp.clip(1.0 + 0.1 * jax.random.normal(seeds[8], (D,), jnp.float32), 0.5, 1.5).astype(jnp.bfloat16)
    offset = noise(seeds[9], (D,), 0.3, 2.0, ((0, 32),))
    expand = noise(seeds[10], (D, FF), D ** -0.5, 0.25, ((0, 32),))
    spread = noise(seeds[11], (FF,), 0.3, 2.0, ((0, 32),))
    contract = noise(seeds[12], (FF, D), FF ** -0.5, 0.125, ((0, 32),))
    settle = noise(seeds[13], (D,), 0.3, 2.0, ((0, 32),))
    temper = jnp.clip(1.0 + 0.1 * jax.random.normal(seeds[14], (D,), jnp.float32), 0.5, 1.5).astype(jnp.bfloat16)
    anchor = noise(seeds[15], (D,), 0.3, 2.0, ((0, 32),))
    return {"tokens": tokens, "first_length": first_length, "cotangent": cotangent, "positions": positions, "inward": inward, "intake": intake, "outward": outward, "outlet": outlet, "steady": steady, "offset": offset, "expand": expand, "spread": spread, "contract": contract, "settle": settle, "temper": temper, "anchor": anchor}


NEGATIVE = -1e+30
HIGHEST = lax.Precision.HIGHEST

@jax.custom_vjp
def low(v):
    return lax.optimization_barrier(v.astype(jnp.bfloat16)).astype(jnp.float32)

@jax.custom_vjp
def low_back(v):
    return v

def low_keep(v):
    return (low(v), None)

def low_pass(kept, grad):
    return (grad,)

def back_keep(v):
    return (v, None)

def back_low(kept, grad):
    return (low(grad),)
low.defvjp(low_keep, low_pass)
low_back.defvjp(back_keep, back_low)

def both(value):
    return low(low_back(value))

def layer_norm(rows, gain, shift):
    center = rows - lax.optimization_barrier(jnp.mean(rows, axis=-1, keepdims=True))
    variance = lax.optimization_barrier(jnp.mean(center * center, axis=-1, keepdims=True))
    return center * lax.rsqrt(variance + 1e-05) * gain + shift

def smooth(values):
    return jax.nn.gelu(values, approximate=True)

def attend(queries, keys, values, first):
    groups, length = (queries.shape[0], queries.shape[1])
    span = min(512, length)
    key_place = jnp.arange(length, dtype=jnp.int32)
    later_key = key_place[None, :] >= first[:, None]
    scale = 1.0 / math.sqrt(HEAD_DIM)

    @jax.checkpoint
    def block(index):
        begin = index * span
        query_block = lax.dynamic_slice_in_dim(queries, begin, span, 1)
        query_place = begin + jnp.arange(span, dtype=jnp.int32)
        later_query = query_place[None, :] >= first[:, None]
        causal = key_place[None, :] <= query_place[:, None]
        allowed = causal[None, :, :] & (later_query[:, :, None] == later_key[:, None, :])
        allowed = allowed[:, None, :, :]
        scores = low_back(jnp.einsum('gqhd,gkhd->ghqk', query_block, keys, precision=HIGHEST))
        logits = jnp.where(allowed, scores * scale, NEGATIVE)
        peak = lax.optimization_barrier(jnp.max(logits, axis=-1, keepdims=True))
        raised = jnp.where(allowed, jnp.exp(logits - peak), 0.0)
        share = low(raised / lax.optimization_barrier(jnp.sum(raised, axis=-1, keepdims=True)))
        return jnp.einsum('ghqk,gkhd->gqhd', share, values, precision=HIGHEST)
    blocks = lax.map(block, jnp.arange(length // span, dtype=jnp.int32))
    return jnp.transpose(blocks, (1, 0, 2, 3, 4)).reshape(groups, length, HEADS * HEAD_DIM)

def forward(tokens_in, first, params):
    table, inward, intake, outward, outlet, steady, offset, expand, spread, contract, settle, temper, anchor = params
    groups, length, width = tokens_in.shape
    places = jnp.arange(length, dtype=jnp.int32)
    later = places[None, :] >= first[:, None]
    place = places[None, :] - jnp.where(later, first[:, None], 0)
    lifted = tokens_in + jnp.take(table, place, axis=0)
    joint = jnp.einsum('gld,de->gle', low(lifted), inward, precision=HIGHEST)
    queries = both(joint[..., :width] + intake[:width])
    keys = both(joint[..., width:2 * width])
    values = both(joint[..., 2 * width:] + intake[width:])
    heads_shape = (groups, length, HEADS, HEAD_DIM)
    mixed = both(attend(queries.reshape(heads_shape), keys.reshape(heads_shape), values.reshape(heads_shape), first))
    branch = low_back(jnp.einsum('gld,de->gle', mixed, outward, precision=HIGHEST) + outlet)
    normed = layer_norm(lifted + branch, steady, offset)
    hidden = low_back(jnp.einsum('gld,df->glf', low(normed), expand, precision=HIGHEST) + spread)
    active = low(smooth(hidden))
    lowered = low_back(jnp.einsum('glf,fd->gld', active, contract, precision=HIGHEST) + settle)
    return layer_norm(normed + lowered, temper, anchor)

def reference(tokens, first_length, cotangent, positions, inward, intake, outward, outlet, steady, offset, expand, spread, contract, settle, temper, anchor):
    params = tuple((p.astype(jnp.float32) for p in (positions, inward, intake, outward, outlet, steady, offset, expand, spread, contract, settle, temper, anchor)))
    groups = MICRO * PACKS // PACK_DEV
    blocks = tokens.astype(jnp.float32).reshape(groups, PACK_DEV, SEQ_LEN, D)
    firsts = first_length.reshape(groups, PACK_DEV).astype(jnp.int32)
    cotangents = cotangent.astype(jnp.float32).reshape(groups, PACK_DEV, SEQ_LEN, D)

    def step(carry, inputs):
        block, first, upstream = inputs
        result, pullback = jax.vjp(lambda values, weights: forward(values, first, weights), block, params)
        block_back, param_back = pullback(upstream)
        carry = jax.tree.map(lambda total, term: total + term, carry, param_back)
        return (carry, (result.astype(jnp.bfloat16), block_back.astype(jnp.bfloat16)))
    zeros = jax.tree.map(jnp.zeros_like, params)
    totals, (results, backs) = lax.scan(step, zeros, (blocks, firsts, cotangents))
    shape = (MICRO, PACKS, SEQ_LEN, D)
    return (results.reshape(shape), backs.reshape(shape), totals[0], totals[1], totals[2], totals[3], totals[4], totals[5], totals[6], totals[7], totals[8], totals[9], totals[10], totals[11], totals[12])
```

```python
import math

import jax
import jax.numpy as jnp
from jax import lax
from jax.sharding import PartitionSpec as P

HEADS = 8
AXES = ("batch", "seq")

NEGATIVE = -1e30


def layer_norm(rows, gain, shift):
    center = rows - jnp.mean(rows, axis=-1, keepdims=True)
    variance = jnp.mean(center * center, axis=-1, keepdims=True)
    return center * lax.rsqrt(variance + 1e-05) * gain + shift


def smooth(values):
    return jax.nn.gelu(values, approximate=True)


def contract_rows(left, right):
    return lax.dot_general(
        left, right, (((0,), (0,)), ((), ())), preferred_element_type=jnp.float32
    )


def times_transposed(left, right):
    return lax.dot_general(
        left, right, (((1,), (1,)), ((), ())), preferred_element_type=jnp.float32
    )


def column_sums(values):
    return jnp.sum(values.astype(jnp.float32), axis=0)


class Links:
    def __init__(self):
        self.count = lax.axis_size(AXES)
        self.bits = self.count.bit_length() - 1
        assert self.count == 1 << self.bits
        self.me = lax.axis_index(AXES)

    def orders(self):
        if self.bits == 5:
            return ((4, 3, 2, 1, 0), (4, 1, 3, 2, 0), (4, 2, 1, 3, 0))
        return (tuple(range(self.bits - 1, -1, -1)),) * 3

    def bit(self, place):
        return (self.me >> place) & 1

    def swap(self, value, mask):
        return lax.ppermute(value, AXES, [(d, d ^ mask) for d in range(self.count)])

    def gather(self, shard, order):
        chunks, rows, columns = shard.shape
        have = []
        for place in order:
            other = self.swap(shard, 1 << place)
            upper = self.bit(place) == 1
            low = jnp.where(upper, other, shard)
            high = jnp.where(upper, shard, other)
            shard = jnp.stack([low, high], axis=1 + sum(1 for h in have if h > place))
            have.append(place)
        return shard.reshape(chunks, self.count * rows, columns)

    def scatter(self, terms, order):
        chunks, total, columns = terms.shape
        rows = total // self.count
        terms = terms.reshape((chunks,) + (2,) * self.bits + (rows, columns))
        left = list(range(self.bits - 1, -1, -1))
        for place in reversed(order):
            axis = 1 + left.index(place)
            left.remove(place)
            mine = self.bit(place)
            keep = lax.dynamic_index_in_dim(terms, mine, axis, keepdims=False)
            send = lax.dynamic_index_in_dim(terms, 1 - mine, axis, keepdims=False)
            other = self.swap(send, 1 << place)
            terms = keep.astype(jnp.float32) + other.astype(jnp.float32)
            if left:
                terms = terms.astype(jnp.bfloat16)
        return terms

    def total(self, values):
        for place in range(self.bits):
            values = values + self.swap(values, 1 << place)
        return values


class Packs:
    def __init__(self, micro_count):
        self.size = lax.axis_size("seq")
        self.rank = lax.axis_index("seq")
        self.share = max(self.size // micro_count, 1)
        assert micro_count * self.share == self.size

    def swap(self, value, mask):
        return lax.ppermute(value, "seq", [(d, d ^ mask) for d in range(self.size)])

    def pick(self, blocks, index):
        return lax.dynamic_index_in_dim(blocks, index, 0, keepdims=False)

    def collect(self, blocks):
        rows, width = blocks.shape[1:]
        whole = jnp.zeros((self.size * rows, width), blocks.dtype)
        for mask in range(self.size):
            piece = self.pick(blocks, (self.rank ^ mask) // self.share)
            if mask:
                piece = self.swap(piece, mask)
            whole = lax.dynamic_update_slice_in_dim(whole, piece, (self.rank ^ mask) * rows, 0)
        return whole

    def spread(self, whole, micro_count):
        rows = whole.shape[0] // self.size
        blocks = jnp.zeros((micro_count, rows, whole.shape[1]), whole.dtype)
        for mask in range(self.size):
            piece = lax.dynamic_slice_in_dim(whole, (self.rank ^ mask) * rows, rows, 0)
            if mask:
                piece = self.swap(piece, mask)
            blocks = lax.dynamic_update_slice_in_dim(
                blocks, piece[None], (self.rank ^ mask) // self.share, 0
            )
        return blocks


def own_places(lengths, owner, count):
    places = []
    start = 0
    for length in lengths:
        places.append(start + owner * (length // count) + jnp.arange(length // count))
        start += length
    return jnp.concatenate(places), start


def local(
    tokens,
    first_length,
    cotangent,
    positions,
    inward,
    intake,
    outward,
    outlet,
    steady,
    offset,
    expand,
    spread,
    contract,
    settle,
    temper,
    anchor,
):
    micro_count, pack_count, block_rows, width = tokens.shape
    assert pack_count == 1
    links = Links()
    packs = Packs(micro_count)
    devices = links.count
    total_rows = block_rows * packs.size
    heads = HEADS
    head_width = width // heads
    scale = 1.0 / math.sqrt(head_width)
    order_a, order_b, order_c = links.orders()
    micro = packs.rank // packs.share
    counted = packs.rank % packs.share == 0

    small = (intake, outlet, steady, offset, spread, settle, temper, anchor)
    lengths = [v.shape[0] * devices for v in small]
    places, small_total = own_places(lengths, links.me, devices)
    own_small = jnp.concatenate(small).astype(jnp.float32)
    spots = lax.broadcasted_iota(jnp.int32, (small_total, own_small.shape[0]), 0)
    smalls = jnp.sum(jnp.where(spots == places[None, :], own_small[None, :], 0.0), axis=1)
    smalls = smalls.reshape(small_total // width, width).astype(jnp.bfloat16)
    smalls = links.total(smalls).astype(jnp.float32)

    first = jnp.sum(jnp.where(jnp.arange(micro_count) == micro, first_length[:, 0], 0))
    rows_in = packs.collect(tokens[:, 0])
    own_rows = width // devices
    table_shard = positions.T.reshape(own_rows, total_rows // width, width).transpose(1, 0, 2)
    inward_shard = inward.reshape(own_rows, 3, width).transpose(1, 0, 2)
    expand_parts = expand.shape[1] // width
    expand_shard = expand.reshape(own_rows, expand_parts, width).transpose(1, 0, 2)
    table_t = links.gather(table_shard, order_a)
    inward_all = links.gather(inward_shard, order_b)
    outward_all = links.gather(outward[None], order_a)[0]
    expand_all = links.gather(expand_shard, order_b)
    contract_all = links.gather(contract[None], order_c)[0]
    upstream = packs.collect(cotangent[:, 0]).astype(jnp.float32)

    table = table_t.transpose(0, 2, 1).reshape(total_rows, width)
    inward_full = inward_all.transpose(1, 0, 2).reshape(width, 3 * width)
    expand_full = expand_all.transpose(1, 0, 2).reshape(width, expand.shape[1])
    flat = smalls.reshape(-1)
    cuts = []
    start = 0
    for length in lengths:
        cuts.append(flat[start : start + length])
        start += length
    intake_f, outlet_f, steady_f, offset_f, spread_f, settle_f, temper_f, anchor_f = cuts

    row = jnp.arange(total_rows)
    later = row >= first
    place = row - jnp.where(later, first, 0)
    lifted = rows_in.astype(jnp.float32) + table[place].astype(jnp.float32)
    lifted_low = lifted.astype(jnp.bfloat16)
    joint = jnp.dot(lifted_low, inward_full, preferred_element_type=jnp.float32)
    queries = (joint[:, :width] + intake_f[:width]).astype(jnp.bfloat16)
    keys = joint[:, width : 2 * width].astype(jnp.bfloat16)
    values = (joint[:, 2 * width :] + intake_f[width:]).astype(jnp.bfloat16)
    qh = queries.reshape(total_rows, heads, head_width)
    kh = keys.reshape(total_rows, heads, head_width)
    vh = values.reshape(total_rows, heads, head_width)
    allowed = (row[None, :] <= row[:, None]) & (later[None, :] == later[:, None])
    allowed = allowed[None]
    logits = jnp.einsum("qhd,khd->hqk", qh, kh, preferred_element_type=jnp.float32) * scale
    logits = jnp.where(allowed, logits, NEGATIVE)
    peak = jnp.max(logits, axis=-1, keepdims=True)
    raised = jnp.where(allowed, jnp.exp(logits - peak), 0.0)
    share = raised / jnp.sum(raised, axis=-1, keepdims=True)
    share_low = share.astype(jnp.bfloat16)
    mixed = jnp.einsum("hqk,khd->qhd", share_low, vh, preferred_element_type=jnp.float32)
    mixed_low = mixed.reshape(total_rows, width).astype(jnp.bfloat16)
    branch = jnp.dot(mixed_low, outward_all, preferred_element_type=jnp.float32) + outlet_f
    normed, first_pull = jax.vjp(layer_norm, lifted + branch, steady_f, offset_f)
    normed_low = normed.astype(jnp.bfloat16)
    hidden = jnp.dot(normed_low, expand_full, preferred_element_type=jnp.float32) + spread_f
    active_low = smooth(hidden).astype(jnp.bfloat16)
    lowered = jnp.dot(active_low, contract_all, preferred_element_type=jnp.float32) + settle_f
    result, final_pull = jax.vjp(layer_norm, normed + lowered, temper_f, anchor_f)
    output = packs.spread(result.astype(jnp.bfloat16), micro_count)

    second_back, temper_grad, anchor_grad = final_pull(upstream)
    lowered_back = second_back.astype(jnp.bfloat16)
    settle_grad = column_sums(lowered_back)
    contract_grad = contract_rows(active_low, lowered_back)
    active_back = times_transposed(lowered_back, contract_all)
    hidden_back = jax.vjp(smooth, hidden)[1](active_back)[0].astype(jnp.bfloat16)
    spread_grad = column_sums(hidden_back)
    expand_grad = contract_rows(normed_low, hidden_back)
    normed_back = times_transposed(hidden_back, expand_full) + second_back
    first_back, steady_grad, offset_grad = first_pull(normed_back)
    branch_back = first_back.astype(jnp.bfloat16)
    outlet_grad = column_sums(branch_back)
    outward_grad = contract_rows(mixed_low, branch_back)
    mixed_back = times_transposed(branch_back, outward_all).astype(jnp.bfloat16)
    mbh = mixed_back.reshape(total_rows, heads, head_width)
    between = jnp.sum(mbh.astype(jnp.float32) * mixed, axis=-1).T
    share_back = jnp.einsum("qhd,khd->hqk", mbh, vh, preferred_element_type=jnp.float32)
    score_back = (scale * share * (share_back - between[..., None])).astype(jnp.bfloat16)
    query_back = jnp.einsum("hqk,khd->qhd", score_back, kh, preferred_element_type=jnp.float32)
    key_back = jnp.einsum("hqk,qhd->khd", score_back, qh, preferred_element_type=jnp.float32)
    value_back = jnp.einsum("hqk,qhd->khd", share_low, mbh, preferred_element_type=jnp.float32)
    joint_back = jnp.concatenate(
        [t.reshape(total_rows, width) for t in (query_back, key_back, value_back)], axis=1
    ).astype(jnp.bfloat16)
    inward_grad = contract_rows(lifted_low, joint_back)
    joint_sums = column_sums(joint_back)
    lifted_back = times_transposed(joint_back, inward_full) + first_back
    tokens_back = packs.spread(lifted_back.astype(jnp.bfloat16), micro_count)
    half = total_rows // 2
    split = first < total_rows
    early = lifted_back[:half] + jnp.where(split, lifted_back[half:], 0.0)
    late = jnp.where(split, 0.0, lifted_back[half:])
    table_grad = jnp.concatenate([early, late], axis=0)

    def send(terms):
        return jnp.where(counted, terms, 0.0).astype(jnp.bfloat16)

    contract_own = links.scatter(send(contract_grad)[None], order_c)[0]
    expand_own = links.scatter(
        send(expand_grad).reshape(width, expand_parts, width).transpose(1, 0, 2), order_b
    )
    outward_own = links.scatter(send(outward_grad)[None], order_a)[0]
    inward_own = links.scatter(
        send(inward_grad).reshape(width, 3, width).transpose(1, 0, 2), order_b
    )
    table_own = links.scatter(
        send(table_grad.T).reshape(width, total_rows // width, width).transpose(1, 0, 2), order_a
    )
    small_grads = jnp.concatenate(
        [
            joint_sums[:width],
            joint_sums[2 * width :],
            outlet_grad,
            steady_grad,
            offset_grad,
            spread_grad,
            settle_grad,
            temper_grad,
            anchor_grad,
        ]
    )
    small_grads = links.total(jnp.where(counted, small_grads, 0.0))
    small_own = jnp.sum(jnp.where(spots == places[None, :], small_grads[:, None], 0.0), axis=0)
    cuts = []
    start = 0
    for length in lengths:
        cuts.append(small_own[start : start + length // devices])
        start += length // devices
    intake_o, outlet_o, steady_o, offset_o, spread_o, settle_o, temper_o, anchor_o = cuts
    return (
        output[:, None],
        tokens_back[:, None],
        table_own.transpose(1, 0, 2).reshape(own_rows, total_rows).T,
        inward_own.transpose(1, 0, 2).reshape(own_rows, 3 * width),
        intake_o,
        outward_own,
        outlet_o,
        steady_o,
        offset_o,
        expand_own.transpose(1, 0, 2).reshape(own_rows, expand.shape[1]),
        spread_o,
        contract_own,
        settle_o,
        temper_o,
        anchor_o,
    )


def solution(mesh):
    rows = P(None, "batch", "seq", None)
    table = P(None, AXES)
    matrix = P(AXES, None)
    vector = P(AXES)
    weights = (
        table,
        matrix,
        vector,
        matrix,
        vector,
        vector,
        vector,
        matrix,
        vector,
        matrix,
        vector,
        vector,
        vector,
    )
    return jax.shard_map(
        local,
        mesh=mesh,
        in_specs=(rows, P(None, "batch"), rows) + weights,
        out_specs=(rows, rows) + weights,
        check_vma=False,
    )
```

```python
import functools

import jax
import jax.numpy as jnp
from jax import lax
from jax.experimental import pallas as pl
from jax.experimental.pallas import tpu as pltpu
from jax.sharding import PartitionSpec as P

AXES = ("batch", "seq")
LANE = 128
TILE = 16
STEP = 256
FAR = 1e30
BEND = 0.7978845608028654
BF = jnp.bfloat16
F32 = jnp.float32
VECTORS = 8


def times(left, right):
    return jnp.dot(left, right, preferred_element_type=F32)


def times_t(left, right):
    return lax.dot_general(left, right, (((1,), (1,)), ((), ())), preferred_element_type=F32)


def t_times(left, right):
    return lax.dot_general(left, right, (((0,), (0,)), ((), ())), preferred_element_type=F32)


def column_sum(values):
    return jnp.sum(values.astype(F32), axis=0, keepdims=True)


def aligned(index, size):
    return pl.ds(pl.multiple_of(index * size, size), size)


def like(shape, kind):
    return jax.ShapeDtypeStruct(shape, kind)


def full(shape):
    return pl.BlockSpec(shape, lambda *_: (0,) * len(shape))


def params(megabytes):
    return pltpu.CompilerParams(vmem_limit_bytes=megabytes * 2**20)


def cost(flops, size, exps=0):
    return pl.CostEstimate(flops=flops, bytes_accessed=size, transcendentals=exps)


class Plan:
    def __init__(self, devices, width, hidden, total_rows):
        self.devices = devices
        self.width = width
        self.hidden = hidden
        self.total_rows = total_rows
        self.own_rows = width // devices
        self.packed = devices == 32 and self.own_rows % TILE == 0
        self.lanes = width // LANE
        self.parts = hidden // width
        self.table_pieces = total_rows // LANE
        self.early_pieces = self.table_pieces + 3 * self.lanes
        self.early_rows = (self.early_pieces + 1) * TILE
        self.late_rows = (self.lanes + hidden // LANE) * TILE + self.lanes * (hidden // devices)
        lengths = [2 * width, width, width, width, hidden, width, width, width]
        self.lengths = lengths
        self.owned = [n // devices for n in lengths]
        self.small_rows = 16
        starts = [0]
        for n in lengths:
            starts.append(starts[-1] + n // LANE)
        self.block_starts = starts

    def place(self, mask):
        return ((mask >> 1) & 3) * 4 + ((mask >> 3) & 3)


def fill_early(plan, me, halves, table_ref, inward_ref, small_ref, stage_ref):
    for mask in range(plan.devices):
        shard = halves[mask & 1].at[plan.place(mask)]
        owner = me ^ mask
        rows = aligned(owner, TILE)
        for piece in range(plan.table_pieces):
            table_ref[piece, rows, :] = shard[piece * TILE : (piece + 1) * TILE, :]
        for piece in range(3 * plan.lanes):
            at = plan.table_pieces + piece
            inward_ref[piece, rows, :] = shard[at * TILE : (at + 1) * TILE, :]
        at = plan.early_pieces * TILE
        stage_ref[pl.ds(owner, 1), :, :] = shard[at : at + TILE, :].astype(F32)[None]
    for vector, length in enumerate(plan.lengths):
        group = LANE // plan.owned[vector]
        for block in range(length // LANE):
            row = jnp.sum(stage_ref[block * group : (block + 1) * group, vector, :], axis=0, keepdims=True)
            at = plan.block_starts[vector] + block
            small_ref[at // plan.lanes : at // plan.lanes + 1, (at % plan.lanes) * LANE : (at % plan.lanes + 1) * LANE] = row


def own_lanes(value, head):
    lane = lax.broadcasted_iota(jnp.int32, value.shape, 1)
    return jnp.where((lane // (LANE // 2)) == head, value, jnp.zeros_like(value))


def causal():
    return lax.broadcasted_iota(jnp.int32, (STEP, STEP), 0) <= lax.broadcasted_iota(
        jnp.int32, (STEP, STEP), 1
    )


def attend_kernel(plan, count, info_ref, *refs):
    pieces, refs = refs[:count], refs[count:]
    if plan.packed:
        halves, refs = refs[:2], refs[2:]
    else:
        table_in, inward_in, small_in = refs[:3]
        refs = refs[3:]
    (lifted_ref, query_ref, key_ref, value_ref, mixed_ref, total_ref, inward_ref, small_ref) = refs[:8]
    low_ref, table_ref, place_ref, stage_ref = refs[8:]
    pair = pl.program_id(0)
    total_rows, width = plan.total_rows, plan.width
    half = total_rows // 2
    split = info_ref[0] < total_rows
    far = jnp.where(split, FAR, 0.0)

    @pl.when(pair == 0)
    def _():
        if plan.packed:
            fill_early(plan, info_ref[1], halves, table_ref, inward_ref, small_ref, stage_ref)
        else:
            table_ref[...] = table_in[...]
            inward_ref[...] = inward_in[...]
            small_ref[...] = small_in[...]
        eye = (
            lax.broadcasted_iota(jnp.int32, (half, half), 0)
            == lax.broadcasted_iota(jnp.int32, (half, half), 1)
        ).astype(BF)
        per_half = half // LANE
        for part in range(2):
            table = jnp.concatenate(
                [table_ref[part * per_half + i] for i in range(per_half)], axis=1
            )
            place_ref[part * half : (part + 1) * half, :] = times_t(eye, table)
        rows = total_rows // count
        for mask in range(count):
            start = (info_ref[2] ^ mask) * rows
            place = start - jnp.where(jnp.logical_and(split, start >= half), half, 0)
            lifted = pieces[mask][...].astype(F32) + place_ref[pl.ds(pl.multiple_of(place, rows), rows), :]
            spot = pl.ds(pl.multiple_of(start, rows), rows)
            lifted_ref[spot, :] = lifted
            low_ref[spot, :] = lifted.astype(BF)

    weights = jnp.concatenate([inward_ref[pair + i * plan.lanes] for i in range(3)], axis=1)
    lanes = aligned(pair, LANE)
    query_bias = small_ref[0:1, lanes]
    value_bias = small_ref[1:2, lanes]
    for block in range(total_rows // STEP):
        spot = slice(block * STEP, (block + 1) * STEP)
        joint = times(low_ref[spot, :], weights)
        query_ref[spot, :] = (joint[:, :LANE] + query_bias).astype(BF) * BF(0.125)
        key_ref[spot, :] = joint[:, LANE : 2 * LANE].astype(BF)
        value_ref[spot, :] = (joint[:, 2 * LANE :] + value_bias).astype(BF)

    keep = causal()
    lower = lax.broadcasted_iota(jnp.int32, (LANE, STEP), 0) < LANE // 2
    for block in range(total_rows // STEP):
        spot = slice(block * STEP, (block + 1) * STEP)
        start = block * STEP
        other = half if start >= half else 0
        query = query_ref[spot, :]
        parts = []
        for head in range(2):
            mine = own_lanes(query, head)
            near = times_t(key_ref[start : start + STEP, :], mine)
            near = jnp.where(keep, near, -FAR)
            peak = jnp.max(near, axis=0, keepdims=True)
            logits = [near]
            if start > other:
                same = times_t(key_ref[other:start, :], mine)
                peak = jnp.maximum(peak, jnp.max(same, axis=0, keepdims=True))
                logits.insert(0, same)
            if other:
                away = times_t(key_ref[:other, :], mine)
                peak = jnp.maximum(peak, jnp.max(away, axis=0, keepdims=True) - far)
            raised = [jnp.exp(piece - peak) for piece in logits]
            total = sum(jnp.sum(piece, axis=0, keepdims=True) for piece in raised)
            low = jnp.concatenate([piece.astype(BF) for piece in raised], axis=0)
            mixed = t_times(value_ref[other : start + STEP, :], low)
            if other:
                away = jnp.exp(away - (peak + far))
                total = total + jnp.sum(away, axis=0, keepdims=True)
                mixed = mixed + t_times(value_ref[:other, :], away.astype(BF))
            parts.append(mixed * (1.0 / total))
            total_ref[0, head : head + 1, spot] = peak + jnp.log(total)
        mixed_ref[spot, :] = jnp.where(lower, parts[0], parts[1]).T.astype(BF)


def attend(plan, info, pieces, weights):
    total_rows, width = plan.total_rows, plan.width
    block = pl.BlockSpec((total_rows, LANE), lambda p, *_: (0, p))
    low = like((total_rows, width), BF)
    inward = (3 * plan.lanes, width, LANE)
    small = (plan.small_rows, width)
    return pl.pallas_call(
        functools.partial(attend_kernel, plan, len(pieces)),
        grid_spec=pltpu.PrefetchScalarGridSpec(
            num_scalar_prefetch=1,
            grid=(plan.lanes,),
            in_specs=[full(v.shape) for v in pieces + weights],
            out_specs=[
                full((total_rows, width)),
                block,
                block,
                block,
                block,
                pl.BlockSpec((1, 8, total_rows), lambda p, *_: (p, 0, 0)),
                full(inward),
                full(small),
            ],
            scratch_shapes=[
                pltpu.VMEM((total_rows, width), BF),
                pltpu.VMEM((plan.table_pieces, width, LANE), BF),
                pltpu.VMEM((total_rows, width), F32),
                pltpu.VMEM((plan.devices, TILE, LANE), F32),
            ],
        ),
        out_shape=[
            like((total_rows, width), F32),
            low,
            low,
            low,
            low,
            like((plan.lanes, 8, total_rows), F32),
            like(inward, BF),
            like(small, F32),
        ],
        compiler_params=params(48),
        cost_estimate=cost(5 * 10**9, 14 * 2**20, 6 * 10**6),
        name="attend",
    )(info, *pieces, *weights)


def norm(rows):
    center = rows - jnp.mean(rows, axis=1, keepdims=True)
    root = lax.rsqrt(jnp.mean(center * center, axis=1, keepdims=True) + 1e-05)
    return center * root, root


def norm_back(upstream, gain, unit, root):
    scaled = upstream * gain
    mean = jnp.mean(scaled, axis=1, keepdims=True)
    slope = jnp.mean(scaled * unit, axis=1, keepdims=True)
    return (scaled - mean - unit * slope) * root


def feed_kernel(plan, count, info_ref, lifted_ref, mixed_ref, *refs):
    upstreams, refs = refs[:count], refs[count:]
    if plan.packed:
        late_in, small_ref = refs[:2]
        refs = refs[2:]
    else:
        outward_in, expand_in, contract_in, small_ref = refs[:4]
        refs = refs[4:]
    results, refs = refs[:count], refs[count:]
    mixed_back_ref, first_back_ref, small_grad_ref = refs[:3]
    refs = refs[3:]
    if plan.packed:
        halves, refs = refs[:2], refs[2:]
    else:
        outward_out, expand_out, contract_out = refs[:3]
        refs = refs[3:]
    (outward_ref, expand_ref, contract_ref, upstream_ref, active_ref, slope_ref,
     outward_sum, expand_sum, contract_sum) = refs
    step = pl.program_id(0)
    width, parts, lanes = plan.width, plan.parts, plan.lanes
    contract_own = plan.hidden // plan.devices
    contract_at = (lanes + parts * lanes) * TILE

    @pl.when(step == 0)
    def _():
        if plan.packed:
            for device in range(plan.devices):
                rows = slice(device * TILE, (device + 1) * TILE)
                shard = late_in.at[device]
                for lane in range(lanes):
                    cut = slice(lane * LANE, (lane + 1) * LANE)
                    outward_ref[rows, cut] = shard[lane * TILE : (lane + 1) * TILE, :]
                    for part in range(parts):
                        at = (lanes + part * lanes + lane) * TILE
                        expand_ref[part, rows, cut] = shard[at : at + TILE, :]
                    at = contract_at + lane * contract_own
                    contract_ref[device * contract_own : (device + 1) * contract_own, cut] = shard[at : at + contract_own, :]
        else:
            outward_ref[...] = outward_in[...]
            expand_ref[...] = expand_in[...]
            contract_ref[...] = contract_in[...]

    for mask in range(count):
        @pl.when(step == mask)
        def _(mask=mask):
            upstream_ref[...] = upstreams[mask][...]

    outlet, steady, offset = (small_ref[i : i + 1, :] for i in (2, 3, 4))
    settle, temper, anchor = (small_ref[i + parts : i + parts + 1, :] for i in (5, 6, 7))
    mixed = mixed_ref[...]
    branch = times(mixed, outward_ref[...]) + outlet
    unit, root = norm(lifted_ref[...] + branch)
    normed = unit * steady + offset
    normed_low = normed.astype(BF)
    lowered = jnp.zeros_like(normed)
    for part in range(parts):
        cut = slice(part * width, (part + 1) * width)
        hidden = times(normed_low, expand_ref[part]) + small_ref[5 + part : 6 + part, :]
        square = hidden * hidden
        bend = jnp.tanh(hidden * (BEND + BEND * 0.044715 * square))
        half = 0.5 + 0.5 * bend
        active = (hidden * half).astype(BF)
        active_ref[:, cut] = active
        slope_ref[:, cut] = half + (0.5 * hidden) * (1.0 - bend * bend) * (
            BEND + 3 * BEND * 0.044715 * square
        )
        lowered = lowered + times(active, contract_ref[cut, :])
    last_unit, last_root = norm(normed + (lowered + settle))
    result = (last_unit * temper + anchor).astype(BF)
    for mask in range(count):
        @pl.when(step == mask)
        def _(mask=mask):
            results[mask][...] = result

    upstream = upstream_ref[...].astype(F32)
    temper_grad = column_sum(upstream * last_unit)
    anchor_grad = column_sum(upstream)
    second_back = norm_back(upstream, temper, last_unit, last_root)
    lowered_back = second_back.astype(BF)
    settle_grad = column_sum(lowered_back)
    normed_back = second_back
    spread_grads = []
    contract_terms = []
    expand_terms = []
    for part in range(parts):
        cut = slice(part * width, (part + 1) * width)
        contract_terms.append(t_times(active_ref[:, cut], lowered_back))
        active_back = times_t(lowered_back, contract_ref[cut, :])
        hidden_back = (active_back * slope_ref[:, cut]).astype(BF)
        spread_grads.append(column_sum(hidden_back))
        expand_terms.append(t_times(normed_low, hidden_back))
        normed_back = normed_back + times_t(hidden_back, expand_ref[part])
    first_back = norm_back(normed_back, steady, unit, root)
    first_back_ref[...] = first_back
    branch_back = first_back.astype(BF)
    mixed_back_ref[...] = times_t(branch_back, outward_ref[...]).astype(BF)
    outward_term = t_times(mixed, branch_back)
    zero = jnp.zeros_like(anchor_grad)
    grads = [zero, zero, column_sum(branch_back), column_sum(normed_back * unit)]
    grads += [column_sum(normed_back)] + spread_grads + [settle_grad, temper_grad, anchor_grad]
    grads += [zero] * (plan.small_rows - len(grads))
    small_term = jnp.concatenate(grads, axis=0)

    @pl.when(step == 0)
    def _():
        small_grad_ref[...] = small_term
        outward_sum[...] = outward_term
        for part in range(parts):
            expand_sum[part] = expand_terms[part]
            contract_sum[part * width : (part + 1) * width, :] = contract_terms[part]

    @pl.when(step > 0)
    def _():
        small_grad_ref[...] += small_term
        outward_sum[...] += outward_term
        for part in range(parts):
            expand_sum[part] += expand_terms[part]
            contract_sum[part * width : (part + 1) * width, :] += contract_terms[part]

    @pl.when(step == count - 1)
    def _():
        if plan.packed:
            for mask in range(plan.devices):
                shard = halves[mask & 1].at[plan.place(mask)]
                owner = info_ref[1] ^ mask
                rows = aligned(owner, TILE)
                wide = aligned(owner, contract_own)
                for lane in range(lanes):
                    cut = slice(lane * LANE, (lane + 1) * LANE)
                    shard[lane * TILE : (lane + 1) * TILE, :] = outward_sum[rows, cut].astype(BF)
                    for part in range(parts):
                        at = (lanes + part * lanes + lane) * TILE
                        shard[at : at + TILE, :] = expand_sum[part, rows, cut].astype(BF)
                    at = contract_at + lane * contract_own
                    shard[at : at + contract_own, :] = contract_sum[wide, cut].astype(BF)
        else:
            outward_out[...] = outward_sum[...].astype(BF)
            expand_out[...] = expand_sum[...].astype(BF)
            contract_out[...] = contract_sum[...].astype(BF)


def feed(plan, info, lifted, mixed, upstreams, weights, small):
    total_rows, width, parts = plan.total_rows, plan.width, plan.parts
    count = len(upstreams)
    size = total_rows // count
    rows = pl.BlockSpec((size, width), lambda i, info: (info[2] ^ i, 0))
    outward, expand, contract = (width, width), (parts, width, width), (parts * width, width)
    if plan.packed:
        grads = [like((plan.devices // 2, plan.late_rows, LANE), BF)] * 2
    else:
        grads = [like(outward, BF), like(expand, BF), like(contract, BF)]
    ends = [like((size, width), BF)] * count
    outs = [like((total_rows, width), BF), like((total_rows, width), F32), like(small.shape, F32)]
    values = pl.pallas_call(
        functools.partial(feed_kernel, plan, count),
        grid_spec=pltpu.PrefetchScalarGridSpec(
            num_scalar_prefetch=1,
            grid=(count,),
            in_specs=[rows, rows] + [full(v.shape) for v in upstreams + weights + [small]],
            out_specs=[full(v.shape) for v in ends]
            + [rows, rows, full(small.shape)]
            + [full(v.shape) for v in grads],
            scratch_shapes=[
                pltpu.VMEM(outward, BF),
                pltpu.VMEM(expand, BF),
                pltpu.VMEM(contract, BF),
                pltpu.VMEM((size, width), BF),
                pltpu.VMEM((size, parts * width), BF),
                pltpu.VMEM((size, parts * width), F32),
                pltpu.VMEM(outward, F32),
                pltpu.VMEM(expand, F32),
                pltpu.VMEM(contract, F32),
            ],
        ),
        out_shape=ends + outs + grads,
        compiler_params=params(60),
        cost_estimate=cost(15 * 10**9, 20 * 2**20, 2 * 10**6),
        name="feed",
    )(info, lifted, mixed, *upstreams, *weights, small)
    return values[:count], values[count : count + 3], values[count + 3 :]


def attend_back_kernel(
    plan, count, info_ref, lifted_ref, query_ref, key_ref, value_ref, mixed_ref, mixed_back_ref,
    total_ref, inward_ref, first_back_ref, small_grad_ref, *refs
):
    tokens, refs = refs[:count], refs[count:]
    if plan.packed:
        halves, refs = refs[:2], refs[2:]
    else:
        table_out, inward_out, small_out = refs[:3]
        refs = refs[3:]
    low_ref, sum_ref, share_ref, score_ref, grad_ref, table_ref, joint_sums, blocks_ref = refs
    pair = pl.program_id(0)
    total_rows, lanes = plan.total_rows, plan.lanes
    half = total_rows // 2
    split = info_ref[0] < total_rows
    far = jnp.where(split, FAR, 0.0)
    blocks = total_rows // STEP

    @pl.when(pair == 0)
    def _():
        low_ref[...] = lifted_ref[...].astype(BF)

    keep = causal()
    lower = lax.broadcasted_iota(jnp.int32, (STEP, LANE), 1) < LANE // 2
    lower_t = lax.broadcasted_iota(jnp.int32, (LANE, STEP), 0) < LANE // 2
    query_parts, key_parts, value_parts = [], [], []
    product = (mixed_ref[...].astype(F32) * mixed_back_ref[...].astype(F32)).T
    scaled_key = key_ref[...] * BF(0.125)
    for head in range(2):
        between = jnp.sum(
            product[head * LANE // 2 : (head + 1) * LANE // 2], axis=0, keepdims=True
        )
        for block in range(blocks):
            start = block * STEP
            spot = slice(start, start + STEP)
            query = own_lanes(query_ref[spot, :], head)
            back = own_lanes(mixed_back_ref[spot, :], head)
            total = total_ref[0, head : head + 1, spot]
            gap = between[:, spot]
            for under in range(block + 1):
                keys = slice(under * STEP, (under + 1) * STEP)
                away = start >= half and under * STEP < half
                logits = times_t(key_ref[keys, :], query)
                share = jnp.exp(logits - (total + far if away else total))
                if under == block:
                    share = jnp.where(keep, share, 0.0)
                share_back = times_t(value_ref[keys, :], back)
                score = share * (share_back - gap)
                share_ref[head, keys, spot] = share.astype(BF)
                score_ref[head, keys, spot] = score.astype(BF)
        queries, keys_, values = [], [], []
        for block in range(blocks):
            start = block * STEP
            spot = slice(start, start + STEP)
            end = start + STEP
            queries.append(t_times(scaled_key[:end], score_ref[head, :end, spot]))
            keys_.append(times(score_ref[head, spot, start:], query_ref[start:, :]))
            values.append(times(share_ref[head, spot, start:], mixed_back_ref[start:, :]))
        query_parts.append(queries)
        key_parts.append(keys_)
        value_parts.append(values)
    weights = jnp.concatenate([inward_ref[pair + i * lanes] for i in range(3)], axis=1)
    joints = []
    for block in range(blocks):
        spot = slice(block * STEP, (block + 1) * STEP)
        query_back = jnp.where(lower_t, query_parts[0][block], query_parts[1][block]).T
        key_back = jnp.where(lower, key_parts[0][block], key_parts[1][block])
        value_back = jnp.where(lower, value_parts[0][block], value_parts[1][block])
        joint = jnp.concatenate([query_back, key_back, value_back], axis=1).astype(BF)
        joints.append(joint)
        term = times_t(joint, weights)

        @pl.when(pair == 0)
        def _():
            sum_ref[spot, :] = term + first_back_ref[spot, :]

        @pl.when(pair > 0)
        def _():
            sum_ref[spot, :] += term

    joint = jnp.concatenate(joints, axis=0)
    grads = t_times(low_ref[...], joint)
    for part in range(3):
        grad_ref[pair + part * lanes] = grads[:, part * LANE : (part + 1) * LANE]
    sums = column_sum(joint)
    joint_sums[pl.ds(pair, 1), :] = sums[:, :LANE]
    joint_sums[pl.ds(pair + lanes, 1), :] = sums[:, 2 * LANE :]

    @pl.when(pair == lanes - 1)
    def _():
        rows = total_rows // count
        for mask in range(count):
            spot = pl.ds(pl.multiple_of((info_ref[2] ^ mask) * rows, rows), rows)
            tokens[mask][...] = sum_ref[spot, :].astype(BF)
        late = sum_ref[half:, :]
        early = sum_ref[:half, :] + jnp.where(split, late, 0.0)
        table_ref[:, :half] = early.T
        table_ref[:, half:] = jnp.where(split, 0.0, late).T
        counted = info_ref[3] > 0
        blocks_ref[: 2 * lanes, :] = joint_sums[: 2 * lanes, :]
        for row in range(2, plan.block_starts[-1] // lanes):
            for lane in range(lanes):
                blocks_ref[row * lanes + lane : row * lanes + lane + 1, :] = small_grad_ref[
                    row : row + 1, lane * LANE : (lane + 1) * LANE
                ]
        if plan.packed:
            for mask in range(plan.devices):
                shard = halves[mask & 1].at[plan.place(mask)]
                owner = info_ref[1] ^ mask
                own = aligned(owner, TILE)
                for piece in range(plan.table_pieces):
                    shard[piece * TILE : (piece + 1) * TILE, :] = table_ref[
                        own, piece * LANE : (piece + 1) * LANE
                    ].astype(BF)
                for piece in range(3 * lanes):
                    at = (plan.table_pieces + piece) * TILE
                    shard[at : at + TILE, :] = grad_ref[piece, own, :].astype(BF)
                rows = [
                    blocks_ref[pl.ds(plan.block_starts[v] + owner * plan.owned[v] // LANE, 1), :]
                    for v in range(VECTORS)
                ]
                rows.append(jnp.zeros((TILE - VECTORS, LANE), F32))
                at = plan.early_pieces * TILE
                shard[at : at + TILE, :] = jnp.concatenate(rows, axis=0).astype(BF)
        else:
            table_out[...] = jnp.where(counted, table_ref[...], 0.0).astype(BF)
            inward_out[...] = jnp.where(counted, grad_ref[...], 0.0).astype(BF)
            small_out[...] = jnp.where(counted, blocks_ref[...], 0.0)


def attend_back(plan, info, count, lifted, saved, mixed_back, inward, first_back, small_grad):
    query, key, value, mixed, totals = saved
    total_rows, width, lanes = plan.total_rows, plan.width, plan.lanes
    block = pl.BlockSpec((total_rows, LANE), lambda p, *_: (0, p))
    blocks = (plan.block_starts[-1], LANE)
    if plan.packed:
        grads = [like((plan.devices // 2, plan.early_rows, LANE), BF)] * 2
    else:
        grads = [like((width, total_rows), BF), like(inward.shape, BF), like(blocks, F32)]
    tokens = [like((total_rows // count, width), BF)] * count
    values = pl.pallas_call(
        functools.partial(attend_back_kernel, plan, count),
        grid_spec=pltpu.PrefetchScalarGridSpec(
            num_scalar_prefetch=1,
            grid=(lanes,),
            in_specs=[
                full(lifted.shape),
                block,
                block,
                block,
                block,
                block,
                pl.BlockSpec((1, 8, total_rows), lambda p, *_: (p, 0, 0)),
                full(inward.shape),
                full(first_back.shape),
                full(small_grad.shape),
            ],
            out_specs=[full(v.shape) for v in tokens + grads],
            scratch_shapes=[
                pltpu.VMEM((total_rows, width), BF),
                pltpu.VMEM((total_rows, width), F32),
                pltpu.VMEM((2, total_rows, total_rows), BF),
                pltpu.VMEM((2, total_rows, total_rows), BF),
                pltpu.VMEM(inward.shape, F32),
                pltpu.VMEM((width, total_rows), F32),
                pltpu.VMEM((8, LANE), F32),
                pltpu.VMEM(blocks, F32),
            ],
        ),
        out_shape=tokens + grads,
        compiler_params=params(60),
        cost_estimate=cost(14 * 10**9, 24 * 2**20, 6 * 10**6),
        name="attend_back",
    )(info, lifted, query, key, value, mixed, mixed_back, totals, inward, first_back, small_grad)
    return values[:count], values[count:]


def pack_early_kernel(plan, info_ref, table_ref, inward_ref, *refs):
    vectors, out_ref = refs[:VECTORS], refs[VECTORS]
    me = info_ref[1]
    for piece in range(plan.table_pieces):
        out_ref[piece * TILE : (piece + 1) * TILE, :] = table_ref[:, piece * LANE : (piece + 1) * LANE]
    for piece in range(3 * plan.lanes):
        at = (plan.table_pieces + piece) * TILE
        out_ref[at : at + TILE, :] = inward_ref[:, piece * LANE : (piece + 1) * LANE]
    lane = lax.broadcasted_iota(jnp.int32, (1, LANE), 1)
    rows = []
    for vector, ref in zip(range(VECTORS), vectors):
        size = plan.owned[vector]
        wide = jnp.concatenate([ref[...].astype(F32)] * (LANE // size), axis=1)
        slot = lax.rem(me, LANE // size)
        rows.append(jnp.where(lane // size == slot, wide, 0.0))
    rows.append(jnp.zeros((TILE - VECTORS, LANE), F32))
    at = plan.early_pieces * TILE
    out_ref[at : at + TILE, :] = jnp.concatenate(rows, axis=0).astype(BF)


def pack_early(plan, info, table, inward, vectors):
    values = [table, inward] + [v.reshape(1, -1) for v in vectors]
    out = (plan.early_rows, LANE)
    return pl.pallas_call(
        functools.partial(pack_early_kernel, plan),
        grid_spec=pltpu.PrefetchScalarGridSpec(
            num_scalar_prefetch=1,
            grid=(1,),
            in_specs=[full(v.shape) for v in values],
            out_specs=full(out),
        ),
        out_shape=like(out, BF),
        name="pack_early",
    )(info, *values)


def pack_late_kernel(plan, outward_ref, expand_ref, contract_ref, out_ref):
    at = 0
    for ref in (outward_ref, expand_ref, contract_ref):
        rows = ref.shape[0]
        for lane in range(ref.shape[1] // LANE):
            out_ref[at : at + rows, :] = ref[:, lane * LANE : (lane + 1) * LANE]
            at += rows


def pack_late(plan, outward, expand, contract):
    return pl.pallas_call(
        functools.partial(pack_late_kernel, plan),
        out_shape=like((plan.late_rows, LANE), BF),
        name="pack_late",
    )(outward, expand, contract)


def fold_kernel(count, *refs):
    total = refs[0][...].astype(F32)
    for ref in refs[1:count]:
        total = total + ref[...].astype(F32)
    size = total.shape[0] // len(refs[count:])
    for index, ref in enumerate(refs[count:]):
        ref[...] = total[index * size : (index + 1) * size].astype(ref.dtype)


def fold(terms, cuts):
    entries, rows, _ = terms[0].shape
    pieces = 4 if rows % 64 == 0 else 3
    size = rows // pieces
    out = like((entries // cuts, rows, LANE), BF)
    return pl.pallas_call(
        functools.partial(fold_kernel, len(terms)),
        grid=(pieces,),
        in_specs=[pl.BlockSpec((entries, size, LANE), lambda i: (0, i, 0))] * len(terms),
        out_specs=[pl.BlockSpec((entries // cuts, size, LANE), lambda i: (0, i, 0))] * cuts,
        out_shape=[out] * cuts,
        cost_estimate=cost(10**6, len(terms) * entries * rows * LANE * 4),
        name="fold",
    )(*terms)


def finish_kernel(plan, count, info_ref, *refs):
    early, late, tokens = refs[:4], refs[4:8], refs[8 : 8 + count]
    (tokens_ref, table_ref, inward_ref, outward_ref, expand_ref, contract_ref) = refs[8 + count : 14 + count]
    vectors = refs[14 + count :]
    early = sum(ref[0].astype(F32) for ref in early)
    late = sum(ref[0].astype(F32) for ref in late)
    for mask in range(count):
        tokens_ref[pl.ds(info_ref[2] ^ mask, 1), :, :] = tokens[mask][...][None]
    for piece in range(plan.table_pieces):
        table_ref[:, piece * LANE : (piece + 1) * LANE] = early[piece * TILE : (piece + 1) * TILE]
    for piece in range(3 * plan.lanes):
        at = (plan.table_pieces + piece) * TILE
        inward_ref[:, piece * LANE : (piece + 1) * LANE] = early[at : at + TILE]
    at = 0
    for ref in (outward_ref, expand_ref, contract_ref):
        rows = ref.shape[0]
        for lane in range(ref.shape[1] // LANE):
            ref[:, lane * LANE : (lane + 1) * LANE] = late[at : at + rows]
            at += rows
    at = plan.early_pieces * TILE
    small = early[at : at + VECTORS]
    for vector, ref in enumerate(vectors):
        size = plan.owned[vector]
        slot = lax.rem(info_ref[1], LANE // size)
        row = pltpu.roll(small, LANE - slot * size, 1)
        ref[...] = row[vector : vector + 1, :size]


def finish(plan, info, micro_count, early, late, tokens):
    rows, width = tokens[0].shape
    own = plan.own_rows
    outs = [
        like((micro_count, rows, width), BF),
        like((own, plan.total_rows), F32),
        like((own, 3 * width), F32),
        like((own, width), F32),
        like((own, plan.hidden), F32),
        like((plan.hidden // plan.devices, width), F32),
    ] + [like((1, n), F32) for n in plan.owned]
    values = early + late + tokens
    return pl.pallas_call(
        functools.partial(finish_kernel, plan, len(tokens)),
        grid_spec=pltpu.PrefetchScalarGridSpec(
            num_scalar_prefetch=1,
            grid=(1,),
            in_specs=[full(v.shape) for v in values],
            out_specs=[full(v.shape) for v in outs],
        ),
        out_shape=outs,
        name="finish",
    )(info, *values)


def settle_kernel(count, share, info_ref, *refs):
    for mask in range(count):
        refs[count][pl.ds((info_ref[2] ^ mask) // share, 1), :, :] = refs[mask][...][None]


def settle_rows(info, micro_count, share, pieces):
    out = (micro_count,) + pieces[0].shape
    return pl.pallas_call(
        functools.partial(settle_kernel, len(pieces), share),
        grid_spec=pltpu.PrefetchScalarGridSpec(
            num_scalar_prefetch=1,
            grid=(1,),
            in_specs=[full(v.shape) for v in pieces],
            out_specs=full(out),
        ),
        out_shape=like(out, BF),
        name="settle_rows",
    )(info, *pieces)


def cut_kernel(*refs):
    refs[2][...] = refs[1][0]


def cut_rows(info, rows, count, share):
    def one(mask):
        return pl.pallas_call(
            cut_kernel,
            grid_spec=pltpu.PrefetchScalarGridSpec(
                num_scalar_prefetch=1,
                grid=(1,),
                in_specs=[
                    pl.BlockSpec((1,) + rows.shape[1:], lambda i, info: ((info[2] ^ mask) // share, 0, 0))
                ],
                out_specs=full(rows.shape[1:]),
            ),
            out_shape=like(rows.shape[1:], BF),
            name="cut_rows",
        )(info, rows)

    return [one(mask) for mask in range(count)]


def local(tokens, first_length, cotangent, positions, inward, intake, outward, outlet, steady, offset,
          expand, spread, contract, settle, temper, anchor):
    micro_count, pack_count, block_rows, width = tokens.shape
    assert pack_count == 1
    devices, count = lax.axis_size(AXES), lax.axis_size("seq")
    me, rank = lax.axis_index(AXES), lax.axis_index("seq")
    share = max(count // micro_count, 1)
    assert share * micro_count == count
    plan = Plan(devices, width, contract.shape[0] * devices, block_rows * count)
    micro = rank // share
    firsts = jnp.where(jnp.arange(micro_count) == micro, first_length[:, 0], 0)
    counted = (rank % share == 0).astype(jnp.int32)
    info = jnp.stack([jnp.sum(firsts), me, rank, counted]).astype(jnp.int32)
    vectors = (intake, outlet, steady, offset, spread, settle, temper, anchor)

    def swap(value, mask):
        return lax.ppermute(value, AXES, [(d, d ^ mask) for d in range(devices)]) if mask else value

    def exchange(pieces):
        return [swap(piece, mask) for mask, piece in enumerate(pieces)]

    rows_in = exchange(cut_rows(info, tokens[:, 0], count, share))
    upstreams = exchange(cut_rows(info, cotangent[:, 0], count, share))
    if plan.packed:
        shard = pack_early(plan, info, positions.T, inward, vectors)[None]
        late_shard = pack_late(plan, outward, expand, contract)
        shard = jnp.concatenate([swap(shard, k << 3) for k in range(4)], axis=0)
        shard = jnp.concatenate([swap(shard, k << 1) for k in range(4)], axis=0)
        early = [shard, swap(shard, 1)]
        late = lax.all_gather(late_shard, AXES, axis=0, tiled=False)
        late = [late]
    else:
        early, late = plain_weights(plan, positions, inward, vectors, outward, expand, contract)
    lifted, query, key, value, mixed, totals, inward_all, small = attend(plan, info, rows_in, early)
    results, (mixed_back, first_back, small_grad), late_grads = feed(
        plan, info, lifted, mixed, upstreams, late, small
    )
    output = settle_rows(info, micro_count, share, exchange(results))
    if plan.packed:
        keep, send = late_grads
        terms = fold([keep, swap(send, 1)], 4)
        terms = [swap(term, k << 1) for k, term in enumerate(terms)]
    token_pieces, early_grads = attend_back(
        plan, info, count, lifted, (query, key, value, mixed, totals), mixed_back, inward_all,
        first_back, small_grad,
    )
    token_pieces = exchange(token_pieces)
    if plan.packed:
        terms = fold(terms, 4)
        late_terms = [swap(term, k << 3) for k, term in enumerate(terms)]
        keep, send = early_grads
        terms = fold([keep, swap(send, 1)], 4)
        terms = fold([swap(term, k << 1) for k, term in enumerate(terms)], 4)
        early_terms = [swap(term, k << 3) for k, term in enumerate(terms)]
        values = finish(plan, info, micro_count, early_terms, late_terms, token_pieces)
        tokens_back, table_t, inward_own, outward_own, expand_own, contract_own = values[:6]
        own = [v.reshape(-1) for v in values[6:]]
        table_own = table_t.T
    else:
        tokens_back = settle_rows(info, micro_count, share, token_pieces)
        table_own, inward_own, outward_own, expand_own, contract_own, own = plain_grads(
            plan, counted, early_grads, late_grads
        )
    return (output[:, None], tokens_back[:, None], table_own, inward_own, own[0], outward_own, own[1], own[2],
            own[3], expand_own, own[4], contract_own, own[5], own[6], own[7])


def plain_weights(plan, positions, inward, vectors, outward, expand, contract):
    lanes, width = plan.lanes, plan.width

    def gather(value, axis=0):
        return lax.all_gather(value, AXES, axis=axis, tiled=True)

    def in_pieces(value, size):
        return value.reshape(value.shape[0], -1, size).transpose(1, 0, 2)

    table = in_pieces(gather(positions, 1).T, LANE)
    small = jnp.concatenate([gather(v) for v in vectors]).astype(F32).reshape(-1, width)
    small = jnp.pad(small, ((0, plan.small_rows - small.shape[0]), (0, 0)))
    early = [table, in_pieces(gather(inward), LANE), small]
    return early, [gather(outward), in_pieces(gather(expand), width), gather(contract)]


def plain_grads(plan, counted, early_grads, late_grads):
    width = plan.width
    table, inward, small = early_grads
    outward, expand, contract = (jnp.where(counted > 0, g, BF(0)) for g in late_grads)

    def scatter(value, axis=0):
        return lax.psum_scatter(value, AXES, scatter_dimension=axis, tiled=True).astype(F32)

    def whole(value):
        return value.transpose(1, 0, 2).reshape(value.shape[1], -1)

    flat = small.reshape(-1)
    own = []
    for vector, length in enumerate(plan.lengths):
        start = plan.block_starts[vector] * LANE
        own.append(scatter(flat[start : start + length]))
    return (scatter(table.T, 1), scatter(whole(inward)), scatter(outward), scatter(whole(expand)),
            scatter(contract), own)


def solution(mesh):
    rows = P(None, "batch", "seq", None)
    table = P(None, AXES)
    matrix = P(AXES, None)
    vector = P(AXES)
    weights = (table, matrix, vector, matrix, vector, vector, vector, matrix, vector, matrix, vector,
               vector, vector)
    return jax.shard_map(
        local,
        mesh=mesh,
        in_specs=(rows, P(None, "batch"), rows) + weights,
        out_specs=(rows, rows) + weights,
        check_vma=False,
    )
```

```python
import functools

import jax
import jax.numpy as jnp
from jax import lax
from jax.experimental import pallas as pl
from jax.experimental.pallas import tpu as pltpu
from jax.sharding import PartitionSpec as P

AXES = ("batch", "seq")
LANE = 128
TILE = 16
STEP = 256
FAR = 1e30
BEND = 0.7978845608028654
BF = jnp.bfloat16
F32 = jnp.float32
VECTORS = 8


def times(left, right):
    return jnp.dot(left, right, preferred_element_type=F32)


def times_t(left, right):
    return lax.dot_general(left, right, (((1,), (1,)), ((), ())), preferred_element_type=F32)


def t_times(left, right):
    return lax.dot_general(left, right, (((0,), (0,)), ((), ())), preferred_element_type=F32)


def column_sum(values):
    return jnp.sum(values.astype(F32), axis=0, keepdims=True)


def aligned(index, size):
    return pl.ds(pl.multiple_of(index * size, size), size)


def like(shape, kind):
    return jax.ShapeDtypeStruct(shape, kind)


def full(shape):
    return pl.BlockSpec(shape, lambda *_: (0,) * len(shape))


def params(megabytes):
    return pltpu.CompilerParams(vmem_limit_bytes=megabytes * 2**20)


def cost(flops, size, exps=0):
    return pl.CostEstimate(flops=flops, bytes_accessed=size, transcendentals=exps)


class Plan:
    def __init__(self, devices, width, hidden, total_rows):
        self.devices = devices
        self.width = width
        self.hidden = hidden
        self.total_rows = total_rows
        self.own_rows = width // devices
        self.packed = devices == 32 and self.own_rows % TILE == 0
        self.lanes = width // LANE
        self.parts = hidden // width
        self.table_pieces = total_rows // LANE
        self.early_pieces = self.table_pieces + 3 * self.lanes
        self.early_rows = (self.early_pieces + 1) * TILE
        self.late_rows = (self.lanes + hidden // LANE) * TILE + self.lanes * (hidden // devices)
        lengths = [2 * width, width, width, width, hidden, width, width, width]
        self.lengths = lengths
        self.owned = [n // devices for n in lengths]
        self.small_rows = 16
        starts = [0]
        for n in lengths:
            starts.append(starts[-1] + n // LANE)
        self.block_starts = starts

    def place(self, mask):
        return ((mask >> 1) & 3) * 4 + ((mask >> 3) & 3)


def fill_early(plan, me, halves, table_ref, inward_ref, small_ref, stage_ref):
    for mask in range(plan.devices):
        shard = halves[mask & 1].at[plan.place(mask)]
        owner = me ^ mask
        rows = aligned(owner, TILE)
        for piece in range(plan.table_pieces):
            table_ref[piece, rows, :] = shard[piece * TILE : (piece + 1) * TILE, :]
        for piece in range(3 * plan.lanes):
            at = plan.table_pieces + piece
            inward_ref[piece, rows, :] = shard[at * TILE : (at + 1) * TILE, :]
        at = plan.early_pieces * TILE
        stage_ref[pl.ds(owner, 1), :, :] = shard[at : at + TILE, :].astype(F32)[None]
    lane = lax.broadcasted_iota(jnp.int32, (1, LANE), 1)
    for vector, length in enumerate(plan.lengths):
        size = plan.owned[vector]
        group = LANE // size
        for block in range(length // LANE):
            row = jnp.zeros((1, LANE), F32)
            for index in range(group):
                own = stage_ref[block * group + index, vector : vector + 1, :]
                row = jnp.where(lane // size == index, own, row)
            at = plan.block_starts[vector] + block
            small_ref[at // plan.lanes : at // plan.lanes + 1, (at % plan.lanes) * LANE : (at % plan.lanes + 1) * LANE] = row


def own_lanes(value, head):
    lane = lax.broadcasted_iota(jnp.int32, value.shape, 1)
    return jnp.where((lane // (LANE // 2)) == head, value, jnp.zeros_like(value))


def causal():
    return lax.broadcasted_iota(jnp.int32, (STEP, STEP), 0) <= lax.broadcasted_iota(
        jnp.int32, (STEP, STEP), 1
    )


def attend_kernel(plan, count, info_ref, *refs):
    pieces, refs = refs[:count], refs[count:]
    if plan.packed:
        halves, refs = refs[:2], refs[2:]
    else:
        table_in, inward_in, small_in = refs[:3]
        refs = refs[3:]
    (lifted_ref, query_ref, key_ref, value_ref, mixed_ref, total_ref, inward_ref, small_ref) = refs[:8]
    low_ref, table_ref, place_ref, stage_ref = refs[8:]
    pair = pl.program_id(0)
    total_rows, width = plan.total_rows, plan.width
    half = total_rows // 2
    split = info_ref[0] < total_rows
    far = jnp.where(split, FAR, 0.0)

    @pl.when(pair == 0)
    def _():
        if plan.packed:
            fill_early(plan, info_ref[1], halves, table_ref, inward_ref, small_ref, stage_ref)
        else:
            table_ref[...] = table_in[...]
            inward_ref[...] = inward_in[...]
            small_ref[...] = small_in[...]
        eye = (
            lax.broadcasted_iota(jnp.int32, (half, half), 0)
            == lax.broadcasted_iota(jnp.int32, (half, half), 1)
        ).astype(BF)
        per_half = half // LANE
        for part in range(2):
            table = jnp.concatenate(
                [table_ref[part * per_half + i] for i in range(per_half)], axis=1
            )
            place_ref[part * half : (part + 1) * half, :] = times_t(eye, table)
        rows = total_rows // count
        for mask in range(count):
            start = (info_ref[2] ^ mask) * rows
            place = start - jnp.where(jnp.logical_and(split, start >= half), half, 0)
            lifted = pieces[mask][...].astype(F32) + place_ref[pl.ds(pl.multiple_of(place, rows), rows), :]
            spot = pl.ds(pl.multiple_of(start, rows), rows)
            lifted_ref[spot, :] = lifted
            low_ref[spot, :] = lifted.astype(BF)

    weights = jnp.concatenate([inward_ref[pair + i * plan.lanes] for i in range(3)], axis=1)
    lanes = aligned(pair, LANE)
    query_bias = small_ref[0:1, lanes]
    value_bias = small_ref[1:2, lanes]
    for block in range(total_rows // STEP):
        spot = slice(block * STEP, (block + 1) * STEP)
        joint = times(low_ref[spot, :], weights)
        query_ref[spot, :] = (joint[:, :LANE] + query_bias).astype(BF) * BF(0.125)
        key_ref[spot, :] = joint[:, LANE : 2 * LANE].astype(BF)
        value_ref[spot, :] = (joint[:, 2 * LANE :] + value_bias).astype(BF)

    keep = causal()
    lower = lax.broadcasted_iota(jnp.int32, (LANE, STEP), 0) < LANE // 2
    for block in range(total_rows // STEP):
        spot = slice(block * STEP, (block + 1) * STEP)
        start = block * STEP
        other = half if start >= half else 0
        query = query_ref[spot, :]
        parts = []
        for head in range(2):
            mine = own_lanes(query, head)
            near = times_t(key_ref[start : start + STEP, :], mine)
            near = jnp.where(keep, near, -FAR)
            peak = jnp.max(near, axis=0, keepdims=True)
            logits = [near]
            if start > other:
                same = times_t(key_ref[other:start, :], mine)
                peak = jnp.maximum(peak, jnp.max(same, axis=0, keepdims=True))
                logits.insert(0, same)
            if other:
                away = times_t(key_ref[:other, :], mine)
                peak = jnp.maximum(peak, jnp.max(away, axis=0, keepdims=True) - far)
            raised = [jnp.exp(piece - peak) for piece in logits]
            total = sum(jnp.sum(piece, axis=0, keepdims=True) for piece in raised)
            low = jnp.concatenate([piece.astype(BF) for piece in raised], axis=0)
            mixed = t_times(value_ref[other : start + STEP, :], low)
            if other:
                away = jnp.exp(away - (peak + far))
                total = total + jnp.sum(away, axis=0, keepdims=True)
                mixed = mixed + t_times(value_ref[:other, :], away.astype(BF))
            parts.append(mixed * (1.0 / total))
            total_ref[0, head : head + 1, spot] = peak + jnp.log(total)
        mixed_ref[spot, :] = jnp.where(lower, parts[0], parts[1]).T.astype(BF)


def attend(plan, info, pieces, weights):
    total_rows, width = plan.total_rows, plan.width
    block = pl.BlockSpec((total_rows, LANE), lambda p, *_: (0, p))
    low = like((total_rows, width), BF)
    inward = (3 * plan.lanes, width, LANE)
    small = (plan.small_rows, width)
    return pl.pallas_call(
        functools.partial(attend_kernel, plan, len(pieces)),
        grid_spec=pltpu.PrefetchScalarGridSpec(
            num_scalar_prefetch=1,
            grid=(plan.lanes,),
            in_specs=[full(v.shape) for v in pieces + weights],
            out_specs=[
                full((total_rows, width)),
                block,
                block,
                block,
                block,
                pl.BlockSpec((1, 8, total_rows), lambda p, *_: (p, 0, 0)),
                full(inward),
                full(small),
            ],
            scratch_shapes=[
                pltpu.VMEM((total_rows, width), BF),
                pltpu.VMEM((plan.table_pieces, width, LANE), BF),
                pltpu.VMEM((total_rows, width), F32),
                pltpu.VMEM((plan.devices, TILE, LANE), F32),
            ],
        ),
        out_shape=[
            like((total_rows, width), F32),
            low,
            low,
            low,
            low,
            like((plan.lanes, 8, total_rows), F32),
            like(inward, BF),
            like(small, F32),
        ],
        compiler_params=params(60),
        cost_estimate=cost(5 * 10**9, 14 * 2**20, 6 * 10**6),
        name="attend",
    )(info, *pieces, *weights)


def norm(rows):
    center = rows - jnp.mean(rows, axis=1, keepdims=True)
    root = lax.rsqrt(jnp.mean(center * center, axis=1, keepdims=True) + 1e-05)
    return center * root, root


def norm_back(upstream, gain, unit, root):
    scaled = upstream * gain
    mean = jnp.mean(scaled, axis=1, keepdims=True)
    slope = jnp.mean(scaled * unit, axis=1, keepdims=True)
    return (scaled - mean - unit * slope) * root


def feed_kernel(plan, count, info_ref, lifted_ref, mixed_ref, *refs):
    upstreams, refs = refs[:count], refs[count:]
    if plan.packed:
        late_in, small_ref = refs[:2]
        refs = refs[2:]
    else:
        outward_in, expand_in, contract_in, small_ref = refs[:4]
        refs = refs[4:]
    results, refs = refs[:count], refs[count:]
    mixed_back_ref, first_back_ref, small_grad_ref = refs[:3]
    refs = refs[3:]
    if plan.packed:
        halves, refs = refs[:2], refs[2:]
    else:
        outward_out, expand_out, contract_out = refs[:3]
        refs = refs[3:]
    (outward_ref, expand_ref, contract_ref, upstream_ref, active_ref, slope_ref,
     outward_sum, expand_sum, contract_sum) = refs
    step = pl.program_id(0)
    width, parts, lanes = plan.width, plan.parts, plan.lanes
    contract_own = plan.hidden // plan.devices
    contract_at = (lanes + parts * lanes) * TILE

    @pl.when(step == 0)
    def _():
        if plan.packed:
            for device in range(plan.devices):
                rows = slice(device * TILE, (device + 1) * TILE)
                shard = late_in.at[device]
                for lane in range(lanes):
                    cut = slice(lane * LANE, (lane + 1) * LANE)
                    outward_ref[rows, cut] = shard[lane * TILE : (lane + 1) * TILE, :]
                    for part in range(parts):
                        at = (lanes + part * lanes + lane) * TILE
                        expand_ref[part, rows, cut] = shard[at : at + TILE, :]
                    at = contract_at + lane * contract_own
                    contract_ref[device * contract_own : (device + 1) * contract_own, cut] = shard[at : at + contract_own, :]
        else:
            outward_ref[...] = outward_in[...]
            expand_ref[...] = expand_in[...]
            contract_ref[...] = contract_in[...]

    for mask in range(count):
        @pl.when(step == mask)
        def _(mask=mask):
            upstream_ref[...] = upstreams[mask][...]

    outlet, steady, offset = (small_ref[i : i + 1, :] for i in (2, 3, 4))
    settle, temper, anchor = (small_ref[i + parts : i + parts + 1, :] for i in (5, 6, 7))
    mixed = mixed_ref[...]
    branch = times(mixed, outward_ref[...]) + outlet
    unit, root = norm(lifted_ref[...] + branch)
    normed = unit * steady + offset
    normed_low = normed.astype(BF)
    lowered = jnp.zeros_like(normed)
    for part in range(parts):
        cut = slice(part * width, (part + 1) * width)
        hidden = times(normed_low, expand_ref[part]) + small_ref[5 + part : 6 + part, :]
        square = hidden * hidden
        bend = jnp.tanh(hidden * (BEND + BEND * 0.044715 * square))
        half = 0.5 + 0.5 * bend
        active = (hidden * half).astype(BF)
        active_ref[:, cut] = active
        slope_ref[:, cut] = half + (0.5 * hidden) * (1.0 - bend * bend) * (
            BEND + 3 * BEND * 0.044715 * square
        )
        lowered = lowered + times(active, contract_ref[cut, :])
    last_unit, last_root = norm(normed + (lowered + settle))
    result = (last_unit * temper + anchor).astype(BF)
    for mask in range(count):
        @pl.when(step == mask)
        def _(mask=mask):
            results[mask][...] = result

    upstream = upstream_ref[...].astype(F32)
    temper_grad = column_sum(upstream * last_unit)
    anchor_grad = column_sum(upstream)
    second_back = norm_back(upstream, temper, last_unit, last_root)
    lowered_back = second_back.astype(BF)
    settle_grad = column_sum(lowered_back)
    normed_back = second_back
    spread_grads = []
    contract_terms = []
    expand_terms = []
    for part in range(parts):
        cut = slice(part * width, (part + 1) * width)
        contract_terms.append(t_times(active_ref[:, cut], lowered_back))
        active_back = times_t(lowered_back, contract_ref[cut, :])
        hidden_back = (active_back * slope_ref[:, cut]).astype(BF)
        spread_grads.append(column_sum(hidden_back))
        expand_terms.append(t_times(normed_low, hidden_back))
        normed_back = normed_back + times_t(hidden_back, expand_ref[part])
    first_back = norm_back(normed_back, steady, unit, root)
    first_back_ref[...] = first_back
    branch_back = first_back.astype(BF)
    mixed_back_ref[...] = times_t(branch_back, outward_ref[...]).astype(BF)
    outward_term = t_times(mixed, branch_back)
    zero = jnp.zeros_like(anchor_grad)
    grads = [zero, zero, column_sum(branch_back), column_sum(normed_back * unit)]
    grads += [column_sum(normed_back)] + spread_grads + [settle_grad, temper_grad, anchor_grad]
    grads += [zero] * (plan.small_rows - len(grads))
    small_term = jnp.concatenate(grads, axis=0)

    @pl.when(step == 0)
    def _():
        small_grad_ref[...] = small_term
        outward_sum[...] = outward_term
        for part in range(parts):
            expand_sum[part] = expand_terms[part]
            contract_sum[part * width : (part + 1) * width, :] = contract_terms[part]

    @pl.when(step > 0)
    def _():
        small_grad_ref[...] += small_term
        outward_sum[...] += outward_term
        for part in range(parts):
            expand_sum[part] += expand_terms[part]
            contract_sum[part * width : (part + 1) * width, :] += contract_terms[part]

    @pl.when(step == count - 1)
    def _():
        if plan.packed:
            for mask in range(plan.devices):
                shard = halves[mask & 1].at[plan.place(mask)]
                owner = info_ref[1] ^ mask
                rows = aligned(owner, TILE)
                wide = aligned(owner, contract_own)
                for lane in range(lanes):
                    cut = slice(lane * LANE, (lane + 1) * LANE)
                    shard[lane * TILE : (lane + 1) * TILE, :] = outward_sum[rows, cut].astype(BF)
                    for part in range(parts):
                        at = (lanes + part * lanes + lane) * TILE
                        shard[at : at + TILE, :] = expand_sum[part, rows, cut].astype(BF)
                    at = contract_at + lane * contract_own
                    shard[at : at + contract_own, :] = contract_sum[wide, cut].astype(BF)
        else:
            outward_out[...] = outward_sum[...].astype(BF)
            expand_out[...] = expand_sum[...].astype(BF)
            contract_out[...] = contract_sum[...].astype(BF)


def feed(plan, info, lifted, mixed, upstreams, weights, small):
    total_rows, width, parts = plan.total_rows, plan.width, plan.parts
    count = len(upstreams)
    size = total_rows // count
    rows = pl.BlockSpec((size, width), lambda i, info: (info[2] ^ i, 0))
    outward, expand, contract = (width, width), (parts, width, width), (parts * width, width)
    if plan.packed:
        grads = [like((plan.devices // 2, plan.late_rows, LANE), BF)] * 2
    else:
        grads = [like(outward, BF), like(expand, BF), like(contract, BF)]
    ends = [like((size, width), BF)] * count
    outs = [like((total_rows, width), BF), like((total_rows, width), F32), like(small.shape, F32)]
    values = pl.pallas_call(
        functools.partial(feed_kernel, plan, count),
        grid_spec=pltpu.PrefetchScalarGridSpec(
            num_scalar_prefetch=1,
            grid=(count,),
            in_specs=[rows, rows] + [full(v.shape) for v in upstreams + weights + [small]],
            out_specs=[full(v.shape) for v in ends]
            + [rows, rows, full(small.shape)]
            + [full(v.shape) for v in grads],
            scratch_shapes=[
                pltpu.VMEM(outward, BF),
                pltpu.VMEM(expand, BF),
                pltpu.VMEM(contract, BF),
                pltpu.VMEM((size, width), BF),
                pltpu.VMEM((size, parts * width), BF),
                pltpu.VMEM((size, parts * width), F32),
                pltpu.VMEM(outward, F32),
                pltpu.VMEM(expand, F32),
                pltpu.VMEM(contract, F32),
            ],
        ),
        out_shape=ends + outs + grads,
        compiler_params=params(60),
        cost_estimate=cost(15 * 10**9, 20 * 2**20, 2 * 10**6),
        name="feed",
    )(info, lifted, mixed, *upstreams, *weights, small)
    return values[:count], values[count : count + 3], values[count + 3 :]


def attend_back_kernel(
    plan, count, info_ref, lifted_ref, query_ref, key_ref, value_ref, mixed_ref, mixed_back_ref,
    total_ref, inward_ref, first_back_ref, small_grad_ref, *refs
):
    tokens, refs = refs[:count], refs[count:]
    if plan.packed:
        halves, refs = refs[:2], refs[2:]
    else:
        table_out, inward_out, small_out = refs[:3]
        refs = refs[3:]
    low_ref, sum_ref, share_ref, score_ref, grad_ref, table_ref, joint_sums, blocks_ref = refs
    pair = pl.program_id(0)
    total_rows, lanes = plan.total_rows, plan.lanes
    half = total_rows // 2
    split = info_ref[0] < total_rows
    far = jnp.where(split, FAR, 0.0)
    blocks = total_rows // STEP

    @pl.when(pair == 0)
    def _():
        low_ref[...] = lifted_ref[...].astype(BF)

    keep = causal()
    lower = lax.broadcasted_iota(jnp.int32, (STEP, LANE), 1) < LANE // 2
    lower_t = lax.broadcasted_iota(jnp.int32, (LANE, STEP), 0) < LANE // 2
    query_parts, key_parts, value_parts = [], [], []
    product = (mixed_ref[...].astype(F32) * mixed_back_ref[...].astype(F32)).T
    scaled_key = key_ref[...] * BF(0.125)
    for head in range(2):
        between = jnp.sum(
            product[head * LANE // 2 : (head + 1) * LANE // 2], axis=0, keepdims=True
        )
        for block in range(blocks):
            start = block * STEP
            spot = slice(start, start + STEP)
            query = own_lanes(query_ref[spot, :], head)
            back = own_lanes(mixed_back_ref[spot, :], head)
            total = total_ref[0, head : head + 1, spot]
            gap = between[:, spot]
            for under in range(block + 1):
                keys = slice(under * STEP, (under + 1) * STEP)
                away = start >= half and under * STEP < half
                logits = times_t(key_ref[keys, :], query)
                share = jnp.exp(logits - (total + far if away else total))
                if under == block:
                    share = jnp.where(keep, share, 0.0)
                share_back = times_t(value_ref[keys, :], back)
                score = share * (share_back - gap)
                share_ref[head, keys, spot] = share.astype(BF)
                score_ref[head, keys, spot] = score.astype(BF)
        queries, keys_, values = [], [], []
        for block in range(blocks):
            start = block * STEP
            spot = slice(start, start + STEP)
            end = start + STEP
            queries.append(t_times(scaled_key[:end], score_ref[head, :end, spot]))
            keys_.append(times(score_ref[head, spot, start:], query_ref[start:, :]))
            values.append(times(share_ref[head, spot, start:], mixed_back_ref[start:, :]))
        query_parts.append(queries)
        key_parts.append(keys_)
        value_parts.append(values)
    weights = jnp.concatenate([inward_ref[pair + i * lanes] for i in range(3)], axis=1)
    joints = []
    for block in range(blocks):
        spot = slice(block * STEP, (block + 1) * STEP)
        query_back = jnp.where(lower_t, query_parts[0][block], query_parts[1][block]).T
        key_back = jnp.where(lower, key_parts[0][block], key_parts[1][block])
        value_back = jnp.where(lower, value_parts[0][block], value_parts[1][block])
        joint = jnp.concatenate([query_back, key_back, value_back], axis=1).astype(BF)
        joints.append(joint)
        term = times_t(joint, weights)

        @pl.when(pair == 0)
        def _():
            sum_ref[spot, :] = term + first_back_ref[spot, :]

        @pl.when(pair > 0)
        def _():
            sum_ref[spot, :] += term

    joint = jnp.concatenate(joints, axis=0)
    grads = t_times(low_ref[...], joint)
    for part in range(3):
        grad_ref[pair + part * lanes] = grads[:, part * LANE : (part + 1) * LANE]
    sums = column_sum(joint)
    joint_sums[pl.ds(pair, 1), :] = sums[:, :LANE]
    joint_sums[pl.ds(pair + lanes, 1), :] = sums[:, 2 * LANE :]

    @pl.when(pair == lanes - 1)
    def _():
        rows = total_rows // count
        for mask in range(count):
            spot = pl.ds(pl.multiple_of((info_ref[2] ^ mask) * rows, rows), rows)
            tokens[mask][...] = sum_ref[spot, :].astype(BF)
        late = sum_ref[half:, :]
        early = sum_ref[:half, :] + jnp.where(split, late, 0.0)
        table_ref[:, :half] = early.T
        table_ref[:, half:] = jnp.where(split, 0.0, late).T
        counted = info_ref[3] > 0
        blocks_ref[: 2 * lanes, :] = joint_sums[: 2 * lanes, :]
        for row in range(2, plan.block_starts[-1] // lanes):
            for lane in range(lanes):
                blocks_ref[row * lanes + lane : row * lanes + lane + 1, :] = small_grad_ref[
                    row : row + 1, lane * LANE : (lane + 1) * LANE
                ]
        if plan.packed:
            for mask in range(plan.devices):
                shard = halves[mask & 1].at[plan.place(mask)]
                owner = info_ref[1] ^ mask
                own = aligned(owner, TILE)
                for piece in range(plan.table_pieces):
                    shard[piece * TILE : (piece + 1) * TILE, :] = table_ref[
                        own, piece * LANE : (piece + 1) * LANE
                    ].astype(BF)
                for piece in range(3 * lanes):
                    at = (plan.table_pieces + piece) * TILE
                    shard[at : at + TILE, :] = grad_ref[piece, own, :].astype(BF)
                rows = [
                    blocks_ref[pl.ds(plan.block_starts[v] + owner * plan.owned[v] // LANE, 1), :]
                    for v in range(VECTORS)
                ]
                rows.append(jnp.zeros((TILE - VECTORS, LANE), F32))
                at = plan.early_pieces * TILE
                shard[at : at + TILE, :] = jnp.concatenate(rows, axis=0).astype(BF)
        else:
            table_out[...] = jnp.where(counted, table_ref[...], 0.0).astype(BF)
            inward_out[...] = jnp.where(counted, grad_ref[...], 0.0).astype(BF)
            small_out[...] = jnp.where(counted, blocks_ref[...], 0.0)


def attend_back(plan, info, count, lifted, saved, mixed_back, inward, first_back, small_grad):
    query, key, value, mixed, totals = saved
    total_rows, width, lanes = plan.total_rows, plan.width, plan.lanes
    block = pl.BlockSpec((total_rows, LANE), lambda p, *_: (0, p))
    blocks = (plan.block_starts[-1], LANE)
    if plan.packed:
        grads = [like((plan.devices // 2, plan.early_rows, LANE), BF)] * 2
    else:
        grads = [like((width, total_rows), BF), like(inward.shape, BF), like(blocks, F32)]
    tokens = [like((total_rows // count, width), BF)] * count
    values = pl.pallas_call(
        functools.partial(attend_back_kernel, plan, count),
        grid_spec=pltpu.PrefetchScalarGridSpec(
            num_scalar_prefetch=1,
            grid=(lanes,),
            in_specs=[
                full(lifted.shape),
                block,
                block,
                block,
                block,
                block,
                pl.BlockSpec((1, 8, total_rows), lambda p, *_: (p, 0, 0)),
                full(inward.shape),
                full(first_back.shape),
                full(small_grad.shape),
            ],
            out_specs=[full(v.shape) for v in tokens + grads],
            scratch_shapes=[
                pltpu.VMEM((total_rows, width), BF),
                pltpu.VMEM((total_rows, width), F32),
                pltpu.VMEM((2, total_rows, total_rows), BF),
                pltpu.VMEM((2, total_rows, total_rows), BF),
                pltpu.VMEM(inward.shape, F32),
                pltpu.VMEM((width, total_rows), F32),
                pltpu.VMEM((8, LANE), F32),
                pltpu.VMEM(blocks, F32),
            ],
        ),
        out_shape=tokens + grads,
        compiler_params=params(60),
        cost_estimate=cost(14 * 10**9, 24 * 2**20, 6 * 10**6),
        name="attend_back",
    )(info, lifted, query, key, value, mixed, mixed_back, totals, inward, first_back, small_grad)
    return values[:count], values[count:]


def pack_early_kernel(plan, table_ref, inward_ref, *refs):
    vectors, out_ref = refs[:VECTORS], refs[VECTORS]
    for piece in range(plan.table_pieces):
        out_ref[piece * TILE : (piece + 1) * TILE, :] = table_ref[:, piece * LANE : (piece + 1) * LANE]
    for piece in range(3 * plan.lanes):
        at = (plan.table_pieces + piece) * TILE
        out_ref[at : at + TILE, :] = inward_ref[:, piece * LANE : (piece + 1) * LANE]
    rows = []
    for size, ref in zip(plan.owned, vectors):
        rows.append(jnp.concatenate([ref[...].astype(F32)] * (LANE // size), axis=1))
    rows.append(jnp.zeros((TILE - VECTORS, LANE), F32))
    at = plan.early_pieces * TILE
    out_ref[at : at + TILE, :] = jnp.concatenate(rows, axis=0).astype(BF)


def pack_early(plan, table, inward, vectors):
    values = [table, inward] + [v.reshape(1, -1) for v in vectors]
    return pl.pallas_call(
        functools.partial(pack_early_kernel, plan),
        out_shape=like((plan.early_rows, LANE), BF),
        name="pack_early",
    )(*values)


def pack_late_kernel(plan, outward_ref, expand_ref, contract_ref, out_ref):
    at = 0
    for ref in (outward_ref, expand_ref, contract_ref):
        rows = ref.shape[0]
        for lane in range(ref.shape[1] // LANE):
            out_ref[at : at + rows, :] = ref[:, lane * LANE : (lane + 1) * LANE]
            at += rows


def pack_late(plan, outward, expand, contract):
    return pl.pallas_call(
        functools.partial(pack_late_kernel, plan),
        out_shape=like((plan.late_rows, LANE), BF),
        name="pack_late",
    )(outward, expand, contract)


def fold_kernel(count, *refs):
    total = refs[0][...].astype(F32)
    for ref in refs[1:count]:
        total = total + ref[...].astype(F32)
    size = total.shape[0] // len(refs[count:])
    for index, ref in enumerate(refs[count:]):
        ref[...] = total[index * size : (index + 1) * size].astype(ref.dtype)


def fold(terms, cuts):
    entries, rows, _ = terms[0].shape
    pieces = 4 if rows % 64 == 0 else 3
    size = rows // pieces
    out = like((entries // cuts, rows, LANE), BF)
    return pl.pallas_call(
        functools.partial(fold_kernel, len(terms)),
        grid=(pieces,),
        in_specs=[pl.BlockSpec((entries, size, LANE), lambda i: (0, i, 0))] * len(terms),
        out_specs=[pl.BlockSpec((entries // cuts, size, LANE), lambda i: (0, i, 0))] * cuts,
        out_shape=[out] * cuts,
        cost_estimate=cost(10**6, len(terms) * entries * rows * LANE * 4),
        name="fold",
    )(*terms)


def finish_kernel(plan, count, info_ref, *refs):
    early, late, tokens = refs[:4], refs[4:8], refs[8 : 8 + count]
    (tokens_ref, table_ref, inward_ref, outward_ref, expand_ref, contract_ref) = refs[8 + count : 14 + count]
    vectors = refs[14 + count :]
    early = sum(ref[0].astype(F32) for ref in early)
    late = sum(ref[0].astype(F32) for ref in late)
    for mask in range(count):
        tokens_ref[pl.ds(info_ref[2] ^ mask, 1), :, :] = tokens[mask][...][None]
    for piece in range(plan.table_pieces):
        table_ref[:, piece * LANE : (piece + 1) * LANE] = early[piece * TILE : (piece + 1) * TILE]
    for piece in range(3 * plan.lanes):
        at = (plan.table_pieces + piece) * TILE
        inward_ref[:, piece * LANE : (piece + 1) * LANE] = early[at : at + TILE]
    at = 0
    for ref in (outward_ref, expand_ref, contract_ref):
        rows = ref.shape[0]
        for lane in range(ref.shape[1] // LANE):
            ref[:, lane * LANE : (lane + 1) * LANE] = late[at : at + rows]
            at += rows
    at = plan.early_pieces * TILE
    small = early[at : at + VECTORS]
    for vector, ref in enumerate(vectors):
        size = plan.owned[vector]
        slot = lax.rem(info_ref[1], LANE // size)
        row = pltpu.roll(small, LANE - slot * size, 1)
        ref[...] = row[vector : vector + 1, :size]


def finish(plan, info, micro_count, early, late, tokens):
    rows, width = tokens[0].shape
    own = plan.own_rows
    outs = [
        like((micro_count, rows, width), BF),
        like((own, plan.total_rows), F32),
        like((own, 3 * width), F32),
        like((own, width), F32),
        like((own, plan.hidden), F32),
        like((plan.hidden // plan.devices, width), F32),
    ] + [like((1, n), F32) for n in plan.owned]
    values = early + late + tokens
    return pl.pallas_call(
        functools.partial(finish_kernel, plan, len(tokens)),
        grid_spec=pltpu.PrefetchScalarGridSpec(
            num_scalar_prefetch=1,
            grid=(1,),
            in_specs=[full(v.shape) for v in values],
            out_specs=[full(v.shape) for v in outs],
        ),
        out_shape=outs,
        name="finish",
    )(info, *values)


def settle_kernel(count, share, info_ref, *refs):
    for mask in range(count):
        refs[count][pl.ds((info_ref[2] ^ mask) // share, 1), :, :] = refs[mask][...][None]


def settle_rows(info, micro_count, share, pieces):
    out = (micro_count,) + pieces[0].shape
    return pl.pallas_call(
        functools.partial(settle_kernel, len(pieces), share),
        grid_spec=pltpu.PrefetchScalarGridSpec(
            num_scalar_prefetch=1,
            grid=(1,),
            in_specs=[full(v.shape) for v in pieces],
            out_specs=full(out),
        ),
        out_shape=like(out, BF),
        name="settle_rows",
    )(info, *pieces)


def cut_kernel(count, share, rows_ref, *refs):
    rank = lax.axis_index("seq")
    for mask in range(count):
        refs[mask][...] = rows_ref[pl.ds((rank ^ mask) // share, 1), :, :][0]


def cut_rows(rows, count, share):
    outs = [like(rows.shape[1:], BF)] * count
    return pl.pallas_call(
        functools.partial(cut_kernel, count, share),
        out_shape=outs,
        cost_estimate=cost(0, 4 * 2**20),
        name="cut_rows",
    )(rows)


def local(tokens, first_length, cotangent, positions, inward, intake, outward, outlet, steady, offset,
          expand, spread, contract, settle, temper, anchor):
    micro_count, pack_count, block_rows, width = tokens.shape
    assert pack_count == 1
    devices, count = lax.axis_size(AXES), lax.axis_size("seq")
    me, rank = lax.axis_index(AXES), lax.axis_index("seq")
    share = max(count // micro_count, 1)
    assert share * micro_count == count
    plan = Plan(devices, width, contract.shape[0] * devices, block_rows * count)
    micro = rank // share
    firsts = jnp.where(jnp.arange(micro_count) == micro, first_length[:, 0], 0)
    counted = (rank % share == 0).astype(jnp.int32)
    info = jnp.stack([jnp.sum(firsts), me, rank, counted]).astype(jnp.int32)
    vectors = (intake, outlet, steady, offset, spread, settle, temper, anchor)

    def swap(value, mask):
        return lax.ppermute(value, AXES, [(d, d ^ mask) for d in range(devices)]) if mask else value

    def exchange(pieces):
        return [swap(piece, mask) for mask, piece in enumerate(pieces)]

    if plan.packed:
        shard = pack_early(plan, positions.T, inward, vectors)[None]
        late_shard = pack_late(plan, outward, expand, contract)
        rows_in = cut_rows(tokens[:, 0], count, share)
        shard, late_shard, rows_in = lax.optimization_barrier((shard, late_shard, rows_in))
        late = [lax.all_gather(late_shard, AXES, axis=0, tiled=False)]
        pieces = [swap(shard, k << 3) for k in range(4)]
        pieces, rows_in = lax.optimization_barrier((pieces, exchange(rows_in)))
        shard = jnp.concatenate(pieces, axis=0)
        pieces = [swap(shard, k << 1) for k in range(4)]
        upstreams = cut_rows(cotangent[:, 0], count, share)
        pieces, upstreams = lax.optimization_barrier((pieces, upstreams))
        shard = jnp.concatenate(pieces, axis=0)
        early = [shard, swap(shard, 1)]
        upstreams = exchange(upstreams)
    else:
        rows_in = exchange(cut_rows(tokens[:, 0], count, share))
        upstreams = exchange(cut_rows(cotangent[:, 0], count, share))
        early, late = plain_weights(plan, positions, inward, vectors, outward, expand, contract)
    lifted, query, key, value, mixed, totals, inward_all, small = attend(plan, info, rows_in, early)
    results, (mixed_back, first_back, small_grad), late_grads = feed(
        plan, info, lifted, mixed, upstreams, late, small
    )
    results = exchange(results)
    if plan.packed:
        keep, send = late_grads
        terms = fold([keep, swap(send, 1)], 4)
        terms, mixed_back = lax.optimization_barrier((terms, mixed_back))
        late_terms = [swap(term, k << 1) for k, term in enumerate(terms)]
    token_pieces, early_grads = attend_back(
        plan, info, count, lifted, (query, key, value, mixed, totals), mixed_back, inward_all,
        first_back, small_grad,
    )
    if plan.packed:
        late_terms, results, token_pieces, early_grads = lax.optimization_barrier(
            (late_terms, results, token_pieces, early_grads)
        )
        keep, send = early_grads
        send = swap(send, 1)
        late_terms = fold(late_terms, 4)
        output = settle_rows(info, micro_count, share, results)
        send, late_terms, output = lax.optimization_barrier((send, late_terms, output))
        terms = fold([keep, send], 4)
        terms, late_terms = lax.optimization_barrier((terms, late_terms))
        terms = [swap(term, k << 1) for k, term in enumerate(terms)]
        late_terms = [swap(term, k << 3) for k, term in enumerate(late_terms)]
        terms, late_terms, token_pieces = lax.optimization_barrier((terms, late_terms, token_pieces))
        token_pieces = exchange(token_pieces)
        terms = fold(terms, 4)
        early_terms = [swap(term, k << 3) for k, term in enumerate(terms)]
        values = finish(plan, info, micro_count, early_terms, late_terms, token_pieces)
        tokens_back, table_t, inward_own, outward_own, expand_own, contract_own = values[:6]
        own = [v.reshape(-1) for v in values[6:]]
        table_own = table_t.T
    else:
        output = settle_rows(info, micro_count, share, results)
        tokens_back = settle_rows(info, micro_count, share, exchange(token_pieces))
        table_own, inward_own, outward_own, expand_own, contract_own, own = plain_grads(
            plan, counted, early_grads, late_grads
        )
    return (output[:, None], tokens_back[:, None], table_own, inward_own, own[0], outward_own, own[1], own[2],
            own[3], expand_own, own[4], contract_own, own[5], own[6], own[7])


def plain_weights(plan, positions, inward, vectors, outward, expand, contract):
    lanes, width = plan.lanes, plan.width

    def gather(value, axis=0):
        return lax.all_gather(value, AXES, axis=axis, tiled=True)

    def in_pieces(value, size):
        return value.reshape(value.shape[0], -1, size).transpose(1, 0, 2)

    table = in_pieces(gather(positions, 1).T, LANE)
    small = jnp.concatenate([gather(v) for v in vectors]).astype(F32).reshape(-1, width)
    small = jnp.pad(small, ((0, plan.small_rows - small.shape[0]), (0, 0)))
    early = [table, in_pieces(gather(inward), LANE), small]
    return early, [gather(outward), in_pieces(gather(expand), width), gather(contract)]


def plain_grads(plan, counted, early_grads, late_grads):
    width = plan.width
    table, inward, small = early_grads
    outward, expand, contract = (jnp.where(counted > 0, g, BF(0)) for g in late_grads)

    def scatter(value, axis=0):
        return lax.psum_scatter(value, AXES, scatter_dimension=axis, tiled=True).astype(F32)

    def whole(value):
        return value.transpose(1, 0, 2).reshape(value.shape[1], -1)

    flat = small.reshape(-1)
    own = []
    for vector, length in enumerate(plan.lengths):
        start = plan.block_starts[vector] * LANE
        own.append(scatter(flat[start : start + length]))
    return (scatter(table.T, 1), scatter(whole(inward)), scatter(outward), scatter(whole(expand)),
            scatter(contract), own)


def solution(mesh):
    rows = P(None, "batch", "seq", None)
    table = P(None, AXES)
    matrix = P(AXES, None)
    vector = P(AXES)
    weights = (table, matrix, vector, matrix, vector, vector, vector, matrix, vector, matrix, vector,
               vector, vector)
    return jax.shard_map(
        local,
        mesh=mesh,
        in_specs=(rows, P(None, "batch"), rows) + weights,
        out_specs=(rows, rows) + weights,
        check_vma=False,
    )
```

```python
import functools

import jax
import jax.numpy as jnp
from jax import lax
from jax.experimental import pallas as pl
from jax.experimental.pallas import tpu as pltpu
from jax.sharding import PartitionSpec as P

AXES = ("batch", "seq")
LANE = 128
TILE = 16
FEED_ROWS = 512
STEP = 256
FAR = 1e30
BEND = 0.7978845608028654
BF = jnp.bfloat16
F32 = jnp.float32
VECTORS = 8


def times(left, right):
    return jnp.dot(left, right, preferred_element_type=F32)


def times_t(left, right):
    return lax.dot_general(left, right, (((1,), (1,)), ((), ())), preferred_element_type=F32)


def t_times(left, right):
    return lax.dot_general(left, right, (((0,), (0,)), ((), ())), preferred_element_type=F32)


def column_sum(values):
    return jnp.sum(values.astype(F32), axis=0, keepdims=True)


def aligned(index, size):
    return pl.ds(pl.multiple_of(index * size, size), size)


def like(shape, kind):
    return jax.ShapeDtypeStruct(shape, kind)


def full(shape):
    return pl.BlockSpec(shape, lambda *_: (0,) * len(shape), pipeline_mode=pl.Buffered(1))


def params(megabytes):
    return pltpu.CompilerParams(vmem_limit_bytes=megabytes * 2**20)


def cost(flops, size, exps=0):
    return pl.CostEstimate(flops=flops, bytes_accessed=size, transcendentals=exps)


class Plan:
    def __init__(self, devices, width, hidden, total_rows):
        self.devices = devices
        self.width = width
        self.hidden = hidden
        self.total_rows = total_rows
        self.own_rows = width // devices
        self.packed = devices == 32 and self.own_rows % TILE == 0
        self.lanes = width // LANE
        self.parts = hidden // width
        self.table_pieces = total_rows // LANE
        self.early_pieces = self.table_pieces + 3 * self.lanes
        self.early_rows = (self.early_pieces + 1) * TILE
        self.late_rows = (self.lanes + hidden // LANE) * TILE + self.lanes * (hidden // devices)
        lengths = [2 * width, width, width, width, hidden, width, width, width]
        self.lengths = lengths
        self.owned = [n // devices for n in lengths]
        self.small_rows = 16
        starts = [0]
        for n in lengths:
            starts.append(starts[-1] + n // LANE)
        self.block_starts = starts

    def place(self, mask):
        return ((mask >> 1) & 3) * 4 + ((mask >> 3) & 3)


def fill_early(plan, me, halves, table_ref, inward_ref, small_ref, stage_ref):
    for mask in range(plan.devices):
        shard = halves[mask & 1].at[plan.place(mask)]
        owner = me ^ mask
        rows = aligned(owner, TILE)
        for piece in range(plan.table_pieces):
            table_ref[piece, rows, :] = shard[piece * TILE : (piece + 1) * TILE, :]
        for piece in range(3 * plan.lanes):
            at = plan.table_pieces + piece
            inward_ref[piece, rows, :] = shard[at * TILE : (at + 1) * TILE, :]
        at = plan.early_pieces * TILE
        stage_ref[pl.ds(owner, 1), :, :] = shard[at : at + TILE, :].astype(F32)[None]
    lane = lax.broadcasted_iota(jnp.int32, (1, LANE), 1)
    for vector, length in enumerate(plan.lengths):
        size = plan.owned[vector]
        group = LANE // size
        for block in range(length // LANE):
            row = jnp.zeros((1, LANE), F32)
            for index in range(group):
                own = stage_ref[block * group + index, vector : vector + 1, :]
                row = jnp.where(lane // size == index, own, row)
            at = plan.block_starts[vector] + block
            small_ref[at // plan.lanes : at // plan.lanes + 1, (at % plan.lanes) * LANE : (at % plan.lanes + 1) * LANE] = row


def own_lanes(value, head):
    lane = lax.broadcasted_iota(jnp.int32, value.shape, 1)
    return jnp.where((lane // (LANE // 2)) == head, value, jnp.zeros_like(value))


def causal():
    return lax.broadcasted_iota(jnp.int32, (STEP, STEP), 0) <= lax.broadcasted_iota(
        jnp.int32, (STEP, STEP), 1
    )


def attend_kernel(plan, count, info_ref, *refs):
    pieces, refs = refs[:count], refs[count:]
    if plan.packed:
        halves, refs = refs[:2], refs[2:]
    else:
        table_in, inward_in, small_in = refs[:3]
        refs = refs[3:]
    (lifted_ref, query_ref, key_ref, value_ref, mixed_ref, total_ref, inward_ref, small_ref) = refs[:8]
    low_ref, table_ref, place_ref, stage_ref = refs[8:]
    pair = pl.program_id(0)
    total_rows, width = plan.total_rows, plan.width
    half = total_rows // 2
    split = info_ref[0] < total_rows
    far = jnp.where(split, FAR, 0.0)

    @pl.when(pair == 0)
    def _():
        if plan.packed:
            fill_early(plan, info_ref[1], halves, table_ref, inward_ref, small_ref, stage_ref)
        else:
            table_ref[...] = table_in[...]
            inward_ref[...] = inward_in[...]
            small_ref[...] = small_in[...]
        eye = (
            lax.broadcasted_iota(jnp.int32, (half, half), 0)
            == lax.broadcasted_iota(jnp.int32, (half, half), 1)
        ).astype(BF)
        per_half = half // LANE
        for part in range(2):
            table = jnp.concatenate(
                [table_ref[part * per_half + i] for i in range(per_half)], axis=1
            )
            place_ref[part * half : (part + 1) * half, :] = times_t(eye, table)
        rows = total_rows // count
        for mask in range(count):
            start = (info_ref[2] ^ mask) * rows
            place = start - jnp.where(jnp.logical_and(split, start >= half), half, 0)
            lifted = pieces[mask][...].astype(F32) + place_ref[pl.ds(pl.multiple_of(place, rows), rows), :]
            spot = pl.ds(pl.multiple_of(start, rows), rows)
            lifted_ref[spot, :] = lifted
            low_ref[spot, :] = lifted.astype(BF)

    weights = jnp.concatenate([inward_ref[pair + i * plan.lanes] for i in range(3)], axis=1)
    lanes = aligned(pair, LANE)
    query_bias = small_ref[0:1, lanes]
    value_bias = small_ref[1:2, lanes]
    for block in range(total_rows // STEP):
        spot = slice(block * STEP, (block + 1) * STEP)
        joint = times(low_ref[spot, :], weights)
        query_ref[spot, :] = (joint[:, :LANE] + query_bias).astype(BF) * BF(0.125)
        key_ref[spot, :] = joint[:, LANE : 2 * LANE].astype(BF)
        value_ref[spot, :] = (joint[:, 2 * LANE :] + value_bias).astype(BF)

    keep = causal()
    lower = lax.broadcasted_iota(jnp.int32, (LANE, STEP), 0) < LANE // 2

    value_t = value_ref[...].T

    def logits_of(block, head):
        start = block * STEP
        other = half if start >= half else 0
        mine = own_lanes(query_ref[start : start + STEP, :], head)
        near = times_t(key_ref[start : start + STEP, :], mine)
        same = times_t(key_ref[other:start, :], mine) if start > other else None
        away = times_t(key_ref[:other, :], mine) if other else None
        return near, same, away

    def mixed_of(block, head, near, same, away):
        start = block * STEP
        other = half if start >= half else 0
        near = jnp.where(keep, near, -FAR)
        peak = jnp.max(near, axis=0, keepdims=True)
        if same is not None:
            peak = jnp.maximum(peak, jnp.max(same, axis=0, keepdims=True))
        if away is not None:
            peak = jnp.maximum(peak, jnp.max(away, axis=0, keepdims=True) - far)
        raised = [jnp.exp(piece - peak) for piece in (same, near) if piece is not None]
        total = sum(jnp.sum(piece, axis=0, keepdims=True) for piece in raised)
        low = jnp.concatenate([piece.astype(BF) for piece in raised], axis=0)
        mixed = times(value_t[:, other : start + STEP], low)
        if away is not None:
            away = jnp.exp(away - (peak + far))
            total = total + jnp.sum(away, axis=0, keepdims=True)
            mixed = mixed + times(value_t[:, :other], away.astype(BF))
        total_ref[0, head : head + 1, start : start + STEP] = peak + jnp.log(total)
        return mixed * (1.0 / total)

    tasks = [(block, head) for block in range(total_rows // STEP) for head in range(2)]
    ahead = logits_of(*tasks[0])
    parts = []
    for index, (block, head) in enumerate(tasks):
        logits, ahead = ahead, logits_of(*tasks[index + 1]) if index + 1 < len(tasks) else None
        parts.append(mixed_of(block, head, *logits))
        if head:
            mixed_ref[block * STEP : (block + 1) * STEP, :] = jnp.where(lower, *parts).T.astype(BF)
            parts = []


def attend(plan, info, pieces, weights):
    total_rows, width = plan.total_rows, plan.width
    block = pl.BlockSpec((total_rows, LANE), lambda p, *_: (0, p))
    low = like((total_rows, width), BF)
    inward = (3 * plan.lanes, width, LANE)
    small = (plan.small_rows, width)
    return pl.pallas_call(
        functools.partial(attend_kernel, plan, len(pieces)),
        grid_spec=pltpu.PrefetchScalarGridSpec(
            num_scalar_prefetch=1,
            grid=(plan.lanes,),
            in_specs=[full(v.shape) for v in pieces + weights],
            out_specs=[
                full((total_rows, width)),
                block,
                block,
                block,
                block,
                pl.BlockSpec((1, 8, total_rows), lambda p, *_: (p, 0, 0)),
                full(inward),
                full(small),
            ],
            scratch_shapes=[
                pltpu.VMEM((total_rows, width), BF),
                pltpu.VMEM((plan.table_pieces, width, LANE), BF),
                pltpu.VMEM((total_rows, width), F32),
                pltpu.VMEM((plan.devices, TILE, LANE), F32),
            ],
        ),
        out_shape=[
            like((total_rows, width), F32),
            low,
            low,
            low,
            low,
            like((plan.lanes, 8, total_rows), F32),
            like(inward, BF),
            like(small, F32),
        ],
        compiler_params=params(60),
        cost_estimate=cost(5 * 10**9, 14 * 2**20, 6 * 10**6),
        name="attend",
    )(info, *pieces, *weights)


def norm(rows):
    center = rows - jnp.mean(rows, axis=1, keepdims=True)
    root = lax.rsqrt(jnp.mean(center * center, axis=1, keepdims=True) + 1e-05)
    return center * root, root


def norm_back(upstream, gain, unit, root):
    scaled = upstream * gain
    mean = jnp.mean(scaled, axis=1, keepdims=True)
    slope = jnp.mean(scaled * unit, axis=1, keepdims=True)
    return (scaled - mean - unit * slope) * root


def feed_kernel(plan, count, info_ref, lifted_ref, mixed_ref, *refs):
    upstreams, refs = refs[:count], refs[count:]
    if plan.packed:
        late_in, small_ref = refs[:2]
        refs = refs[2:]
    else:
        outward_in, expand_in, contract_in, small_ref = refs[:4]
        refs = refs[4:]
    results, refs = refs[:count], refs[count:]
    mixed_back_ref, first_back_ref, small_grad_ref = refs[:3]
    refs = refs[3:]
    if plan.packed:
        halves, refs = refs[:2], refs[2:]
    else:
        outward_out, expand_out, contract_out = refs[:3]
        refs = refs[3:]
    (outward_ref, expand_ref, contract_ref, upstream_ref, result_ref, slope_ref, active_all, hidden_all, normed_all,
     lowered_all, branch_all, mixed_all, whole_ref, expand_sum, contract_sum) = refs
    step = pl.program_id(0)
    width, parts, lanes = plan.width, plan.parts, plan.lanes
    contract_own = plan.hidden // plan.devices
    contract_at = (lanes + parts * lanes) * TILE

    @pl.when(step == 0)
    def _():
        if plan.packed:
            for device in range(plan.devices):
                rows = slice(device * TILE, (device + 1) * TILE)
                shard = late_in.at[device]
                for lane in range(lanes):
                    cut = slice(lane * LANE, (lane + 1) * LANE)
                    outward_ref[rows, cut] = shard[lane * TILE : (lane + 1) * TILE, :]
                    for part in range(parts):
                        at = (lanes + part * lanes + lane) * TILE
                        expand_ref[part, rows, cut] = shard[at : at + TILE, :]
                    at = contract_at + lane * contract_own
                    contract_ref[device * contract_own : (device + 1) * contract_own, cut] = shard[at : at + contract_own, :]
        else:
            outward_ref[...] = outward_in[...]
            expand_ref[...] = expand_in[...]
            contract_ref[...] = contract_in[...]

    size = lifted_ref.shape[0]
    here = pl.ds(pl.multiple_of(step * size, size), size)
    rows = plan.total_rows // count
    group = size // rows

    def spot(mask):
        return pl.ds(pl.multiple_of(((info_ref[2] ^ mask) % group) * rows, rows), rows)

    for mask in range(count):
        @pl.when(step == mask // group)
        def _(mask=mask):
            upstream_ref[spot(mask), :] = upstreams[mask][...]

    outlet, steady, offset = (small_ref[i : i + 1, :] for i in (2, 3, 4))
    settle, temper, anchor = (small_ref[i + parts : i + parts + 1, :] for i in (5, 6, 7))
    mixed = mixed_ref[...]
    branch = times(mixed, outward_ref[...]) + outlet
    unit, root = norm(lifted_ref[...] + branch)
    normed = unit * steady + offset
    normed_low = normed.astype(BF)
    normed_all[here, :] = normed_low
    mixed_all[here, :] = mixed
    lowered = jnp.zeros_like(normed)
    for part in range(parts):
        cut = slice(part * width, (part + 1) * width)
        hidden = times(normed_low, expand_ref[part]) + small_ref[5 + part : 6 + part, :]
        square = hidden * hidden
        bend = jnp.tanh(hidden * (BEND + BEND * 0.044715 * square))
        half = 0.5 + 0.5 * bend
        active = (hidden * half).astype(BF)
        active_all[here, cut] = active
        slope_ref[:, cut] = half + (0.5 * hidden) * (1.0 - bend * bend) * (
            BEND + 3 * BEND * 0.044715 * square
        )
        lowered = lowered + times(active, contract_ref[cut, :])
    last_unit, last_root = norm(normed + (lowered + settle))
    result_ref[...] = (last_unit * temper + anchor).astype(BF)
    upstream = upstream_ref[...].astype(F32)
    temper_grad = column_sum(upstream * last_unit)
    anchor_grad = column_sum(upstream)
    second_back = norm_back(upstream, temper, last_unit, last_root)
    lowered_back = second_back.astype(BF)
    lowered_all[here, :] = lowered_back
    settle_grad = column_sum(lowered_back)
    normed_back = second_back
    spread_grads = []
    for part in range(parts):
        cut = slice(part * width, (part + 1) * width)
        active_back = times_t(lowered_back, contract_ref[cut, :])
        hidden_back = (active_back * slope_ref[:, cut]).astype(BF)
        spread_grads.append(column_sum(hidden_back))
        hidden_all[here, cut] = hidden_back
        normed_back = normed_back + times_t(hidden_back, expand_ref[part])
    first_back = norm_back(normed_back, steady, unit, root)
    first_back_ref[...] = first_back
    branch_back = first_back.astype(BF)
    mixed_back_ref[...] = times_t(branch_back, outward_ref[...]).astype(BF)
    branch_all[here, :] = branch_back
    zero = jnp.zeros_like(anchor_grad)
    grads = [zero, zero, column_sum(branch_back), column_sum(normed_back * unit)]
    grads += [column_sum(normed_back)] + spread_grads + [settle_grad, temper_grad, anchor_grad]
    grads += [zero] * (plan.small_rows - len(grads))
    small_term = jnp.concatenate(grads, axis=0)
    for mask in range(count):
        @pl.when(step == mask // group)
        def _(mask=mask):
            results[mask][...] = result_ref[spot(mask), :]

    @pl.when(step == 0)
    def _():
        small_grad_ref[...] = small_term

    @pl.when(step > 0)
    def _():
        small_grad_ref[...] += small_term

    @pl.when(step == pl.num_programs(0) - 1)
    def _():
        outward = t_times(mixed_all[...], branch_all[...])
        if plan.packed:
            me = info_ref[1]
            whole_ref[...] = outward
            for mask in range(plan.devices):
                shard = halves[mask & 1].at[plan.place(mask)]
                rows = aligned(me ^ mask, TILE)
                for lane in range(lanes):
                    cut = slice(lane * LANE, (lane + 1) * LANE)
                    shard[lane * TILE : (lane + 1) * TILE, :] = whole_ref[rows, cut].astype(BF)
        else:
            outward_out[...] = outward.astype(BF)
        per_part = plan.devices // parts
        for mask_part in range(parts):
            part = (me // per_part) ^ mask_part if plan.packed else mask_part
            cut = pl.ds(pl.multiple_of(part * width, width), width)
            expand = t_times(normed_all[...], hidden_all[:, cut])
            contract = t_times(active_all[:, cut], lowered_all[...])
            if not plan.packed:
                expand_out[mask_part] = expand.astype(BF)
                contract_out[cut, :] = contract.astype(BF)
                continue
            expand_sum[...] = expand
            contract_sum[...] = contract
            for mask in range(plan.devices):
                shard = halves[mask & 1].at[plan.place(mask)]
                rows = aligned(me ^ mask, TILE)
                for lane in range(lanes):
                    at = aligned(lanes + part * lanes + lane, TILE)
                    shard[at, :] = expand_sum[rows, lane * LANE : (lane + 1) * LANE].astype(BF)
            for index in range(per_part):
                mask = mask_part * per_part + index
                shard = halves[mask & 1].at[plan.place(mask)]
                rows = aligned((me ^ mask) % per_part, contract_own)
                for lane in range(lanes):
                    at = contract_at + lane * contract_own
                    shard[at : at + contract_own, :] = contract_sum[
                        rows, lane * LANE : (lane + 1) * LANE
                    ].astype(BF)


def feed(plan, info, lifted, mixed, upstreams, weights, small):
    total_rows, width, parts = plan.total_rows, plan.width, plan.parts
    count = len(upstreams)
    piece = total_rows // count
    size = max(piece, FEED_ROWS)
    group = size // piece
    rows = pl.BlockSpec((size, width), lambda i, info: ((info[2] // group) ^ i, 0))
    outward, expand, contract = (width, width), (parts, width, width), (parts * width, width)
    if plan.packed:
        grads = [like((plan.devices // 2, plan.late_rows, LANE), BF)] * 2
    else:
        grads = [like(outward, BF), like(expand, BF), like(contract, BF)]
    ends = [like((piece, width), BF)] * count
    outs = [like((total_rows, width), BF), like((total_rows, width), F32), like(small.shape, F32)]
    values = pl.pallas_call(
        functools.partial(feed_kernel, plan, count),
        grid_spec=pltpu.PrefetchScalarGridSpec(
            num_scalar_prefetch=1,
            grid=(total_rows // size,),
            in_specs=[rows, rows] + [full(v.shape) for v in upstreams + weights + [small]],
            out_specs=[full(v.shape) for v in ends]
            + [rows, rows, full(small.shape)]
            + [full(v.shape) for v in grads],
            scratch_shapes=[
                pltpu.VMEM(outward, BF),
                pltpu.VMEM(expand, BF),
                pltpu.VMEM(contract, BF),
                pltpu.VMEM((size, width), BF),
                pltpu.VMEM((size, width), BF),
                pltpu.VMEM((size, parts * width), F32),
                pltpu.VMEM((total_rows, parts * width), BF),
                pltpu.VMEM((total_rows, parts * width), BF),
                pltpu.VMEM((total_rows, width), BF),
                pltpu.VMEM((total_rows, width), BF),
                pltpu.VMEM((total_rows, width), BF),
                pltpu.VMEM((total_rows, width), BF),
                pltpu.VMEM(outward, F32),
                pltpu.VMEM(outward, F32),
                pltpu.VMEM(outward, F32),
            ],
        ),
        out_shape=ends + outs + grads,
        compiler_params=params(60),
        cost_estimate=cost(15 * 10**9, 20 * 2**20, 2 * 10**6),
        name="feed",
    )(info, lifted, mixed, *upstreams, *weights, small)
    return values[:count], values[count : count + 3], values[count + 3 :]


def attend_back_kernel(
    plan, count, info_ref, lifted_ref, query_ref, key_ref, value_ref, mixed_ref, mixed_back_ref,
    total_ref, inward_ref, first_back_ref, small_grad_ref, *refs
):
    tokens, refs = refs[:count], refs[count:]
    if plan.packed:
        halves, refs = refs[:2], refs[2:]
    else:
        table_out, inward_out, small_out = refs[:3]
        refs = refs[3:]
    joint_ref, sum_ref, share_ref, score_ref, grad_ref, table_ref, joint_sums, blocks_ref = refs
    pair = pl.program_id(0)
    total_rows, lanes = plan.total_rows, plan.lanes
    half = total_rows // 2
    split = info_ref[0] < total_rows
    far = jnp.where(split, FAR, 0.0)
    blocks = total_rows // STEP

    keep = causal()
    lower = lax.broadcasted_iota(jnp.int32, (STEP, LANE), 1) < LANE // 2
    lower_t = lax.broadcasted_iota(jnp.int32, (LANE, STEP), 0) < LANE // 2
    product = (mixed_ref[...].astype(F32) * mixed_back_ref[...].astype(F32)).T
    scaled_key = (key_ref[...] * BF(0.125)).T
    betweens = [
        jnp.sum(product[head * LANE // 2 : (head + 1) * LANE // 2], axis=0, keepdims=True)
        for head in range(2)
    ]

    def logits_of(block, head):
        spot = slice(block * STEP, (block + 1) * STEP)
        keys = slice(0, (block + 1) * STEP)
        query = own_lanes(query_ref[spot, :], head)
        back = own_lanes(mixed_back_ref[spot, :], head)
        return times_t(key_ref[keys, :], query), times_t(value_ref[keys, :], back)

    def scores_of(block, head, logits, share_back):
        start = block * STEP
        spot = slice(start, start + STEP)
        total = total_ref[0, head : head + 1, spot]
        gap = betweens[head][:, spot]
        for under in range(block + 1):
            keys = slice(under * STEP, (under + 1) * STEP)
            away = start >= half and under * STEP < half
            share = jnp.exp(logits[keys] - (total + far if away else total))
            if under == block:
                share = jnp.where(keep, share, 0.0)
            score = share * (share_back[keys] - gap)
            share_ref[head, keys, spot] = share.astype(BF)
            score_ref[head, keys, spot] = score.astype(BF)

    def backs_of(block, head):
        start = block * STEP
        spot = slice(start, start + STEP)
        end = start + STEP
        query_back = times(scaled_key[:, :end], score_ref[head, :end, spot])
        key_back = times(score_ref[head, spot, start:], query_ref[start:, :])
        value_back = times(share_ref[head, spot, start:], mixed_back_ref[start:, :])
        return query_back, key_back, value_back

    tasks = [(block, head) for block in reversed(range(blocks)) for head in range(2)]
    ahead = logits_of(*tasks[0])
    parts = []
    for index, (block, head) in enumerate(tasks):
        logits, ahead = ahead, logits_of(*tasks[index + 1]) if index + 1 < len(tasks) else None
        scores_of(block, head, *logits)
        parts.append(backs_of(block, head))
        if head:
            spot = slice(block * STEP, (block + 1) * STEP)
            query_back = jnp.where(lower_t, parts[0][0], parts[1][0]).T
            key_back = jnp.where(lower, parts[0][1], parts[1][1])
            value_back = jnp.where(lower, parts[0][2], parts[1][2])
            for part, back in enumerate((query_back, key_back, value_back)):
                joint_ref[spot, aligned(pair + part * lanes, LANE)] = back.astype(BF)
            parts = []

    @pl.when(pair == lanes - 1)
    def _():
        low = lifted_ref[...].astype(BF).T
        weights = jnp.concatenate([inward_ref[i] for i in range(3 * lanes)], axis=1)
        for block in range(blocks):
            spot = slice(block * STEP, (block + 1) * STEP)
            sum_ref[spot, :] = first_back_ref[spot, :] + times_t(joint_ref[spot, :], weights)
        for part in range(3):
            joint = joint_ref[:, part * plan.width : (part + 1) * plan.width]
            grads = times(low, joint)
            for lane in range(lanes):
                grad_ref[part * lanes + lane] = grads[:, lane * LANE : (lane + 1) * LANE]
            if part != 1:
                sums = column_sum(joint)
                for lane in range(lanes):
                    at = lane if part == 0 else lane + lanes
                    joint_sums[at : at + 1, :] = sums[:, lane * LANE : (lane + 1) * LANE]
        rows = total_rows // count
        for mask in range(count):
            spot = pl.ds(pl.multiple_of((info_ref[2] ^ mask) * rows, rows), rows)
            tokens[mask][...] = sum_ref[spot, :].astype(BF)
        late = sum_ref[half:, :]
        early = sum_ref[:half, :] + jnp.where(split, late, 0.0)
        table_ref[:, :half] = early.T
        table_ref[:, half:] = jnp.where(split, 0.0, late).T
        counted = info_ref[3] > 0
        blocks_ref[: 2 * lanes, :] = joint_sums[: 2 * lanes, :]
        for row in range(2, plan.block_starts[-1] // lanes):
            for lane in range(lanes):
                blocks_ref[row * lanes + lane : row * lanes + lane + 1, :] = small_grad_ref[
                    row : row + 1, lane * LANE : (lane + 1) * LANE
                ]
        if plan.packed:
            for mask in range(plan.devices):
                shard = halves[mask & 1].at[plan.place(mask)]
                owner = info_ref[1] ^ mask
                own = aligned(owner, TILE)
                for piece in range(plan.table_pieces):
                    shard[piece * TILE : (piece + 1) * TILE, :] = table_ref[
                        own, piece * LANE : (piece + 1) * LANE
                    ].astype(BF)
                for piece in range(3 * lanes):
                    at = (plan.table_pieces + piece) * TILE
                    shard[at : at + TILE, :] = grad_ref[piece, own, :].astype(BF)
                rows = [
                    blocks_ref[pl.ds(plan.block_starts[v] + owner * plan.owned[v] // LANE, 1), :]
                    for v in range(VECTORS)
                ]
                rows.append(jnp.zeros((TILE - VECTORS, LANE), F32))
                at = plan.early_pieces * TILE
                shard[at : at + TILE, :] = jnp.concatenate(rows, axis=0).astype(BF)
        else:
            table_out[...] = jnp.where(counted, table_ref[...], 0.0).astype(BF)
            inward_out[...] = jnp.where(counted, grad_ref[...], 0.0).astype(BF)
            small_out[...] = jnp.where(counted, blocks_ref[...], 0.0)


def attend_back(plan, info, count, lifted, saved, mixed_back, inward, first_back, small_grad):
    query, key, value, mixed, totals = saved
    total_rows, width, lanes = plan.total_rows, plan.width, plan.lanes
    block = pl.BlockSpec((total_rows, LANE), lambda p, *_: (0, p))
    blocks = (plan.block_starts[-1], LANE)
    if plan.packed:
        grads = [like((plan.devices // 2, plan.early_rows, LANE), BF)] * 2
    else:
        grads = [like((width, total_rows), BF), like(inward.shape, BF), like(blocks, F32)]
    tokens = [like((total_rows // count, width), BF)] * count
    values = pl.pallas_call(
        functools.partial(attend_back_kernel, plan, count),
        grid_spec=pltpu.PrefetchScalarGridSpec(
            num_scalar_prefetch=1,
            grid=(lanes,),
            in_specs=[
                full(lifted.shape),
                block,
                block,
                block,
                block,
                block,
                pl.BlockSpec((1, 8, total_rows), lambda p, *_: (p, 0, 0)),
                full(inward.shape),
                full(first_back.shape),
                full(small_grad.shape),
            ],
            out_specs=[full(v.shape) for v in tokens + grads],
            scratch_shapes=[
                pltpu.VMEM((total_rows, 3 * width), BF),
                pltpu.VMEM((total_rows, width), F32),
                pltpu.VMEM((2, total_rows, total_rows), BF),
                pltpu.VMEM((2, total_rows, total_rows), BF),
                pltpu.VMEM(inward.shape, F32),
                pltpu.VMEM((width, total_rows), F32),
                pltpu.VMEM((8, LANE), F32),
                pltpu.VMEM(blocks, F32),
            ],
        ),
        out_shape=tokens + grads,
        compiler_params=params(60),
        cost_estimate=cost(14 * 10**9, 24 * 2**20, 6 * 10**6),
        name="attend_back",
    )(info, lifted, query, key, value, mixed, mixed_back, totals, inward, first_back, small_grad)
    return values[:count], values[count:]


def pack_early_kernel(plan, table_ref, inward_ref, *refs):
    vectors, out_ref = refs[:VECTORS], refs[VECTORS]
    for piece in range(plan.table_pieces):
        out_ref[piece * TILE : (piece + 1) * TILE, :] = table_ref[:, piece * LANE : (piece + 1) * LANE]
    for piece in range(3 * plan.lanes):
        at = (plan.table_pieces + piece) * TILE
        out_ref[at : at + TILE, :] = inward_ref[:, piece * LANE : (piece + 1) * LANE]
    rows = []
    for size, ref in zip(plan.owned, vectors):
        rows.append(jnp.concatenate([ref[...].astype(F32)] * (LANE // size), axis=1))
    rows.append(jnp.zeros((TILE - VECTORS, LANE), F32))
    at = plan.early_pieces * TILE
    out_ref[at : at + TILE, :] = jnp.concatenate(rows, axis=0).astype(BF)


def pack_early(plan, table, inward, vectors):
    values = [table, inward] + [v.reshape(1, -1) for v in vectors]
    return pl.pallas_call(
        functools.partial(pack_early_kernel, plan),
        out_shape=like((plan.early_rows, LANE), BF),
        name="pack_early",
    )(*values)


def pack_late_kernel(plan, outward_ref, expand_ref, contract_ref, out_ref):
    at = 0
    for ref in (outward_ref, expand_ref, contract_ref):
        rows = ref.shape[0]
        for lane in range(ref.shape[1] // LANE):
            out_ref[at : at + rows, :] = ref[:, lane * LANE : (lane + 1) * LANE]
            at += rows


def pack_late(plan, outward, expand, contract):
    return pl.pallas_call(
        functools.partial(pack_late_kernel, plan),
        out_shape=like((plan.late_rows, LANE), BF),
        name="pack_late",
    )(outward, expand, contract)


def fold_kernel(count, *refs):
    total = refs[0][...].astype(F32)
    for ref in refs[1:count]:
        total = total + ref[...].astype(F32)
    size = total.shape[0] // len(refs[count:])
    for index, ref in enumerate(refs[count:]):
        ref[...] = total[index * size : (index + 1) * size].astype(ref.dtype)


def fold(terms, cuts):
    entries, rows, _ = terms[0].shape
    pieces = 4 if rows % 64 == 0 else 3
    size = rows // pieces
    out = like((entries // cuts, rows, LANE), BF)
    return pl.pallas_call(
        functools.partial(fold_kernel, len(terms)),
        grid=(pieces,),
        in_specs=[pl.BlockSpec((entries, size, LANE), lambda i: (0, i, 0))] * len(terms),
        out_specs=[pl.BlockSpec((entries // cuts, size, LANE), lambda i: (0, i, 0))] * cuts,
        out_shape=[out] * cuts,
        cost_estimate=cost(10**6, len(terms) * entries * rows * LANE * 4),
        name="fold",
    )(*terms)


def finish_kernel(plan, count, info_ref, *refs):
    early, late, tokens = refs[:4], refs[4:8], refs[8 : 8 + count]
    (tokens_ref, table_ref, inward_ref, outward_ref, expand_ref, contract_ref) = refs[8 + count : 14 + count]
    vectors = refs[14 + count :]
    early = sum(ref[0].astype(F32) for ref in early)
    late = sum(ref[0].astype(F32) for ref in late)
    for mask in range(count):
        tokens_ref[pl.ds(info_ref[2] ^ mask, 1), :, :] = tokens[mask][...][None]
    for piece in range(plan.table_pieces):
        table_ref[:, piece * LANE : (piece + 1) * LANE] = early[piece * TILE : (piece + 1) * TILE]
    for piece in range(3 * plan.lanes):
        at = (plan.table_pieces + piece) * TILE
        inward_ref[:, piece * LANE : (piece + 1) * LANE] = early[at : at + TILE]
    at = 0
    for ref in (outward_ref, expand_ref, contract_ref):
        rows = ref.shape[0]
        for lane in range(ref.shape[1] // LANE):
            ref[:, lane * LANE : (lane + 1) * LANE] = late[at : at + rows]
            at += rows
    at = plan.early_pieces * TILE
    small = early[at : at + VECTORS]
    for vector, ref in enumerate(vectors):
        size = plan.owned[vector]
        slot = lax.rem(info_ref[1], LANE // size)
        row = pltpu.roll(small, LANE - slot * size, 1)
        ref[...] = row[vector : vector + 1, :size]


def finish(plan, info, micro_count, early, late, tokens):
    rows, width = tokens[0].shape
    own = plan.own_rows
    outs = [
        like((micro_count, rows, width), BF),
        like((own, plan.total_rows), F32),
        like((own, 3 * width), F32),
        like((own, width), F32),
        like((own, plan.hidden), F32),
        like((plan.hidden // plan.devices, width), F32),
    ] + [like((1, n), F32) for n in plan.owned]
    values = early + late + tokens
    return pl.pallas_call(
        functools.partial(finish_kernel, plan, len(tokens)),
        grid_spec=pltpu.PrefetchScalarGridSpec(
            num_scalar_prefetch=1,
            grid=(1,),
            in_specs=[full(v.shape) for v in values],
            out_specs=[full(v.shape) for v in outs],
        ),
        out_shape=outs,
        name="finish",
    )(info, *values)


def settle_kernel(count, share, info_ref, *refs):
    for mask in range(count):
        refs[count][pl.ds((info_ref[2] ^ mask) // share, 1), :, :] = refs[mask][...][None]


def settle_rows(info, micro_count, share, pieces):
    out = (micro_count,) + pieces[0].shape
    return pl.pallas_call(
        functools.partial(settle_kernel, len(pieces), share),
        grid_spec=pltpu.PrefetchScalarGridSpec(
            num_scalar_prefetch=1,
            grid=(1,),
            in_specs=[full(v.shape) for v in pieces],
            out_specs=full(out),
        ),
        out_shape=like(out, BF),
        name="settle_rows",
    )(info, *pieces)


def cut_kernel(count, share, rows_ref, *refs):
    rank = lax.axis_index("seq")
    for mask in range(count):
        refs[mask][...] = rows_ref[pl.ds((rank ^ mask) // share, 1), :, :][0]


def cut_rows(rows, count, share):
    outs = [like(rows.shape[1:], BF)] * count
    return pl.pallas_call(
        functools.partial(cut_kernel, count, share),
        out_shape=outs,
        cost_estimate=cost(0, 4 * 2**20),
        name="cut_rows",
    )(rows)


def local(tokens, first_length, cotangent, positions, inward, intake, outward, outlet, steady, offset,
          expand, spread, contract, settle, temper, anchor):
    micro_count, pack_count, block_rows, width = tokens.shape
    assert pack_count == 1
    devices, count = lax.axis_size(AXES), lax.axis_size("seq")
    me, rank = lax.axis_index(AXES), lax.axis_index("seq")
    share = max(count // micro_count, 1)
    assert share * micro_count == count
    plan = Plan(devices, width, contract.shape[0] * devices, block_rows * count)
    micro = rank // share
    firsts = jnp.where(jnp.arange(micro_count) == micro, first_length[:, 0], 0)
    counted = (rank % share == 0).astype(jnp.int32)
    info = jnp.stack([jnp.sum(firsts), me, rank, counted]).astype(jnp.int32)
    vectors = (intake, outlet, steady, offset, spread, settle, temper, anchor)

    def swap(value, mask):
        return lax.ppermute(value, AXES, [(d, d ^ mask) for d in range(devices)]) if mask else value

    def exchange(pieces):
        return [swap(piece, mask) for mask, piece in enumerate(pieces)]

    if plan.packed:
        shard = pack_early(plan, positions.T, inward, vectors)[None]
        late_shard = pack_late(plan, outward, expand, contract)
        rows_in = cut_rows(tokens[:, 0], count, share)
        shard, late_shard, rows_in = lax.optimization_barrier((shard, late_shard, rows_in))
        late = [lax.all_gather(late_shard, AXES, axis=0, tiled=False)]
        pieces = [swap(shard, k << 3) for k in range(4)]
        pieces, rows_in = lax.optimization_barrier((pieces, exchange(rows_in)))
        shard = jnp.concatenate(pieces, axis=0)
        pieces = [swap(shard, k << 1) for k in range(4)]
        upstreams = cut_rows(cotangent[:, 0], count, share)
        pieces, upstreams = lax.optimization_barrier((pieces, upstreams))
        shard = jnp.concatenate(pieces, axis=0)
        early = [shard, swap(shard, 1)]
        upstreams = exchange(upstreams)
    else:
        rows_in = exchange(cut_rows(tokens[:, 0], count, share))
        upstreams = exchange(cut_rows(cotangent[:, 0], count, share))
        early, late = plain_weights(plan, positions, inward, vectors, outward, expand, contract)
    lifted, query, key, value, mixed, totals, inward_all, small = attend(plan, info, rows_in, early)
    results, (mixed_back, first_back, small_grad), late_grads = feed(
        plan, info, lifted, mixed, upstreams, late, small
    )
    results = exchange(results)
    if plan.packed:
        keep, send = late_grads
        terms = fold([keep, swap(send, 1)], 4)
        terms, mixed_back = lax.optimization_barrier((terms, mixed_back))
        late_terms = [swap(term, k << 1) for k, term in enumerate(terms)]
    token_pieces, early_grads = attend_back(
        plan, info, count, lifted, (query, key, value, mixed, totals), mixed_back, inward_all,
        first_back, small_grad,
    )
    if plan.packed:
        late_terms, results, token_pieces, early_grads = lax.optimization_barrier(
            (late_terms, results, token_pieces, early_grads)
        )
        keep, send = early_grads
        send = swap(send, 1)
        late_terms = fold(late_terms, 4)
        output = settle_rows(info, micro_count, share, results)
        send, late_terms, output = lax.optimization_barrier((send, late_terms, output))
        terms = fold([keep, send], 4)
        terms, late_terms = lax.optimization_barrier((terms, late_terms))
        terms = [swap(term, k << 1) for k, term in enumerate(terms)]
        late_terms = [swap(term, k << 3) for k, term in enumerate(late_terms)]
        terms, late_terms, token_pieces = lax.optimization_barrier((terms, late_terms, token_pieces))
        token_pieces = exchange(token_pieces)
        terms = fold(terms, 4)
        early_terms = [swap(term, k << 3) for k, term in enumerate(terms)]
        values = finish(plan, info, micro_count, early_terms, late_terms, token_pieces)
        tokens_back, table_t, inward_own, outward_own, expand_own, contract_own = values[:6]
        own = [v.reshape(-1) for v in values[6:]]
        table_own = table_t.T
    else:
        output = settle_rows(info, micro_count, share, results)
        tokens_back = settle_rows(info, micro_count, share, exchange(token_pieces))
        table_own, inward_own, outward_own, expand_own, contract_own, own = plain_grads(
            plan, counted, early_grads, late_grads
        )
    return (output[:, None], tokens_back[:, None], table_own, inward_own, own[0], outward_own, own[1], own[2],
            own[3], expand_own, own[4], contract_own, own[5], own[6], own[7])


def plain_weights(plan, positions, inward, vectors, outward, expand, contract):
    lanes, width = plan.lanes, plan.width

    def gather(value, axis=0):
        return lax.all_gather(value, AXES, axis=axis, tiled=True)

    def in_pieces(value, size):
        return value.reshape(value.shape[0], -1, size).transpose(1, 0, 2)

    table = in_pieces(gather(positions, 1).T, LANE)
    small = jnp.concatenate([gather(v) for v in vectors]).astype(F32).reshape(-1, width)
    small = jnp.pad(small, ((0, plan.small_rows - small.shape[0]), (0, 0)))
    early = [table, in_pieces(gather(inward), LANE), small]
    return early, [gather(outward), in_pieces(gather(expand), width), gather(contract)]


def plain_grads(plan, counted, early_grads, late_grads):
    width = plan.width
    table, inward, small = early_grads
    outward, expand, contract = (jnp.where(counted > 0, g, BF(0)) for g in late_grads)

    def scatter(value, axis=0):
        return lax.psum_scatter(value, AXES, scatter_dimension=axis, tiled=True).astype(F32)

    def whole(value):
        return value.transpose(1, 0, 2).reshape(value.shape[1], -1)

    flat = small.reshape(-1)
    own = []
    for vector, length in enumerate(plan.lengths):
        start = plan.block_starts[vector] * LANE
        own.append(scatter(flat[start : start + length]))
    return (scatter(table.T, 1), scatter(whole(inward)), scatter(outward), scatter(whole(expand)),
            scatter(contract), own)


def solution(mesh):
    rows = P(None, "batch", "seq", None)
    table = P(None, AXES)
    matrix = P(AXES, None)
    vector = P(AXES)
    weights = (table, matrix, vector, matrix, vector, vector, vector, matrix, vector, matrix, vector,
               vector, vector)
    return jax.shard_map(
        local,
        mesh=mesh,
        in_specs=(rows, P(None, "batch"), rows) + weights,
        out_specs=(rows, rows) + weights,
        check_vma=False,
    )
```

```python
import functools

import jax
import jax.numpy as jnp
from jax import lax
from jax.experimental import pallas as pl
from jax.experimental.pallas import tpu as pltpu
from jax.sharding import PartitionSpec as P

AXES = ("batch", "seq")
LANE = 128
TILE = 16
FEED_ROWS = 512
STEP = 256
FAR = 1e30
BEND = 0.7978845608028654
BF = jnp.bfloat16
F32 = jnp.float32
VECTORS = 8


def times(left, right):
    return jnp.dot(left, right, preferred_element_type=F32)


def times_t(left, right):
    return lax.dot_general(left, right, (((1,), (1,)), ((), ())), preferred_element_type=F32)


def t_times(left, right):
    return lax.dot_general(left, right, (((0,), (0,)), ((), ())), preferred_element_type=F32)


def column_sum(values):
    return jnp.sum(values.astype(F32), axis=0, keepdims=True)


def aligned(index, size):
    return pl.ds(pl.multiple_of(index * size, size), size)


def like(shape, kind):
    return jax.ShapeDtypeStruct(shape, kind)


def full(shape):
    return pl.BlockSpec(shape, lambda *_: (0,) * len(shape), pipeline_mode=pl.Buffered(1))


def params(megabytes):
    return pltpu.CompilerParams(vmem_limit_bytes=megabytes * 2**20)


def cost(flops, size, exps=0):
    return pl.CostEstimate(flops=flops, bytes_accessed=size, transcendentals=exps)


class Plan:
    def __init__(self, devices, width, hidden, total_rows):
        self.devices = devices
        self.width = width
        self.hidden = hidden
        self.total_rows = total_rows
        self.own_rows = width // devices
        self.packed = devices == 32 and self.own_rows % TILE == 0
        self.lanes = width // LANE
        self.parts = hidden // width
        self.table_pieces = total_rows // LANE
        self.early_pieces = self.table_pieces + 3 * self.lanes
        self.early_rows = (self.early_pieces + 1) * TILE
        self.late_rows = (self.lanes + hidden // LANE) * TILE + self.lanes * (hidden // devices)
        lengths = [2 * width, width, width, width, hidden, width, width, width]
        self.lengths = lengths
        self.owned = [n // devices for n in lengths]
        self.small_rows = 16
        self.z_order = (0, 16, 8, 24)
        starts = [0]
        for n in lengths:
            starts.append(starts[-1] + n // LANE)
        self.block_starts = starts

    def place(self, mask):
        return ((mask >> 1) & 3) * 4 + self.z_order.index(mask & 24)

    def grad_piece(self, half, mask, at, rows):
        cut = self.late_rows // 2
        if at < cut:
            assert at + rows <= cut
            return half.at[self.place(mask), at : at + rows, :]
        swapped = (mask & ~6) | ((mask >> 1) & 2) | ((mask & 2) << 1)
        return half.at[16 + self.place(swapped), at - cut : at - cut + rows, :]


def fill_early(plan, me, halves, table_ref, inward_ref, small_ref, stage_ref):
    for mask in range(plan.devices):
        shard = halves[mask & 1].at[plan.place(mask)]
        owner = me ^ mask
        rows = aligned(owner, TILE)
        for piece in range(plan.table_pieces):
            table_ref[piece, rows, :] = shard[piece * TILE : (piece + 1) * TILE, :]
        for piece in range(3 * plan.lanes):
            at = plan.table_pieces + piece
            inward_ref[piece, rows, :] = shard[at * TILE : (at + 1) * TILE, :]
        at = plan.early_pieces * TILE
        stage_ref[pl.ds(owner, 1), :, :] = shard[at : at + TILE, :].astype(F32)[None]
    lane = lax.broadcasted_iota(jnp.int32, (1, LANE), 1)
    for vector, length in enumerate(plan.lengths):
        size = plan.owned[vector]
        group = LANE // size
        for block in range(length // LANE):
            row = jnp.zeros((1, LANE), F32)
            for index in range(group):
                own = stage_ref[block * group + index, vector : vector + 1, :]
                row = jnp.where(lane // size == index, own, row)
            at = plan.block_starts[vector] + block
            small_ref[at // plan.lanes : at // plan.lanes + 1, (at % plan.lanes) * LANE : (at % plan.lanes + 1) * LANE] = row


def own_lanes(value, head):
    lane = lax.broadcasted_iota(jnp.int32, value.shape, 1)
    return jnp.where((lane // (LANE // 2)) == head, value, jnp.zeros_like(value))


def causal():
    return lax.broadcasted_iota(jnp.int32, (STEP, STEP), 0) <= lax.broadcasted_iota(
        jnp.int32, (STEP, STEP), 1
    )


def attend_kernel(plan, count, info_ref, *refs):
    pieces, refs = refs[:count], refs[count:]
    if plan.packed:
        halves, refs = refs[:2], refs[2:]
    else:
        table_in, inward_in, small_in = refs[:3]
        refs = refs[3:]
    (lifted_ref, query_ref, key_ref, value_ref, mixed_ref, total_ref, inward_ref, small_ref) = refs[:8]
    low_ref, table_ref, place_ref, stage_ref = refs[8:]
    pair = pl.program_id(0)
    total_rows, width = plan.total_rows, plan.width
    half = total_rows // 2
    split = info_ref[0] < total_rows
    far = jnp.where(split, FAR, 0.0)

    @pl.when(pair == 0)
    def _():
        if plan.packed:
            fill_early(plan, info_ref[1], halves, table_ref, inward_ref, small_ref, stage_ref)
        else:
            table_ref[...] = table_in[...]
            inward_ref[...] = inward_in[...]
            small_ref[...] = small_in[...]
        eye = (
            lax.broadcasted_iota(jnp.int32, (half, half), 0)
            == lax.broadcasted_iota(jnp.int32, (half, half), 1)
        ).astype(BF)
        per_half = half // LANE
        for part in range(2):
            table = jnp.concatenate(
                [table_ref[part * per_half + i] for i in range(per_half)], axis=1
            )
            place_ref[part * half : (part + 1) * half, :] = times_t(eye, table)
        rows = total_rows // count
        for mask in range(count):
            start = (info_ref[2] ^ mask) * rows
            place = start - jnp.where(jnp.logical_and(split, start >= half), half, 0)
            lifted = pieces[mask][...].astype(F32) + place_ref[pl.ds(pl.multiple_of(place, rows), rows), :]
            spot = pl.ds(pl.multiple_of(start, rows), rows)
            lifted_ref[spot, :] = lifted
            low_ref[spot, :] = lifted.astype(BF)

    weights = jnp.concatenate([inward_ref[pair + i * plan.lanes] for i in range(3)], axis=1)
    lanes = aligned(pair, LANE)
    query_bias = small_ref[0:1, lanes]
    value_bias = small_ref[1:2, lanes]
    for block in range(total_rows // STEP):
        spot = slice(block * STEP, (block + 1) * STEP)
        joint = times(low_ref[spot, :], weights)
        query_ref[spot, :] = (joint[:, :LANE] + query_bias).astype(BF) * BF(0.125)
        key_ref[spot, :] = joint[:, LANE : 2 * LANE].astype(BF)
        value_ref[spot, :] = (joint[:, 2 * LANE :] + value_bias).astype(BF)

    keep = causal()
    lower = lax.broadcasted_iota(jnp.int32, (LANE, STEP), 0) < LANE // 2

    value_t = value_ref[...].T

    def logits_of(block, head):
        start = block * STEP
        other = half if start >= half else 0
        mine = own_lanes(query_ref[start : start + STEP, :], head)
        near = times_t(key_ref[start : start + STEP, :], mine)
        same = times_t(key_ref[other:start, :], mine) if start > other else None
        away = times_t(key_ref[:other, :], mine) if other else None
        return near, same, away

    def mixed_of(block, head, near, same, away):
        start = block * STEP
        other = half if start >= half else 0
        near = jnp.where(keep, near, -FAR)
        peak = jnp.max(near, axis=0, keepdims=True)
        if same is not None:
            peak = jnp.maximum(peak, jnp.max(same, axis=0, keepdims=True))
        if away is not None:
            peak = jnp.maximum(peak, jnp.max(away, axis=0, keepdims=True) - far)
        raised = [jnp.exp(piece - peak) for piece in (same, near) if piece is not None]
        total = sum(jnp.sum(piece, axis=0, keepdims=True) for piece in raised)
        low = jnp.concatenate([piece.astype(BF) for piece in raised], axis=0)
        mixed = times(value_t[:, other : start + STEP], low)
        if away is not None:
            away = jnp.exp(away - (peak + far))
            total = total + jnp.sum(away, axis=0, keepdims=True)
            mixed = mixed + times(value_t[:, :other], away.astype(BF))
        total_ref[0, head : head + 1, start : start + STEP] = peak + jnp.log(total)
        return mixed * (1.0 / total)

    tasks = [(block, head) for block in range(total_rows // STEP) for head in range(2)]
    ahead = logits_of(*tasks[0])
    parts = []
    for index, (block, head) in enumerate(tasks):
        logits, ahead = ahead, logits_of(*tasks[index + 1]) if index + 1 < len(tasks) else None
        parts.append(mixed_of(block, head, *logits))
        if head:
            mixed_ref[block * STEP : (block + 1) * STEP, :] = jnp.where(lower, *parts).T.astype(BF)
            parts = []


def attend(plan, info, count, pieces, weights):
    total_rows, width = plan.total_rows, plan.width
    block = pl.BlockSpec((total_rows, LANE), lambda p, *_: (0, p))
    low = pltpu.HBM((total_rows, width), BF)
    inward = (3 * plan.lanes, width, LANE)
    small = (plan.small_rows, width)
    return pl.pallas_call(
        functools.partial(attend_kernel, plan, count),
        grid_spec=pltpu.PrefetchScalarGridSpec(
            num_scalar_prefetch=1,
            grid=(plan.lanes,),
            in_specs=[full(v.shape) for v in pieces + weights],
            out_specs=[
                full((total_rows, width)),
                block,
                block,
                block,
                block,
                pl.BlockSpec((1, 8, total_rows), lambda p, *_: (p, 0, 0)),
                full(inward),
                full(small),
            ],
            scratch_shapes=[
                pltpu.VMEM((total_rows, width), BF),
                pltpu.VMEM((plan.table_pieces, width, LANE), BF),
                pltpu.VMEM((total_rows, width), F32),
                pltpu.VMEM((plan.devices, TILE, LANE), F32),
            ],
        ),
        out_shape=[
            pltpu.HBM((total_rows, width), F32),
            low,
            low,
            low,
            low,
            pltpu.HBM((plan.lanes, 8, total_rows), F32),
            pltpu.HBM(inward, BF),
            pltpu.HBM(small, F32),
        ],
        compiler_params=params(36),
        cost_estimate=cost(5 * 10**9, 14 * 2**20, 6 * 10**6),
        name="attend",
    )(info, *pieces, *weights)


def norm(rows):
    center = rows - jnp.mean(rows, axis=1, keepdims=True)
    root = lax.rsqrt(jnp.mean(center * center, axis=1, keepdims=True) + 1e-05)
    return center * root, root


def norm_back(upstream, gain, unit, root):
    scaled = upstream * gain
    mean = jnp.mean(scaled, axis=1, keepdims=True)
    slope = jnp.mean(scaled * unit, axis=1, keepdims=True)
    return (scaled - mean - unit * slope) * root


def feed_kernel(plan, count, info_ref, lifted_ref, mixed_ref, *refs):
    upstreams, refs = refs[:count], refs[count:]
    if plan.packed:
        late_halves, small_ref = refs[:2], refs[2]
        refs = refs[3:]
    else:
        outward_in, expand_in, contract_in, small_ref = refs[:4]
        refs = refs[4:]
    results, refs = refs[:count], refs[count:]
    mixed_back_ref, first_back_ref, small_grad_ref = refs[:3]
    refs = refs[3:]
    if plan.packed:
        halves, refs = refs[:2], refs[2:]
    else:
        outward_out, expand_out, contract_out = refs[:3]
        refs = refs[3:]
    (outward_ref, expand_ref, contract_ref, upstream_ref, result_ref, slope_ref, active_all, hidden_all, normed_all,
     lowered_all, branch_all, mixed_all, whole_ref, expand_sum, contract_sum) = refs
    step = pl.program_id(0)
    width, parts, lanes = plan.width, plan.parts, plan.lanes
    contract_own = plan.hidden // plan.devices
    contract_at = (lanes + parts * lanes) * TILE

    @pl.when(step == 0)
    def _():
        if plan.packed:
            for mask in range(plan.devices):
                shard = late_halves[mask & 1].at[plan.place(mask)]
                owner = info_ref[1] ^ mask
                rows, wide = aligned(owner, TILE), aligned(owner, contract_own)
                for lane in range(lanes):
                    cut = slice(lane * LANE, (lane + 1) * LANE)
                    outward_ref[rows, cut] = shard[lane * TILE : (lane + 1) * TILE, :]
                    for part in range(parts):
                        at = (lanes + part * lanes + lane) * TILE
                        expand_ref[part, rows, cut] = shard[at : at + TILE, :]
                    at = contract_at + lane * contract_own
                    contract_ref[wide, cut] = shard[at : at + contract_own, :]
        else:
            outward_ref[...] = outward_in[...]
            expand_ref[...] = expand_in[...]
            contract_ref[...] = contract_in[...]

    size = lifted_ref.shape[0]
    here = pl.ds(pl.multiple_of(step * size, size), size)
    rows = plan.total_rows // count
    group = size // rows

    def spot(mask):
        return pl.ds(pl.multiple_of(((info_ref[2] ^ mask) % group) * rows, rows), rows)

    for mask in range(count):
        @pl.when(step == mask // group)
        def _(mask=mask):
            upstream_ref[spot(mask), :] = upstreams[mask][...]

    outlet, steady, offset = (small_ref[i : i + 1, :] for i in (2, 3, 4))
    settle, temper, anchor = (small_ref[i + parts : i + parts + 1, :] for i in (5, 6, 7))
    mixed = mixed_ref[...]
    branch = times(mixed, outward_ref[...]) + outlet
    unit, root = norm(lifted_ref[...] + branch)
    normed = unit * steady + offset
    normed_low = normed.astype(BF)
    normed_all[here, :] = normed_low
    mixed_all[here, :] = mixed
    lowered = jnp.zeros_like(normed)
    for part in range(parts):
        cut = slice(part * width, (part + 1) * width)
        hidden = times(normed_low, expand_ref[part]) + small_ref[5 + part : 6 + part, :]
        square = hidden * hidden
        bend = jnp.tanh(hidden * (BEND + BEND * 0.044715 * square))
        half = 0.5 + 0.5 * bend
        active = (hidden * half).astype(BF)
        active_all[here, cut] = active
        slope_ref[:, cut] = half + (0.5 * hidden) * (1.0 - bend * bend) * (
            BEND + 3 * BEND * 0.044715 * square
        )
        lowered = lowered + times(active, contract_ref[cut, :])
    last_unit, last_root = norm(normed + (lowered + settle))
    result_ref[...] = (last_unit * temper + anchor).astype(BF)
    upstream = upstream_ref[...].astype(F32)
    temper_grad = column_sum(upstream * last_unit)
    anchor_grad = column_sum(upstream)
    second_back = norm_back(upstream, temper, last_unit, last_root)
    lowered_back = second_back.astype(BF)
    lowered_all[here, :] = lowered_back
    settle_grad = column_sum(lowered_back)
    normed_back = second_back
    spread_grads = []
    for part in range(parts):
        cut = slice(part * width, (part + 1) * width)
        active_back = times_t(lowered_back, contract_ref[cut, :])
        hidden_back = (active_back * slope_ref[:, cut]).astype(BF)
        spread_grads.append(column_sum(hidden_back))
        hidden_all[here, cut] = hidden_back
        normed_back = normed_back + times_t(hidden_back, expand_ref[part])
    first_back = norm_back(normed_back, steady, unit, root)
    first_back_ref[...] = first_back
    branch_back = first_back.astype(BF)
    mixed_back_ref[...] = times_t(branch_back, outward_ref[...]).astype(BF)
    branch_all[here, :] = branch_back
    zero = jnp.zeros_like(anchor_grad)
    grads = [zero, zero, column_sum(branch_back), column_sum(normed_back * unit)]
    grads += [column_sum(normed_back)] + spread_grads + [settle_grad, temper_grad, anchor_grad]
    grads += [zero] * (plan.small_rows - len(grads))
    small_term = jnp.concatenate(grads, axis=0)
    for mask in range(count):
        @pl.when(step == mask // group)
        def _(mask=mask):
            results[mask][...] = result_ref[spot(mask), :]

    @pl.when(step == 0)
    def _():
        small_grad_ref[...] = small_term

    @pl.when(step > 0)
    def _():
        small_grad_ref[...] += small_term

    @pl.when(step == pl.num_programs(0) - 1)
    def _():
        outward = t_times(mixed_all[...], branch_all[...])
        if plan.packed:
            me = info_ref[1]
            whole_ref[...] = outward
            for mask in range(plan.devices):
                half = halves[mask & 1]
                rows = aligned(me ^ mask, TILE)
                for lane in range(lanes):
                    cut = slice(lane * LANE, (lane + 1) * LANE)
                    plan.grad_piece(half, mask, lane * TILE, TILE)[...] = whole_ref[rows, cut].astype(BF)
        else:
            outward_out[...] = outward.astype(BF)
        per_part = plan.devices // parts
        for part in range(parts):
            cut = slice(part * width, (part + 1) * width)
            expand = t_times(normed_all[...], hidden_all[:, cut])
            if not plan.packed:
                expand_out[part] = expand.astype(BF)
                continue
            expand_sum[...] = expand
            for mask in range(plan.devices):
                rows = aligned(me ^ mask, TILE)
                for lane in range(lanes):
                    at = (lanes + part * lanes + lane) * TILE
                    plan.grad_piece(halves[mask & 1], mask, at, TILE)[...] = expand_sum[
                        rows, lane * LANE : (lane + 1) * LANE
                    ].astype(BF)
        for mask_part in range(parts):
            part = (me // per_part) ^ mask_part if plan.packed else mask_part
            cut = pl.ds(pl.multiple_of(part * width, width), width)
            contract = t_times(active_all[:, cut], lowered_all[...])
            if not plan.packed:
                contract_out[cut, :] = contract.astype(BF)
                continue
            contract_sum[...] = contract
            for index in range(per_part):
                mask = mask_part * per_part + index
                rows = aligned((me ^ mask) % per_part, contract_own)
                for lane in range(lanes):
                    at = contract_at + lane * contract_own
                    plan.grad_piece(halves[mask & 1], mask, at, contract_own)[...] = contract_sum[
                        rows, lane * LANE : (lane + 1) * LANE
                    ].astype(BF)


def feed(plan, info, count, lifted, mixed, upstreams, weights, small):
    total_rows, width, parts = plan.total_rows, plan.width, plan.parts
    piece = total_rows // count
    size = max(piece, FEED_ROWS)
    group = size // piece
    rows = pl.BlockSpec((size, width), lambda i, info: ((info[2] // group) ^ i, 0))
    outward, expand, contract = (width, width), (parts, width, width), (parts * width, width)
    if plan.packed:
        grads = [like((plan.devices, plan.late_rows // 2, LANE), BF)] * 2
    else:
        grads = [like(outward, BF), like(expand, BF), like(contract, BF)]
    ends = [like((piece, width), BF)] * count
    outs = [like((total_rows, width), BF), like((total_rows, width), F32), like(small.shape, F32)]
    values = pl.pallas_call(
        functools.partial(feed_kernel, plan, count),
        grid_spec=pltpu.PrefetchScalarGridSpec(
            num_scalar_prefetch=1,
            grid=(total_rows // size,),
            in_specs=[rows, rows] + [full(v.shape) for v in upstreams + weights + [small]],
            out_specs=[full(v.shape) for v in ends]
            + [rows, rows, full(small.shape)]
            + [full(v.shape) for v in grads],
            scratch_shapes=[
                pltpu.VMEM(outward, BF),
                pltpu.VMEM(expand, BF),
                pltpu.VMEM(contract, BF),
                pltpu.VMEM((size, width), BF),
                pltpu.VMEM((size, width), BF),
                pltpu.VMEM((size, parts * width), F32),
                pltpu.VMEM((total_rows, parts * width), BF),
                pltpu.VMEM((total_rows, parts * width), BF),
                pltpu.VMEM((total_rows, width), BF),
                pltpu.VMEM((total_rows, width), BF),
                pltpu.VMEM((total_rows, width), BF),
                pltpu.VMEM((total_rows, width), BF),
                pltpu.VMEM(outward, F32),
                pltpu.VMEM(outward, F32),
                pltpu.VMEM(outward, F32),
            ],
        ),
        out_shape=ends + outs + grads,
        compiler_params=params(60),
        cost_estimate=cost(15 * 10**9, 20 * 2**20, 2 * 10**6),
        name="feed",
    )(info, lifted, mixed, *upstreams, *weights, small)
    return values[:count], values[count : count + 3], values[count + 3 :]


def attend_back_kernel(
    plan, count, info_ref, lifted_ref, query_ref, key_ref, value_ref, mixed_ref, mixed_back_ref,
    total_ref, inward_ref, first_back_ref, small_grad_ref, *refs
):
    tokens, refs = refs[:count], refs[count:]
    if plan.packed:
        halves, refs = refs[:2], refs[2:]
    else:
        table_out, inward_out, small_out = refs[:3]
        refs = refs[3:]
    joint_ref, sum_ref, share_ref, score_ref, grad_ref, table_ref, joint_sums, blocks_ref = refs
    pair = pl.program_id(0)
    total_rows, lanes = plan.total_rows, plan.lanes
    half = total_rows // 2
    split = info_ref[0] < total_rows
    far = jnp.where(split, FAR, 0.0)
    blocks = total_rows // STEP

    keep = causal()
    lower = lax.broadcasted_iota(jnp.int32, (STEP, LANE), 1) < LANE // 2
    lower_t = lax.broadcasted_iota(jnp.int32, (LANE, STEP), 0) < LANE // 2
    product = (mixed_ref[...].astype(F32) * mixed_back_ref[...].astype(F32)).T
    scaled_key = (key_ref[...] * BF(0.125)).T
    betweens = [
        jnp.sum(product[head * LANE // 2 : (head + 1) * LANE // 2], axis=0, keepdims=True)
        for head in range(2)
    ]

    def logits_of(block, head):
        spot = slice(block * STEP, (block + 1) * STEP)
        keys = slice(0, (block + 1) * STEP)
        query = own_lanes(query_ref[spot, :], head)
        back = own_lanes(mixed_back_ref[spot, :], head)
        return times_t(key_ref[keys, :], query), times_t(value_ref[keys, :], back)

    def scores_of(block, head, logits, share_back):
        start = block * STEP
        spot = slice(start, start + STEP)
        total = total_ref[0, head : head + 1, spot]
        gap = betweens[head][:, spot]
        for under in range(block + 1):
            keys = slice(under * STEP, (under + 1) * STEP)
            away = start >= half and under * STEP < half
            share = jnp.exp(logits[keys] - (total + far if away else total))
            if under == block:
                share = jnp.where(keep, share, 0.0)
            score = share * (share_back[keys] - gap)
            share_ref[head, keys, spot] = share.astype(BF)
            score_ref[head, keys, spot] = score.astype(BF)

    def backs_of(block, head):
        start = block * STEP
        spot = slice(start, start + STEP)
        end = start + STEP
        query_back = times(scaled_key[:, :end], score_ref[head, :end, spot])
        key_back = times(score_ref[head, spot, start:], query_ref[start:, :])
        value_back = times(share_ref[head, spot, start:], mixed_back_ref[start:, :])
        return query_back, key_back, value_back

    tasks = [(block, head) for block in reversed(range(blocks)) for head in range(2)]
    ahead = logits_of(*tasks[0])
    parts = []
    for index, (block, head) in enumerate(tasks):
        logits, ahead = ahead, logits_of(*tasks[index + 1]) if index + 1 < len(tasks) else None
        scores_of(block, head, *logits)
        parts.append(backs_of(block, head))
        if head:
            spot = slice(block * STEP, (block + 1) * STEP)
            query_back = jnp.where(lower_t, parts[0][0], parts[1][0]).T
            key_back = jnp.where(lower, parts[0][1], parts[1][1])
            value_back = jnp.where(lower, parts[0][2], parts[1][2])
            for part, back in enumerate((query_back, key_back, value_back)):
                joint_ref[spot, aligned(pair + part * lanes, LANE)] = back.astype(BF)
            parts = []

    @pl.when(pair == lanes - 1)
    def _():
        low = lifted_ref[...].astype(BF).T
        weights = jnp.concatenate([inward_ref[i] for i in range(3 * lanes)], axis=1)
        for block in range(blocks):
            spot = slice(block * STEP, (block + 1) * STEP)
            sum_ref[spot, :] = first_back_ref[spot, :] + times_t(joint_ref[spot, :], weights)
        for part in range(3):
            joint = joint_ref[:, part * plan.width : (part + 1) * plan.width]
            grads = times(low, joint)
            for lane in range(lanes):
                grad_ref[part * lanes + lane] = grads[:, lane * LANE : (lane + 1) * LANE]
            if part != 1:
                sums = column_sum(joint)
                for lane in range(lanes):
                    at = lane if part == 0 else lane + lanes
                    joint_sums[at : at + 1, :] = sums[:, lane * LANE : (lane + 1) * LANE]
        rows = total_rows // count
        for mask in range(count):
            spot = pl.ds(pl.multiple_of((info_ref[2] ^ mask) * rows, rows), rows)
            tokens[mask][...] = sum_ref[spot, :].astype(BF)
        late = sum_ref[half:, :]
        early = sum_ref[:half, :] + jnp.where(split, late, 0.0)
        table_ref[:, :half] = early.T
        table_ref[:, half:] = jnp.where(split, 0.0, late).T
        counted = info_ref[3] > 0
        blocks_ref[: 2 * lanes, :] = joint_sums[: 2 * lanes, :]
        for row in range(2, plan.block_starts[-1] // lanes):
            for lane in range(lanes):
                blocks_ref[row * lanes + lane : row * lanes + lane + 1, :] = small_grad_ref[
                    row : row + 1, lane * LANE : (lane + 1) * LANE
                ]
        if plan.packed:
            for mask in range(plan.devices):
                shard = halves[mask & 1].at[plan.place(mask)]
                owner = info_ref[1] ^ mask
                own = aligned(owner, TILE)
                for piece in range(plan.table_pieces):
                    shard[piece * TILE : (piece + 1) * TILE, :] = table_ref[
                        own, piece * LANE : (piece + 1) * LANE
                    ].astype(BF)
                for piece in range(3 * lanes):
                    at = (plan.table_pieces + piece) * TILE
                    shard[at : at + TILE, :] = grad_ref[piece, own, :].astype(BF)
                rows = [
                    blocks_ref[pl.ds(plan.block_starts[v] + owner * plan.owned[v] // LANE, 1), :]
                    for v in range(VECTORS)
                ]
                rows.append(jnp.zeros((TILE - VECTORS, LANE), F32))
                at = plan.early_pieces * TILE
                shard[at : at + TILE, :] = jnp.concatenate(rows, axis=0).astype(BF)
        else:
            table_out[...] = jnp.where(counted, table_ref[...], 0.0).astype(BF)
            inward_out[...] = jnp.where(counted, grad_ref[...], 0.0).astype(BF)
            small_out[...] = jnp.where(counted, blocks_ref[...], 0.0)


def attend_back(plan, info, count, lifted, saved, mixed_back, inward, first_back, small_grad):
    query, key, value, mixed, totals = saved
    total_rows, width, lanes = plan.total_rows, plan.width, plan.lanes
    block = pl.BlockSpec((total_rows, LANE), lambda p, *_: (0, p))
    blocks = (plan.block_starts[-1], LANE)
    if plan.packed:
        grads = [like((plan.devices // 2, plan.early_rows, LANE), BF)] * 2
    else:
        grads = [like((width, total_rows), BF), like(inward.shape, BF), like(blocks, F32)]
    tokens = [like((total_rows // count, width), BF)] * count
    values = pl.pallas_call(
        functools.partial(attend_back_kernel, plan, count),
        grid_spec=pltpu.PrefetchScalarGridSpec(
            num_scalar_prefetch=1,
            grid=(lanes,),
            in_specs=[
                full(lifted.shape),
                block,
                block,
                block,
                block,
                block,
                pl.BlockSpec((1, 8, total_rows), lambda p, *_: (p, 0, 0)),
                full(inward.shape),
                full(first_back.shape),
                full(small_grad.shape),
            ],
            out_specs=[full(v.shape) for v in tokens + grads],
            scratch_shapes=[
                pltpu.VMEM((total_rows, 3 * width), BF),
                pltpu.VMEM((total_rows, width), F32),
                pltpu.VMEM((2, total_rows, total_rows), BF),
                pltpu.VMEM((2, total_rows, total_rows), BF),
                pltpu.VMEM(inward.shape, F32),
                pltpu.VMEM((width, total_rows), F32),
                pltpu.VMEM((8, LANE), F32),
                pltpu.VMEM(blocks, F32),
            ],
        ),
        out_shape=tokens + grads,
        compiler_params=params(44),
        cost_estimate=cost(14 * 10**9, 24 * 2**20, 6 * 10**6),
        name="attend_back",
    )(info, lifted, query, key, value, mixed, mixed_back, totals, inward, first_back, small_grad)
    return values[:count], values[count:]


def pack_early_kernel(plan, table_ref, inward_ref, *refs):
    vectors, out_ref = refs[:VECTORS], refs[VECTORS]
    for piece in range(plan.table_pieces):
        out_ref[piece * TILE : (piece + 1) * TILE, :] = table_ref[:, piece * LANE : (piece + 1) * LANE]
    for piece in range(3 * plan.lanes):
        at = (plan.table_pieces + piece) * TILE
        out_ref[at : at + TILE, :] = inward_ref[:, piece * LANE : (piece + 1) * LANE]
    rows = []
    for size, ref in zip(plan.owned, vectors):
        rows.append(jnp.concatenate([ref[...].astype(F32)] * (LANE // size), axis=1))
    rows.append(jnp.zeros((TILE - VECTORS, LANE), F32))
    at = plan.early_pieces * TILE
    out_ref[at : at + TILE, :] = jnp.concatenate(rows, axis=0).astype(BF)


def pack_early(plan, table, inward, vectors):
    values = [table, inward] + [v.reshape(1, -1) for v in vectors]
    return pl.pallas_call(
        functools.partial(pack_early_kernel, plan),
        out_shape=like((plan.early_rows, LANE), BF),
        name="pack_early",
    )(*values)


def pack_late_kernel(plan, outward_ref, expand_ref, contract_ref, out_ref):
    at = 0
    for ref in (outward_ref, expand_ref, contract_ref):
        rows = ref.shape[0]
        for lane in range(ref.shape[1] // LANE):
            out_ref[at : at + rows, :] = ref[:, lane * LANE : (lane + 1) * LANE]
            at += rows


def pack_late(plan, outward, expand, contract):
    return pl.pallas_call(
        functools.partial(pack_late_kernel, plan),
        out_shape=like((plan.late_rows, LANE), BF),
        name="pack_late",
    )(outward, expand, contract)


def fold(terms, cuts):
    size = terms[0].shape[0] // cuts
    return [
        sum(term[index * size : (index + 1) * size].astype(F32) for term in terms).astype(BF)
        for index in range(cuts)
    ]


def finish_kernel(plan, info_ref, *refs):
    early, late, refs = refs[:4], refs[4:8], refs[8:]
    table_ref, inward_ref, outward_ref, expand_ref, contract_ref = refs[:5]
    vectors = refs[5:]
    early = sum(ref[0].astype(F32) for ref in early)
    late = sum(ref[0].astype(F32) for ref in late)
    for piece in range(plan.table_pieces):
        table_ref[:, piece * LANE : (piece + 1) * LANE] = early[piece * TILE : (piece + 1) * TILE]
    for piece in range(3 * plan.lanes):
        at = (plan.table_pieces + piece) * TILE
        inward_ref[:, piece * LANE : (piece + 1) * LANE] = early[at : at + TILE]
    at = 0
    for ref in (outward_ref, expand_ref, contract_ref):
        rows = ref.shape[0]
        for lane in range(ref.shape[1] // LANE):
            ref[:, lane * LANE : (lane + 1) * LANE] = late[at : at + rows]
            at += rows
    at = plan.early_pieces * TILE
    small = early[at : at + VECTORS]
    for vector, ref in enumerate(vectors):
        size = plan.owned[vector]
        slot = lax.rem(info_ref[1], LANE // size)
        row = pltpu.roll(small, LANE - slot * size, 1)
        ref[...] = row[vector : vector + 1, :size]


def finish(plan, info, early, late):
    own, width = plan.own_rows, plan.width
    outs = [
        like((own, plan.total_rows), F32),
        like((own, 3 * width), F32),
        like((own, width), F32),
        like((own, plan.hidden), F32),
        like((plan.hidden // plan.devices, width), F32),
    ] + [like((1, n), F32) for n in plan.owned]
    values = early + late
    return pl.pallas_call(
        functools.partial(finish_kernel, plan),
        grid_spec=pltpu.PrefetchScalarGridSpec(
            num_scalar_prefetch=1,
            grid=(1,),
            in_specs=[full(v.shape) for v in values],
            out_specs=[full(v.shape) for v in outs],
        ),
        out_shape=outs,
        name="finish",
    )(info, *values)


def ordered(rank, pieces):
    for bit in (1, 2):
        flip = (rank & bit) > 0
        pieces = [jnp.where(flip, pieces[i ^ bit], pieces[i]) for i in range(4)]
    return jnp.stack(pieces)


def settle_kernel(count, share, info_ref, *refs):
    for mask in range(count):
        refs[count][pl.ds((info_ref[2] ^ mask) // share, 1), :, :] = refs[mask][...][None]


def settle_rows(info, micro_count, share, pieces):
    out = (micro_count,) + pieces[0].shape
    return pl.pallas_call(
        functools.partial(settle_kernel, len(pieces), share),
        grid_spec=pltpu.PrefetchScalarGridSpec(
            num_scalar_prefetch=1,
            grid=(1,),
            in_specs=[full(v.shape) for v in pieces],
            out_specs=full(out),
        ),
        out_shape=like(out, BF),
        name="settle_rows",
    )(info, *pieces)


def cut_kernel(count, share, rows_ref, *refs):
    rank = lax.axis_index("seq")
    for mask in range(count):
        refs[mask][...] = rows_ref[pl.ds((rank ^ mask) // share, 1), :, :][0]


def cut_rows(rows, count, share):
    outs = [like(rows.shape[1:], BF)] * count
    return pl.pallas_call(
        functools.partial(cut_kernel, count, share),
        out_shape=outs,
        cost_estimate=cost(0, 4 * 2**20),
        name="cut_rows",
    )(rows)


def local(tokens, first_length, cotangent, positions, inward, intake, outward, outlet, steady, offset,
          expand, spread, contract, settle, temper, anchor):
    micro_count, pack_count, block_rows, width = tokens.shape
    assert pack_count == 1
    devices, count = lax.axis_size(AXES), lax.axis_size("seq")
    me, rank = lax.axis_index(AXES), lax.axis_index("seq")
    share = max(count // micro_count, 1)
    assert share * micro_count == count
    plan = Plan(devices, width, contract.shape[0] * devices, block_rows * count)
    micro = rank // share
    firsts = jnp.where(jnp.arange(micro_count) == micro, first_length[:, 0], 0)
    counted = (rank % share == 0).astype(jnp.int32)
    info = jnp.stack([jnp.sum(firsts), me, rank, counted]).astype(jnp.int32)
    vectors = (intake, outlet, steady, offset, spread, settle, temper, anchor)

    def swap(value, mask):
        return lax.ppermute(value, AXES, [(d, d ^ mask) for d in range(devices)]) if mask else value

    def exchange(pieces):
        return [swap(piece, mask) for mask, piece in enumerate(pieces)]

    def in_order(pieces):
        if count != 4 or share != 1:
            return settle_rows(info, micro_count, share, pieces)
        return ordered(rank, pieces)

    if plan.packed:
        rows_in = cut_rows(tokens[:, 0], count, share)
        rows_in, inward = lax.optimization_barrier((rows_in, inward))
        rows_in = exchange(rows_in)
        shard = pack_early(plan, positions.T, inward, vectors)[None]
        shard, rows_in[1], outward = lax.optimization_barrier((shard, rows_in[1], outward))
        pieces = [swap(shard, mask) for mask in plan.z_order]
        late = pack_late(plan, outward, expand, contract)[None]
        pieces, rows_in, info, late, cotangent = lax.optimization_barrier(
            (pieces, rows_in, info, late, cotangent)
        )
        shard = jnp.concatenate(pieces, axis=0)
        pieces = [swap(shard, k << 1) for k in range(4)]
        late = [swap(late, mask) for mask in plan.z_order]
        upstreams = cut_rows(cotangent[:, 0], count, share)
        pieces, upstreams, late = lax.optimization_barrier((pieces, list(upstreams), late))
        late = jnp.concatenate(late, axis=0)
        late_x, late_y = swap(late, 2), swap(late, 4)
        shard = jnp.concatenate(pieces, axis=0)
        early = [shard, swap(shard, 1)]
        upstreams[1] = swap(upstreams[1], 1)
        early, late_x, late_y, upstreams = lax.optimization_barrier((early, late_x, late_y, upstreams))
        late_xy = swap(late_x, 4)
        upstreams[2:] = [swap(upstreams[mask], mask) for mask in (2, 3)]
    else:
        rows_in = exchange(cut_rows(tokens[:, 0], count, share))
        upstreams = exchange(cut_rows(cotangent[:, 0], count, share))
        early, late = plain_weights(plan, positions, inward, vectors, outward, expand, contract)
    lifted, query, key, value, mixed, totals, inward_all, small = attend(plan, info, count, rows_in, early)
    if plan.packed:
        late_xy, upstreams, mixed = lax.optimization_barrier((late_xy, upstreams, mixed))
        late = jnp.concatenate([late, late_x, late_y, late_xy], axis=0)
        late = [late, swap(late, 1)]
    results, (mixed_back, first_back, small_grad), late_grads = feed(
        plan, info, count, lifted, mixed, upstreams, late, small
    )
    results = exchange(results)
    if plan.packed:
        keep, send = late_grads
        one, one_send, two, two_send = fold([keep, swap(send, 1)], 4)
        one, one_send, two, two_send, mixed_back = lax.optimization_barrier(
            (one, one_send, two, two_send, mixed_back)
        )
        one_other, two_other = swap(one_send, 4), swap(two_send, 2)
    token_pieces, early_grads = attend_back(
        plan, info, count, lifted, (query, key, value, mixed, totals), mixed_back, inward_all,
        first_back, small_grad,
    )
    if plan.packed:
        one_other, two_other, results, token_pieces, early_grads = lax.optimization_barrier(
            (one_other, two_other, results, token_pieces, early_grads)
        )
        keep, send = early_grads
        send = swap(send, 1)
        one, one_send = fold([one, one_other], 2)
        two, two_send = fold([two, two_other], 2)
        one, one_send, two, two_send, keep = lax.optimization_barrier((one, one_send, two, two_send, keep))
        one_other, two_other = swap(one_send, 2), swap(two_send, 4)
        terms = fold([keep, send], 4)
        terms, results, token_pieces = lax.optimization_barrier((terms, results, token_pieces))
        terms = [swap(term, k << 1) for k, term in enumerate(terms)]
        one_other, two_other, terms[2], results = lax.optimization_barrier(
            (one_other, two_other, terms[2], results)
        )
        ones, twos = fold([one, one_other], 4), fold([two, two_other], 4)
        late_terms = [jnp.concatenate(pair, axis=1) for pair in zip(ones, twos)]
        late_terms = [swap(term, mask) for term, mask in zip(late_terms, plan.z_order)]
        output = in_order(results)
        terms, late_terms, output, token_pieces = lax.optimization_barrier(
            (terms, late_terms, output, token_pieces)
        )
        terms = fold(terms, 4)
        early_terms = [swap(term, mask) for term, mask in zip(terms, plan.z_order)]
        tokens_back = in_order(exchange(token_pieces))
        values = finish(plan, info, early_terms, late_terms)
        table_t, inward_own, outward_own, expand_own, contract_own = values[:5]
        own = [v.reshape(-1) for v in values[5:]]
        table_own = table_t.T
    else:
        output = in_order(results)
        tokens_back = in_order(exchange(token_pieces))
        table_own, inward_own, outward_own, expand_own, contract_own, own = plain_grads(
            plan, counted, early_grads, late_grads
        )
    return (output[:, None], tokens_back[:, None], table_own, inward_own, own[0], outward_own, own[1], own[2],
            own[3], expand_own, own[4], contract_own, own[5], own[6], own[7])


def plain_weights(plan, positions, inward, vectors, outward, expand, contract):
    lanes, width = plan.lanes, plan.width

    def gather(value, axis=0):
        return lax.all_gather(value, AXES, axis=axis, tiled=True)

    def in_pieces(value, size):
        return value.reshape(value.shape[0], -1, size).transpose(1, 0, 2)

    table = in_pieces(gather(positions, 1).T, LANE)
    small = jnp.concatenate([gather(v) for v in vectors]).astype(F32).reshape(-1, width)
    small = jnp.pad(small, ((0, plan.small_rows - small.shape[0]), (0, 0)))
    early = [table, in_pieces(gather(inward), LANE), small]
    return early, [gather(outward), in_pieces(gather(expand), width), gather(contract)]


def plain_grads(plan, counted, early_grads, late_grads):
    width = plan.width
    table, inward, small = early_grads
    outward, expand, contract = (jnp.where(counted > 0, g, BF(0)) for g in late_grads)

    def scatter(value, axis=0):
        return lax.psum_scatter(value, AXES, scatter_dimension=axis, tiled=True).astype(F32)

    def whole(value):
        return value.transpose(1, 0, 2).reshape(value.shape[1], -1)

    flat = small.reshape(-1)
    own = []
    for vector, length in enumerate(plan.lengths):
        start = plan.block_starts[vector] * LANE
        own.append(scatter(flat[start : start + length]))
    return (scatter(table.T, 1), scatter(whole(inward)), scatter(outward), scatter(whole(expand)),
            scatter(contract), own)


def solution(mesh):
    rows = P(None, "batch", "seq", None)
    table = P(None, AXES)
    matrix = P(AXES, None)
    vector = P(AXES)
    weights = (table, matrix, vector, matrix, vector, vector, vector, matrix, vector, matrix, vector,
               vector, vector)
    return jax.shard_map(
        local,
        mesh=mesh,
        in_specs=(rows, P(None, "batch"), rows) + weights,
        out_specs=(rows, rows) + weights,
        check_vma=False,
    )
```

```python
import functools

import jax
import jax.numpy as jnp
from jax import lax
from jax.experimental import pallas as pl
from jax.experimental.pallas import tpu as pltpu
from jax.sharding import PartitionSpec as P

AXES = ("batch", "seq")
LANE = 128
TILE = 16
FEED_ROWS = 512
STEP = 256
FAR = 1e30
BEND = 0.7978845608028654
BF = jnp.bfloat16
F32 = jnp.float32
VECTORS = 8


def times(left, right):
    return jnp.dot(left, right, preferred_element_type=F32)


def times_t(left, right):
    return lax.dot_general(left, right, (((1,), (1,)), ((), ())), preferred_element_type=F32)


def t_times(left, right):
    return lax.dot_general(left, right, (((0,), (0,)), ((), ())), preferred_element_type=F32)


def column_sum(values):
    return jnp.sum(values.astype(F32), axis=0, keepdims=True)


def aligned(index, size):
    return pl.ds(pl.multiple_of(index * size, size), size)


def like(shape, kind):
    return jax.ShapeDtypeStruct(shape, kind)


def full(shape):
    return pl.BlockSpec(shape, lambda *_: (0,) * len(shape), pipeline_mode=pl.Buffered(1))


def params(megabytes):
    return pltpu.CompilerParams(vmem_limit_bytes=megabytes * 2**20)


def cost(flops, size, exps=0):
    return pl.CostEstimate(flops=flops, bytes_accessed=size, transcendentals=exps)


class Plan:
    def __init__(self, devices, width, hidden, total_rows):
        self.devices = devices
        self.width = width
        self.hidden = hidden
        self.total_rows = total_rows
        self.own_rows = width // devices
        self.packed = devices == 32 and self.own_rows % TILE == 0
        self.lanes = width // LANE
        self.parts = hidden // width
        self.table_pieces = total_rows // LANE
        self.early_pieces = self.table_pieces + 3 * self.lanes
        self.early_rows = (self.early_pieces + 1) * TILE
        self.late_rows = (self.lanes + hidden // LANE) * TILE + self.lanes * (hidden // devices)
        lengths = [2 * width, width, width, width, hidden, width, width, width]
        self.lengths = lengths
        self.owned = [n // devices for n in lengths]
        self.small_rows = 16
        self.z_order = (0, 16, 8, 24)
        starts = [0]
        for n in lengths:
            starts.append(starts[-1] + n // LANE)
        self.block_starts = starts

    def place(self, mask):
        return ((mask >> 1) & 3) * 4 + self.z_order.index(mask & 24)

    def grad_piece(self, half, mask, at, rows):
        cut = self.late_rows // 2
        first = at < cut
        assert not first or at + rows <= cut
        swapped = mask if first else (mask & ~6) | ((mask >> 1) & 2) | ((mask & 2) << 1)
        place = self.place(swapped)
        start = at if first else at - cut
        return half[place // 8].at[place % 8 + (0 if first else 8), start : start + rows, :]


def fill_early(plan, me, halves, table_ref, inward_ref, small_ref, stage_ref):
    for mask in range(plan.devices):
        shard = halves[mask & 1].at[plan.place(mask)]
        owner = me ^ mask
        rows = aligned(owner, TILE)
        for piece in range(plan.table_pieces):
            table_ref[piece, rows, :] = shard[piece * TILE : (piece + 1) * TILE, :]
        for piece in range(3 * plan.lanes):
            at = plan.table_pieces + piece
            inward_ref[piece, rows, :] = shard[at * TILE : (at + 1) * TILE, :]
        at = plan.early_pieces * TILE
        stage_ref[pl.ds(owner, 1), :, :] = shard[at : at + TILE, :].astype(F32)[None]
    lane = lax.broadcasted_iota(jnp.int32, (1, LANE), 1)
    for vector, length in enumerate(plan.lengths):
        size = plan.owned[vector]
        group = LANE // size
        for block in range(length // LANE):
            row = jnp.zeros((1, LANE), F32)
            for index in range(group):
                own = stage_ref[block * group + index, vector : vector + 1, :]
                row = jnp.where(lane // size == index, own, row)
            at = plan.block_starts[vector] + block
            small_ref[at // plan.lanes : at // plan.lanes + 1, (at % plan.lanes) * LANE : (at % plan.lanes + 1) * LANE] = row


def own_lanes(value, head):
    lane = lax.broadcasted_iota(jnp.int32, value.shape, 1)
    return jnp.where((lane // (LANE // 2)) == head, value, jnp.zeros_like(value))


def causal():
    return lax.broadcasted_iota(jnp.int32, (STEP, STEP), 0) <= lax.broadcasted_iota(
        jnp.int32, (STEP, STEP), 1
    )


def attend_kernel(plan, count, info_ref, *refs):
    pieces, refs = refs[:count], refs[count:]
    if plan.packed:
        halves, refs = refs[:2], refs[2:]
    else:
        table_in, inward_in, small_in = refs[:3]
        refs = refs[3:]
    (lifted_ref, query_ref, key_ref, value_ref, mixed_ref, total_ref, inward_ref, small_ref) = refs[:8]
    low_ref, table_ref, place_ref, stage_ref = refs[8:]
    pair = pl.program_id(0)
    total_rows, width = plan.total_rows, plan.width
    half = total_rows // 2
    split = info_ref[0] < total_rows
    far = jnp.where(split, FAR, 0.0)

    @pl.when(pair == 0)
    def _():
        if plan.packed:
            fill_early(plan, info_ref[1], halves, table_ref, inward_ref, small_ref, stage_ref)
        else:
            table_ref[...] = table_in[...]
            inward_ref[...] = inward_in[...]
            small_ref[...] = small_in[...]
        eye = (
            lax.broadcasted_iota(jnp.int32, (half, half), 0)
            == lax.broadcasted_iota(jnp.int32, (half, half), 1)
        ).astype(BF)
        per_half = half // LANE
        for part in range(2):
            table = jnp.concatenate(
                [table_ref[part * per_half + i] for i in range(per_half)], axis=1
            )
            place_ref[part * half : (part + 1) * half, :] = times_t(eye, table)
        rows = total_rows // count
        for mask in range(count):
            start = (info_ref[2] ^ mask) * rows
            place = start - jnp.where(jnp.logical_and(split, start >= half), half, 0)
            lifted = pieces[mask][...].astype(F32) + place_ref[pl.ds(pl.multiple_of(place, rows), rows), :]
            spot = pl.ds(pl.multiple_of(start, rows), rows)
            lifted_ref[spot, :] = lifted
            low_ref[spot, :] = lifted.astype(BF)

    weights = jnp.concatenate([inward_ref[pair + i * plan.lanes] for i in range(3)], axis=1)
    lanes = aligned(pair, LANE)
    query_bias = small_ref[0:1, lanes]
    value_bias = small_ref[1:2, lanes]
    for block in range(total_rows // STEP):
        spot = slice(block * STEP, (block + 1) * STEP)
        joint = times(low_ref[spot, :], weights)
        query_ref[spot, :] = (joint[:, :LANE] + query_bias).astype(BF) * BF(0.125)
        key_ref[spot, :] = joint[:, LANE : 2 * LANE].astype(BF)
        value_ref[spot, :] = (joint[:, 2 * LANE :] + value_bias).astype(BF)

    keep = causal()
    lower = lax.broadcasted_iota(jnp.int32, (LANE, STEP), 0) < LANE // 2

    value_t = value_ref[...].T

    def logits_of(block, head):
        start = block * STEP
        other = half if start >= half else 0
        mine = own_lanes(query_ref[start : start + STEP, :], head)
        near = times_t(key_ref[start : start + STEP, :], mine)
        same = times_t(key_ref[other:start, :], mine) if start > other else None
        away = times_t(key_ref[:other, :], mine) if other else None
        return near, same, away

    def mixed_of(block, head, near, same, away):
        start = block * STEP
        other = half if start >= half else 0
        near = jnp.where(keep, near, -FAR)
        peak = jnp.max(near, axis=0, keepdims=True)
        if same is not None:
            peak = jnp.maximum(peak, jnp.max(same, axis=0, keepdims=True))
        if away is not None:
            peak = jnp.maximum(peak, jnp.max(away, axis=0, keepdims=True) - far)
        raised = [jnp.exp(piece - peak) for piece in (same, near) if piece is not None]
        total = sum(jnp.sum(piece, axis=0, keepdims=True) for piece in raised)
        low = jnp.concatenate([piece.astype(BF) for piece in raised], axis=0)
        mixed = times(value_t[:, other : start + STEP], low)
        if away is not None:
            away = jnp.exp(away - (peak + far))
            total = total + jnp.sum(away, axis=0, keepdims=True)
            mixed = mixed + times(value_t[:, :other], away.astype(BF))
        total_ref[0, head : head + 1, start : start + STEP] = peak + jnp.log(total)
        return mixed * (1.0 / total)

    tasks = [(block, head) for block in range(total_rows // STEP) for head in range(2)]
    ahead = logits_of(*tasks[0])
    parts = []
    for index, (block, head) in enumerate(tasks):
        logits, ahead = ahead, logits_of(*tasks[index + 1]) if index + 1 < len(tasks) else None
        parts.append(mixed_of(block, head, *logits))
        if head:
            mixed_ref[block * STEP : (block + 1) * STEP, :] = jnp.where(lower, *parts).T.astype(BF)
            parts = []


def attend(plan, info, count, pieces, weights):
    total_rows, width = plan.total_rows, plan.width
    block = pl.BlockSpec((total_rows, LANE), lambda p, *_: (0, p))
    low = pltpu.HBM((total_rows, width), BF)
    inward = (3 * plan.lanes, width, LANE)
    small = (plan.small_rows, width)
    return pl.pallas_call(
        functools.partial(attend_kernel, plan, count),
        grid_spec=pltpu.PrefetchScalarGridSpec(
            num_scalar_prefetch=1,
            grid=(plan.lanes,),
            in_specs=[full(v.shape) for v in pieces + weights],
            out_specs=[
                full((total_rows, width)),
                block,
                block,
                block,
                block,
                pl.BlockSpec((1, 8, total_rows), lambda p, *_: (p, 0, 0)),
                full(inward),
                full(small),
            ],
            scratch_shapes=[
                pltpu.VMEM((total_rows, width), BF),
                pltpu.VMEM((plan.table_pieces, width, LANE), BF),
                pltpu.VMEM((total_rows, width), F32),
                pltpu.VMEM((plan.devices, TILE, LANE), F32),
            ],
        ),
        out_shape=[
            pltpu.HBM((total_rows, width), F32),
            low,
            low,
            low,
            low,
            pltpu.HBM((plan.lanes, 8, total_rows), F32),
            pltpu.HBM(inward, BF),
            pltpu.HBM(small, F32),
        ],
        compiler_params=params(36),
        cost_estimate=cost(5 * 10**9, 14 * 2**20, 6 * 10**6),
        name="attend",
    )(info, *pieces, *weights)


def norm(rows):
    center = rows - jnp.mean(rows, axis=1, keepdims=True)
    root = lax.rsqrt(jnp.mean(center * center, axis=1, keepdims=True) + 1e-05)
    return center * root, root


def norm_back(upstream, gain, unit, root):
    scaled = upstream * gain
    mean = jnp.mean(scaled, axis=1, keepdims=True)
    slope = jnp.mean(scaled * unit, axis=1, keepdims=True)
    return (scaled - mean - unit * slope) * root


def feed_kernel(plan, count, info_ref, lifted_ref, mixed_ref, *refs):
    upstreams, refs = refs[:count], refs[count:]
    if plan.packed:
        late_quarters, small_ref = refs[:8], refs[8]
        refs = refs[9:]
    else:
        outward_in, expand_in, contract_in, small_ref = refs[:4]
        refs = refs[4:]
    results, refs = refs[:count], refs[count:]
    mixed_back_ref, first_back_ref, small_grad_ref = refs[:3]
    refs = refs[3:]
    if plan.packed:
        halves, refs = (refs[:2], refs[2:4]), refs[4:]
    else:
        outward_out, expand_out, contract_out = refs[:3]
        refs = refs[3:]
    (outward_ref, expand_ref, contract_ref, upstream_ref, result_ref, slope_ref, active_all, hidden_all, normed_all,
     lowered_all, branch_all, mixed_all, whole_ref, expand_sum, contract_sum) = refs
    step = pl.program_id(0)
    width, parts, lanes = plan.width, plan.parts, plan.lanes
    contract_own = plan.hidden // plan.devices
    contract_at = (lanes + parts * lanes) * TILE

    @pl.when(step == 0)
    def _():
        if plan.packed:
            for mask in range(plan.devices):
                at = plan.place(mask)
                shard = late_quarters[(mask & 1) * 4 + at // 4].at[at % 4]
                owner = info_ref[1] ^ mask
                rows, wide = aligned(owner, TILE), aligned(owner, contract_own)
                for lane in range(lanes):
                    cut = slice(lane * LANE, (lane + 1) * LANE)
                    outward_ref[rows, cut] = shard[lane * TILE : (lane + 1) * TILE, :]
                    for part in range(parts):
                        at = (lanes + part * lanes + lane) * TILE
                        expand_ref[part, rows, cut] = shard[at : at + TILE, :]
                    at = contract_at + lane * contract_own
                    contract_ref[wide, cut] = shard[at : at + contract_own, :]
        else:
            outward_ref[...] = outward_in[...]
            expand_ref[...] = expand_in[...]
            contract_ref[...] = contract_in[...]

    size = lifted_ref.shape[0]
    here = pl.ds(pl.multiple_of(step * size, size), size)
    rows = plan.total_rows // count
    group = size // rows

    def spot(mask):
        return pl.ds(pl.multiple_of(((info_ref[2] ^ mask) % group) * rows, rows), rows)

    for mask in range(count):
        @pl.when(step == mask // group)
        def _(mask=mask):
            upstream_ref[spot(mask), :] = upstreams[mask][...]

    outlet, steady, offset = (small_ref[i : i + 1, :] for i in (2, 3, 4))
    settle, temper, anchor = (small_ref[i + parts : i + parts + 1, :] for i in (5, 6, 7))
    mixed = mixed_ref[...]
    branch = times(mixed, outward_ref[...]) + outlet
    unit, root = norm(lifted_ref[...] + branch)
    normed = unit * steady + offset
    normed_low = normed.astype(BF)
    normed_all[here, :] = normed_low
    mixed_all[here, :] = mixed
    lowered = jnp.zeros_like(normed)
    for part in range(parts):
        cut = slice(part * width, (part + 1) * width)
        hidden = times(normed_low, expand_ref[part]) + small_ref[5 + part : 6 + part, :]
        square = hidden * hidden
        bend = jnp.tanh(hidden * (BEND + BEND * 0.044715 * square))
        half = 0.5 + 0.5 * bend
        active = (hidden * half).astype(BF)
        active_all[here, cut] = active
        slope_ref[:, cut] = half + (0.5 * hidden) * (1.0 - bend * bend) * (
            BEND + 3 * BEND * 0.044715 * square
        )
        lowered = lowered + times(active, contract_ref[cut, :])
    last_unit, last_root = norm(normed + (lowered + settle))
    result_ref[...] = (last_unit * temper + anchor).astype(BF)
    upstream = upstream_ref[...].astype(F32)
    temper_grad = column_sum(upstream * last_unit)
    anchor_grad = column_sum(upstream)
    second_back = norm_back(upstream, temper, last_unit, last_root)
    lowered_back = second_back.astype(BF)
    lowered_all[here, :] = lowered_back
    settle_grad = column_sum(lowered_back)
    normed_back = second_back
    spread_grads = []
    for part in range(parts):
        cut = slice(part * width, (part + 1) * width)
        active_back = times_t(lowered_back, contract_ref[cut, :])
        hidden_back = (active_back * slope_ref[:, cut]).astype(BF)
        spread_grads.append(column_sum(hidden_back))
        hidden_all[here, cut] = hidden_back
        normed_back = normed_back + times_t(hidden_back, expand_ref[part])
    first_back = norm_back(normed_back, steady, unit, root)
    first_back_ref[...] = first_back
    branch_back = first_back.astype(BF)
    mixed_back_ref[...] = times_t(branch_back, outward_ref[...]).astype(BF)
    branch_all[here, :] = branch_back
    zero = jnp.zeros_like(anchor_grad)
    grads = [zero, zero, column_sum(branch_back), column_sum(normed_back * unit)]
    grads += [column_sum(normed_back)] + spread_grads + [settle_grad, temper_grad, anchor_grad]
    grads += [zero] * (plan.small_rows - len(grads))
    small_term = jnp.concatenate(grads, axis=0)
    for mask in range(count):
        @pl.when(step == mask // group)
        def _(mask=mask):
            results[mask][...] = result_ref[spot(mask), :]

    @pl.when(step == 0)
    def _():
        small_grad_ref[...] = small_term

    @pl.when(step > 0)
    def _():
        small_grad_ref[...] += small_term

    @pl.when(step == pl.num_programs(0) - 1)
    def _():
        outward = t_times(mixed_all[...], branch_all[...])
        if plan.packed:
            me = info_ref[1]
            whole_ref[...] = outward
            for mask in range(plan.devices):
                half = halves[mask & 1]
                rows = aligned(me ^ mask, TILE)
                for lane in range(lanes):
                    cut = slice(lane * LANE, (lane + 1) * LANE)
                    plan.grad_piece(half, mask, lane * TILE, TILE)[...] = whole_ref[rows, cut].astype(BF)
        else:
            outward_out[...] = outward.astype(BF)
        per_part = plan.devices // parts
        for part in range(parts):
            cut = slice(part * width, (part + 1) * width)
            expand = t_times(normed_all[...], hidden_all[:, cut])
            if not plan.packed:
                expand_out[part] = expand.astype(BF)
                continue
            expand_sum[...] = expand
            for mask in range(plan.devices):
                rows = aligned(me ^ mask, TILE)
                for lane in range(lanes):
                    at = (lanes + part * lanes + lane) * TILE
                    plan.grad_piece(halves[mask & 1], mask, at, TILE)[...] = expand_sum[
                        rows, lane * LANE : (lane + 1) * LANE
                    ].astype(BF)
        for mask_part in range(parts):
            part = (me // per_part) ^ mask_part if plan.packed else mask_part
            cut = pl.ds(pl.multiple_of(part * width, width), width)
            contract = t_times(active_all[:, cut], lowered_all[...])
            if not plan.packed:
                contract_out[cut, :] = contract.astype(BF)
                continue
            contract_sum[...] = contract
            for index in range(per_part):
                mask = mask_part * per_part + index
                rows = aligned((me ^ mask) % per_part, contract_own)
                for lane in range(lanes):
                    at = contract_at + lane * contract_own
                    plan.grad_piece(halves[mask & 1], mask, at, contract_own)[...] = contract_sum[
                        rows, lane * LANE : (lane + 1) * LANE
                    ].astype(BF)


def feed(plan, info, count, lifted, mixed, upstreams, weights, small):
    total_rows, width, parts = plan.total_rows, plan.width, plan.parts
    piece = total_rows // count
    size = max(piece, FEED_ROWS)
    group = size // piece
    rows = pl.BlockSpec((size, width), lambda i, info: ((info[2] // group) ^ i, 0))
    outward, expand, contract = (width, width), (parts, width, width), (parts * width, width)
    if plan.packed:
        grads = [like((plan.devices // 2, plan.late_rows // 2, LANE), BF)] * 4
    else:
        grads = [like(outward, BF), like(expand, BF), like(contract, BF)]
    ends = [like((piece, width), BF)] * count
    outs = [like((total_rows, width), BF), like((total_rows, width), F32), like(small.shape, F32)]
    values = pl.pallas_call(
        functools.partial(feed_kernel, plan, count),
        grid_spec=pltpu.PrefetchScalarGridSpec(
            num_scalar_prefetch=1,
            grid=(total_rows // size,),
            in_specs=[rows, rows] + [full(v.shape) for v in upstreams + weights + [small]],
            out_specs=[full(v.shape) for v in ends]
            + [rows, rows, full(small.shape)]
            + [full(v.shape) for v in grads],
            scratch_shapes=[
                pltpu.VMEM(outward, BF),
                pltpu.VMEM(expand, BF),
                pltpu.VMEM(contract, BF),
                pltpu.VMEM((size, width), BF),
                pltpu.VMEM((size, width), BF),
                pltpu.VMEM((size, parts * width), F32),
                pltpu.VMEM((total_rows, parts * width), BF),
                pltpu.VMEM((total_rows, parts * width), BF),
                pltpu.VMEM((total_rows, width), BF),
                pltpu.VMEM((total_rows, width), BF),
                pltpu.VMEM((total_rows, width), BF),
                pltpu.VMEM((total_rows, width), BF),
                pltpu.VMEM(outward, F32),
                pltpu.VMEM(outward, F32),
                pltpu.VMEM(outward, F32),
            ],
        ),
        out_shape=ends + outs + grads,
        compiler_params=params(60),
        cost_estimate=cost(15 * 10**9, 20 * 2**20, 2 * 10**6),
        name="feed",
    )(info, lifted, mixed, *upstreams, *weights, small)
    return values[:count], values[count : count + 3], values[count + 3 :]


def attend_back_kernel(
    plan, count, info_ref, lifted_ref, query_ref, key_ref, value_ref, mixed_ref, mixed_back_ref,
    total_ref, inward_ref, first_back_ref, small_grad_ref, *refs
):
    tokens, refs = refs[:count], refs[count:]
    if plan.packed:
        halves, refs = refs[:2], refs[2:]
    else:
        table_out, inward_out, small_out = refs[:3]
        refs = refs[3:]
    joint_ref, sum_ref, share_ref, score_ref, grad_ref, table_ref, joint_sums, blocks_ref = refs
    pair = pl.program_id(0)
    total_rows, lanes = plan.total_rows, plan.lanes
    half = total_rows // 2
    split = info_ref[0] < total_rows
    far = jnp.where(split, FAR, 0.0)
    blocks = total_rows // STEP

    keep = causal()
    lower = lax.broadcasted_iota(jnp.int32, (STEP, LANE), 1) < LANE // 2
    lower_t = lax.broadcasted_iota(jnp.int32, (LANE, STEP), 0) < LANE // 2
    product = (mixed_ref[...].astype(F32) * mixed_back_ref[...].astype(F32)).T
    scaled_key = (key_ref[...] * BF(0.125)).T
    betweens = [
        jnp.sum(product[head * LANE // 2 : (head + 1) * LANE // 2], axis=0, keepdims=True)
        for head in range(2)
    ]

    def logits_of(block, head):
        spot = slice(block * STEP, (block + 1) * STEP)
        keys = slice(0, (block + 1) * STEP)
        query = own_lanes(query_ref[spot, :], head)
        back = own_lanes(mixed_back_ref[spot, :], head)
        return times_t(key_ref[keys, :], query), times_t(value_ref[keys, :], back)

    def scores_of(block, head, logits, share_back):
        start = block * STEP
        spot = slice(start, start + STEP)
        total = total_ref[0, head : head + 1, spot]
        gap = betweens[head][:, spot]
        for under in range(block + 1):
            keys = slice(under * STEP, (under + 1) * STEP)
            away = start >= half and under * STEP < half
            share = jnp.exp(logits[keys] - (total + far if away else total))
            if under == block:
                share = jnp.where(keep, share, 0.0)
            score = share * (share_back[keys] - gap)
            share_ref[head, keys, spot] = share.astype(BF)
            score_ref[head, keys, spot] = score.astype(BF)

    def backs_of(block, head):
        start = block * STEP
        spot = slice(start, start + STEP)
        end = start + STEP
        query_back = times(scaled_key[:, :end], score_ref[head, :end, spot])
        key_back = times(score_ref[head, spot, start:], query_ref[start:, :])
        value_back = times(share_ref[head, spot, start:], mixed_back_ref[start:, :])
        return query_back, key_back, value_back

    tasks = [(block, head) for block in reversed(range(blocks)) for head in range(2)]
    ahead = logits_of(*tasks[0])
    parts = []
    for index, (block, head) in enumerate(tasks):
        logits, ahead = ahead, logits_of(*tasks[index + 1]) if index + 1 < len(tasks) else None
        scores_of(block, head, *logits)
        parts.append(backs_of(block, head))
        if head:
            spot = slice(block * STEP, (block + 1) * STEP)
            query_back = jnp.where(lower_t, parts[0][0], parts[1][0]).T
            key_back = jnp.where(lower, parts[0][1], parts[1][1])
            value_back = jnp.where(lower, parts[0][2], parts[1][2])
            for part, back in enumerate((query_back, key_back, value_back)):
                joint_ref[spot, aligned(pair + part * lanes, LANE)] = back.astype(BF)
            parts = []

    @pl.when(pair == lanes - 1)
    def _():
        low = lifted_ref[...].astype(BF).T
        weights = jnp.concatenate([inward_ref[i] for i in range(3 * lanes)], axis=1)
        for block in range(blocks):
            spot = slice(block * STEP, (block + 1) * STEP)
            sum_ref[spot, :] = first_back_ref[spot, :] + times_t(joint_ref[spot, :], weights)
        for part in range(3):
            joint = joint_ref[:, part * plan.width : (part + 1) * plan.width]
            grads = times(low, joint)
            for lane in range(lanes):
                grad_ref[part * lanes + lane] = grads[:, lane * LANE : (lane + 1) * LANE]
            if part != 1:
                sums = column_sum(joint)
                for lane in range(lanes):
                    at = lane if part == 0 else lane + lanes
                    joint_sums[at : at + 1, :] = sums[:, lane * LANE : (lane + 1) * LANE]
        rows = total_rows // count
        for mask in range(count):
            spot = pl.ds(pl.multiple_of((info_ref[2] ^ mask) * rows, rows), rows)
            tokens[mask][...] = sum_ref[spot, :].astype(BF)
        late = sum_ref[half:, :]
        early = sum_ref[:half, :] + jnp.where(split, late, 0.0)
        table_ref[:, :half] = early.T
        table_ref[:, half:] = jnp.where(split, 0.0, late).T
        counted = info_ref[3] > 0
        blocks_ref[: 2 * lanes, :] = joint_sums[: 2 * lanes, :]
        for row in range(2, plan.block_starts[-1] // lanes):
            for lane in range(lanes):
                blocks_ref[row * lanes + lane : row * lanes + lane + 1, :] = small_grad_ref[
                    row : row + 1, lane * LANE : (lane + 1) * LANE
                ]
        if plan.packed:
            for mask in range(plan.devices):
                shard = halves[mask & 1].at[plan.place(mask)]
                owner = info_ref[1] ^ mask
                own = aligned(owner, TILE)
                for piece in range(plan.table_pieces):
                    shard[piece * TILE : (piece + 1) * TILE, :] = table_ref[
                        own, piece * LANE : (piece + 1) * LANE
                    ].astype(BF)
                for piece in range(3 * lanes):
                    at = (plan.table_pieces + piece) * TILE
                    shard[at : at + TILE, :] = grad_ref[piece, own, :].astype(BF)
                rows = [
                    blocks_ref[pl.ds(plan.block_starts[v] + owner * plan.owned[v] // LANE, 1), :]
                    for v in range(VECTORS)
                ]
                rows.append(jnp.zeros((TILE - VECTORS, LANE), F32))
                at = plan.early_pieces * TILE
                shard[at : at + TILE, :] = jnp.concatenate(rows, axis=0).astype(BF)
        else:
            table_out[...] = jnp.where(counted, table_ref[...], 0.0).astype(BF)
            inward_out[...] = jnp.where(counted, grad_ref[...], 0.0).astype(BF)
            small_out[...] = jnp.where(counted, blocks_ref[...], 0.0)


def attend_back(plan, info, count, lifted, saved, mixed_back, inward, first_back, small_grad):
    query, key, value, mixed, totals = saved
    total_rows, width, lanes = plan.total_rows, plan.width, plan.lanes
    block = pl.BlockSpec((total_rows, LANE), lambda p, *_: (0, p))
    blocks = (plan.block_starts[-1], LANE)
    if plan.packed:
        grads = [like((plan.devices // 2, plan.early_rows, LANE), BF)] * 2
    else:
        grads = [like((width, total_rows), BF), like(inward.shape, BF), like(blocks, F32)]
    tokens = [like((total_rows // count, width), BF)] * count
    values = pl.pallas_call(
        functools.partial(attend_back_kernel, plan, count),
        grid_spec=pltpu.PrefetchScalarGridSpec(
            num_scalar_prefetch=1,
            grid=(lanes,),
            in_specs=[
                full(lifted.shape),
                block,
                block,
                block,
                block,
                block,
                pl.BlockSpec((1, 8, total_rows), lambda p, *_: (p, 0, 0)),
                full(inward.shape),
                full(first_back.shape),
                full(small_grad.shape),
            ],
            out_specs=[full(v.shape) for v in tokens + grads],
            scratch_shapes=[
                pltpu.VMEM((total_rows, 3 * width), BF),
                pltpu.VMEM((total_rows, width), F32),
                pltpu.VMEM((2, total_rows, total_rows), BF),
                pltpu.VMEM((2, total_rows, total_rows), BF),
                pltpu.VMEM(inward.shape, F32),
                pltpu.VMEM((width, total_rows), F32),
                pltpu.VMEM((8, LANE), F32),
                pltpu.VMEM(blocks, F32),
            ],
        ),
        out_shape=tokens + grads,
        compiler_params=params(56),
        cost_estimate=cost(14 * 10**9, 24 * 2**20, 6 * 10**6),
        name="attend_back",
    )(info, lifted, query, key, value, mixed, mixed_back, totals, inward, first_back, small_grad)
    return values[:count], values[count:]


def pack_kernel(plan, count, share, rows_ref, table_ref, inward_ref, *refs):
    vectors, refs = refs[:VECTORS], refs[VECTORS:]
    outward_ref, expand_ref, contract_ref = refs[:3]
    pieces, early_ref, late_ref = refs[3 : 3 + count], refs[3 + count], refs[4 + count]
    rank = lax.axis_index("seq")
    for mask in range(count):
        pieces[mask][...] = rows_ref[pl.ds((rank ^ mask) // share, 1), :, :][0]
    at = 0
    for ref in (table_ref, inward_ref):
        for lane in range(ref.shape[1] // LANE):
            early_ref[0, at : at + TILE, :] = ref[:, lane * LANE : (lane + 1) * LANE]
            at += TILE
    rows = []
    for size, ref in zip(plan.owned, vectors):
        rows.append(jnp.concatenate([ref[...].astype(F32)] * (LANE // size), axis=1))
    rows.append(jnp.zeros((TILE - VECTORS, LANE), F32))
    early_ref[0, at : at + TILE, :] = jnp.concatenate(rows, axis=0).astype(BF)
    at = 0
    for ref in (outward_ref, expand_ref, contract_ref):
        rows = ref.shape[0]
        for lane in range(ref.shape[1] // LANE):
            late_ref[0, at : at + rows, :] = ref[:, lane * LANE : (lane + 1) * LANE]
            at += rows


def pack(plan, count, share, rows, table, inward, vectors, outward, expand, contract):
    vectors = [v.reshape(1, -1) for v in vectors]
    outs = [like(rows.shape[1:], BF)] * count
    outs += [like((1, plan.early_rows, LANE), BF), like((1, plan.late_rows, LANE), BF)]
    values = pl.pallas_call(
        functools.partial(pack_kernel, plan, count, share),
        out_shape=outs,
        cost_estimate=cost(0, 4 * 2**20),
        name="pack",
    )(rows, table, inward, *vectors, outward, expand, contract)
    return values[:count], values[count], values[count + 1]


def fold(terms, cuts):
    size = terms[0].shape[0] // cuts
    return [
        sum(term[index * size : (index + 1) * size].astype(F32) for term in terms).astype(BF)
        for index in range(cuts)
    ]


def finish_kernel(plan, info_ref, *refs):
    early, late, refs = refs[:4], refs[4:8], refs[8:]
    table_ref, inward_ref, outward_ref, expand_ref, contract_ref = refs[:5]
    vectors = refs[5:]
    early = sum(ref[0].astype(F32) for ref in early)
    late = sum(ref[0].astype(F32) for ref in late)
    for piece in range(plan.table_pieces):
        table_ref[:, piece * LANE : (piece + 1) * LANE] = early[piece * TILE : (piece + 1) * TILE]
    for piece in range(3 * plan.lanes):
        at = (plan.table_pieces + piece) * TILE
        inward_ref[:, piece * LANE : (piece + 1) * LANE] = early[at : at + TILE]
    at = 0
    for ref in (outward_ref, expand_ref, contract_ref):
        rows = ref.shape[0]
        for lane in range(ref.shape[1] // LANE):
            ref[:, lane * LANE : (lane + 1) * LANE] = late[at : at + rows]
            at += rows
    at = plan.early_pieces * TILE
    small = early[at : at + VECTORS]
    for vector, ref in enumerate(vectors):
        size = plan.owned[vector]
        slot = lax.rem(info_ref[1], LANE // size)
        row = pltpu.roll(small, LANE - slot * size, 1)
        ref[...] = row[vector : vector + 1, :size]


def finish(plan, info, early, late):
    own, width = plan.own_rows, plan.width
    outs = [
        like((own, plan.total_rows), F32),
        like((own, 3 * width), F32),
        like((own, width), F32),
        like((own, plan.hidden), F32),
        like((plan.hidden // plan.devices, width), F32),
    ] + [like((1, n), F32) for n in plan.owned]
    values = early + late
    return pl.pallas_call(
        functools.partial(finish_kernel, plan),
        grid_spec=pltpu.PrefetchScalarGridSpec(
            num_scalar_prefetch=1,
            grid=(1,),
            in_specs=[full(v.shape) for v in values],
            out_specs=[full(v.shape) for v in outs],
        ),
        out_shape=outs,
        name="finish",
    )(info, *values)


def ordered(rank, pieces):
    for bit in (1, 2):
        flip = (rank & bit) > 0
        pieces = [jnp.where(flip, pieces[i ^ bit], pieces[i]) for i in range(4)]
    return jnp.stack(pieces)


def settle_kernel(count, share, info_ref, *refs):
    for mask in range(count):
        refs[count][pl.ds((info_ref[2] ^ mask) // share, 1), :, :] = refs[mask][...][None]


def settle_rows(info, micro_count, share, pieces):
    out = (micro_count,) + pieces[0].shape
    return pl.pallas_call(
        functools.partial(settle_kernel, len(pieces), share),
        grid_spec=pltpu.PrefetchScalarGridSpec(
            num_scalar_prefetch=1,
            grid=(1,),
            in_specs=[full(v.shape) for v in pieces],
            out_specs=full(out),
        ),
        out_shape=like(out, BF),
        name="settle_rows",
    )(info, *pieces)


def cut_kernel(count, share, rows_ref, *refs):
    rank = lax.axis_index("seq")
    for mask in range(count):
        refs[mask][...] = rows_ref[pl.ds((rank ^ mask) // share, 1), :, :][0]


def cut_rows(rows, count, share):
    outs = [like(rows.shape[1:], BF)] * count
    return pl.pallas_call(
        functools.partial(cut_kernel, count, share),
        out_shape=outs,
        cost_estimate=cost(0, 4 * 2**20),
        name="cut_rows",
    )(rows)


def local(tokens, first_length, cotangent, positions, inward, intake, outward, outlet, steady, offset,
          expand, spread, contract, settle, temper, anchor):
    micro_count, pack_count, block_rows, width = tokens.shape
    assert pack_count == 1
    devices, count = lax.axis_size(AXES), lax.axis_size("seq")
    me, rank = lax.axis_index(AXES), lax.axis_index("seq")
    share = max(count // micro_count, 1)
    assert share * micro_count == count
    plan = Plan(devices, width, contract.shape[0] * devices, block_rows * count)
    micro = rank // share
    counted = (rank % share == 0).astype(jnp.int32)

    def info_of(lengths):
        first = jnp.sum(jnp.where(jnp.arange(micro_count) == micro, lengths[:, 0], 0))
        return jnp.stack([first, me, rank, counted]).astype(jnp.int32)

    vectors = (intake, outlet, steady, offset, spread, settle, temper, anchor)

    def swap(value, mask):
        return lax.ppermute(value, AXES, [(d, d ^ mask) for d in range(devices)]) if mask else value

    def exchange(pieces):
        return [swap(piece, mask) for mask, piece in enumerate(pieces)]

    def in_order(pieces):
        if count != 4 or share != 1:
            return settle_rows(info, micro_count, share, pieces)
        return ordered(rank, pieces)

    if plan.packed:
        rows_in, shard, late = pack(
            plan, count, share, tokens[:, 0], positions.T, inward, vectors, outward, expand, contract
        )
        rows_in = exchange(rows_in)
        shard, rows_in[1] = lax.optimization_barrier((shard, rows_in[1]))
        pieces = [swap(shard, mask) for mask in plan.z_order]
        pieces, rows_in, late, cotangent, first_length = lax.optimization_barrier(
            (pieces, rows_in, late, cotangent, first_length)
        )
        info = info_of(first_length)
        shard = jnp.concatenate(pieces, axis=0)
        pieces = [swap(shard, k << 1) for k in range(4)]
        late = [swap(late, mask) for mask in plan.z_order]
        upstreams = cut_rows(cotangent[:, 0], count, share)
        pieces, upstreams, late, info = lax.optimization_barrier((pieces, list(upstreams), late, info))
        late = jnp.concatenate(late, axis=0)
        late_x, late_y = swap(late, 2), swap(late, 4)
        shard = jnp.concatenate(pieces, axis=0)
        early = [shard, swap(shard, 1)]
        upstreams[1] = swap(upstreams[1], 1)
        late_core = swap(late, 1)
        early, late_core, late_x, late_y, upstreams = lax.optimization_barrier(
            (early, late_core, late_x, late_y, upstreams)
        )
        late_xy = swap(late_x, 4)
        upstreams[2:] = [swap(upstreams[mask], mask) for mask in (2, 3)]
        late_cores = [late_core, swap(late_x, 1), swap(late_y, 1)]
    else:
        info = info_of(first_length)
        rows_in = exchange(cut_rows(tokens[:, 0], count, share))
        upstreams = exchange(cut_rows(cotangent[:, 0], count, share))
        early, late = plain_weights(plan, positions, inward, vectors, outward, expand, contract)
    lifted, query, key, value, mixed, totals, inward_all, small = attend(plan, info, count, rows_in, early)
    if plan.packed:
        late_xy, late_cores, upstreams, mixed = lax.optimization_barrier(
            (late_xy, late_cores, upstreams, mixed)
        )
        late = [late, late_x, late_y, late_xy] + late_cores + [swap(late_xy, 1)]
    results, (mixed_back, first_back, small_grad), late_grads = feed(
        plan, info, count, lifted, mixed, upstreams, late, small
    )
    results = exchange(results)
    if plan.packed:
        stay_keep, go_keep, stay_send, go_send = late_grads
        one_send, two_send = fold([go_keep, swap(go_send, 1)], 2)
        stay_other = swap(stay_send, 1)
        one_send, two_send, mixed_back = lax.optimization_barrier((one_send, two_send, mixed_back))
        one_other, two_other = swap(one_send, 4), swap(two_send, 2)
    token_pieces, early_grads = attend_back(
        plan, info, count, lifted, (query, key, value, mixed, totals), mixed_back, inward_all,
        first_back, small_grad,
    )
    if plan.packed:
        one_other, two_other, stay_other, results, token_pieces, early_grads = lax.optimization_barrier(
            (one_other, two_other, stay_other, results, token_pieces, early_grads)
        )
        keep, send = early_grads
        send = swap(send, 1)
        one, one_send = fold([stay_keep[:8], stay_other[:8], one_other], 2)
        two, two_send = fold([stay_keep[8:], stay_other[8:], two_other], 2)
        one, one_send, two, two_send, keep = lax.optimization_barrier((one, one_send, two, two_send, keep))
        one_other, two_other = swap(one_send, 2), swap(two_send, 4)
        terms = fold([keep, send], 4)
        terms, results, token_pieces, one_other, two_other = lax.optimization_barrier(
            (terms, results, token_pieces, one_other, two_other)
        )
        terms = [swap(term, k << 1) for k, term in enumerate(terms)]
        ones, twos = fold([one, one_other], 4), fold([two, two_other], 4)
        late_terms = [jnp.concatenate(pair, axis=1) for pair in zip(ones, twos)]
        late_terms = [swap(term, mask) for term, mask in zip(late_terms, plan.z_order)]
        output = in_order(results)
        token_pieces = list(token_pieces)
        token_pieces[1] = swap(token_pieces[1], 1)
        terms, late_terms, output, token_pieces = lax.optimization_barrier(
            (terms, late_terms, output, token_pieces)
        )
        terms = fold(terms, 4)
        early_terms = [swap(term, mask) for term, mask in zip(terms, plan.z_order)]
        token_pieces[2:] = [swap(token_pieces[mask], mask) for mask in (2, 3)]
        tokens_back = in_order(token_pieces)
        values = finish(plan, info, early_terms, late_terms)
        table_t, inward_own, outward_own, expand_own, contract_own = values[:5]
        own = [v.reshape(-1) for v in values[5:]]
        table_own = table_t.T
    else:
        output = in_order(results)
        tokens_back = in_order(exchange(token_pieces))
        table_own, inward_own, outward_own, expand_own, contract_own, own = plain_grads(
            plan, counted, early_grads, late_grads
        )
    return (output[:, None], tokens_back[:, None], table_own, inward_own, own[0], outward_own, own[1], own[2],
            own[3], expand_own, own[4], contract_own, own[5], own[6], own[7])


def plain_weights(plan, positions, inward, vectors, outward, expand, contract):
    lanes, width = plan.lanes, plan.width

    def gather(value, axis=0):
        return lax.all_gather(value, AXES, axis=axis, tiled=True)

    def in_pieces(value, size):
        return value.reshape(value.shape[0], -1, size).transpose(1, 0, 2)

    table = in_pieces(gather(positions, 1).T, LANE)
    small = jnp.concatenate([gather(v) for v in vectors]).astype(F32).reshape(-1, width)
    small = jnp.pad(small, ((0, plan.small_rows - small.shape[0]), (0, 0)))
    early = [table, in_pieces(gather(inward), LANE), small]
    return early, [gather(outward), in_pieces(gather(expand), width), gather(contract)]


def plain_grads(plan, counted, early_grads, late_grads):
    width = plan.width
    table, inward, small = early_grads
    outward, expand, contract = (jnp.where(counted > 0, g, BF(0)) for g in late_grads)

    def scatter(value, axis=0):
        return lax.psum_scatter(value, AXES, scatter_dimension=axis, tiled=True).astype(F32)

    def whole(value):
        return value.transpose(1, 0, 2).reshape(value.shape[1], -1)

    flat = small.reshape(-1)
    own = []
    for vector, length in enumerate(plan.lengths):
        start = plan.block_starts[vector] * LANE
        own.append(scatter(flat[start : start + length]))
    return (scatter(table.T, 1), scatter(whole(inward)), scatter(outward), scatter(whole(expand)),
            scatter(contract), own)


def solution(mesh):
    rows = P(None, "batch", "seq", None)
    table = P(None, AXES)
    matrix = P(AXES, None)
    vector = P(AXES)
    weights = (table, matrix, vector, matrix, vector, vector, vector, matrix, vector, matrix, vector,
               vector, vector)
    return jax.shard_map(
        local,
        mesh=mesh,
        in_specs=(rows, P(None, "batch"), rows) + weights,
        out_specs=(rows, rows) + weights,
        check_vma=False,
    )
```

```python
import functools

import jax
import jax.numpy as jnp
from jax import lax
from jax.experimental import pallas as pl
from jax.experimental.pallas import tpu as pltpu
from jax.sharding import PartitionSpec as P

AXES = ("batch", "seq")
LANE = 128
TILE = 16
FEED_ROWS = 512
STEP = 256
FAR = 1e30
BEND = 0.7978845608028654
BF = jnp.bfloat16
F32 = jnp.float32
VECTORS = 8


def times(left, right):
    return jnp.dot(left, right, preferred_element_type=F32)


def times_t(left, right):
    return lax.dot_general(left, right, (((1,), (1,)), ((), ())), preferred_element_type=F32)


def t_times(left, right):
    return lax.dot_general(left, right, (((0,), (0,)), ((), ())), preferred_element_type=F32)


def column_sum(values):
    return jnp.sum(values.astype(F32), axis=0, keepdims=True)


def aligned(index, size):
    return pl.ds(pl.multiple_of(index * size, size), size)


def like(shape, kind):
    return jax.ShapeDtypeStruct(shape, kind)


def full(shape):
    return pl.BlockSpec(shape, lambda *_: (0,) * len(shape), pipeline_mode=pl.Buffered(1))


HELD = pl.BlockSpec(memory_space=pltpu.VMEM)


def hold(values):
    return [pltpu.with_memory_space_constraint(v, pltpu.VMEM) for v in values]


def params(megabytes):
    return pltpu.CompilerParams(vmem_limit_bytes=megabytes * 2**20)


def cost(flops, size, exps=0):
    return pl.CostEstimate(flops=flops, bytes_accessed=size, transcendentals=exps)


class Plan:
    def __init__(self, devices, width, hidden, total_rows):
        self.devices = devices
        self.width = width
        self.hidden = hidden
        self.total_rows = total_rows
        self.own_rows = width // devices
        self.packed = devices == 32 and self.own_rows % TILE == 0
        self.lanes = width // LANE
        self.parts = hidden // width
        self.table_pieces = total_rows // LANE
        self.early_pieces = self.table_pieces + 3 * self.lanes
        self.early_rows = (self.early_pieces + 1) * TILE
        self.late_rows = (self.lanes + hidden // LANE) * TILE + self.lanes * (hidden // devices)
        lengths = [2 * width, width, width, width, hidden, width, width, width]
        self.lengths = lengths
        self.owned = [n // devices for n in lengths]
        self.small_rows = 16
        self.z_order = (0, 16, 8, 24)
        starts = [0]
        for n in lengths:
            starts.append(starts[-1] + n // LANE)
        self.block_starts = starts

    def place(self, mask):
        return ((mask >> 1) & 3) * 4 + self.z_order.index(mask & 24)

    def grad_piece(self, half, mask, at, rows):
        cut = self.late_rows // 2
        first = at < cut
        assert not first or at + rows <= cut
        swapped = mask if first else (mask & ~6) | ((mask >> 1) & 2) | ((mask & 2) << 1)
        place = self.place(swapped)
        start = at if first else at - cut
        return half[place // 8].at[place % 8 + (0 if first else 8), start : start + rows, :]


def fill_early(plan, me, halves, table_ref, inward_ref, small_ref, stage_ref):
    for mask in range(plan.devices):
        shard = halves[mask & 1].at[plan.place(mask)]
        owner = me ^ mask
        rows = aligned(owner, TILE)
        for piece in range(plan.table_pieces):
            table_ref[piece, rows, :] = shard[piece * TILE : (piece + 1) * TILE, :]
        for piece in range(3 * plan.lanes):
            at = plan.table_pieces + piece
            inward_ref[piece, rows, :] = shard[at * TILE : (at + 1) * TILE, :]
        at = plan.early_pieces * TILE
        stage_ref[pl.ds(owner, 1), :, :] = shard[at : at + TILE, :].astype(F32)[None]
    lane = lax.broadcasted_iota(jnp.int32, (1, LANE), 1)
    for vector, length in enumerate(plan.lengths):
        size = plan.owned[vector]
        group = LANE // size
        for block in range(length // LANE):
            row = jnp.zeros((1, LANE), F32)
            for index in range(group):
                own = stage_ref[block * group + index, vector : vector + 1, :]
                row = jnp.where(lane // size == index, own, row)
            at = plan.block_starts[vector] + block
            small_ref[at // plan.lanes : at // plan.lanes + 1, (at % plan.lanes) * LANE : (at % plan.lanes + 1) * LANE] = row


def own_lanes(value, head):
    lane = lax.broadcasted_iota(jnp.int32, value.shape, 1)
    return jnp.where((lane // (LANE // 2)) == head, value, jnp.zeros_like(value))


def causal():
    return lax.broadcasted_iota(jnp.int32, (STEP, STEP), 0) <= lax.broadcasted_iota(
        jnp.int32, (STEP, STEP), 1
    )


def attend_kernel(plan, count, info_ref, *refs):
    pieces, refs = refs[:count], refs[count:]
    if plan.packed:
        halves, refs = refs[:2], refs[2:]
    else:
        table_in, inward_in, small_in = refs[:3]
        refs = refs[3:]
    (lifted_out, query_ref, key_ref, value_ref, mixed_ref, total_ref, inward_out, small_ref) = refs[:8]
    low_ref, table_ref, place_ref, stage_ref, lifted_ref, inward_ref, copied = refs[8:]
    pair = pl.program_id(0)
    copies = [
        pltpu.make_async_copy(lifted_ref, lifted_out, copied.at[0]),
        pltpu.make_async_copy(inward_ref, inward_out, copied.at[1]),
    ]
    total_rows, width = plan.total_rows, plan.width
    half = total_rows // 2
    split = info_ref[0] < total_rows
    far = jnp.where(split, FAR, 0.0)

    @pl.when(pair == 0)
    def _():
        if plan.packed:
            fill_early(plan, info_ref[1], halves, table_ref, inward_ref, small_ref, stage_ref)
        else:
            table_ref[...] = table_in[...]
            inward_ref[...] = inward_in[...]
            small_ref[...] = small_in[...]
        eye = (
            lax.broadcasted_iota(jnp.int32, (half, half), 0)
            == lax.broadcasted_iota(jnp.int32, (half, half), 1)
        ).astype(BF)
        per_half = half // LANE
        for part in range(2):
            table = jnp.concatenate(
                [table_ref[part * per_half + i] for i in range(per_half)], axis=1
            )
            place_ref[part * half : (part + 1) * half, :] = times_t(eye, table)
        rows = total_rows // count
        for mask in range(count):
            start = (info_ref[2] ^ mask) * rows
            place = start - jnp.where(jnp.logical_and(split, start >= half), half, 0)
            lifted = pieces[mask][...].astype(F32) + place_ref[pl.ds(pl.multiple_of(place, rows), rows), :]
            spot = pl.ds(pl.multiple_of(start, rows), rows)
            lifted_ref[spot, :] = lifted
            low_ref[spot, :] = lifted.astype(BF)
        for copy in copies:
            copy.start()

    weights = jnp.concatenate([inward_ref[pair + i * plan.lanes] for i in range(3)], axis=1)
    lanes = aligned(pair, LANE)
    query_bias = small_ref[0:1, lanes]
    value_bias = small_ref[1:2, lanes]
    for block in range(total_rows // STEP):
        spot = slice(block * STEP, (block + 1) * STEP)
        joint = times(low_ref[spot, :], weights)
        query_ref[spot, :] = (joint[:, :LANE] + query_bias).astype(BF) * BF(0.125)
        key_ref[spot, :] = joint[:, LANE : 2 * LANE].astype(BF)
        value_ref[spot, :] = (joint[:, 2 * LANE :] + value_bias).astype(BF)

    keep = causal()
    lower = lax.broadcasted_iota(jnp.int32, (LANE, STEP), 0) < LANE // 2

    value_t = value_ref[...].T

    def logits_of(block, head):
        start = block * STEP
        other = half if start >= half else 0
        mine = own_lanes(query_ref[start : start + STEP, :], head)
        near = times_t(key_ref[start : start + STEP, :], mine)
        same = times_t(key_ref[other:start, :], mine) if start > other else None
        away = times_t(key_ref[:other, :], mine) if other else None
        return near, same, away

    def mixed_of(block, head, near, same, away):
        start = block * STEP
        other = half if start >= half else 0
        near = jnp.where(keep, near, -FAR)
        peak = jnp.max(near, axis=0, keepdims=True)
        if same is not None:
            peak = jnp.maximum(peak, jnp.max(same, axis=0, keepdims=True))
        if away is not None:
            peak = jnp.maximum(peak, jnp.max(away, axis=0, keepdims=True) - far)
        raised = [jnp.exp(piece - peak) for piece in (same, near) if piece is not None]
        total = sum(jnp.sum(piece, axis=0, keepdims=True) for piece in raised)
        low = jnp.concatenate([piece.astype(BF) for piece in raised], axis=0)
        mixed = times(value_t[:, other : start + STEP], low)
        if away is not None:
            away = jnp.exp(away - (peak + far))
            total = total + jnp.sum(away, axis=0, keepdims=True)
            mixed = mixed + times(value_t[:, :other], away.astype(BF))
        total_ref[0, head : head + 1, start : start + STEP] = peak + jnp.log(total)
        return mixed * (1.0 / total)

    tasks = [(block, head) for block in range(total_rows // STEP) for head in range(2)]
    ahead = logits_of(*tasks[0])
    parts = []
    for index, (block, head) in enumerate(tasks):
        logits, ahead = ahead, logits_of(*tasks[index + 1]) if index + 1 < len(tasks) else None
        parts.append(mixed_of(block, head, *logits))
        if head:
            mixed_ref[block * STEP : (block + 1) * STEP, :] = jnp.where(lower, *parts).T.astype(BF)
            parts = []

    @pl.when(pair == pl.num_programs(0) - 1)
    def _():
        for copy in copies:
            copy.wait()


def attend(plan, info, count, pieces, weights):
    total_rows, width = plan.total_rows, plan.width
    block = pl.BlockSpec((total_rows, LANE), lambda p, *_: (0, p))
    low = pltpu.HBM((total_rows, width), BF)
    inward = (3 * plan.lanes, width, LANE)
    small = (plan.small_rows, width)
    return pl.pallas_call(
        functools.partial(attend_kernel, plan, count),
        grid_spec=pltpu.PrefetchScalarGridSpec(
            num_scalar_prefetch=1,
            grid=(plan.lanes,),
            in_specs=[HELD for v in pieces + weights],
            out_specs=[
                pl.BlockSpec(memory_space=pl.ANY),
                block,
                block,
                block,
                block,
                pl.BlockSpec((1, 8, total_rows), lambda p, *_: (p, 0, 0)),
                pl.BlockSpec(memory_space=pl.ANY),
                full(small),
            ],
            scratch_shapes=[
                pltpu.VMEM((total_rows, width), BF),
                pltpu.VMEM((plan.table_pieces, width, LANE), BF),
                pltpu.VMEM((total_rows, width), F32),
                pltpu.VMEM((plan.devices, TILE, LANE), F32),
                pltpu.VMEM((total_rows, width), F32),
                pltpu.VMEM(inward, BF),
                pltpu.SemaphoreType.DMA((2,)),
            ],
        ),
        out_shape=[
            pltpu.HBM((total_rows, width), F32),
            low,
            low,
            low,
            low,
            pltpu.HBM((plan.lanes, 8, total_rows), F32),
            pltpu.HBM(inward, BF),
            pltpu.HBM(small, F32),
        ],
        compiler_params=params(36),
        cost_estimate=cost(5 * 10**9, 14 * 2**20, 6 * 10**6),
        name="attend",
    )(info, *hold(pieces), *hold(weights))


def norm(rows):
    center = rows - jnp.mean(rows, axis=1, keepdims=True)
    root = lax.rsqrt(jnp.mean(center * center, axis=1, keepdims=True) + 1e-05)
    return center * root, root


def norm_back(upstream, gain, unit, root):
    scaled = upstream * gain
    mean = jnp.mean(scaled, axis=1, keepdims=True)
    slope = jnp.mean(scaled * unit, axis=1, keepdims=True)
    return (scaled - mean - unit * slope) * root


def feed_kernel(plan, count, info_ref, lifted_ref, mixed_ref, *refs):
    upstreams, refs = refs[:count], refs[count:]
    if plan.packed:
        late_quarters, small_ref = refs[:8], refs[8]
        refs = refs[9:]
    else:
        outward_in, expand_in, contract_in, small_ref = refs[:4]
        refs = refs[4:]
    results, refs = refs[:count], refs[count:]
    mixed_back_ref, first_back_ref, small_grad_ref = refs[:3]
    refs = refs[3:]
    if plan.packed:
        halves, refs = (refs[:2], refs[2:4]), refs[4:]
    else:
        outward_out, expand_out, contract_out = refs[:3]
        refs = refs[3:]
    (outward_ref, expand_ref, contract_ref, upstream_ref, result_ref, slope_ref, active_all, hidden_all, normed_all,
     lowered_all, branch_all, mixed_all, whole_ref, expand_sum, contract_sum) = refs
    step = pl.program_id(0)
    width, parts, lanes = plan.width, plan.parts, plan.lanes
    contract_own = plan.hidden // plan.devices
    contract_at = (lanes + parts * lanes) * TILE

    @pl.when(step == 0)
    def _():
        if plan.packed:
            for mask in range(plan.devices):
                at = plan.place(mask)
                shard = late_quarters[(mask & 1) * 4 + at // 4].at[at % 4]
                owner = info_ref[1] ^ mask
                rows, wide = aligned(owner, TILE), aligned(owner, contract_own)
                for lane in range(lanes):
                    cut = slice(lane * LANE, (lane + 1) * LANE)
                    outward_ref[rows, cut] = shard[lane * TILE : (lane + 1) * TILE, :]
                    for part in range(parts):
                        at = (lanes + part * lanes + lane) * TILE
                        expand_ref[part, rows, cut] = shard[at : at + TILE, :]
                    at = contract_at + lane * contract_own
                    contract_ref[wide, cut] = shard[at : at + contract_own, :]
        else:
            outward_ref[...] = outward_in[...]
            expand_ref[...] = expand_in[...]
            contract_ref[...] = contract_in[...]

    size = lifted_ref.shape[0]
    here = pl.ds(pl.multiple_of(step * size, size), size)
    rows = plan.total_rows // count
    group = size // rows

    def spot(mask):
        return pl.ds(pl.multiple_of(((info_ref[2] ^ mask) % group) * rows, rows), rows)

    for mask in range(count):
        @pl.when(step == mask // group)
        def _(mask=mask):
            upstream_ref[spot(mask), :] = upstreams[mask][...]

    outlet, steady, offset = (small_ref[i : i + 1, :] for i in (2, 3, 4))
    settle, temper, anchor = (small_ref[i + parts : i + parts + 1, :] for i in (5, 6, 7))
    mixed = mixed_ref[...]
    branch = times(mixed, outward_ref[...]) + outlet
    unit, root = norm(lifted_ref[...] + branch)
    normed = unit * steady + offset
    normed_low = normed.astype(BF)
    normed_all[here, :] = normed_low
    mixed_all[here, :] = mixed
    lowered = jnp.zeros_like(normed)
    for part in range(parts):
        cut = slice(part * width, (part + 1) * width)
        hidden = times(normed_low, expand_ref[part]) + small_ref[5 + part : 6 + part, :]
        square = hidden * hidden
        bend = jnp.tanh(hidden * (BEND + BEND * 0.044715 * square))
        half = 0.5 + 0.5 * bend
        active = (hidden * half).astype(BF)
        active_all[here, cut] = active
        slope_ref[:, cut] = half + (0.5 * hidden) * (1.0 - bend * bend) * (
            BEND + 3 * BEND * 0.044715 * square
        )
        lowered = lowered + times(active, contract_ref[cut, :])
    last_unit, last_root = norm(normed + (lowered + settle))
    result_ref[...] = (last_unit * temper + anchor).astype(BF)
    upstream = upstream_ref[...].astype(F32)
    temper_grad = column_sum(upstream * last_unit)
    anchor_grad = column_sum(upstream)
    second_back = norm_back(upstream, temper, last_unit, last_root)
    lowered_back = second_back.astype(BF)
    lowered_all[here, :] = lowered_back
    settle_grad = column_sum(lowered_back)
    normed_back = second_back
    spread_grads = []
    for part in range(parts):
        cut = slice(part * width, (part + 1) * width)
        active_back = times_t(lowered_back, contract_ref[cut, :])
        hidden_back = (active_back * slope_ref[:, cut]).astype(BF)
        spread_grads.append(column_sum(hidden_back))
        hidden_all[here, cut] = hidden_back
        normed_back = normed_back + times_t(hidden_back, expand_ref[part])
    first_back = norm_back(normed_back, steady, unit, root)
    first_back_ref[...] = first_back
    branch_back = first_back.astype(BF)
    mixed_back_ref[...] = times_t(branch_back, outward_ref[...]).astype(BF)
    branch_all[here, :] = branch_back
    zero = jnp.zeros_like(anchor_grad)
    grads = [zero, zero, column_sum(branch_back), column_sum(normed_back * unit)]
    grads += [column_sum(normed_back)] + spread_grads + [settle_grad, temper_grad, anchor_grad]
    grads += [zero] * (plan.small_rows - len(grads))
    small_term = jnp.concatenate(grads, axis=0)
    for mask in range(count):
        @pl.when(step == mask // group)
        def _(mask=mask):
            results[mask][...] = result_ref[spot(mask), :]

    @pl.when(step == 0)
    def _():
        small_grad_ref[...] = small_term

    @pl.when(step > 0)
    def _():
        small_grad_ref[...] += small_term

    @pl.when(step == pl.num_programs(0) - 1)
    def _():
        outward = t_times(mixed_all[...], branch_all[...])
        if plan.packed:
            me = info_ref[1]
            whole_ref[...] = outward
            for mask in range(plan.devices):
                half = halves[mask & 1]
                rows = aligned(me ^ mask, TILE)
                for lane in range(lanes):
                    cut = slice(lane * LANE, (lane + 1) * LANE)
                    plan.grad_piece(half, mask, lane * TILE, TILE)[...] = whole_ref[rows, cut].astype(BF)
        else:
            outward_out[...] = outward.astype(BF)
        per_part = plan.devices // parts
        for part in range(parts):
            cut = slice(part * width, (part + 1) * width)
            expand = t_times(normed_all[...], hidden_all[:, cut])
            if not plan.packed:
                expand_out[part] = expand.astype(BF)
                continue
            expand_sum[...] = expand
            for mask in range(plan.devices):
                rows = aligned(me ^ mask, TILE)
                for lane in range(lanes):
                    at = (lanes + part * lanes + lane) * TILE
                    plan.grad_piece(halves[mask & 1], mask, at, TILE)[...] = expand_sum[
                        rows, lane * LANE : (lane + 1) * LANE
                    ].astype(BF)
        for mask_part in range(parts):
            part = (me // per_part) ^ mask_part if plan.packed else mask_part
            cut = pl.ds(pl.multiple_of(part * width, width), width)
            contract = t_times(active_all[:, cut], lowered_all[...])
            if not plan.packed:
                contract_out[cut, :] = contract.astype(BF)
                continue
            contract_sum[...] = contract
            for index in range(per_part):
                mask = mask_part * per_part + index
                rows = aligned((me ^ mask) % per_part, contract_own)
                for lane in range(lanes):
                    at = contract_at + lane * contract_own
                    plan.grad_piece(halves[mask & 1], mask, at, contract_own)[...] = contract_sum[
                        rows, lane * LANE : (lane + 1) * LANE
                    ].astype(BF)


def feed(plan, info, count, lifted, mixed, upstreams, weights, small):
    total_rows, width, parts = plan.total_rows, plan.width, plan.parts
    piece = total_rows // count
    size = max(piece, FEED_ROWS)
    group = size // piece
    rows = pl.BlockSpec((size, width), lambda i, info: ((info[2] // group) ^ i, 0))
    outward, expand, contract = (width, width), (parts, width, width), (parts * width, width)
    if plan.packed:
        grads = [pltpu.VMEM((plan.devices // 2, plan.late_rows // 2, LANE), BF)] * 4
    else:
        grads = [pltpu.VMEM(outward, BF), pltpu.VMEM(expand, BF), pltpu.VMEM(contract, BF)]
    ends = [like((piece, width), BF)] * count
    outs = [like((total_rows, width), BF), like((total_rows, width), F32), like(small.shape, F32)]
    values = pl.pallas_call(
        functools.partial(feed_kernel, plan, count),
        grid_spec=pltpu.PrefetchScalarGridSpec(
            num_scalar_prefetch=1,
            grid=(total_rows // size,),
            in_specs=[rows, rows]
            + [full(v.shape) for v in upstreams]
            + [HELD for v in weights]
            + [full(small.shape)],
            out_specs=[full(v.shape) for v in ends]
            + [rows, rows, full(small.shape)]
            + [HELD for v in grads],
            scratch_shapes=[
                pltpu.VMEM(outward, BF),
                pltpu.VMEM(expand, BF),
                pltpu.VMEM(contract, BF),
                pltpu.VMEM((size, width), BF),
                pltpu.VMEM((size, width), BF),
                pltpu.VMEM((size, parts * width), F32),
                pltpu.VMEM((total_rows, parts * width), BF),
                pltpu.VMEM((total_rows, parts * width), BF),
                pltpu.VMEM((total_rows, width), BF),
                pltpu.VMEM((total_rows, width), BF),
                pltpu.VMEM((total_rows, width), BF),
                pltpu.VMEM((total_rows, width), BF),
                pltpu.VMEM(outward, F32),
                pltpu.VMEM(outward, F32),
                pltpu.VMEM(outward, F32),
            ],
        ),
        out_shape=ends + outs + grads,
        compiler_params=params(51),
        cost_estimate=cost(15 * 10**9, 20 * 2**20, 2 * 10**6),
        name="feed",
    )(info, lifted, mixed, *upstreams, *hold(weights), small)
    return values[:count], values[count : count + 3], values[count + 3 :]


def attend_back_kernel(
    plan, count, info_ref, lifted_ref, query_ref, key_ref, value_ref, mixed_ref, mixed_back_ref,
    total_ref, inward_ref, first_back_ref, small_grad_ref, *refs
):
    tokens, refs = refs[:count], refs[count:]
    if plan.packed:
        halves, refs = refs[:2], refs[2:]
    else:
        table_out, inward_out, small_out = refs[:3]
        refs = refs[3:]
    (joint_ref, sum_ref, share_ref, score_ref, grad_ref, table_ref, joint_sums, blocks_ref,
     lifted_here, inward_here, copied) = refs
    pair = pl.program_id(0)
    copies = [
        pltpu.make_async_copy(source, target, copied.at[index])
        for index, (source, target) in enumerate(
            ((lifted_ref, lifted_here), (inward_ref, inward_here), (first_back_ref, sum_ref))
        )
    ]

    @pl.when(pair == 0)
    def _():
        for copy in copies:
            copy.start()

    total_rows, lanes = plan.total_rows, plan.lanes
    half = total_rows // 2
    split = info_ref[0] < total_rows
    far = jnp.where(split, FAR, 0.0)
    blocks = total_rows // STEP

    keep = causal()
    lower = lax.broadcasted_iota(jnp.int32, (STEP, LANE), 1) < LANE // 2
    lower_t = lax.broadcasted_iota(jnp.int32, (LANE, STEP), 0) < LANE // 2
    product = (mixed_ref[...].astype(F32) * mixed_back_ref[...].astype(F32)).T
    scaled_key = (key_ref[...] * BF(0.125)).T
    betweens = [
        jnp.sum(product[head * LANE // 2 : (head + 1) * LANE // 2], axis=0, keepdims=True)
        for head in range(2)
    ]

    def logits_of(block, head):
        spot = slice(block * STEP, (block + 1) * STEP)
        keys = slice(0, (block + 1) * STEP)
        query = own_lanes(query_ref[spot, :], head)
        back = own_lanes(mixed_back_ref[spot, :], head)
        return times_t(key_ref[keys, :], query), times_t(value_ref[keys, :], back)

    def scores_of(block, head, logits, share_back):
        start = block * STEP
        spot = slice(start, start + STEP)
        total = total_ref[0, head : head + 1, spot]
        gap = betweens[head][:, spot]
        for under in range(block + 1):
            keys = slice(under * STEP, (under + 1) * STEP)
            away = start >= half and under * STEP < half
            share = jnp.exp(logits[keys] - (total + far if away else total))
            if under == block:
                share = jnp.where(keep, share, 0.0)
            score = share * (share_back[keys] - gap)
            share_ref[head, keys, spot] = share.astype(BF)
            score_ref[head, keys, spot] = score.astype(BF)

    def backs_of(block, head):
        start = block * STEP
        spot = slice(start, start + STEP)
        end = start + STEP
        query_back = times(scaled_key[:, :end], score_ref[head, :end, spot])
        key_back = times(score_ref[head, spot, start:], query_ref[start:, :])
        value_back = times(share_ref[head, spot, start:], mixed_back_ref[start:, :])
        return query_back, key_back, value_back

    tasks = [(block, head) for block in reversed(range(blocks)) for head in range(2)]
    ahead = logits_of(*tasks[0])
    parts = []
    for index, (block, head) in enumerate(tasks):
        logits, ahead = ahead, logits_of(*tasks[index + 1]) if index + 1 < len(tasks) else None
        scores_of(block, head, *logits)
        parts.append(backs_of(block, head))
        if head:
            spot = slice(block * STEP, (block + 1) * STEP)
            query_back = jnp.where(lower_t, parts[0][0], parts[1][0]).T
            key_back = jnp.where(lower, parts[0][1], parts[1][1])
            value_back = jnp.where(lower, parts[0][2], parts[1][2])
            for part, back in enumerate((query_back, key_back, value_back)):
                joint_ref[spot, aligned(pair + part * lanes, LANE)] = back.astype(BF)
            parts = []

    @pl.when(pair == lanes - 1)
    def _():
        for copy in copies:
            copy.wait()
        low = lifted_here[...].astype(BF).T
        weights = jnp.concatenate([inward_here[i] for i in range(3 * lanes)], axis=1)
        for block in range(blocks):
            spot = slice(block * STEP, (block + 1) * STEP)
            sum_ref[spot, :] += times_t(joint_ref[spot, :], weights)
        for part in range(3):
            joint = joint_ref[:, part * plan.width : (part + 1) * plan.width]
            grads = times(low, joint)
            for lane in range(lanes):
                grad_ref[part * lanes + lane] = grads[:, lane * LANE : (lane + 1) * LANE]
            if part != 1:
                sums = column_sum(joint)
                for lane in range(lanes):
                    at = lane if part == 0 else lane + lanes
                    joint_sums[at : at + 1, :] = sums[:, lane * LANE : (lane + 1) * LANE]
        rows = total_rows // count
        for mask in range(count):
            spot = pl.ds(pl.multiple_of((info_ref[2] ^ mask) * rows, rows), rows)
            tokens[mask][...] = sum_ref[spot, :].astype(BF)
        late = sum_ref[half:, :]
        early = sum_ref[:half, :] + jnp.where(split, late, 0.0)
        table_ref[:, :half] = early.T
        table_ref[:, half:] = jnp.where(split, 0.0, late).T
        counted = info_ref[3] > 0
        blocks_ref[: 2 * lanes, :] = joint_sums[: 2 * lanes, :]
        for row in range(2, plan.block_starts[-1] // lanes):
            for lane in range(lanes):
                blocks_ref[row * lanes + lane : row * lanes + lane + 1, :] = small_grad_ref[
                    row : row + 1, lane * LANE : (lane + 1) * LANE
                ]
        if plan.packed:
            for mask in range(plan.devices):
                shard = halves[mask & 1].at[plan.place(mask)]
                owner = info_ref[1] ^ mask
                own = aligned(owner, TILE)
                for piece in range(plan.table_pieces):
                    shard[piece * TILE : (piece + 1) * TILE, :] = table_ref[
                        own, piece * LANE : (piece + 1) * LANE
                    ].astype(BF)
                for piece in range(3 * lanes):
                    at = (plan.table_pieces + piece) * TILE
                    shard[at : at + TILE, :] = grad_ref[piece, own, :].astype(BF)
                rows = [
                    blocks_ref[pl.ds(plan.block_starts[v] + owner * plan.owned[v] // LANE, 1), :]
                    for v in range(VECTORS)
                ]
                rows.append(jnp.zeros((TILE - VECTORS, LANE), F32))
                at = plan.early_pieces * TILE
                shard[at : at + TILE, :] = jnp.concatenate(rows, axis=0).astype(BF)
        else:
            table_out[...] = jnp.where(counted, table_ref[...], 0.0).astype(BF)
            inward_out[...] = jnp.where(counted, grad_ref[...], 0.0).astype(BF)
            small_out[...] = jnp.where(counted, blocks_ref[...], 0.0)


def attend_back(plan, info, count, lifted, saved, mixed_back, inward, first_back, small_grad):
    query, key, value, mixed, totals = saved
    total_rows, width, lanes = plan.total_rows, plan.width, plan.lanes
    block = pl.BlockSpec((total_rows, LANE), lambda p, *_: (0, p))
    blocks = (plan.block_starts[-1], LANE)
    if plan.packed:
        grads = [pltpu.VMEM((plan.devices // 2, plan.early_rows, LANE), BF)] * 2
    else:
        grads = [pltpu.VMEM((width, total_rows), BF), pltpu.VMEM(inward.shape, BF), pltpu.VMEM(blocks, F32)]
    tokens = [pltpu.VMEM((total_rows // count, width), BF)] * count
    values = pl.pallas_call(
        functools.partial(attend_back_kernel, plan, count),
        grid_spec=pltpu.PrefetchScalarGridSpec(
            num_scalar_prefetch=1,
            grid=(lanes,),
            in_specs=[
                pl.BlockSpec(memory_space=pl.ANY),
                block,
                block,
                block,
                block,
                block,
                pl.BlockSpec((1, 8, total_rows), lambda p, *_: (p, 0, 0)),
                pl.BlockSpec(memory_space=pl.ANY),
                pl.BlockSpec(memory_space=pl.ANY),
                full(small_grad.shape),
            ],
            out_specs=[HELD for v in tokens + grads],
            scratch_shapes=[
                pltpu.VMEM((total_rows, 3 * width), BF),
                pltpu.VMEM((total_rows, width), F32),
                pltpu.VMEM((2, total_rows, total_rows), BF),
                pltpu.VMEM((2, total_rows, total_rows), BF),
                pltpu.VMEM(inward.shape, F32),
                pltpu.VMEM((width, total_rows), F32),
                pltpu.VMEM((8, LANE), F32),
                pltpu.VMEM(blocks, F32),
                pltpu.VMEM(lifted.shape, F32),
                pltpu.VMEM(inward.shape, BF),
                pltpu.SemaphoreType.DMA((3,)),
            ],
        ),
        out_shape=tokens + grads,
        compiler_params=params(56),
        cost_estimate=cost(14 * 10**9, 24 * 2**20, 6 * 10**6),
        name="attend_back",
    )(info, lifted, query, key, value, mixed, mixed_back, totals, inward, first_back, small_grad)
    return values[:count], values[count:]


def pack_kernel(plan, count, share, rows_ref, table_ref, inward_ref, *refs):
    vectors, refs = refs[:VECTORS], refs[VECTORS:]
    outward_ref, expand_ref, contract_ref = refs[:3]
    pieces, early_ref, late_ref = refs[3 : 3 + count], refs[3 + count], refs[4 + count]
    rank = lax.axis_index("seq")
    for mask in range(count):
        pieces[mask][...] = rows_ref[pl.ds((rank ^ mask) // share, 1), :, :][0]
    at = 0
    for ref in (table_ref, inward_ref):
        for lane in range(ref.shape[1] // LANE):
            early_ref[0, at : at + TILE, :] = ref[:, lane * LANE : (lane + 1) * LANE]
            at += TILE
    rows = []
    for size, ref in zip(plan.owned, vectors):
        rows.append(jnp.concatenate([ref[...].astype(F32)] * (LANE // size), axis=1))
    rows.append(jnp.zeros((TILE - VECTORS, LANE), F32))
    early_ref[0, at : at + TILE, :] = jnp.concatenate(rows, axis=0).astype(BF)
    at = 0
    for ref in (outward_ref, expand_ref, contract_ref):
        rows = ref.shape[0]
        for lane in range(ref.shape[1] // LANE):
            late_ref[0, at : at + rows, :] = ref[:, lane * LANE : (lane + 1) * LANE]
            at += rows


def pack(plan, count, share, rows, table, inward, vectors, outward, expand, contract):
    vectors = [v.reshape(1, -1) for v in vectors]
    outs = [like(rows.shape[1:], BF)] * count
    outs += [like((1, plan.early_rows, LANE), BF), like((1, plan.late_rows, LANE), BF)]
    values = pl.pallas_call(
        functools.partial(pack_kernel, plan, count, share),
        out_shape=outs,
        cost_estimate=cost(0, 4 * 2**20),
        name="pack",
    )(rows, table, inward, *vectors, outward, expand, contract)
    return values[:count], values[count], values[count + 1]


def fold(terms, cuts):
    size = terms[0].shape[0] // cuts
    return [
        sum(term[index * size : (index + 1) * size].astype(F32) for term in terms).astype(BF)
        for index in range(cuts)
    ]


def finish_kernel(plan, info_ref, *refs):
    early, late, refs = refs[:4], refs[4:8], refs[8:]
    table_ref, inward_ref, outward_ref, expand_ref, contract_ref = refs[:5]
    vectors = refs[5:]
    early = sum(ref[0].astype(F32) for ref in early)
    late = sum(ref[0].astype(F32) for ref in late)
    for piece in range(plan.table_pieces):
        table_ref[:, piece * LANE : (piece + 1) * LANE] = early[piece * TILE : (piece + 1) * TILE]
    for piece in range(3 * plan.lanes):
        at = (plan.table_pieces + piece) * TILE
        inward_ref[:, piece * LANE : (piece + 1) * LANE] = early[at : at + TILE]
    at = 0
    for ref in (outward_ref, expand_ref, contract_ref):
        rows = ref.shape[0]
        for lane in range(ref.shape[1] // LANE):
            ref[:, lane * LANE : (lane + 1) * LANE] = late[at : at + rows]
            at += rows
    at = plan.early_pieces * TILE
    small = early[at : at + VECTORS]
    for vector, ref in enumerate(vectors):
        size = plan.owned[vector]
        slot = lax.rem(info_ref[1], LANE // size)
        row = pltpu.roll(small, LANE - slot * size, 1)
        ref[...] = row[vector : vector + 1, :size]


def finish(plan, info, early, late):
    own, width = plan.own_rows, plan.width
    outs = [
        like((own, plan.total_rows), F32),
        like((own, 3 * width), F32),
        like((own, width), F32),
        like((own, plan.hidden), F32),
        like((plan.hidden // plan.devices, width), F32),
    ] + [like((1, n), F32) for n in plan.owned]
    values = early + late
    return pl.pallas_call(
        functools.partial(finish_kernel, plan),
        grid_spec=pltpu.PrefetchScalarGridSpec(
            num_scalar_prefetch=1,
            grid=(1,),
            in_specs=[HELD for v in values],
            out_specs=[full(v.shape) for v in outs],
        ),
        out_shape=outs,
        name="finish",
    )(info, *hold(values))


def ordered(rank, pieces):
    for bit in (1, 2):
        flip = (rank & bit) > 0
        pieces = [jnp.where(flip, pieces[i ^ bit], pieces[i]) for i in range(4)]
    return jnp.stack(pieces)


def settle_kernel(count, share, info_ref, *refs):
    for mask in range(count):
        refs[count][pl.ds((info_ref[2] ^ mask) // share, 1), :, :] = refs[mask][...][None]


def settle_rows(info, micro_count, share, pieces):
    out = (micro_count,) + pieces[0].shape
    return pl.pallas_call(
        functools.partial(settle_kernel, len(pieces), share),
        grid_spec=pltpu.PrefetchScalarGridSpec(
            num_scalar_prefetch=1,
            grid=(1,),
            in_specs=[full(v.shape) for v in pieces],
            out_specs=full(out),
        ),
        out_shape=like(out, BF),
        name="settle_rows",
    )(info, *pieces)


def cut_kernel(count, share, rows_ref, *refs):
    rank = lax.axis_index("seq")
    for mask in range(count):
        refs[mask][...] = rows_ref[pl.ds((rank ^ mask) // share, 1), :, :][0]


def cut_rows(rows, count, share):
    outs = [like(rows.shape[1:], BF)] * count
    return pl.pallas_call(
        functools.partial(cut_kernel, count, share),
        out_shape=outs,
        cost_estimate=cost(0, 4 * 2**20),
        name="cut_rows",
    )(rows)


def local(tokens, first_length, cotangent, positions, inward, intake, outward, outlet, steady, offset,
          expand, spread, contract, settle, temper, anchor):
    micro_count, pack_count, block_rows, width = tokens.shape
    assert pack_count == 1
    devices, count = lax.axis_size(AXES), lax.axis_size("seq")
    me, rank = lax.axis_index(AXES), lax.axis_index("seq")
    share = max(count // micro_count, 1)
    assert share * micro_count == count
    plan = Plan(devices, width, contract.shape[0] * devices, block_rows * count)
    micro = rank // share
    counted = (rank % share == 0).astype(jnp.int32)

    def info_of(lengths):
        first = jnp.sum(jnp.where(jnp.arange(micro_count) == micro, lengths[:, 0], 0))
        return jnp.stack([first, me, rank, counted]).astype(jnp.int32)

    vectors = (intake, outlet, steady, offset, spread, settle, temper, anchor)

    def swap(value, mask):
        return lax.ppermute(value, AXES, [(d, d ^ mask) for d in range(devices)]) if mask else value

    def exchange(pieces):
        return [swap(piece, mask) for mask, piece in enumerate(pieces)]

    def in_order(pieces):
        if count != 4 or share != 1:
            return settle_rows(info, micro_count, share, pieces)
        return ordered(rank, pieces)

    if plan.packed:
        rows_in, shard, late = pack(
            plan, count, share, tokens[:, 0], positions.T, inward, vectors, outward, expand, contract
        )
        rows_in = exchange(rows_in)
        shard, rows_in[1] = lax.optimization_barrier((shard, rows_in[1]))
        pieces = [swap(shard, mask) for mask in plan.z_order]
        pieces, rows_in, late, cotangent, first_length = lax.optimization_barrier(
            (pieces, rows_in, late, cotangent, first_length)
        )
        info = info_of(first_length)
        shard = jnp.concatenate(pieces, axis=0)
        pieces = [swap(shard, k << 1) for k in range(4)]
        late = [swap(late, mask) for mask in plan.z_order]
        upstreams = cut_rows(cotangent[:, 0], count, share)
        pieces, upstreams, late, info = lax.optimization_barrier((pieces, list(upstreams), late, info))
        late = jnp.concatenate(late, axis=0)
        late_x, late_y = swap(late, 2), swap(late, 4)
        shard = jnp.concatenate(pieces, axis=0)
        early = [shard, swap(shard, 1)]
        upstreams[1] = swap(upstreams[1], 1)
        late_core = swap(late, 1)
        early, late_core, late_x, late_y, upstreams = lax.optimization_barrier(
            (early, late_core, late_x, late_y, upstreams)
        )
        late_xy = swap(late_x, 4)
        upstreams[2:] = [swap(upstreams[mask], mask) for mask in (2, 3)]
        late_cores = [late_core, swap(late_x, 1), swap(late_y, 1)]
    else:
        info = info_of(first_length)
        rows_in = exchange(cut_rows(tokens[:, 0], count, share))
        upstreams = exchange(cut_rows(cotangent[:, 0], count, share))
        early, late = plain_weights(plan, positions, inward, vectors, outward, expand, contract)
    lifted, query, key, value, mixed, totals, inward_all, small = attend(plan, info, count, rows_in, early)
    if plan.packed:
        late_xy, late_cores, upstreams, mixed = lax.optimization_barrier(
            (late_xy, late_cores, upstreams, mixed)
        )
        late = [late, late_x, late_y, late_xy] + late_cores + [swap(late_xy, 1)]
    results, (mixed_back, first_back, small_grad), late_grads = feed(
        plan, info, count, lifted, mixed, upstreams, late, small
    )
    results = exchange(results)
    if plan.packed:
        stay_keep, go_keep, stay_send, go_send = late_grads
        one_send, two_send = fold([go_keep, swap(go_send, 1)], 2)
        stay_other = swap(stay_send, 1)
        one_send, two_send, mixed_back = lax.optimization_barrier((one_send, two_send, mixed_back))
        one_other, two_other = swap(one_send, 4), swap(two_send, 2)
    token_pieces, early_grads = attend_back(
        plan, info, count, lifted, (query, key, value, mixed, totals), mixed_back, inward_all,
        first_back, small_grad,
    )
    if plan.packed:
        one_other, two_other, stay_other, results, token_pieces, early_grads = lax.optimization_barrier(
            (one_other, two_other, stay_other, results, token_pieces, early_grads)
        )
        keep, send = early_grads
        send = swap(send, 1)
        one, one_send = fold([stay_keep[:8], stay_other[:8], one_other], 2)
        two, two_send = fold([stay_keep[8:], stay_other[8:], two_other], 2)
        one, one_send, two, two_send, keep = lax.optimization_barrier((one, one_send, two, two_send, keep))
        one_other, two_other = swap(one_send, 2), swap(two_send, 4)
        terms = fold([keep, send], 4)
        terms, results, token_pieces, one_other, two_other = lax.optimization_barrier(
            (terms, results, token_pieces, one_other, two_other)
        )
        terms = [swap(term, k << 1) for k, term in enumerate(terms)]
        ones, twos = fold([one, one_other], 4), fold([two, two_other], 4)
        late_terms = [jnp.concatenate(pair, axis=1) for pair in zip(ones, twos)]
        late_terms = [swap(term, mask) for term, mask in zip(late_terms, plan.z_order)]
        output = in_order(results)
        token_pieces = list(token_pieces)
        token_pieces[1] = swap(token_pieces[1], 1)
        terms, late_terms, output, token_pieces = lax.optimization_barrier(
            (terms, late_terms, output, token_pieces)
        )
        terms = fold(terms, 4)
        early_terms = [swap(term, mask) for term, mask in zip(terms, plan.z_order)]
        token_pieces[2:] = [swap(token_pieces[mask], mask) for mask in (2, 3)]
        tokens_back = in_order(token_pieces)
        values = finish(plan, info, early_terms, late_terms)
        table_t, inward_own, outward_own, expand_own, contract_own = values[:5]
        own = [v.reshape(-1) for v in values[5:]]
        table_own = table_t.T
    else:
        output = in_order(results)
        tokens_back = in_order(exchange(token_pieces))
        table_own, inward_own, outward_own, expand_own, contract_own, own = plain_grads(
            plan, counted, early_grads, late_grads
        )
    return (output[:, None], tokens_back[:, None], table_own, inward_own, own[0], outward_own, own[1], own[2],
            own[3], expand_own, own[4], contract_own, own[5], own[6], own[7])


def plain_weights(plan, positions, inward, vectors, outward, expand, contract):
    lanes, width = plan.lanes, plan.width

    def gather(value, axis=0):
        return lax.all_gather(value, AXES, axis=axis, tiled=True)

    def in_pieces(value, size):
        return value.reshape(value.shape[0], -1, size).transpose(1, 0, 2)

    table = in_pieces(gather(positions, 1).T, LANE)
    small = jnp.concatenate([gather(v) for v in vectors]).astype(F32).reshape(-1, width)
    small = jnp.pad(small, ((0, plan.small_rows - small.shape[0]), (0, 0)))
    early = [table, in_pieces(gather(inward), LANE), small]
    return early, [gather(outward), in_pieces(gather(expand), width), gather(contract)]


def plain_grads(plan, counted, early_grads, late_grads):
    width = plan.width
    table, inward, small = early_grads
    outward, expand, contract = (jnp.where(counted > 0, g, BF(0)) for g in late_grads)

    def scatter(value, axis=0):
        return lax.psum_scatter(value, AXES, scatter_dimension=axis, tiled=True).astype(F32)

    def whole(value):
        return value.transpose(1, 0, 2).reshape(value.shape[1], -1)

    flat = small.reshape(-1)
    own = []
    for vector, length in enumerate(plan.lengths):
        start = plan.block_starts[vector] * LANE
        own.append(scatter(flat[start : start + length]))
    return (scatter(table.T, 1), scatter(whole(inward)), scatter(outward), scatter(whole(expand)),
            scatter(contract), own)


def solution(mesh):
    rows = P(None, "batch", "seq", None)
    table = P(None, AXES)
    matrix = P(AXES, None)
    vector = P(AXES)
    weights = (table, matrix, vector, matrix, vector, vector, vector, matrix, vector, matrix, vector,
               vector, vector)
    return jax.shard_map(
        local,
        mesh=mesh,
        in_specs=(rows, P(None, "batch"), rows) + weights,
        out_specs=(rows, rows) + weights,
        check_vma=False,
    )
```

```python
import functools

import jax
import jax.numpy as jnp
from jax import lax
from jax.experimental import pallas as pl
from jax.experimental.pallas import tpu as pltpu
from jax.sharding import PartitionSpec as P

AXES = ("batch", "seq")
LANE = 128
TILE = 16
FEED_ROWS = 512
STEP = 256
FAR = 1e30
BEND = 0.7978845608028654
BF = jnp.bfloat16
F32 = jnp.float32
VECTORS = 8


def times(left, right):
    return jnp.dot(left, right, preferred_element_type=F32)


def times_t(left, right):
    return lax.dot_general(left, right, (((1,), (1,)), ((), ())), preferred_element_type=F32)


def t_times(left, right):
    return lax.dot_general(left, right, (((0,), (0,)), ((), ())), preferred_element_type=F32)


def column_sum(values):
    return jnp.sum(values.astype(F32), axis=0, keepdims=True)


def aligned(index, size):
    return pl.ds(pl.multiple_of(index * size, size), size)


def like(shape, kind):
    return jax.ShapeDtypeStruct(shape, kind)


def full(shape):
    return pl.BlockSpec(shape, lambda *_: (0,) * len(shape), pipeline_mode=pl.Buffered(1))


HELD = pl.BlockSpec(memory_space=pltpu.VMEM)


def hold(values):
    return [pltpu.with_memory_space_constraint(v, pltpu.VMEM) for v in values]


def stay(values):
    return [pltpu.with_memory_space_constraint(v, pltpu.HBM) for v in values]


def params(megabytes):
    return pltpu.CompilerParams(vmem_limit_bytes=megabytes * 2**20)


def cost(flops, size, exps=0):
    return pl.CostEstimate(flops=flops, bytes_accessed=size, transcendentals=exps)


class Plan:
    def __init__(self, devices, width, hidden, total_rows):
        self.devices = devices
        self.width = width
        self.hidden = hidden
        self.total_rows = total_rows
        self.own_rows = width // devices
        self.packed = devices == 32 and self.own_rows % TILE == 0
        self.lanes = width // LANE
        self.parts = hidden // width
        self.table_pieces = total_rows // LANE
        self.early_pieces = self.table_pieces + 3 * self.lanes
        self.early_rows = (self.early_pieces + 1) * TILE
        self.late_rows = (self.lanes + hidden // LANE) * TILE + self.lanes * (hidden // devices)
        self.late_cut = (self.lanes + hidden // LANE) * TILE + hidden // devices
        lengths = [2 * width, width, width, width, hidden, width, width, width]
        self.lengths = lengths
        self.owned = [n // devices for n in lengths]
        self.small_rows = 16
        self.z_order = (0, 16, 8, 24)
        starts = [0]
        for n in lengths:
            starts.append(starts[-1] + n // LANE)
        self.block_starts = starts

    def place(self, mask):
        return ((mask >> 1) & 3) * 4 + self.z_order.index(mask & 24)

    def grad_piece(self, half, mask, at, rows):
        first = at < self.late_cut
        assert not first or at + rows <= self.late_cut
        swapped = mask if first else (mask & ~6) | ((mask >> 1) & 2) | ((mask & 2) << 1)
        place = self.place(swapped)
        last_rows = self.late_rows - self.late_cut
        if first:
            start = (place % 8) * self.late_cut + at
        else:
            start = 8 * self.late_cut + (place % 8) * last_rows + at - self.late_cut
        return half[place // 8].at[start : start + rows, :]


def fill_early(plan, me, halves, table_ref, inward_ref, small_ref, stage_ref):
    for mask in range(plan.devices):
        shard = halves[mask & 1].at[plan.place(mask)]
        owner = me ^ mask
        rows = aligned(owner, TILE)
        for piece in range(plan.table_pieces):
            table_ref[piece, rows, :] = shard[piece * TILE : (piece + 1) * TILE, :]
        for piece in range(3 * plan.lanes):
            at = plan.table_pieces + piece
            inward_ref[piece, rows, :] = shard[at * TILE : (at + 1) * TILE, :]
        at = plan.early_pieces * TILE
        stage_ref[pl.ds(owner, 1), :, :] = shard[at : at + TILE, :].astype(F32)[None]
    lane = lax.broadcasted_iota(jnp.int32, (1, LANE), 1)
    for vector, length in enumerate(plan.lengths):
        size = plan.owned[vector]
        group = LANE // size
        for block in range(length // LANE):
            row = jnp.zeros((1, LANE), F32)
            for index in range(group):
                own = stage_ref[block * group + index, vector : vector + 1, :]
                row = jnp.where(lane // size == index, own, row)
            at = plan.block_starts[vector] + block
            small_ref[at // plan.lanes : at // plan.lanes + 1, (at % plan.lanes) * LANE : (at % plan.lanes + 1) * LANE] = row


def own_lanes(value, head):
    lane = lax.broadcasted_iota(jnp.int32, value.shape, 1)
    return jnp.where((lane // (LANE // 2)) == head, value, jnp.zeros_like(value))


def causal():
    return lax.broadcasted_iota(jnp.int32, (STEP, STEP), 0) <= lax.broadcasted_iota(
        jnp.int32, (STEP, STEP), 1
    )


def attend_kernel(plan, count, info_ref, *refs):
    pieces, refs = refs[:count], refs[count:]
    if plan.packed:
        halves, refs = refs[:2], refs[2:]
    else:
        table_in, inward_in, small_in = refs[:3]
        refs = refs[3:]
    (lifted_ref, query_ref, key_ref, value_ref, mixed_ref, total_ref, inward_ref, small_ref) = refs[:8]
    low_ref, table_ref, place_ref, stage_ref = refs[8:]
    pair = pl.program_id(0)
    total_rows, width = plan.total_rows, plan.width
    half = total_rows // 2
    split = info_ref[0] < total_rows
    far = jnp.where(split, FAR, 0.0)

    @pl.when(pair == 0)
    def _():
        if plan.packed:
            fill_early(plan, info_ref[1], halves, table_ref, inward_ref, small_ref, stage_ref)
        else:
            table_ref[...] = table_in[...]
            inward_ref[...] = inward_in[...]
            small_ref[...] = small_in[...]
        eye = (
            lax.broadcasted_iota(jnp.int32, (half, half), 0)
            == lax.broadcasted_iota(jnp.int32, (half, half), 1)
        ).astype(BF)
        per_half = half // LANE
        for part in range(2):
            table = jnp.concatenate(
                [table_ref[part * per_half + i] for i in range(per_half)], axis=1
            )
            place_ref[part * half : (part + 1) * half, :] = times_t(eye, table)
        rows = total_rows // count
        for mask in range(count):
            start = (info_ref[2] ^ mask) * rows
            place = start - jnp.where(jnp.logical_and(split, start >= half), half, 0)
            lifted = pieces[mask][...].astype(F32) + place_ref[pl.ds(pl.multiple_of(place, rows), rows), :]
            spot = pl.ds(pl.multiple_of(start, rows), rows)
            lifted_ref[spot, :] = lifted
            low_ref[spot, :] = lifted.astype(BF)

    weights = jnp.concatenate([inward_ref[pair + i * plan.lanes] for i in range(3)], axis=1)
    lanes = aligned(pair, LANE)
    query_bias = small_ref[0:1, lanes]
    value_bias = small_ref[1:2, lanes]
    for block in range(total_rows // STEP):
        spot = slice(block * STEP, (block + 1) * STEP)
        joint = times(low_ref[spot, :], weights)
        query_ref[spot, :] = (joint[:, :LANE] + query_bias).astype(BF) * BF(0.125)
        key_ref[spot, :] = joint[:, LANE : 2 * LANE].astype(BF)
        value_ref[spot, :] = (joint[:, 2 * LANE :] + value_bias).astype(BF)

    keep = causal()
    lower = lax.broadcasted_iota(jnp.int32, (LANE, STEP), 0) < LANE // 2

    value_t = value_ref[...].T

    def logits_of(block, head):
        start = block * STEP
        other = half if start >= half else 0
        mine = own_lanes(query_ref[start : start + STEP, :], head)
        near = times_t(key_ref[start : start + STEP, :], mine)
        same = times_t(key_ref[other:start, :], mine) if start > other else None
        away = times_t(key_ref[:other, :], mine) if other else None
        return near, same, away

    def mixed_of(block, head, near, same, away):
        start = block * STEP
        other = half if start >= half else 0
        near = jnp.where(keep, near, -FAR)
        peak = jnp.max(near, axis=0, keepdims=True)
        if same is not None:
            peak = jnp.maximum(peak, jnp.max(same, axis=0, keepdims=True))
        if away is not None:
            peak = jnp.maximum(peak, jnp.max(away, axis=0, keepdims=True) - far)
        raised = [jnp.exp(piece - peak) for piece in (same, near) if piece is not None]
        total = sum(jnp.sum(piece, axis=0, keepdims=True) for piece in raised)
        low = jnp.concatenate([piece.astype(BF) for piece in raised], axis=0)
        mixed = times(value_t[:, other : start + STEP], low)
        if away is not None:
            away = jnp.exp(away - (peak + far))
            total = total + jnp.sum(away, axis=0, keepdims=True)
            mixed = mixed + times(value_t[:, :other], away.astype(BF))
        total_ref[0, head : head + 1, start : start + STEP] = peak + jnp.log(total)
        return mixed * (1.0 / total)

    tasks = [(block, head) for block in range(total_rows // STEP) for head in range(2)]
    ahead = logits_of(*tasks[0])
    parts = []
    for index, (block, head) in enumerate(tasks):
        logits, ahead = ahead, logits_of(*tasks[index + 1]) if index + 1 < len(tasks) else None
        parts.append(mixed_of(block, head, *logits))
        if head:
            mixed_ref[block * STEP : (block + 1) * STEP, :] = jnp.where(lower, *parts).T.astype(BF)
            parts = []


def attend(plan, info, count, pieces, weights):
    total_rows, width = plan.total_rows, plan.width
    block = pl.BlockSpec((total_rows, LANE), lambda p, *_: (0, p))
    low = pltpu.HBM((total_rows, width), BF)
    inward = (3 * plan.lanes, width, LANE)
    small = (plan.small_rows, width)
    return pl.pallas_call(
        functools.partial(attend_kernel, plan, count),
        grid_spec=pltpu.PrefetchScalarGridSpec(
            num_scalar_prefetch=1,
            grid=(plan.lanes,),
            in_specs=[HELD for v in pieces + weights],
            out_specs=[
                full((total_rows, width)),
                block,
                block,
                block,
                block,
                pl.BlockSpec((1, 8, total_rows), lambda p, *_: (p, 0, 0)),
                full(inward),
                full(small),
            ],
            scratch_shapes=[
                pltpu.VMEM((total_rows, width), BF),
                pltpu.VMEM((plan.table_pieces, width, LANE), BF),
                pltpu.VMEM((total_rows, width), F32),
                pltpu.VMEM((plan.devices, TILE, LANE), F32),
            ],
        ),
        out_shape=[
            pltpu.HBM((total_rows, width), F32),
            low,
            low,
            low,
            low,
            pltpu.HBM((plan.lanes, 8, total_rows), F32),
            pltpu.HBM(inward, BF),
            pltpu.HBM(small, F32),
        ],
        compiler_params=params(36),
        cost_estimate=cost(5 * 10**9, 14 * 2**20, 6 * 10**6),
        name="attend",
    )(info, *hold(pieces), *hold(weights))


def norm(rows):
    center = rows - jnp.mean(rows, axis=1, keepdims=True)
    root = lax.rsqrt(jnp.mean(center * center, axis=1, keepdims=True) + 1e-05)
    return center * root, root


def norm_back(upstream, gain, unit, root):
    scaled = upstream * gain
    mean = jnp.mean(scaled, axis=1, keepdims=True)
    slope = jnp.mean(scaled * unit, axis=1, keepdims=True)
    return (scaled - mean - unit * slope) * root


def feed_kernel(plan, count, info_ref, lifted_ref, mixed_ref, *refs):
    upstreams, refs = refs[:count], refs[count:]
    if plan.packed:
        late_quarters, small_ref = refs[:8], refs[8]
        refs = refs[9:]
    else:
        outward_in, expand_in, contract_in, small_ref = refs[:4]
        refs = refs[4:]
    results, refs = refs[:count], refs[count:]
    mixed_back_ref, first_back_ref, small_grad_ref = refs[:3]
    refs = refs[3:]
    if plan.packed:
        halves, refs = (refs[:2], refs[2:4]), refs[4:]
    else:
        outward_out, expand_out, contract_out = refs[:3]
        refs = refs[3:]
    (outward_ref, expand_ref, contract_ref, upstream_ref, result_ref, slope_ref, active_all, hidden_all, normed_all,
     lowered_all, branch_all, mixed_all, whole_ref, expand_sum, contract_sum) = refs
    step = pl.program_id(0)
    width, parts, lanes = plan.width, plan.parts, plan.lanes
    contract_own = plan.hidden // plan.devices
    contract_at = (lanes + parts * lanes) * TILE

    @pl.when(step == 0)
    def _():
        if plan.packed:
            for mask in range(plan.devices):
                at = plan.place(mask)
                shard = late_quarters[(mask & 1) * 4 + at // 4].at[at % 4]
                owner = info_ref[1] ^ mask
                rows, wide = aligned(owner, TILE), aligned(owner, contract_own)
                for lane in range(lanes):
                    cut = slice(lane * LANE, (lane + 1) * LANE)
                    outward_ref[rows, cut] = shard[lane * TILE : (lane + 1) * TILE, :]
                    for part in range(parts):
                        at = (lanes + part * lanes + lane) * TILE
                        expand_ref[part, rows, cut] = shard[at : at + TILE, :]
                    at = contract_at + lane * contract_own
                    contract_ref[wide, cut] = shard[at : at + contract_own, :]
        else:
            outward_ref[...] = outward_in[...]
            expand_ref[...] = expand_in[...]
            contract_ref[...] = contract_in[...]

    size = lifted_ref.shape[0]
    here = pl.ds(pl.multiple_of(step * size, size), size)
    rows = plan.total_rows // count
    group = size // rows

    def spot(mask):
        return pl.ds(pl.multiple_of(((info_ref[2] ^ mask) % group) * rows, rows), rows)

    for mask in range(count):
        @pl.when(step == mask // group)
        def _(mask=mask):
            upstream_ref[spot(mask), :] = upstreams[mask][...]

    outlet, steady, offset = (small_ref[i : i + 1, :] for i in (2, 3, 4))
    settle, temper, anchor = (small_ref[i + parts : i + parts + 1, :] for i in (5, 6, 7))
    mixed = mixed_ref[...]
    branch = times(mixed, outward_ref[...]) + outlet
    unit, root = norm(lifted_ref[...] + branch)
    normed = unit * steady + offset
    normed_low = normed.astype(BF)
    normed_all[here, :] = normed_low
    mixed_all[here, :] = mixed
    lowered = jnp.zeros_like(normed)
    for part in range(parts):
        cut = slice(part * width, (part + 1) * width)
        hidden = times(normed_low, expand_ref[part]) + small_ref[5 + part : 6 + part, :]
        square = hidden * hidden
        bend = jnp.tanh(hidden * (BEND + BEND * 0.044715 * square))
        half = 0.5 + 0.5 * bend
        active = (hidden * half).astype(BF)
        active_all[here, cut] = active
        slope_ref[:, cut] = half + (0.5 * hidden) * (1.0 - bend * bend) * (
            BEND + 3 * BEND * 0.044715 * square
        )
        lowered = lowered + times(active, contract_ref[cut, :])
    last_unit, last_root = norm(normed + (lowered + settle))
    result_ref[...] = (last_unit * temper + anchor).astype(BF)
    upstream = upstream_ref[...].astype(F32)
    temper_grad = column_sum(upstream * last_unit)
    anchor_grad = column_sum(upstream)
    second_back = norm_back(upstream, temper, last_unit, last_root)
    lowered_back = second_back.astype(BF)
    lowered_all[here, :] = lowered_back
    settle_grad = column_sum(lowered_back)
    normed_back = second_back
    spread_grads = []
    for part in range(parts):
        cut = slice(part * width, (part + 1) * width)
        active_back = times_t(lowered_back, contract_ref[cut, :])
        hidden_back = (active_back * slope_ref[:, cut]).astype(BF)
        spread_grads.append(column_sum(hidden_back))
        hidden_all[here, cut] = hidden_back
        normed_back = normed_back + times_t(hidden_back, expand_ref[part])
    first_back = norm_back(normed_back, steady, unit, root)
    first_back_ref[...] = first_back
    branch_back = first_back.astype(BF)
    mixed_back_ref[...] = times_t(branch_back, outward_ref[...]).astype(BF)
    branch_all[here, :] = branch_back
    zero = jnp.zeros_like(anchor_grad)
    grads = [zero, zero, column_sum(branch_back), column_sum(normed_back * unit)]
    grads += [column_sum(normed_back)] + spread_grads + [settle_grad, temper_grad, anchor_grad]
    grads += [zero] * (plan.small_rows - len(grads))
    small_term = jnp.concatenate(grads, axis=0)
    for mask in range(count):
        @pl.when(step == mask // group)
        def _(mask=mask):
            results[mask][...] = result_ref[spot(mask), :]

    @pl.when(step == 0)
    def _():
        small_grad_ref[...] = small_term

    @pl.when(step > 0)
    def _():
        small_grad_ref[...] += small_term

    @pl.when(step == pl.num_programs(0) - 1)
    def _():
        outward = t_times(mixed_all[...], branch_all[...])
        if plan.packed:
            me = info_ref[1]
            whole_ref[...] = outward
            for mask in range(plan.devices):
                half = halves[mask & 1]
                rows = aligned(me ^ mask, TILE)
                for lane in range(lanes):
                    cut = slice(lane * LANE, (lane + 1) * LANE)
                    plan.grad_piece(half, mask, lane * TILE, TILE)[...] = whole_ref[rows, cut].astype(BF)
        else:
            outward_out[...] = outward.astype(BF)
        per_part = plan.devices // parts
        for part in range(parts):
            cut = slice(part * width, (part + 1) * width)
            expand = t_times(normed_all[...], hidden_all[:, cut])
            if not plan.packed:
                expand_out[part] = expand.astype(BF)
                continue
            expand_sum[...] = expand
            for mask in range(plan.devices):
                rows = aligned(me ^ mask, TILE)
                for lane in range(lanes):
                    at = (lanes + part * lanes + lane) * TILE
                    plan.grad_piece(halves[mask & 1], mask, at, TILE)[...] = expand_sum[
                        rows, lane * LANE : (lane + 1) * LANE
                    ].astype(BF)
        for mask_part in range(parts):
            part = (me // per_part) ^ mask_part if plan.packed else mask_part
            cut = pl.ds(pl.multiple_of(part * width, width), width)
            contract = t_times(active_all[:, cut], lowered_all[...])
            if not plan.packed:
                contract_out[cut, :] = contract.astype(BF)
                continue
            contract_sum[...] = contract
            for index in range(per_part):
                mask = mask_part * per_part + index
                rows = aligned((me ^ mask) % per_part, contract_own)
                for lane in range(lanes):
                    at = contract_at + lane * contract_own
                    plan.grad_piece(halves[mask & 1], mask, at, contract_own)[...] = contract_sum[
                        rows, lane * LANE : (lane + 1) * LANE
                    ].astype(BF)


def feed(plan, info, count, lifted, mixed, upstreams, weights, small):
    total_rows, width, parts = plan.total_rows, plan.width, plan.parts
    piece = total_rows // count
    size = max(piece, FEED_ROWS)
    group = size // piece
    rows = pl.BlockSpec((size, width), lambda i, info: ((info[2] // group) ^ i, 0))
    outward, expand, contract = (width, width), (parts, width, width), (parts * width, width)
    if plan.packed:
        grads = [pltpu.VMEM((8 * plan.late_rows, LANE), BF)] * 4
    else:
        grads = [pltpu.VMEM(outward, BF), pltpu.VMEM(expand, BF), pltpu.VMEM(contract, BF)]
    ends = [like((piece, width), BF)] * count
    outs = [like((total_rows, width), BF), like((total_rows, width), F32), like(small.shape, F32)]
    values = pl.pallas_call(
        functools.partial(feed_kernel, plan, count),
        grid_spec=pltpu.PrefetchScalarGridSpec(
            num_scalar_prefetch=1,
            grid=(total_rows // size,),
            in_specs=[rows, rows]
            + [full(v.shape) for v in upstreams]
            + [HELD for v in weights]
            + [full(small.shape)],
            out_specs=[full(v.shape) for v in ends]
            + [rows, rows, full(small.shape)]
            + [HELD for v in grads],
            scratch_shapes=[
                pltpu.VMEM(outward, BF),
                pltpu.VMEM(expand, BF),
                pltpu.VMEM(contract, BF),
                pltpu.VMEM((size, width), BF),
                pltpu.VMEM((size, width), BF),
                pltpu.VMEM((size, parts * width), F32),
                pltpu.VMEM((total_rows, parts * width), BF),
                pltpu.VMEM((total_rows, parts * width), BF),
                pltpu.VMEM((total_rows, width), BF),
                pltpu.VMEM((total_rows, width), BF),
                pltpu.VMEM((total_rows, width), BF),
                pltpu.VMEM((total_rows, width), BF),
                pltpu.VMEM(outward, F32),
                pltpu.VMEM(outward, F32),
                pltpu.VMEM(outward, F32),
            ],
        ),
        out_shape=ends + outs + grads,
        compiler_params=params(51),
        cost_estimate=cost(15 * 10**9, 20 * 2**20, 2 * 10**6),
        name="feed",
    )(info, lifted, mixed, *upstreams, *hold(weights), small)
    return values[:count], values[count : count + 3], values[count + 3 :]


def attend_back_kernel(
    plan, count, info_ref, lifted_ref, query_ref, key_ref, value_ref, mixed_ref, mixed_back_ref,
    total_ref, inward_ref, first_back_ref, small_grad_ref, *refs
):
    tokens, refs = refs[:count], refs[count:]
    if plan.packed:
        halves, refs = refs[:2], refs[2:]
    else:
        table_out, inward_out, small_out = refs[:3]
        refs = refs[3:]
    (joint_ref, sum_ref, share_ref, score_ref, grad_ref, table_ref, joint_sums, blocks_ref,
     lifted_here, inward_here, copied) = refs
    pair = pl.program_id(0)
    copies = [
        pltpu.make_async_copy(source, target, copied.at[index])
        for index, (source, target) in enumerate(
            ((lifted_ref, lifted_here), (inward_ref, inward_here), (first_back_ref, sum_ref))
        )
    ]

    @pl.when(pair == 0)
    def _():
        for copy in copies:
            copy.start()

    total_rows, lanes = plan.total_rows, plan.lanes
    half = total_rows // 2
    split = info_ref[0] < total_rows
    far = jnp.where(split, FAR, 0.0)
    blocks = total_rows // STEP

    keep = causal()
    lower = lax.broadcasted_iota(jnp.int32, (STEP, LANE), 1) < LANE // 2
    lower_t = lax.broadcasted_iota(jnp.int32, (LANE, STEP), 0) < LANE // 2
    product = (mixed_ref[...].astype(F32) * mixed_back_ref[...].astype(F32)).T
    scaled_key = (key_ref[...] * BF(0.125)).T
    betweens = [
        jnp.sum(product[head * LANE // 2 : (head + 1) * LANE // 2], axis=0, keepdims=True)
        for head in range(2)
    ]

    def logits_of(block, head):
        spot = slice(block * STEP, (block + 1) * STEP)
        keys = slice(0, (block + 1) * STEP)
        query = own_lanes(query_ref[spot, :], head)
        back = own_lanes(mixed_back_ref[spot, :], head)
        return times_t(key_ref[keys, :], query), times_t(value_ref[keys, :], back)

    def scores_of(block, head, logits, share_back):
        start = block * STEP
        spot = slice(start, start + STEP)
        total = total_ref[0, head : head + 1, spot]
        gap = betweens[head][:, spot]
        for under in range(block + 1):
            keys = slice(under * STEP, (under + 1) * STEP)
            away = start >= half and under * STEP < half
            share = jnp.exp(logits[keys] - (total + far if away else total))
            if under == block:
                share = jnp.where(keep, share, 0.0)
            score = share * (share_back[keys] - gap)
            share_ref[head, keys, spot] = share.astype(BF)
            score_ref[head, keys, spot] = score.astype(BF)

    def backs_of(block, head):
        start = block * STEP
        spot = slice(start, start + STEP)
        end = start + STEP
        query_back = times(scaled_key[:, :end], score_ref[head, :end, spot])
        key_back = times(score_ref[head, spot, start:], query_ref[start:, :])
        value_back = times(share_ref[head, spot, start:], mixed_back_ref[start:, :])
        return query_back, key_back, value_back

    tasks = [(block, head) for block in reversed(range(blocks)) for head in range(2)]
    ahead = logits_of(*tasks[0])
    parts = []
    for index, (block, head) in enumerate(tasks):
        logits, ahead = ahead, logits_of(*tasks[index + 1]) if index + 1 < len(tasks) else None
        scores_of(block, head, *logits)
        parts.append(backs_of(block, head))
        if head:
            spot = slice(block * STEP, (block + 1) * STEP)
            query_back = jnp.where(lower_t, parts[0][0], parts[1][0]).T
            key_back = jnp.where(lower, parts[0][1], parts[1][1])
            value_back = jnp.where(lower, parts[0][2], parts[1][2])
            for part, back in enumerate((query_back, key_back, value_back)):
                joint_ref[spot, aligned(pair + part * lanes, LANE)] = back.astype(BF)
            parts = []

    @pl.when(pair == lanes - 1)
    def _():
        for copy in copies:
            copy.wait()
        low = lifted_here[...].astype(BF).T
        weights = jnp.concatenate([inward_here[i] for i in range(3 * lanes)], axis=1)
        for block in range(blocks):
            spot = slice(block * STEP, (block + 1) * STEP)
            sum_ref[spot, :] += times_t(joint_ref[spot, :], weights)
        for part in range(3):
            joint = joint_ref[:, part * plan.width : (part + 1) * plan.width]
            grads = times(low, joint)
            for lane in range(lanes):
                grad_ref[part * lanes + lane] = grads[:, lane * LANE : (lane + 1) * LANE]
            if part != 1:
                sums = column_sum(joint)
                for lane in range(lanes):
                    at = lane if part == 0 else lane + lanes
                    joint_sums[at : at + 1, :] = sums[:, lane * LANE : (lane + 1) * LANE]
        rows = total_rows // count
        for mask in range(count):
            spot = pl.ds(pl.multiple_of((info_ref[2] ^ mask) * rows, rows), rows)
            tokens[mask][...] = sum_ref[spot, :].astype(BF)
        late = sum_ref[half:, :]
        early = sum_ref[:half, :] + jnp.where(split, late, 0.0)
        table_ref[:, :half] = early.T
        table_ref[:, half:] = jnp.where(split, 0.0, late).T
        counted = info_ref[3] > 0
        blocks_ref[: 2 * lanes, :] = joint_sums[: 2 * lanes, :]
        for row in range(2, plan.block_starts[-1] // lanes):
            for lane in range(lanes):
                blocks_ref[row * lanes + lane : row * lanes + lane + 1, :] = small_grad_ref[
                    row : row + 1, lane * LANE : (lane + 1) * LANE
                ]
        if plan.packed:
            for mask in range(plan.devices):
                shard = halves[mask & 1].at[plan.place(mask)]
                owner = info_ref[1] ^ mask
                own = aligned(owner, TILE)
                for piece in range(plan.table_pieces):
                    shard[piece * TILE : (piece + 1) * TILE, :] = table_ref[
                        own, piece * LANE : (piece + 1) * LANE
                    ].astype(BF)
                for piece in range(3 * lanes):
                    at = (plan.table_pieces + piece) * TILE
                    shard[at : at + TILE, :] = grad_ref[piece, own, :].astype(BF)
                rows = [
                    blocks_ref[pl.ds(plan.block_starts[v] + owner * plan.owned[v] // LANE, 1), :]
                    for v in range(VECTORS)
                ]
                rows.append(jnp.zeros((TILE - VECTORS, LANE), F32))
                at = plan.early_pieces * TILE
                shard[at : at + TILE, :] = jnp.concatenate(rows, axis=0).astype(BF)
        else:
            table_out[...] = jnp.where(counted, table_ref[...], 0.0).astype(BF)
            inward_out[...] = jnp.where(counted, grad_ref[...], 0.0).astype(BF)
            small_out[...] = jnp.where(counted, blocks_ref[...], 0.0)


def attend_back(plan, info, count, lifted, saved, mixed_back, inward, first_back, small_grad):
    query, key, value, mixed, totals = saved
    total_rows, width, lanes = plan.total_rows, plan.width, plan.lanes
    block = pl.BlockSpec((total_rows, LANE), lambda p, *_: (0, p))
    blocks = (plan.block_starts[-1], LANE)
    if plan.packed:
        grads = [pltpu.VMEM((plan.devices // 2, plan.early_rows, LANE), BF)] * 2
    else:
        grads = [pltpu.VMEM((width, total_rows), BF), pltpu.VMEM(inward.shape, BF), pltpu.VMEM(blocks, F32)]
    tokens = [pltpu.VMEM((total_rows // count, width), BF)] * count
    values = pl.pallas_call(
        functools.partial(attend_back_kernel, plan, count),
        grid_spec=pltpu.PrefetchScalarGridSpec(
            num_scalar_prefetch=1,
            grid=(lanes,),
            in_specs=[
                pl.BlockSpec(memory_space=pl.ANY),
                block,
                block,
                block,
                block,
                block,
                pl.BlockSpec((1, 8, total_rows), lambda p, *_: (p, 0, 0)),
                pl.BlockSpec(memory_space=pl.ANY),
                pl.BlockSpec(memory_space=pl.ANY),
                full(small_grad.shape),
            ],
            out_specs=[HELD for v in tokens + grads],
            scratch_shapes=[
                pltpu.VMEM((total_rows, 3 * width), BF),
                pltpu.VMEM((total_rows, width), F32),
                pltpu.VMEM((2, total_rows, total_rows), BF),
                pltpu.VMEM((2, total_rows, total_rows), BF),
                pltpu.VMEM(inward.shape, F32),
                pltpu.VMEM((width, total_rows), F32),
                pltpu.VMEM((8, LANE), F32),
                pltpu.VMEM(blocks, F32),
                pltpu.VMEM(lifted.shape, F32),
                pltpu.VMEM(inward.shape, BF),
                pltpu.SemaphoreType.DMA((3,)),
            ],
        ),
        out_shape=tokens + grads,
        compiler_params=params(40),
        cost_estimate=cost(14 * 10**9, 24 * 2**20, 6 * 10**6),
        name="attend_back",
    )(info, *stay([lifted, query, key, value, mixed, mixed_back, totals, inward, first_back]), small_grad)
    return values[:count], values[count:]


def pack_kernel(plan, count, share, rows_ref, table_ref, inward_ref, *refs):
    vectors, refs = refs[:VECTORS], refs[VECTORS:]
    outward_ref, expand_ref, contract_ref = refs[:3]
    pieces, early_ref, late_ref = refs[3 : 3 + count], refs[3 + count], refs[4 + count]
    rank = lax.axis_index("seq")
    for mask in range(count):
        pieces[mask][...] = rows_ref[pl.ds((rank ^ mask) // share, 1), :, :][0]
    at = 0
    for ref in (table_ref, inward_ref):
        for lane in range(ref.shape[1] // LANE):
            early_ref[0, at : at + TILE, :] = ref[:, lane * LANE : (lane + 1) * LANE]
            at += TILE
    rows = []
    for size, ref in zip(plan.owned, vectors):
        rows.append(jnp.concatenate([ref[...].astype(F32)] * (LANE // size), axis=1))
    rows.append(jnp.zeros((TILE - VECTORS, LANE), F32))
    early_ref[0, at : at + TILE, :] = jnp.concatenate(rows, axis=0).astype(BF)
    at = 0
    for ref in (outward_ref, expand_ref, contract_ref):
        rows = ref.shape[0]
        for lane in range(ref.shape[1] // LANE):
            late_ref[0, at : at + rows, :] = ref[:, lane * LANE : (lane + 1) * LANE]
            at += rows


def pack(plan, count, share, rows, table, inward, vectors, outward, expand, contract):
    vectors = [v.reshape(1, -1) for v in vectors]
    outs = [like(rows.shape[1:], BF)] * count
    outs += [like((1, plan.early_rows, LANE), BF), like((1, plan.late_rows, LANE), BF)]
    values = pl.pallas_call(
        functools.partial(pack_kernel, plan, count, share),
        out_shape=outs,
        cost_estimate=cost(0, 4 * 2**20),
        name="pack",
    )(rows, table, inward, *vectors, outward, expand, contract)
    return values[:count], values[count], values[count + 1]


def fold(terms, cuts):
    size = terms[0].shape[0] // cuts
    return [
        sum(term[index * size : (index + 1) * size].astype(F32) for term in terms).astype(BF)
        for index in range(cuts)
    ]


def finish_kernel(plan, info_ref, *refs):
    early, late, refs = refs[:4], refs[4:8], refs[8:]
    table_ref, inward_ref, outward_ref, expand_ref, contract_ref = refs[:5]
    vectors = refs[5:]
    early = sum(ref[0].astype(F32) for ref in early)
    late = sum(ref[...].astype(F32) for ref in late)
    for piece in range(plan.table_pieces):
        table_ref[:, piece * LANE : (piece + 1) * LANE] = early[piece * TILE : (piece + 1) * TILE]
    for piece in range(3 * plan.lanes):
        at = (plan.table_pieces + piece) * TILE
        inward_ref[:, piece * LANE : (piece + 1) * LANE] = early[at : at + TILE]
    at = 0
    for ref in (outward_ref, expand_ref, contract_ref):
        rows = ref.shape[0]
        for lane in range(ref.shape[1] // LANE):
            ref[:, lane * LANE : (lane + 1) * LANE] = late[at : at + rows]
            at += rows
    at = plan.early_pieces * TILE
    small = early[at : at + VECTORS]
    for vector, ref in enumerate(vectors):
        size = plan.owned[vector]
        slot = lax.rem(info_ref[1], LANE // size)
        row = pltpu.roll(small, LANE - slot * size, 1)
        ref[...] = row[vector : vector + 1, :size]


def finish(plan, info, early, late):
    own, width = plan.own_rows, plan.width
    outs = [
        like((own, plan.total_rows), F32),
        like((own, 3 * width), F32),
        like((own, width), F32),
        like((own, plan.hidden), F32),
        like((plan.hidden // plan.devices, width), F32),
    ] + [like((1, n), F32) for n in plan.owned]
    values = early + late
    return pl.pallas_call(
        functools.partial(finish_kernel, plan),
        grid_spec=pltpu.PrefetchScalarGridSpec(
            num_scalar_prefetch=1,
            grid=(1,),
            in_specs=[HELD for v in values],
            out_specs=[full(v.shape) for v in outs],
        ),
        out_shape=outs,
        name="finish",
    )(info, *hold(values))


def ordered(rank, pieces):
    for bit in (1, 2):
        flip = (rank & bit) > 0
        pieces = [jnp.where(flip, pieces[i ^ bit], pieces[i]) for i in range(4)]
    return jnp.stack(pieces)


def settle_kernel(count, share, info_ref, *refs):
    for mask in range(count):
        refs[count][pl.ds((info_ref[2] ^ mask) // share, 1), :, :] = refs[mask][...][None]


def settle_rows(info, micro_count, share, pieces):
    out = (micro_count,) + pieces[0].shape
    return pl.pallas_call(
        functools.partial(settle_kernel, len(pieces), share),
        grid_spec=pltpu.PrefetchScalarGridSpec(
            num_scalar_prefetch=1,
            grid=(1,),
            in_specs=[full(v.shape) for v in pieces],
            out_specs=full(out),
        ),
        out_shape=like(out, BF),
        cost_estimate=cost(0, 48 * 2**20),
        name="settle_rows",
    )(info, *pieces)


def cut_kernel(count, share, rows_ref, *refs):
    rank = lax.axis_index("seq")
    for mask in range(count):
        refs[mask][...] = rows_ref[pl.ds((rank ^ mask) // share, 1), :, :][0]


def cut_rows(rows, count, share):
    outs = [like(rows.shape[1:], BF)] * count
    return pl.pallas_call(
        functools.partial(cut_kernel, count, share),
        out_shape=outs,
        cost_estimate=cost(0, 4 * 2**20),
        name="cut_rows",
    )(rows)


def local(tokens, first_length, cotangent, positions, inward, intake, outward, outlet, steady, offset,
          expand, spread, contract, settle, temper, anchor):
    micro_count, pack_count, block_rows, width = tokens.shape
    assert pack_count == 1
    devices, count = lax.axis_size(AXES), lax.axis_size("seq")
    me, rank = lax.axis_index(AXES), lax.axis_index("seq")
    share = max(count // micro_count, 1)
    assert share * micro_count == count
    plan = Plan(devices, width, contract.shape[0] * devices, block_rows * count)
    micro = rank // share
    counted = (rank % share == 0).astype(jnp.int32)

    def info_of(lengths):
        first = jnp.sum(jnp.where(jnp.arange(micro_count) == micro, lengths[:, 0], 0))
        return jnp.stack([first, me, rank, counted]).astype(jnp.int32)

    vectors = (intake, outlet, steady, offset, spread, settle, temper, anchor)

    def swap(value, mask):
        return lax.ppermute(value, AXES, [(d, d ^ mask) for d in range(devices)]) if mask else value

    def exchange(pieces):
        return [swap(piece, mask) for mask, piece in enumerate(pieces)]

    def in_order(pieces):
        if count != 4 or share != 1:
            return settle_rows(info, micro_count, share, pieces)
        return ordered(rank, pieces)

    if plan.packed:
        rows_in, shard, late = pack(
            plan, count, share, tokens[:, 0], positions.T, inward, vectors, outward, expand, contract
        )
        rows_in = exchange(rows_in)
        shard, rows_in[1] = lax.optimization_barrier((shard, rows_in[1]))
        pieces = [swap(shard, mask) for mask in plan.z_order]
        pieces, rows_in, late, cotangent, first_length = lax.optimization_barrier(
            (pieces, rows_in, late, cotangent, first_length)
        )
        info = info_of(first_length)
        shard = jnp.concatenate(pieces, axis=0)
        pieces = [swap(shard, k << 1) for k in range(4)]
        late = [swap(late, mask) for mask in plan.z_order]
        upstreams = cut_rows(cotangent[:, 0], count, share)
        pieces, upstreams, late, info = lax.optimization_barrier((pieces, list(upstreams), late, info))
        late = jnp.concatenate(late, axis=0)
        late_x, late_y = swap(late, 2), swap(late, 4)
        shard = jnp.concatenate(pieces, axis=0)
        early = [shard, swap(shard, 1)]
        upstreams[1] = swap(upstreams[1], 1)
        late_core = swap(late, 1)
        early, late_core, late_x, late_y, upstreams = lax.optimization_barrier(
            (early, late_core, late_x, late_y, upstreams)
        )
        late_xy = swap(late_x, 4)
        upstreams[2:] = [swap(upstreams[mask], mask) for mask in (2, 3)]
        late_cores = [late_core, swap(late_x, 1), swap(late_y, 1)]
    else:
        info = info_of(first_length)
        rows_in = exchange(cut_rows(tokens[:, 0], count, share))
        upstreams = exchange(cut_rows(cotangent[:, 0], count, share))
        early, late = plain_weights(plan, positions, inward, vectors, outward, expand, contract)
    lifted, query, key, value, mixed, totals, inward_all, small = attend(plan, info, count, rows_in, early)
    if plan.packed:
        late_xy, late_cores, upstreams, mixed = lax.optimization_barrier(
            (late_xy, late_cores, upstreams, mixed)
        )
        late = [late, late_x, late_y, late_xy] + late_cores + [swap(late_xy, 1)]
    results, (mixed_back, first_back, small_grad), late_grads = feed(
        plan, info, count, lifted, mixed, upstreams, late, small
    )
    results = exchange(results)
    if plan.packed:
        stay_keep, go_keep, stay_send, go_send = late_grads
        cut = 8 * plan.late_cut
        go = [go_keep, swap(go_send, 1)]
        one_send, two_send = fold([v[:cut] for v in go], 1) + fold([v[cut:] for v in go], 1)
        stay_other = swap(stay_send, 1)
        one_send, two_send, mixed_back = lax.optimization_barrier((one_send, two_send, mixed_back))
        one_other, two_other = swap(one_send, 4), swap(two_send, 2)
    token_pieces, early_grads = attend_back(
        plan, info, count, lifted, (query, key, value, mixed, totals), mixed_back, inward_all,
        first_back, small_grad,
    )
    if plan.packed:
        one_other, two_other, stay_other, results, token_pieces, early_grads = lax.optimization_barrier(
            (one_other, two_other, stay_other, results, token_pieces, early_grads)
        )
        keep, send = early_grads
        send = swap(send, 1)
        one, one_send = fold([stay_keep[:cut], stay_other[:cut], one_other], 2)
        two, two_send = fold([stay_keep[cut:], stay_other[cut:], two_other], 2)
        one, one_send, two, two_send, keep = lax.optimization_barrier((one, one_send, two, two_send, keep))
        one_other, two_other = swap(one_send, 2), swap(two_send, 4)
        terms = fold([keep, send], 4)
        terms, results, token_pieces = lax.optimization_barrier((terms, results, token_pieces))
        terms = [swap(term, k << 1) for k, term in enumerate(terms)]
        output = settle_rows(info, micro_count, share, results)
        one_other, two_other, output = lax.optimization_barrier((one_other, two_other, output))
        ones, twos = fold([one, one_other], 4), fold([two, two_other], 4)
        late_terms = [jnp.concatenate(pair, axis=0) for pair in zip(ones, twos)]
        late_terms = [swap(term, mask) for term, mask in zip(late_terms, plan.z_order)]
        token_pieces = list(token_pieces)
        token_pieces[1] = swap(token_pieces[1], 1)
        terms, late_terms, output, token_pieces = lax.optimization_barrier(
            (terms, late_terms, output, token_pieces)
        )
        terms = fold(terms, 4)
        early_terms = [swap(term, mask) for term, mask in zip(terms, plan.z_order)]
        token_pieces[2:] = [swap(token_pieces[mask], mask) for mask in (2, 3)]
        tokens_back = in_order(token_pieces)
        values = finish(plan, info, early_terms, late_terms)
        table_t, inward_own, outward_own, expand_own, contract_own = values[:5]
        own = [v.reshape(-1) for v in values[5:]]
        table_own = table_t.T
    else:
        output = in_order(results)
        tokens_back = in_order(exchange(token_pieces))
        table_own, inward_own, outward_own, expand_own, contract_own, own = plain_grads(
            plan, counted, early_grads, late_grads
        )
    return (output[:, None], tokens_back[:, None], table_own, inward_own, own[0], outward_own, own[1], own[2],
            own[3], expand_own, own[4], contract_own, own[5], own[6], own[7])


def plain_weights(plan, positions, inward, vectors, outward, expand, contract):
    lanes, width = plan.lanes, plan.width

    def gather(value, axis=0):
        return lax.all_gather(value, AXES, axis=axis, tiled=True)

    def in_pieces(value, size):
        return value.reshape(value.shape[0], -1, size).transpose(1, 0, 2)

    table = in_pieces(gather(positions, 1).T, LANE)
    small = jnp.concatenate([gather(v) for v in vectors]).astype(F32).reshape(-1, width)
    small = jnp.pad(small, ((0, plan.small_rows - small.shape[0]), (0, 0)))
    early = [table, in_pieces(gather(inward), LANE), small]
    return early, [gather(outward), in_pieces(gather(expand), width), gather(contract)]


def plain_grads(plan, counted, early_grads, late_grads):
    width = plan.width
    table, inward, small = early_grads
    outward, expand, contract = (jnp.where(counted > 0, g, BF(0)) for g in late_grads)

    def scatter(value, axis=0):
        return lax.psum_scatter(value, AXES, scatter_dimension=axis, tiled=True).astype(F32)

    def whole(value):
        return value.transpose(1, 0, 2).reshape(value.shape[1], -1)

    flat = small.reshape(-1)
    own = []
    for vector, length in enumerate(plan.lengths):
        start = plan.block_starts[vector] * LANE
        own.append(scatter(flat[start : start + length]))
    return (scatter(table.T, 1), scatter(whole(inward)), scatter(outward), scatter(whole(expand)),
            scatter(contract), own)


def solution(mesh):
    rows = P(None, "batch", "seq", None)
    table = P(None, AXES)
    matrix = P(AXES, None)
    vector = P(AXES)
    weights = (table, matrix, vector, matrix, vector, vector, vector, matrix, vector, matrix, vector,
               vector, vector)
    return jax.shard_map(
        local,
        mesh=mesh,
        in_specs=(rows, P(None, "batch"), rows) + weights,
        out_specs=(rows, rows) + weights,
        check_vma=False,
    )
```

```python
import functools

import jax
import jax.numpy as jnp
from jax import lax
from jax.experimental import pallas as pl
from jax.experimental.pallas import tpu as pltpu
from jax.sharding import PartitionSpec as P

AXES = ("batch", "seq")
LANE = 128
TILE = 16
FEED_ROWS = 512
STEP = 256
FAR = 1e30
BEND = 0.7978845608028654
BF = jnp.bfloat16
F32 = jnp.float32
VECTORS = 8


def times(left, right):
    return jnp.dot(left, right, preferred_element_type=F32)


def times_t(left, right):
    return lax.dot_general(left, right, (((1,), (1,)), ((), ())), preferred_element_type=F32)


def t_times(left, right):
    return lax.dot_general(left, right, (((0,), (0,)), ((), ())), preferred_element_type=F32)


def column_sum(values):
    return jnp.sum(values.astype(F32), axis=0, keepdims=True)


def aligned(index, size):
    return pl.ds(pl.multiple_of(index * size, size), size)


def like(shape, kind):
    return jax.ShapeDtypeStruct(shape, kind)


def full(shape):
    return pl.BlockSpec(shape, lambda *_: (0,) * len(shape), pipeline_mode=pl.Buffered(1))


HELD = pl.BlockSpec(memory_space=pltpu.VMEM)


def hold(values):
    return [pltpu.with_memory_space_constraint(v, pltpu.VMEM) for v in values]


def stay(values):
    return [pltpu.with_memory_space_constraint(v, pltpu.HBM) for v in values]


def params(megabytes):
    return pltpu.CompilerParams(vmem_limit_bytes=megabytes * 2**20)


def cost(flops, size, exps=0):
    return pl.CostEstimate(flops=flops, bytes_accessed=size, transcendentals=exps)


class Plan:
    def __init__(self, devices, width, hidden, total_rows):
        self.devices = devices
        self.width = width
        self.hidden = hidden
        self.total_rows = total_rows
        self.own_rows = width // devices
        self.packed = devices == 32 and self.own_rows % TILE == 0
        self.lanes = width // LANE
        self.parts = hidden // width
        self.table_pieces = total_rows // LANE
        self.early_pieces = self.table_pieces + 3 * self.lanes
        self.early_rows = (self.early_pieces + 1) * TILE
        self.late_rows = (self.lanes + hidden // LANE) * TILE + self.lanes * (hidden // devices)
        self.late_cut = (self.lanes + hidden // LANE) * TILE + hidden // devices
        lengths = [2 * width, width, width, width, hidden, width, width, width]
        self.lengths = lengths
        self.owned = [n // devices for n in lengths]
        self.small_rows = 16
        self.z_order = (0, 16, 8, 24)
        starts = [0]
        for n in lengths:
            starts.append(starts[-1] + n // LANE)
        self.block_starts = starts

    def place(self, mask):
        return ((mask >> 1) & 3) * 4 + self.z_order.index(mask & 24)

    def grad_piece(self, half, mask, at, rows):
        first = at < self.late_cut
        assert not first or at + rows <= self.late_cut
        swapped = mask if first else (mask & ~6) | ((mask >> 1) & 2) | ((mask & 2) << 1)
        place = self.place(swapped)
        last_rows = self.late_rows - self.late_cut
        if first:
            start = (place % 8) * self.late_cut + at
        else:
            start = 8 * self.late_cut + (place % 8) * last_rows + at - self.late_cut
        return half[place // 8].at[start : start + rows, :]


def fill_early(plan, me, halves, table_ref, inward_ref, small_ref, stage_ref):
    for mask in range(plan.devices):
        shard = halves[mask & 1].at[plan.place(mask)]
        owner = me ^ mask
        rows = aligned(owner, TILE)
        for piece in range(plan.table_pieces):
            table_ref[piece, rows, :] = shard[piece * TILE : (piece + 1) * TILE, :]
        for piece in range(3 * plan.lanes):
            at = plan.table_pieces + piece
            inward_ref[piece, rows, :] = shard[at * TILE : (at + 1) * TILE, :]
        at = plan.early_pieces * TILE
        stage_ref[pl.ds(owner, 1), :, :] = shard[at : at + TILE, :].astype(F32)[None]
    lane = lax.broadcasted_iota(jnp.int32, (1, LANE), 1)
    for vector, length in enumerate(plan.lengths):
        size = plan.owned[vector]
        group = LANE // size
        for block in range(length // LANE):
            row = jnp.zeros((1, LANE), F32)
            for index in range(group):
                own = stage_ref[block * group + index, vector : vector + 1, :]
                row = jnp.where(lane // size == index, own, row)
            at = plan.block_starts[vector] + block
            small_ref[at // plan.lanes : at // plan.lanes + 1, (at % plan.lanes) * LANE : (at % plan.lanes + 1) * LANE] = row


def own_lanes(value, head):
    lane = lax.broadcasted_iota(jnp.int32, value.shape, 1)
    return jnp.where((lane // (LANE // 2)) == head, value, jnp.zeros_like(value))


def causal():
    return lax.broadcasted_iota(jnp.int32, (STEP, STEP), 0) <= lax.broadcasted_iota(
        jnp.int32, (STEP, STEP), 1
    )


def attend_kernel(plan, count, info_ref, *refs):
    pieces, refs = refs[:count], refs[count:]
    if plan.packed:
        halves, refs = refs[:2], refs[2:]
    else:
        table_in, inward_in, small_in = refs[:3]
        refs = refs[3:]
    (lifted_ref, query_ref, key_ref, value_ref, mixed_ref, total_ref, inward_ref, small_ref) = refs[:8]
    low_ref, table_ref, place_ref, stage_ref = refs[8:]
    pair = pl.program_id(0)
    total_rows, width = plan.total_rows, plan.width
    half = total_rows // 2
    split = info_ref[0] < total_rows
    far = jnp.where(split, FAR, 0.0)

    @pl.when(pair == 0)
    def _():
        if plan.packed:
            fill_early(plan, info_ref[1], halves, table_ref, inward_ref, small_ref, stage_ref)
        else:
            table_ref[...] = table_in[...]
            inward_ref[...] = inward_in[...]
            small_ref[...] = small_in[...]
        eye = (
            lax.broadcasted_iota(jnp.int32, (half, half), 0)
            == lax.broadcasted_iota(jnp.int32, (half, half), 1)
        ).astype(BF)
        per_half = half // LANE
        for part in range(2):
            table = jnp.concatenate(
                [table_ref[part * per_half + i] for i in range(per_half)], axis=1
            )
            place_ref[part * half : (part + 1) * half, :] = times_t(eye, table)
        rows = total_rows // count
        for mask in range(count):
            start = (info_ref[2] ^ mask) * rows
            place = start - jnp.where(jnp.logical_and(split, start >= half), half, 0)
            lifted = pieces[mask][...].astype(F32) + place_ref[pl.ds(pl.multiple_of(place, rows), rows), :]
            spot = pl.ds(pl.multiple_of(start, rows), rows)
            lifted_ref[spot, :] = lifted
            low_ref[spot, :] = lifted.astype(BF)

    weights = jnp.concatenate([inward_ref[pair + i * plan.lanes] for i in range(3)], axis=1)
    lanes = aligned(pair, LANE)
    query_bias = small_ref[0:1, lanes]
    value_bias = small_ref[1:2, lanes]
    for block in range(total_rows // STEP):
        spot = slice(block * STEP, (block + 1) * STEP)
        joint = times(low_ref[spot, :], weights)
        query_ref[spot, :] = (joint[:, :LANE] + query_bias).astype(BF) * BF(0.125)
        key_ref[spot, :] = joint[:, LANE : 2 * LANE].astype(BF)
        value_ref[spot, :] = (joint[:, 2 * LANE :] + value_bias).astype(BF)

    keep = causal()
    lower = lax.broadcasted_iota(jnp.int32, (LANE, STEP), 0) < LANE // 2

    value_t = value_ref[...].T

    def logits_of(block, head):
        start = block * STEP
        other = half if start >= half else 0
        mine = own_lanes(query_ref[start : start + STEP, :], head)
        near = times_t(key_ref[start : start + STEP, :], mine)
        same = times_t(key_ref[other:start, :], mine) if start > other else None
        away = times_t(key_ref[:other, :], mine) if other else None
        return near, same, away

    def mixed_of(block, head, near, same, away):
        start = block * STEP
        other = half if start >= half else 0
        near = jnp.where(keep, near, -FAR)
        peak = jnp.max(near, axis=0, keepdims=True)
        if same is not None:
            peak = jnp.maximum(peak, jnp.max(same, axis=0, keepdims=True))
        if away is not None:
            peak = jnp.maximum(peak, jnp.max(away, axis=0, keepdims=True) - far)
        raised = [jnp.exp(piece - peak) for piece in (same, near) if piece is not None]
        total = sum(jnp.sum(piece, axis=0, keepdims=True) for piece in raised)
        low = jnp.concatenate([piece.astype(BF) for piece in raised], axis=0)
        mixed = times(value_t[:, other : start + STEP], low)
        if away is not None:
            away = jnp.exp(away - (peak + far))
            total = total + jnp.sum(away, axis=0, keepdims=True)
            mixed = mixed + times(value_t[:, :other], away.astype(BF))
        total_ref[0, head : head + 1, start : start + STEP] = peak + jnp.log(total)
        return mixed * (1.0 / total)

    tasks = [(block, head) for block in range(total_rows // STEP) for head in range(2)]
    ahead = logits_of(*tasks[0])
    parts = []
    for index, (block, head) in enumerate(tasks):
        logits, ahead = ahead, logits_of(*tasks[index + 1]) if index + 1 < len(tasks) else None
        parts.append(mixed_of(block, head, *logits))
        if head:
            mixed_ref[block * STEP : (block + 1) * STEP, :] = jnp.where(lower, *parts).T.astype(BF)
            parts = []


def attend(plan, info, count, pieces, weights):
    total_rows, width = plan.total_rows, plan.width
    block = pl.BlockSpec((total_rows, LANE), lambda p, *_: (0, p))
    low = pltpu.HBM((total_rows, width), BF)
    inward = (3 * plan.lanes, width, LANE)
    small = (plan.small_rows, width)
    return pl.pallas_call(
        functools.partial(attend_kernel, plan, count),
        grid_spec=pltpu.PrefetchScalarGridSpec(
            num_scalar_prefetch=1,
            grid=(plan.lanes,),
            in_specs=[HELD for v in pieces + weights],
            out_specs=[
                full((total_rows, width)),
                block,
                block,
                block,
                block,
                pl.BlockSpec((1, 8, total_rows), lambda p, *_: (p, 0, 0)),
                full(inward),
                full(small),
            ],
            scratch_shapes=[
                pltpu.VMEM((total_rows, width), BF),
                pltpu.VMEM((plan.table_pieces, width, LANE), BF),
                pltpu.VMEM((total_rows, width), F32),
                pltpu.VMEM((plan.devices, TILE, LANE), F32),
            ],
        ),
        out_shape=[
            pltpu.HBM((total_rows, width), F32),
            low,
            low,
            low,
            low,
            pltpu.HBM((plan.lanes, 8, total_rows), F32),
            pltpu.HBM(inward, BF),
            pltpu.HBM(small, F32),
        ],
        compiler_params=params(36),
        cost_estimate=cost(5 * 10**9, 14 * 2**20, 6 * 10**6),
        name="attend",
    )(info, *hold(pieces), *hold(weights))


def norm(rows):
    center = rows - jnp.mean(rows, axis=1, keepdims=True)
    root = lax.rsqrt(jnp.mean(center * center, axis=1, keepdims=True) + 1e-05)
    return center * root, root


def norm_back(upstream, gain, unit, root):
    scaled = upstream * gain
    mean = jnp.mean(scaled, axis=1, keepdims=True)
    slope = jnp.mean(scaled * unit, axis=1, keepdims=True)
    return (scaled - mean - unit * slope) * root


def feed_kernel(plan, count, info_ref, lifted_ref, mixed_ref, *refs):
    upstreams, refs = refs[:count], refs[count:]
    if plan.packed:
        late_quarters, small_ref = refs[:8], refs[8]
        refs = refs[9:]
    else:
        outward_in, expand_in, contract_in, small_ref = refs[:4]
        refs = refs[4:]
    results, refs = refs[:count], refs[count:]
    mixed_back_ref, first_back_ref, small_grad_ref = refs[:3]
    refs = refs[3:]
    if plan.packed:
        halves, refs = (refs[:2], refs[2:4]), refs[4:]
    else:
        outward_out, expand_out, contract_out = refs[:3]
        refs = refs[3:]
    (outward_ref, expand_ref, contract_ref, upstream_ref, result_ref, slope_ref, active_all, hidden_all, normed_all,
     lowered_all, branch_all, mixed_all, whole_ref, expand_sum, contract_sum) = refs
    step = pl.program_id(0)
    width, parts, lanes = plan.width, plan.parts, plan.lanes
    contract_own = plan.hidden // plan.devices
    contract_at = (lanes + parts * lanes) * TILE

    @pl.when(step == 0)
    def _():
        if plan.packed:
            for mask in range(plan.devices):
                at = plan.place(mask)
                shard = late_quarters[(mask & 1) * 4 + at // 4].at[at % 4]
                owner = info_ref[1] ^ mask
                rows, wide = aligned(owner, TILE), aligned(owner, contract_own)
                for lane in range(lanes):
                    cut = slice(lane * LANE, (lane + 1) * LANE)
                    outward_ref[rows, cut] = shard[lane * TILE : (lane + 1) * TILE, :]
                    for part in range(parts):
                        at = (lanes + part * lanes + lane) * TILE
                        expand_ref[part, rows, cut] = shard[at : at + TILE, :]
                    at = contract_at + lane * contract_own
                    contract_ref[wide, cut] = shard[at : at + contract_own, :]
        else:
            outward_ref[...] = outward_in[...]
            expand_ref[...] = expand_in[...]
            contract_ref[...] = contract_in[...]

    size = lifted_ref.shape[0]
    here = pl.ds(pl.multiple_of(step * size, size), size)
    rows = plan.total_rows // count
    group = size // rows

    def spot(mask):
        return pl.ds(pl.multiple_of(((info_ref[2] ^ mask) % group) * rows, rows), rows)

    for mask in range(count):
        @pl.when(step == mask // group)
        def _(mask=mask):
            upstream_ref[spot(mask), :] = upstreams[mask][...]

    outlet, steady, offset = (small_ref[i : i + 1, :] for i in (2, 3, 4))
    settle, temper, anchor = (small_ref[i + parts : i + parts + 1, :] for i in (5, 6, 7))
    mixed = mixed_ref[...]
    branch = times(mixed, outward_ref[...]) + outlet
    unit, root = norm(lifted_ref[...] + branch)
    normed = unit * steady + offset
    normed_low = normed.astype(BF)
    normed_all[here, :] = normed_low
    mixed_all[here, :] = mixed
    lowered = jnp.zeros_like(normed)
    for part in range(parts):
        cut = slice(part * width, (part + 1) * width)
        hidden = times(normed_low, expand_ref[part]) + small_ref[5 + part : 6 + part, :]
        square = hidden * hidden
        bend = jnp.tanh(hidden * (BEND + BEND * 0.044715 * square))
        half = 0.5 + 0.5 * bend
        active = (hidden * half).astype(BF)
        active_all[here, cut] = active
        slope_ref[:, cut] = half + (0.5 * hidden) * (1.0 - bend * bend) * (
            BEND + 3 * BEND * 0.044715 * square
        )
        lowered = lowered + times(active, contract_ref[cut, :])
    last_unit, last_root = norm(normed + (lowered + settle))
    result_ref[...] = (last_unit * temper + anchor).astype(BF)
    upstream = upstream_ref[...].astype(F32)
    temper_grad = column_sum(upstream * last_unit)
    anchor_grad = column_sum(upstream)
    second_back = norm_back(upstream, temper, last_unit, last_root)
    lowered_back = second_back.astype(BF)
    lowered_all[here, :] = lowered_back
    settle_grad = column_sum(lowered_back)
    normed_back = second_back
    spread_grads = []
    for part in range(parts):
        cut = slice(part * width, (part + 1) * width)
        active_back = times_t(lowered_back, contract_ref[cut, :])
        hidden_back = (active_back * slope_ref[:, cut]).astype(BF)
        spread_grads.append(column_sum(hidden_back))
        hidden_all[here, cut] = hidden_back
        normed_back = normed_back + times_t(hidden_back, expand_ref[part])
    first_back = norm_back(normed_back, steady, unit, root)
    first_back_ref[...] = first_back
    branch_back = first_back.astype(BF)
    mixed_back_ref[...] = times_t(branch_back, outward_ref[...]).astype(BF)
    branch_all[here, :] = branch_back
    zero = jnp.zeros_like(anchor_grad)
    grads = [zero, zero, column_sum(branch_back), column_sum(normed_back * unit)]
    grads += [column_sum(normed_back)] + spread_grads + [settle_grad, temper_grad, anchor_grad]
    grads += [zero] * (plan.small_rows - len(grads))
    small_term = jnp.concatenate(grads, axis=0)
    for mask in range(count):
        @pl.when(step == mask // group)
        def _(mask=mask):
            results[mask][...] = result_ref[spot(mask), :]

    @pl.when(step == 0)
    def _():
        small_grad_ref[...] = small_term

    @pl.when(step > 0)
    def _():
        small_grad_ref[...] += small_term

    @pl.when(step == pl.num_programs(0) - 1)
    def _():
        outward = t_times(mixed_all[...], branch_all[...])
        if plan.packed:
            me = info_ref[1]
            whole_ref[...] = outward
            for mask in range(plan.devices):
                half = halves[mask & 1]
                rows = aligned(me ^ mask, TILE)
                for lane in range(lanes):
                    cut = slice(lane * LANE, (lane + 1) * LANE)
                    plan.grad_piece(half, mask, lane * TILE, TILE)[...] = whole_ref[rows, cut].astype(BF)
        else:
            outward_out[...] = outward.astype(BF)
        per_part = plan.devices // parts
        for part in range(parts):
            cut = slice(part * width, (part + 1) * width)
            expand = t_times(normed_all[...], hidden_all[:, cut])
            if not plan.packed:
                expand_out[part] = expand.astype(BF)
                continue
            expand_sum[...] = expand
            for mask in range(plan.devices):
                rows = aligned(me ^ mask, TILE)
                for lane in range(lanes):
                    at = (lanes + part * lanes + lane) * TILE
                    plan.grad_piece(halves[mask & 1], mask, at, TILE)[...] = expand_sum[
                        rows, lane * LANE : (lane + 1) * LANE
                    ].astype(BF)
        for mask_part in range(parts):
            part = (me // per_part) ^ mask_part if plan.packed else mask_part
            cut = pl.ds(pl.multiple_of(part * width, width), width)
            contract = t_times(active_all[:, cut], lowered_all[...])
            if not plan.packed:
                contract_out[cut, :] = contract.astype(BF)
                continue
            contract_sum[...] = contract
            for index in range(per_part):
                mask = mask_part * per_part + index
                rows = aligned((me ^ mask) % per_part, contract_own)
                for lane in range(lanes):
                    at = contract_at + lane * contract_own
                    plan.grad_piece(halves[mask & 1], mask, at, contract_own)[...] = contract_sum[
                        rows, lane * LANE : (lane + 1) * LANE
                    ].astype(BF)


def feed(plan, info, count, lifted, mixed, upstreams, weights, small):
    total_rows, width, parts = plan.total_rows, plan.width, plan.parts
    piece = total_rows // count
    size = max(piece, FEED_ROWS)
    group = size // piece
    rows = pl.BlockSpec((size, width), lambda i, info: ((info[2] // group) ^ i, 0))
    outward, expand, contract = (width, width), (parts, width, width), (parts * width, width)
    if plan.packed:
        grads = [pltpu.VMEM((8 * plan.late_rows, LANE), BF)] * 4
    else:
        grads = [pltpu.VMEM(outward, BF), pltpu.VMEM(expand, BF), pltpu.VMEM(contract, BF)]
    ends = [pltpu.VMEM((piece, width), BF)] * count
    outs = [like((total_rows, width), BF), like((total_rows, width), F32), like(small.shape, F32)]
    values = pl.pallas_call(
        functools.partial(feed_kernel, plan, count),
        grid_spec=pltpu.PrefetchScalarGridSpec(
            num_scalar_prefetch=1,
            grid=(total_rows // size,),
            in_specs=[rows, rows]
            + [HELD for v in upstreams + weights]
            + [full(small.shape)],
            out_specs=[HELD for v in ends]
            + [rows, rows, full(small.shape)]
            + [HELD for v in grads],
            scratch_shapes=[
                pltpu.VMEM(outward, BF),
                pltpu.VMEM(expand, BF),
                pltpu.VMEM(contract, BF),
                pltpu.VMEM((size, width), BF),
                pltpu.VMEM((size, width), BF),
                pltpu.VMEM((size, parts * width), F32),
                pltpu.VMEM((total_rows, parts * width), BF),
                pltpu.VMEM((total_rows, parts * width), BF),
                pltpu.VMEM((total_rows, width), BF),
                pltpu.VMEM((total_rows, width), BF),
                pltpu.VMEM((total_rows, width), BF),
                pltpu.VMEM((total_rows, width), BF),
                pltpu.VMEM(outward, F32),
                pltpu.VMEM(outward, F32),
                pltpu.VMEM(outward, F32),
            ],
        ),
        out_shape=ends + outs + grads,
        compiler_params=params(50),
        cost_estimate=cost(15 * 10**9, 20 * 2**20, 2 * 10**6),
        name="feed",
    )(info, lifted, mixed, *hold(upstreams), *hold(weights), small)
    return values[:count], values[count : count + 3], values[count + 3 :]


def attend_back_kernel(
    plan, count, info_ref, lifted_ref, query_ref, key_ref, value_ref, mixed_ref, mixed_back_ref,
    total_ref, inward_ref, first_back_ref, small_grad_ref, *refs
):
    tokens, refs = refs[:count], refs[count:]
    if plan.packed:
        halves, refs = refs[:2], refs[2:]
    else:
        table_out, inward_out, small_out = refs[:3]
        refs = refs[3:]
    (joint_ref, sum_ref, share_ref, score_ref, grad_ref, table_ref, joint_sums, blocks_ref,
     lifted_here, inward_here, copied) = refs
    pair = pl.program_id(0)
    copies = [
        pltpu.make_async_copy(source, target, copied.at[index])
        for index, (source, target) in enumerate(
            ((lifted_ref, lifted_here), (inward_ref, inward_here), (first_back_ref, sum_ref))
        )
    ]

    @pl.when(pair == 0)
    def _():
        for copy in copies:
            copy.start()

    total_rows, lanes = plan.total_rows, plan.lanes
    half = total_rows // 2
    split = info_ref[0] < total_rows
    far = jnp.where(split, FAR, 0.0)
    blocks = total_rows // STEP

    keep = causal()
    lower = lax.broadcasted_iota(jnp.int32, (STEP, LANE), 1) < LANE // 2
    lower_t = lax.broadcasted_iota(jnp.int32, (LANE, STEP), 0) < LANE // 2
    product = (mixed_ref[...].astype(F32) * mixed_back_ref[...].astype(F32)).T
    scaled_key = (key_ref[...] * BF(0.125)).T
    betweens = [
        jnp.sum(product[head * LANE // 2 : (head + 1) * LANE // 2], axis=0, keepdims=True)
        for head in range(2)
    ]

    def logits_of(block, head):
        spot = slice(block * STEP, (block + 1) * STEP)
        keys = slice(0, (block + 1) * STEP)
        query = own_lanes(query_ref[spot, :], head)
        back = own_lanes(mixed_back_ref[spot, :], head)
        return times_t(key_ref[keys, :], query), times_t(value_ref[keys, :], back)

    def scores_of(block, head, logits, share_back):
        start = block * STEP
        spot = slice(start, start + STEP)
        total = total_ref[0, head : head + 1, spot]
        gap = betweens[head][:, spot]
        for under in range(block + 1):
            keys = slice(under * STEP, (under + 1) * STEP)
            away = start >= half and under * STEP < half
            share = jnp.exp(logits[keys] - (total + far if away else total))
            if under == block:
                share = jnp.where(keep, share, 0.0)
            score = share * (share_back[keys] - gap)
            share_ref[head, keys, spot] = share.astype(BF)
            score_ref[head, keys, spot] = score.astype(BF)

    def backs_of(block, head):
        start = block * STEP
        spot = slice(start, start + STEP)
        end = start + STEP
        query_back = times(scaled_key[:, :end], score_ref[head, :end, spot])
        key_back = times(score_ref[head, spot, start:], query_ref[start:, :])
        value_back = times(share_ref[head, spot, start:], mixed_back_ref[start:, :])
        return query_back, key_back, value_back

    tasks = [(block, head) for block in reversed(range(blocks)) for head in range(2)]
    ahead = logits_of(*tasks[0])
    parts = []
    for index, (block, head) in enumerate(tasks):
        logits, ahead = ahead, logits_of(*tasks[index + 1]) if index + 1 < len(tasks) else None
        scores_of(block, head, *logits)
        parts.append(backs_of(block, head))
        if head:
            spot = slice(block * STEP, (block + 1) * STEP)
            query_back = jnp.where(lower_t, parts[0][0], parts[1][0]).T
            key_back = jnp.where(lower, parts[0][1], parts[1][1])
            value_back = jnp.where(lower, parts[0][2], parts[1][2])
            for part, back in enumerate((query_back, key_back, value_back)):
                joint_ref[spot, aligned(pair + part * lanes, LANE)] = back.astype(BF)
            parts = []

    @pl.when(pair == lanes - 1)
    def _():
        for copy in copies:
            copy.wait()
        low = lifted_here[...].astype(BF).T
        weights = jnp.concatenate([inward_here[i] for i in range(3 * lanes)], axis=1)
        for block in range(blocks):
            spot = slice(block * STEP, (block + 1) * STEP)
            sum_ref[spot, :] += times_t(joint_ref[spot, :], weights)
        for part in range(3):
            joint = joint_ref[:, part * plan.width : (part + 1) * plan.width]
            grads = times(low, joint)
            for lane in range(lanes):
                grad_ref[part * lanes + lane] = grads[:, lane * LANE : (lane + 1) * LANE]
            if part != 1:
                sums = column_sum(joint)
                for lane in range(lanes):
                    at = lane if part == 0 else lane + lanes
                    joint_sums[at : at + 1, :] = sums[:, lane * LANE : (lane + 1) * LANE]
        rows = total_rows // count
        for mask in range(count):
            spot = pl.ds(pl.multiple_of((info_ref[2] ^ mask) * rows, rows), rows)
            tokens[mask][...] = sum_ref[spot, :].astype(BF)
        late = sum_ref[half:, :]
        early = sum_ref[:half, :] + jnp.where(split, late, 0.0)
        table_ref[:, :half] = early.T
        table_ref[:, half:] = jnp.where(split, 0.0, late).T
        counted = info_ref[3] > 0
        blocks_ref[: 2 * lanes, :] = joint_sums[: 2 * lanes, :]
        for row in range(2, plan.block_starts[-1] // lanes):
            for lane in range(lanes):
                blocks_ref[row * lanes + lane : row * lanes + lane + 1, :] = small_grad_ref[
                    row : row + 1, lane * LANE : (lane + 1) * LANE
                ]
        if plan.packed:
            for mask in range(plan.devices):
                shard = halves[mask & 1].at[plan.place(mask)]
                owner = info_ref[1] ^ mask
                own = aligned(owner, TILE)
                for piece in range(plan.table_pieces):
                    shard[piece * TILE : (piece + 1) * TILE, :] = table_ref[
                        own, piece * LANE : (piece + 1) * LANE
                    ].astype(BF)
                for piece in range(3 * lanes):
                    at = (plan.table_pieces + piece) * TILE
                    shard[at : at + TILE, :] = grad_ref[piece, own, :].astype(BF)
                rows = [
                    blocks_ref[pl.ds(plan.block_starts[v] + owner * plan.owned[v] // LANE, 1), :]
                    for v in range(VECTORS)
                ]
                rows.append(jnp.zeros((TILE - VECTORS, LANE), F32))
                at = plan.early_pieces * TILE
                shard[at : at + TILE, :] = jnp.concatenate(rows, axis=0).astype(BF)
        else:
            table_out[...] = jnp.where(counted, table_ref[...], 0.0).astype(BF)
            inward_out[...] = jnp.where(counted, grad_ref[...], 0.0).astype(BF)
            small_out[...] = jnp.where(counted, blocks_ref[...], 0.0)


def attend_back(plan, info, count, lifted, saved, mixed_back, inward, first_back, small_grad):
    query, key, value, mixed, totals = saved
    total_rows, width, lanes = plan.total_rows, plan.width, plan.lanes
    block = pl.BlockSpec((total_rows, LANE), lambda p, *_: (0, p))
    blocks = (plan.block_starts[-1], LANE)
    if plan.packed:
        grads = [pltpu.VMEM((plan.devices // 2, plan.early_rows, LANE), BF)] * 2
    else:
        grads = [pltpu.VMEM((width, total_rows), BF), pltpu.VMEM(inward.shape, BF), pltpu.VMEM(blocks, F32)]
    tokens = [pltpu.VMEM((total_rows // count, width), BF)] * count
    values = pl.pallas_call(
        functools.partial(attend_back_kernel, plan, count),
        grid_spec=pltpu.PrefetchScalarGridSpec(
            num_scalar_prefetch=1,
            grid=(lanes,),
            in_specs=[
                pl.BlockSpec(memory_space=pl.ANY),
                block,
                block,
                block,
                block,
                block,
                pl.BlockSpec((1, 8, total_rows), lambda p, *_: (p, 0, 0)),
                pl.BlockSpec(memory_space=pl.ANY),
                pl.BlockSpec(memory_space=pl.ANY),
                full(small_grad.shape),
            ],
            out_specs=[HELD for v in tokens + grads],
            scratch_shapes=[
                pltpu.VMEM((total_rows, 3 * width), BF),
                pltpu.VMEM((total_rows, width), F32),
                pltpu.VMEM((2, total_rows, total_rows), BF),
                pltpu.VMEM((2, total_rows, total_rows), BF),
                pltpu.VMEM(inward.shape, F32),
                pltpu.VMEM((width, total_rows), F32),
                pltpu.VMEM((8, LANE), F32),
                pltpu.VMEM(blocks, F32),
                pltpu.VMEM(lifted.shape, F32),
                pltpu.VMEM(inward.shape, BF),
                pltpu.SemaphoreType.DMA((3,)),
            ],
        ),
        out_shape=tokens + grads,
        compiler_params=params(40),
        cost_estimate=cost(14 * 10**9, 24 * 2**20, 6 * 10**6),
        name="attend_back",
    )(info, *stay([lifted, query, key, value, mixed, mixed_back, totals, inward, first_back]), small_grad)
    return values[:count], values[count:]


def pack_kernel(plan, count, share, rows_ref, table_ref, inward_ref, *refs):
    vectors, refs = refs[:VECTORS], refs[VECTORS:]
    outward_ref, expand_ref, contract_ref = refs[:3]
    pieces, early_ref, late_ref = refs[3 : 3 + count], refs[3 + count], refs[4 + count]
    rank = lax.axis_index("seq")
    for mask in range(count):
        pieces[mask][...] = rows_ref[pl.ds((rank ^ mask) // share, 1), :, :][0]
    at = 0
    for ref in (table_ref, inward_ref):
        for lane in range(ref.shape[1] // LANE):
            early_ref[0, at : at + TILE, :] = ref[:, lane * LANE : (lane + 1) * LANE]
            at += TILE
    rows = []
    for size, ref in zip(plan.owned, vectors):
        rows.append(jnp.concatenate([ref[...].astype(F32)] * (LANE // size), axis=1))
    rows.append(jnp.zeros((TILE - VECTORS, LANE), F32))
    early_ref[0, at : at + TILE, :] = jnp.concatenate(rows, axis=0).astype(BF)
    at = 0
    for ref in (outward_ref, expand_ref, contract_ref):
        rows = ref.shape[0]
        for lane in range(ref.shape[1] // LANE):
            late_ref[0, at : at + rows, :] = ref[:, lane * LANE : (lane + 1) * LANE]
            at += rows


def pack(plan, count, share, rows, table, inward, vectors, outward, expand, contract):
    vectors = [v.reshape(1, -1) for v in vectors]
    outs = [like(rows.shape[1:], BF)] * count
    outs += [like((1, plan.early_rows, LANE), BF), like((1, plan.late_rows, LANE), BF)]
    values = pl.pallas_call(
        functools.partial(pack_kernel, plan, count, share),
        out_shape=outs,
        cost_estimate=cost(0, 4 * 2**20),
        name="pack",
    )(rows, table, inward, *vectors, outward, expand, contract)
    return values[:count], values[count], values[count + 1]


def fold(terms, cuts):
    size = terms[0].shape[0] // cuts
    return [
        sum(term[index * size : (index + 1) * size].astype(F32) for term in terms).astype(BF)
        for index in range(cuts)
    ]


def finish_kernel(plan, info_ref, *refs):
    early, late, refs = refs[:4], refs[4:8], refs[8:]
    table_ref, inward_ref, outward_ref, expand_ref, contract_ref = refs[:5]
    vectors = refs[5:]
    early = sum(ref[0].astype(F32) for ref in early)
    late = sum(ref[...].astype(F32) for ref in late)
    for piece in range(plan.table_pieces):
        table_ref[:, piece * LANE : (piece + 1) * LANE] = early[piece * TILE : (piece + 1) * TILE]
    for piece in range(3 * plan.lanes):
        at = (plan.table_pieces + piece) * TILE
        inward_ref[:, piece * LANE : (piece + 1) * LANE] = early[at : at + TILE]
    at = 0
    for ref in (outward_ref, expand_ref, contract_ref):
        rows = ref.shape[0]
        for lane in range(ref.shape[1] // LANE):
            ref[:, lane * LANE : (lane + 1) * LANE] = late[at : at + rows]
            at += rows
    at = plan.early_pieces * TILE
    small = early[at : at + VECTORS]
    for vector, ref in enumerate(vectors):
        size = plan.owned[vector]
        slot = lax.rem(info_ref[1], LANE // size)
        row = pltpu.roll(small, LANE - slot * size, 1)
        ref[...] = row[vector : vector + 1, :size]


def finish(plan, info, early, late):
    own, width = plan.own_rows, plan.width
    outs = [
        like((own, plan.total_rows), F32),
        like((own, 3 * width), F32),
        like((own, width), F32),
        like((own, plan.hidden), F32),
        like((plan.hidden // plan.devices, width), F32),
    ] + [like((1, n), F32) for n in plan.owned]
    values = early + late
    return pl.pallas_call(
        functools.partial(finish_kernel, plan),
        grid_spec=pltpu.PrefetchScalarGridSpec(
            num_scalar_prefetch=1,
            grid=(1,),
            in_specs=[HELD for v in values],
            out_specs=[full(v.shape) for v in outs],
        ),
        out_shape=outs,
        name="finish",
    )(info, *hold(values))


def ordered(rank, pieces):
    for bit in (1, 2):
        flip = (rank & bit) > 0
        pieces = [jnp.where(flip, pieces[i ^ bit], pieces[i]) for i in range(4)]
    return jnp.stack(pieces)


def settle_kernel(count, share, info_ref, *refs):
    for mask in range(count):
        refs[count][pl.ds((info_ref[2] ^ mask) // share, 1), :, :] = refs[mask][...][None]


def settle_rows(info, micro_count, share, pieces):
    out = (micro_count,) + pieces[0].shape
    return pl.pallas_call(
        functools.partial(settle_kernel, len(pieces), share),
        grid_spec=pltpu.PrefetchScalarGridSpec(
            num_scalar_prefetch=1,
            grid=(1,),
            in_specs=[full(v.shape) for v in pieces],
            out_specs=full(out),
        ),
        out_shape=like(out, BF),
        cost_estimate=cost(0, 48 * 2**20),
        name="settle_rows",
    )(info, *pieces)


def cut_kernel(count, share, rows_ref, *refs):
    rank = lax.axis_index("seq")
    for mask in range(count):
        refs[mask][...] = rows_ref[pl.ds((rank ^ mask) // share, 1), :, :][0]


def cut_rows(rows, count, share):
    outs = [like(rows.shape[1:], BF)] * count
    return pl.pallas_call(
        functools.partial(cut_kernel, count, share),
        out_shape=outs,
        cost_estimate=cost(0, 4 * 2**20),
        name="cut_rows",
    )(rows)


def local(tokens, first_length, cotangent, positions, inward, intake, outward, outlet, steady, offset,
          expand, spread, contract, settle, temper, anchor):
    micro_count, pack_count, block_rows, width = tokens.shape
    assert pack_count == 1
    devices, count = lax.axis_size(AXES), lax.axis_size("seq")
    me, rank = lax.axis_index(AXES), lax.axis_index("seq")
    share = max(count // micro_count, 1)
    assert share * micro_count == count
    plan = Plan(devices, width, contract.shape[0] * devices, block_rows * count)
    micro = rank // share
    counted = (rank % share == 0).astype(jnp.int32)

    def info_of(lengths):
        first = jnp.sum(jnp.where(jnp.arange(micro_count) == micro, lengths[:, 0], 0))
        return jnp.stack([first, me, rank, counted]).astype(jnp.int32)

    vectors = (intake, outlet, steady, offset, spread, settle, temper, anchor)

    def swap(value, mask):
        return lax.ppermute(value, AXES, [(d, d ^ mask) for d in range(devices)]) if mask else value

    def exchange(pieces):
        return [swap(piece, mask) for mask, piece in enumerate(pieces)]

    def in_order(pieces):
        if count != 4 or share != 1:
            return settle_rows(info, micro_count, share, pieces)
        return ordered(rank, pieces)

    if plan.packed:
        rows_in, shard, late = pack(
            plan, count, share, tokens[:, 0], positions.T, inward, vectors, outward, expand, contract
        )
        rows_in = exchange(rows_in)
        shard, rows_in[1] = lax.optimization_barrier((shard, rows_in[1]))
        pieces = [swap(shard, mask) for mask in plan.z_order]
        pieces, rows_in, late, cotangent, first_length = lax.optimization_barrier(
            (pieces, rows_in, late, cotangent, first_length)
        )
        info = info_of(first_length)
        shard = jnp.concatenate(pieces, axis=0)
        pieces = [swap(shard, k << 1) for k in range(4)]
        late = [swap(late, mask) for mask in plan.z_order]
        upstreams = cut_rows(cotangent[:, 0], count, share)
        pieces, upstreams, late, info = lax.optimization_barrier((pieces, list(upstreams), late, info))
        late = jnp.concatenate(late, axis=0)
        late_x, late_y = swap(late, 2), swap(late, 4)
        shard = jnp.concatenate(pieces, axis=0)
        early = [shard, swap(shard, 1)]
        upstreams[1] = swap(upstreams[1], 1)
        late_core = swap(late, 1)
        early, late_core, late_x, late_y, upstreams = lax.optimization_barrier(
            (early, late_core, late_x, late_y, upstreams)
        )
        late_xy = swap(late_x, 4)
        upstreams[2:] = [swap(upstreams[mask], mask) for mask in (2, 3)]
        late_cores = [late_core, swap(late_x, 1), swap(late_y, 1)]
    else:
        info = info_of(first_length)
        rows_in = exchange(cut_rows(tokens[:, 0], count, share))
        upstreams = exchange(cut_rows(cotangent[:, 0], count, share))
        early, late = plain_weights(plan, positions, inward, vectors, outward, expand, contract)
    lifted, query, key, value, mixed, totals, inward_all, small = attend(plan, info, count, rows_in, early)
    if plan.packed:
        late_xy, late_cores, upstreams, mixed = lax.optimization_barrier(
            (late_xy, late_cores, upstreams, mixed)
        )
        late = [late, late_x, late_y, late_xy] + late_cores + [swap(late_xy, 1)]
    results, (mixed_back, first_back, small_grad), late_grads = feed(
        plan, info, count, lifted, mixed, upstreams, late, small
    )
    results = exchange(results)
    if plan.packed:
        stay_keep, go_keep, stay_send, go_send = late_grads
        cut = 8 * plan.late_cut
        go = [go_keep, swap(go_send, 1)]
        one_send, two_send = fold([v[:cut] for v in go], 1) + fold([v[cut:] for v in go], 1)
        stay_other = swap(stay_send, 1)
        one_send, two_send, mixed_back = lax.optimization_barrier((one_send, two_send, mixed_back))
        one_other, two_other = swap(one_send, 4), swap(two_send, 2)
    token_pieces, early_grads = attend_back(
        plan, info, count, lifted, (query, key, value, mixed, totals), mixed_back, inward_all,
        first_back, small_grad,
    )
    if plan.packed:
        one_other, two_other, stay_other, results, token_pieces, early_grads = lax.optimization_barrier(
            (one_other, two_other, stay_other, results, token_pieces, early_grads)
        )
        keep, send = early_grads
        send = swap(send, 1)
        one, one_send = fold([stay_keep[:cut], stay_other[:cut], one_other], 2)
        two, two_send = fold([stay_keep[cut:], stay_other[cut:], two_other], 2)
        one, one_send, two, two_send, keep = lax.optimization_barrier((one, one_send, two, two_send, keep))
        one_other, two_other = swap(one_send, 2), swap(two_send, 4)
        terms = fold([keep, send], 4)
        terms, results, token_pieces = lax.optimization_barrier((terms, results, token_pieces))
        terms = [swap(term, k << 1) for k, term in enumerate(terms)]
        output = settle_rows(info, micro_count, share, results)
        one_other, two_other, output = lax.optimization_barrier((one_other, two_other, output))
        ones, twos = fold([one, one_other], 4), fold([two, two_other], 4)
        late_terms = [jnp.concatenate(pair, axis=0) for pair in zip(ones, twos)]
        late_terms = [swap(term, mask) for term, mask in zip(late_terms, plan.z_order)]
        token_pieces = list(token_pieces)
        token_pieces[1] = swap(token_pieces[1], 1)
        terms, late_terms, output, token_pieces = lax.optimization_barrier(
            (terms, late_terms, output, token_pieces)
        )
        terms = fold(terms, 4)
        early_terms = [swap(term, mask) for term, mask in zip(terms, plan.z_order)]
        token_pieces[2:] = [swap(token_pieces[mask], mask) for mask in (2, 3)]
        early_terms, token_pieces = lax.optimization_barrier((early_terms, token_pieces))
        tokens_back = in_order(token_pieces)
        values = finish(plan, info, early_terms, late_terms)
        table_t, inward_own, outward_own, expand_own, contract_own = values[:5]
        own = [v.reshape(-1) for v in values[5:]]
        table_own = table_t.T
    else:
        output = in_order(results)
        tokens_back = in_order(exchange(token_pieces))
        table_own, inward_own, outward_own, expand_own, contract_own, own = plain_grads(
            plan, counted, early_grads, late_grads
        )
    return (output[:, None], tokens_back[:, None], table_own, inward_own, own[0], outward_own, own[1], own[2],
            own[3], expand_own, own[4], contract_own, own[5], own[6], own[7])


def plain_weights(plan, positions, inward, vectors, outward, expand, contract):
    lanes, width = plan.lanes, plan.width

    def gather(value, axis=0):
        return lax.all_gather(value, AXES, axis=axis, tiled=True)

    def in_pieces(value, size):
        return value.reshape(value.shape[0], -1, size).transpose(1, 0, 2)

    table = in_pieces(gather(positions, 1).T, LANE)
    small = jnp.concatenate([gather(v) for v in vectors]).astype(F32).reshape(-1, width)
    small = jnp.pad(small, ((0, plan.small_rows - small.shape[0]), (0, 0)))
    early = [table, in_pieces(gather(inward), LANE), small]
    return early, [gather(outward), in_pieces(gather(expand), width), gather(contract)]


def plain_grads(plan, counted, early_grads, late_grads):
    width = plan.width
    table, inward, small = early_grads
    outward, expand, contract = (jnp.where(counted > 0, g, BF(0)) for g in late_grads)

    def scatter(value, axis=0):
        return lax.psum_scatter(value, AXES, scatter_dimension=axis, tiled=True).astype(F32)

    def whole(value):
        return value.transpose(1, 0, 2).reshape(value.shape[1], -1)

    flat = small.reshape(-1)
    own = []
    for vector, length in enumerate(plan.lengths):
        start = plan.block_starts[vector] * LANE
        own.append(scatter(flat[start : start + length]))
    return (scatter(table.T, 1), scatter(whole(inward)), scatter(outward), scatter(whole(expand)),
            scatter(contract), own)


def solution(mesh):
    rows = P(None, "batch", "seq", None)
    table = P(None, AXES)
    matrix = P(AXES, None)
    vector = P(AXES)
    weights = (table, matrix, vector, matrix, vector, vector, vector, matrix, vector, matrix, vector,
               vector, vector)
    return jax.shard_map(
        local,
        mesh=mesh,
        in_specs=(rows, P(None, "batch"), rows) + weights,
        out_specs=(rows, rows) + weights,
        check_vma=False,
    )
```

```python
import functools

import jax
import jax.numpy as jnp
from jax import lax
from jax.experimental import pallas as pl
from jax.experimental.pallas import tpu as pltpu
from jax.sharding import PartitionSpec as P

AXES = ("batch", "seq")
LANE = 128
TILE = 16
FEED_ROWS = 512
STEP = 256
FAR = 1e30
BEND = 0.7978845608028654
BF = jnp.bfloat16
F32 = jnp.float32
VECTORS = 8


def times(left, right):
    return jnp.dot(left, right, preferred_element_type=F32)


def times_t(left, right):
    return lax.dot_general(left, right, (((1,), (1,)), ((), ())), preferred_element_type=F32)


def t_times(left, right):
    return lax.dot_general(left, right, (((0,), (0,)), ((), ())), preferred_element_type=F32)


def column_sum(values):
    return jnp.sum(values.astype(F32), axis=0, keepdims=True)


def aligned(index, size):
    return pl.ds(pl.multiple_of(index * size, size), size)


def like(shape, kind):
    return jax.ShapeDtypeStruct(shape, kind)


def full(shape):
    return pl.BlockSpec(shape, lambda *_: (0,) * len(shape), pipeline_mode=pl.Buffered(1))


HELD = pl.BlockSpec(memory_space=pltpu.VMEM)


def hold(values):
    return [pltpu.with_memory_space_constraint(v, pltpu.VMEM) for v in values]


def stay(values):
    return [pltpu.with_memory_space_constraint(v, pltpu.HBM) for v in values]


def params(megabytes):
    return pltpu.CompilerParams(vmem_limit_bytes=megabytes * 2**20)


def cost(flops, size, exps=0):
    return pl.CostEstimate(flops=flops, bytes_accessed=size, transcendentals=exps)


class Plan:
    def __init__(self, devices, width, hidden, total_rows):
        self.devices = devices
        self.width = width
        self.hidden = hidden
        self.total_rows = total_rows
        self.own_rows = width // devices
        self.packed = devices == 32 and self.own_rows % TILE == 0
        self.lanes = width // LANE
        self.parts = hidden // width
        self.table_pieces = total_rows // LANE
        self.early_pieces = self.table_pieces + 3 * self.lanes
        self.early_rows = (self.early_pieces + 1) * TILE
        self.late_rows = (self.lanes + hidden // LANE) * TILE + self.lanes * (hidden // devices)
        self.late_cut = (self.lanes + hidden // LANE) * TILE + hidden // devices
        lengths = [2 * width, width, width, width, hidden, width, width, width]
        self.lengths = lengths
        self.owned = [n // devices for n in lengths]
        self.small_rows = 16
        self.z_order = (0, 16, 8, 24)
        starts = [0]
        for n in lengths:
            starts.append(starts[-1] + n // LANE)
        self.block_starts = starts

    def place(self, mask):
        return ((mask >> 1) & 3) * 4 + self.z_order.index(mask & 24)

    def grad_piece(self, half, mask, at, rows):
        first = at < self.late_cut
        assert not first or at + rows <= self.late_cut
        swapped = mask if first else (mask & ~6) | ((mask >> 1) & 2) | ((mask & 2) << 1)
        place = self.place(swapped)
        last_rows = self.late_rows - self.late_cut
        if first:
            start = (place % 8) * self.late_cut + at
        else:
            start = 8 * self.late_cut + (place % 8) * last_rows + at - self.late_cut
        return half[place // 8].at[start : start + rows, :]


def fill_early(plan, me, halves, table_ref, inward_ref, small_ref, stage_ref):
    for mask in range(plan.devices):
        shard = halves[mask & 1].at[plan.place(mask)]
        owner = me ^ mask
        rows = aligned(owner, TILE)
        for piece in range(plan.table_pieces):
            table_ref[piece, rows, :] = shard[piece * TILE : (piece + 1) * TILE, :]
        for piece in range(3 * plan.lanes):
            at = plan.table_pieces + piece
            inward_ref[piece, rows, :] = shard[at * TILE : (at + 1) * TILE, :]
        at = plan.early_pieces * TILE
        stage_ref[pl.ds(owner, 1), :, :] = shard[at : at + TILE, :].astype(F32)[None]
    lane = lax.broadcasted_iota(jnp.int32, (1, LANE), 1)
    for vector, length in enumerate(plan.lengths):
        size = plan.owned[vector]
        group = LANE // size
        for block in range(length // LANE):
            row = jnp.zeros((1, LANE), F32)
            for index in range(group):
                own = stage_ref[block * group + index, vector : vector + 1, :]
                row = jnp.where(lane // size == index, own, row)
            at = plan.block_starts[vector] + block
            small_ref[at // plan.lanes : at // plan.lanes + 1, (at % plan.lanes) * LANE : (at % plan.lanes + 1) * LANE] = row


def own_lanes(value, head):
    lane = lax.broadcasted_iota(jnp.int32, value.shape, 1)
    return jnp.where((lane // (LANE // 2)) == head, value, jnp.zeros_like(value))


def causal():
    return lax.broadcasted_iota(jnp.int32, (STEP, STEP), 0) <= lax.broadcasted_iota(
        jnp.int32, (STEP, STEP), 1
    )


def attend_kernel(plan, count, info_ref, *refs):
    pieces, refs = refs[:count], refs[count:]
    if plan.packed:
        halves, refs = refs[:2], refs[2:]
    else:
        table_in, inward_in, small_in = refs[:3]
        refs = refs[3:]
    (lifted_ref, query_ref, key_ref, value_ref, mixed_ref, total_ref, inward_ref, small_ref) = refs[:8]
    low_ref, table_ref, place_ref, stage_ref = refs[8:]
    pair = pl.program_id(0)
    total_rows, width = plan.total_rows, plan.width
    half = total_rows // 2
    split = info_ref[0] < total_rows
    far = jnp.where(split, FAR, 0.0)

    @pl.when(pair == 0)
    def _():
        if plan.packed:
            fill_early(plan, info_ref[1], halves, table_ref, inward_ref, small_ref, stage_ref)
        else:
            table_ref[...] = table_in[...]
            inward_ref[...] = inward_in[...]
            small_ref[...] = small_in[...]
        eye = (
            lax.broadcasted_iota(jnp.int32, (half, half), 0)
            == lax.broadcasted_iota(jnp.int32, (half, half), 1)
        ).astype(BF)
        per_half = half // LANE
        for part in range(2):
            table = jnp.concatenate(
                [table_ref[part * per_half + i] for i in range(per_half)], axis=1
            )
            place_ref[part * half : (part + 1) * half, :] = times_t(eye, table)
        rows = total_rows // count
        for mask in range(count):
            start = (info_ref[2] ^ mask) * rows
            place = start - jnp.where(jnp.logical_and(split, start >= half), half, 0)
            lifted = pieces[mask][...].astype(F32) + place_ref[pl.ds(pl.multiple_of(place, rows), rows), :]
            spot = pl.ds(pl.multiple_of(start, rows), rows)
            lifted_ref[spot, :] = lifted
            low_ref[spot, :] = lifted.astype(BF)

    weights = jnp.concatenate([inward_ref[pair + i * plan.lanes] for i in range(3)], axis=1)
    lanes = aligned(pair, LANE)
    query_bias = small_ref[0:1, lanes]
    value_bias = small_ref[1:2, lanes]
    for block in range(total_rows // STEP):
        spot = slice(block * STEP, (block + 1) * STEP)
        joint = times(low_ref[spot, :], weights)
        query_ref[spot, :] = (joint[:, :LANE] + query_bias).astype(BF) * BF(0.125)
        key_ref[spot, :] = joint[:, LANE : 2 * LANE].astype(BF)
        value_ref[spot, :] = (joint[:, 2 * LANE :] + value_bias).astype(BF)

    keep = causal()
    lower = lax.broadcasted_iota(jnp.int32, (LANE, STEP), 0) < LANE // 2

    value_t = value_ref[...].T

    def logits_of(block, head):
        start = block * STEP
        other = half if start >= half else 0
        mine = own_lanes(query_ref[start : start + STEP, :], head)
        near = times_t(key_ref[start : start + STEP, :], mine)
        same = times_t(key_ref[other:start, :], mine) if start > other else None
        away = times_t(key_ref[:other, :], mine) if other else None
        return near, same, away

    def mixed_of(block, head, near, same, away):
        start = block * STEP
        other = half if start >= half else 0
        near = jnp.where(keep, near, -FAR)
        peak = jnp.max(near, axis=0, keepdims=True)
        if same is not None:
            peak = jnp.maximum(peak, jnp.max(same, axis=0, keepdims=True))
        if away is not None:
            peak = jnp.maximum(peak, jnp.max(away, axis=0, keepdims=True) - far)
        raised = [jnp.exp(piece - peak) for piece in (same, near) if piece is not None]
        total = sum(jnp.sum(piece, axis=0, keepdims=True) for piece in raised)
        low = jnp.concatenate([piece.astype(BF) for piece in raised], axis=0)
        mixed = times(value_t[:, other : start + STEP], low)
        if away is not None:
            away = jnp.exp(away - (peak + far))
            total = total + jnp.sum(away, axis=0, keepdims=True)
            mixed = mixed + times(value_t[:, :other], away.astype(BF))
        total_ref[0, head : head + 1, start : start + STEP] = peak + jnp.log(total)
        return mixed * (1.0 / total)

    tasks = [(block, head) for block in range(total_rows // STEP) for head in range(2)]
    ahead = logits_of(*tasks[0])
    parts = []
    for index, (block, head) in enumerate(tasks):
        logits, ahead = ahead, logits_of(*tasks[index + 1]) if index + 1 < len(tasks) else None
        parts.append(mixed_of(block, head, *logits))
        if head:
            mixed_ref[block * STEP : (block + 1) * STEP, :] = jnp.where(lower, *parts).T.astype(BF)
            parts = []


def attend(plan, info, count, pieces, weights):
    total_rows, width = plan.total_rows, plan.width
    block = pl.BlockSpec((total_rows, LANE), lambda p, *_: (0, p))
    low = pltpu.HBM((total_rows, width), BF)
    inward = (3 * plan.lanes, width, LANE)
    small = (plan.small_rows, width)
    return pl.pallas_call(
        functools.partial(attend_kernel, plan, count),
        grid_spec=pltpu.PrefetchScalarGridSpec(
            num_scalar_prefetch=1,
            grid=(plan.lanes,),
            in_specs=[HELD for v in pieces + weights],
            out_specs=[
                full((total_rows, width)),
                block,
                block,
                block,
                block,
                pl.BlockSpec((1, 8, total_rows), lambda p, *_: (p, 0, 0)),
                full(inward),
                full(small),
            ],
            scratch_shapes=[
                pltpu.VMEM((total_rows, width), BF),
                pltpu.VMEM((plan.table_pieces, width, LANE), BF),
                pltpu.VMEM((total_rows, width), F32),
                pltpu.VMEM((plan.devices, TILE, LANE), F32),
            ],
        ),
        out_shape=[
            pltpu.HBM((total_rows, width), F32),
            low,
            low,
            low,
            low,
            pltpu.HBM((plan.lanes, 8, total_rows), F32),
            pltpu.HBM(inward, BF),
            pltpu.HBM(small, F32),
        ],
        compiler_params=params(36),
        cost_estimate=cost(5 * 10**9, 14 * 2**20, 6 * 10**6),
        name="attend",
    )(info, *hold(pieces), *hold(weights))


def norm(rows):
    center = rows - jnp.mean(rows, axis=1, keepdims=True)
    root = lax.rsqrt(jnp.mean(center * center, axis=1, keepdims=True) + 1e-05)
    return center * root, root


def norm_back(upstream, gain, unit, root):
    scaled = upstream * gain
    mean = jnp.mean(scaled, axis=1, keepdims=True)
    slope = jnp.mean(scaled * unit, axis=1, keepdims=True)
    return (scaled - mean - unit * slope) * root


def feed_kernel(plan, count, info_ref, lifted_ref, mixed_ref, *refs):
    upstreams, refs = refs[:count], refs[count:]
    if plan.packed:
        late_quarters, small_ref = refs[:8], refs[8]
        refs = refs[9:]
    else:
        outward_in, expand_in, contract_in, small_ref = refs[:4]
        refs = refs[4:]
    results, refs = refs[:count], refs[count:]
    mixed_back_ref, first_back_ref, small_grad_ref = refs[:3]
    refs = refs[3:]
    if plan.packed:
        halves, refs = (refs[:2], refs[2:4]), refs[4:]
    else:
        outward_out, expand_out, contract_out = refs[:3]
        refs = refs[3:]
    (outward_ref, expand_ref, contract_ref, upstream_ref, result_ref, slope_ref, active_all, hidden_all, normed_all,
     lowered_all, branch_all, mixed_all, whole_ref, expand_sum, contract_sum) = refs
    step = pl.program_id(0)
    width, parts, lanes = plan.width, plan.parts, plan.lanes
    contract_own = plan.hidden // plan.devices
    contract_at = (lanes + parts * lanes) * TILE

    @pl.when(step == 0)
    def _():
        if plan.packed:
            for mask in range(plan.devices):
                at = plan.place(mask)
                shard = late_quarters[(mask & 1) * 4 + at // 4].at[at % 4]
                owner = info_ref[1] ^ mask
                rows, wide = aligned(owner, TILE), aligned(owner, contract_own)
                for lane in range(lanes):
                    cut = slice(lane * LANE, (lane + 1) * LANE)
                    outward_ref[rows, cut] = shard[lane * TILE : (lane + 1) * TILE, :]
                    for part in range(parts):
                        at = (lanes + part * lanes + lane) * TILE
                        expand_ref[part, rows, cut] = shard[at : at + TILE, :]
                    at = contract_at + lane * contract_own
                    contract_ref[wide, cut] = shard[at : at + contract_own, :]
        else:
            outward_ref[...] = outward_in[...]
            expand_ref[...] = expand_in[...]
            contract_ref[...] = contract_in[...]

    size = lifted_ref.shape[0]
    here = pl.ds(pl.multiple_of(step * size, size), size)
    rows = plan.total_rows // count
    group = size // rows

    def spot(mask):
        return pl.ds(pl.multiple_of(((info_ref[2] ^ mask) % group) * rows, rows), rows)

    for mask in range(count):
        @pl.when(step == mask // group)
        def _(mask=mask):
            upstream_ref[spot(mask), :] = upstreams[mask][...]

    outlet, steady, offset = (small_ref[i : i + 1, :] for i in (2, 3, 4))
    settle, temper, anchor = (small_ref[i + parts : i + parts + 1, :] for i in (5, 6, 7))
    mixed = mixed_ref[...]
    branch = times(mixed, outward_ref[...]) + outlet
    unit, root = norm(lifted_ref[...] + branch)
    normed = unit * steady + offset
    normed_low = normed.astype(BF)
    normed_all[here, :] = normed_low
    mixed_all[here, :] = mixed
    lowered = jnp.zeros_like(normed)
    for part in range(parts):
        cut = slice(part * width, (part + 1) * width)
        hidden = times(normed_low, expand_ref[part]) + small_ref[5 + part : 6 + part, :]
        square = hidden * hidden
        bend = jnp.tanh(hidden * (BEND + BEND * 0.044715 * square))
        half = 0.5 + 0.5 * bend
        active = (hidden * half).astype(BF)
        active_all[here, cut] = active
        slope_ref[:, cut] = half + (0.5 * hidden) * (1.0 - bend * bend) * (
            BEND + 3 * BEND * 0.044715 * square
        )
        lowered = lowered + times(active, contract_ref[cut, :])
    last_unit, last_root = norm(normed + (lowered + settle))
    result_ref[...] = (last_unit * temper + anchor).astype(BF)
    upstream = upstream_ref[...].astype(F32)
    temper_grad = column_sum(upstream * last_unit)
    anchor_grad = column_sum(upstream)
    second_back = norm_back(upstream, temper, last_unit, last_root)
    lowered_back = second_back.astype(BF)
    lowered_all[here, :] = lowered_back
    settle_grad = column_sum(lowered_back)
    normed_back = second_back
    spread_grads = []
    for part in range(parts):
        cut = slice(part * width, (part + 1) * width)
        active_back = times_t(lowered_back, contract_ref[cut, :])
        hidden_back = (active_back * slope_ref[:, cut]).astype(BF)
        spread_grads.append(column_sum(hidden_back))
        hidden_all[here, cut] = hidden_back
        normed_back = normed_back + times_t(hidden_back, expand_ref[part])
    first_back = norm_back(normed_back, steady, unit, root)
    first_back_ref[...] = first_back
    branch_back = first_back.astype(BF)
    mixed_back_ref[...] = times_t(branch_back, outward_ref[...]).astype(BF)
    branch_all[here, :] = branch_back
    zero = jnp.zeros_like(anchor_grad)
    grads = [zero, zero, column_sum(branch_back), column_sum(normed_back * unit)]
    grads += [column_sum(normed_back)] + spread_grads + [settle_grad, temper_grad, anchor_grad]
    grads += [zero] * (plan.small_rows - len(grads))
    small_term = jnp.concatenate(grads, axis=0)
    for mask in range(count):
        @pl.when(step == mask // group)
        def _(mask=mask):
            results[mask][...] = result_ref[spot(mask), :]

    @pl.when(step == 0)
    def _():
        small_grad_ref[...] = small_term

    @pl.when(step > 0)
    def _():
        small_grad_ref[...] += small_term

    @pl.when(step == pl.num_programs(0) - 1)
    def _():
        outward = t_times(mixed_all[...], branch_all[...])
        if plan.packed:
            me = info_ref[1]
            whole_ref[...] = outward
            for mask in range(plan.devices):
                half = halves[mask & 1]
                rows = aligned(me ^ mask, TILE)
                for lane in range(lanes):
                    cut = slice(lane * LANE, (lane + 1) * LANE)
                    plan.grad_piece(half, mask, lane * TILE, TILE)[...] = whole_ref[rows, cut].astype(BF)
        else:
            outward_out[...] = outward.astype(BF)
        per_part = plan.devices // parts
        for part in range(parts):
            cut = slice(part * width, (part + 1) * width)
            expand = t_times(normed_all[...], hidden_all[:, cut])
            if not plan.packed:
                expand_out[part] = expand.astype(BF)
                continue
            expand_sum[...] = expand
            for mask in range(plan.devices):
                rows = aligned(me ^ mask, TILE)
                for lane in range(lanes):
                    at = (lanes + part * lanes + lane) * TILE
                    plan.grad_piece(halves[mask & 1], mask, at, TILE)[...] = expand_sum[
                        rows, lane * LANE : (lane + 1) * LANE
                    ].astype(BF)
        for mask_part in range(parts):
            part = (me // per_part) ^ mask_part if plan.packed else mask_part
            cut = pl.ds(pl.multiple_of(part * width, width), width)
            contract = t_times(active_all[:, cut], lowered_all[...])
            if not plan.packed:
                contract_out[cut, :] = contract.astype(BF)
                continue
            contract_sum[...] = contract
            for index in range(per_part):
                mask = mask_part * per_part + index
                rows = aligned((me ^ mask) % per_part, contract_own)
                for lane in range(lanes):
                    at = contract_at + lane * contract_own
                    plan.grad_piece(halves[mask & 1], mask, at, contract_own)[...] = contract_sum[
                        rows, lane * LANE : (lane + 1) * LANE
                    ].astype(BF)


def feed(plan, info, count, lifted, mixed, upstreams, weights, small):
    total_rows, width, parts = plan.total_rows, plan.width, plan.parts
    piece = total_rows // count
    size = max(piece, FEED_ROWS)
    group = size // piece
    rows = pl.BlockSpec((size, width), lambda i, info: ((info[2] // group) ^ i, 0))
    outward, expand, contract = (width, width), (parts, width, width), (parts * width, width)
    if plan.packed:
        grads = [pltpu.VMEM((8 * plan.late_rows, LANE), BF)] * 4
    else:
        grads = [pltpu.VMEM(outward, BF), pltpu.VMEM(expand, BF), pltpu.VMEM(contract, BF)]
    ends = [pltpu.VMEM((piece, width), BF)] * count
    outs = [like((total_rows, width), BF), like((total_rows, width), F32), like(small.shape, F32)]
    values = pl.pallas_call(
        functools.partial(feed_kernel, plan, count),
        grid_spec=pltpu.PrefetchScalarGridSpec(
            num_scalar_prefetch=1,
            grid=(total_rows // size,),
            in_specs=[rows, rows]
            + [HELD for v in upstreams + weights]
            + [full(small.shape)],
            out_specs=[HELD for v in ends]
            + [rows, rows, full(small.shape)]
            + [HELD for v in grads],
            scratch_shapes=[
                pltpu.VMEM(outward, BF),
                pltpu.VMEM(expand, BF),
                pltpu.VMEM(contract, BF),
                pltpu.VMEM((size, width), BF),
                pltpu.VMEM((size, width), BF),
                pltpu.VMEM((size, parts * width), F32),
                pltpu.VMEM((total_rows, parts * width), BF),
                pltpu.VMEM((total_rows, parts * width), BF),
                pltpu.VMEM((total_rows, width), BF),
                pltpu.VMEM((total_rows, width), BF),
                pltpu.VMEM((total_rows, width), BF),
                pltpu.VMEM((total_rows, width), BF),
                pltpu.VMEM(outward, F32),
                pltpu.VMEM(outward, F32),
                pltpu.VMEM(outward, F32),
            ],
        ),
        out_shape=ends + outs + grads,
        compiler_params=params(50),
        cost_estimate=cost(15 * 10**9, 20 * 2**20, 2 * 10**6),
        name="feed",
    )(info, lifted, mixed, *hold(upstreams), *hold(weights), small)
    return values[:count], values[count : count + 3], values[count + 3 :]


def attend_back_kernel(
    plan, count, info_ref, lifted_ref, query_ref, key_ref, value_ref, mixed_ref, mixed_back_ref,
    total_ref, inward_ref, first_back_ref, small_grad_ref, *refs
):
    tokens, refs = refs[:count], refs[count:]
    if plan.packed:
        halves, refs = refs[:2], refs[2:]
    else:
        table_out, inward_out, small_out = refs[:3]
        refs = refs[3:]
    (joint_ref, sum_ref, share_ref, score_ref, grad_ref, table_ref, joint_sums, blocks_ref,
     lifted_here, inward_here, copied) = refs
    pair = pl.program_id(0)
    copies = [
        pltpu.make_async_copy(source, target, copied.at[index])
        for index, (source, target) in enumerate(
            ((lifted_ref, lifted_here), (inward_ref, inward_here), (first_back_ref, sum_ref))
        )
    ]

    @pl.when(pair == 0)
    def _():
        for copy in copies:
            copy.start()

    total_rows, lanes = plan.total_rows, plan.lanes
    half = total_rows // 2
    split = info_ref[0] < total_rows
    far = jnp.where(split, FAR, 0.0)
    blocks = total_rows // STEP

    keep = causal()
    lower = lax.broadcasted_iota(jnp.int32, (STEP, LANE), 1) < LANE // 2
    lower_t = lax.broadcasted_iota(jnp.int32, (LANE, STEP), 0) < LANE // 2
    product = (mixed_ref[...].astype(F32) * mixed_back_ref[...].astype(F32)).T
    scaled_key = (key_ref[...] * BF(0.125)).T
    betweens = [
        jnp.sum(product[head * LANE // 2 : (head + 1) * LANE // 2], axis=0, keepdims=True)
        for head in range(2)
    ]

    def logits_of(block, head):
        spot = slice(block * STEP, (block + 1) * STEP)
        keys = slice(0, (block + 1) * STEP)
        query = own_lanes(query_ref[spot, :], head)
        back = own_lanes(mixed_back_ref[spot, :], head)
        return times_t(key_ref[keys, :], query), times_t(value_ref[keys, :], back)

    def scores_of(block, head, logits, share_back):
        start = block * STEP
        spot = slice(start, start + STEP)
        total = total_ref[0, head : head + 1, spot]
        gap = betweens[head][:, spot]
        for under in range(block + 1):
            keys = slice(under * STEP, (under + 1) * STEP)
            away = start >= half and under * STEP < half
            share = jnp.exp(logits[keys] - (total + far if away else total))
            if under == block:
                share = jnp.where(keep, share, 0.0)
            score = share * (share_back[keys] - gap)
            share_ref[head, keys, spot] = share.astype(BF)
            score_ref[head, keys, spot] = score.astype(BF)

    def backs_of(block, head):
        start = block * STEP
        spot = slice(start, start + STEP)
        end = start + STEP
        query_back = times(scaled_key[:, :end], score_ref[head, :end, spot])
        key_back = times(score_ref[head, spot, start:], query_ref[start:, :])
        value_back = times(share_ref[head, spot, start:], mixed_back_ref[start:, :])
        return query_back, key_back, value_back

    tasks = [(block, head) for block in reversed(range(blocks)) for head in range(2)]
    ahead = logits_of(*tasks[0])
    parts = []
    for index, (block, head) in enumerate(tasks):
        logits, ahead = ahead, logits_of(*tasks[index + 1]) if index + 1 < len(tasks) else None
        scores_of(block, head, *logits)
        parts.append(backs_of(block, head))
        if head:
            spot = slice(block * STEP, (block + 1) * STEP)
            query_back = jnp.where(lower_t, parts[0][0], parts[1][0]).T
            key_back = jnp.where(lower, parts[0][1], parts[1][1])
            value_back = jnp.where(lower, parts[0][2], parts[1][2])
            for part, back in enumerate((query_back, key_back, value_back)):
                joint_ref[spot, aligned(pair + part * lanes, LANE)] = back.astype(BF)
            parts = []

    @pl.when(pair == lanes - 1)
    def _():
        for copy in copies:
            copy.wait()
        low = lifted_here[...].astype(BF).T
        weights = jnp.concatenate([inward_here[i] for i in range(3 * lanes)], axis=1)
        for block in range(blocks):
            spot = slice(block * STEP, (block + 1) * STEP)
            sum_ref[spot, :] += times_t(joint_ref[spot, :], weights)
        for part in range(3):
            joint = joint_ref[:, part * plan.width : (part + 1) * plan.width]
            grads = times(low, joint)
            for lane in range(lanes):
                grad_ref[part * lanes + lane] = grads[:, lane * LANE : (lane + 1) * LANE]
            if part != 1:
                sums = column_sum(joint)
                for lane in range(lanes):
                    at = lane if part == 0 else lane + lanes
                    joint_sums[at : at + 1, :] = sums[:, lane * LANE : (lane + 1) * LANE]
        rows = total_rows // count
        for mask in range(count):
            spot = pl.ds(pl.multiple_of((info_ref[2] ^ mask) * rows, rows), rows)
            tokens[mask][...] = sum_ref[spot, :].astype(BF)
        late = sum_ref[half:, :]
        early = sum_ref[:half, :] + jnp.where(split, late, 0.0)
        table_ref[:, :half] = early.T
        table_ref[:, half:] = jnp.where(split, 0.0, late).T
        counted = info_ref[3] > 0
        blocks_ref[: 2 * lanes, :] = joint_sums[: 2 * lanes, :]
        for row in range(2, plan.block_starts[-1] // lanes):
            for lane in range(lanes):
                blocks_ref[row * lanes + lane : row * lanes + lane + 1, :] = small_grad_ref[
                    row : row + 1, lane * LANE : (lane + 1) * LANE
                ]
        if plan.packed:
            for mask in range(plan.devices):
                shard = halves[mask & 1].at[plan.place(mask)]
                owner = info_ref[1] ^ mask
                own = aligned(owner, TILE)
                for piece in range(plan.table_pieces):
                    shard[piece * TILE : (piece + 1) * TILE, :] = table_ref[
                        own, piece * LANE : (piece + 1) * LANE
                    ].astype(BF)
                for piece in range(3 * lanes):
                    at = (plan.table_pieces + piece) * TILE
                    shard[at : at + TILE, :] = grad_ref[piece, own, :].astype(BF)
                rows = [
                    blocks_ref[pl.ds(plan.block_starts[v] + owner * plan.owned[v] // LANE, 1), :]
                    for v in range(VECTORS)
                ]
                rows.append(jnp.zeros((TILE - VECTORS, LANE), F32))
                at = plan.early_pieces * TILE
                shard[at : at + TILE, :] = jnp.concatenate(rows, axis=0).astype(BF)
        else:
            table_out[...] = jnp.where(counted, table_ref[...], 0.0).astype(BF)
            inward_out[...] = jnp.where(counted, grad_ref[...], 0.0).astype(BF)
            small_out[...] = jnp.where(counted, blocks_ref[...], 0.0)


def attend_back(plan, info, count, lifted, saved, mixed_back, inward, first_back, small_grad):
    query, key, value, mixed, totals = saved
    total_rows, width, lanes = plan.total_rows, plan.width, plan.lanes
    block = pl.BlockSpec((total_rows, LANE), lambda p, *_: (0, p))
    blocks = (plan.block_starts[-1], LANE)
    if plan.packed:
        grads = [pltpu.VMEM((plan.devices // 2, plan.early_rows, LANE), BF)] * 2
    else:
        grads = [pltpu.VMEM((width, total_rows), BF), pltpu.VMEM(inward.shape, BF), pltpu.VMEM(blocks, F32)]
    tokens = [pltpu.VMEM((total_rows // count, width), BF)] * count
    values = pl.pallas_call(
        functools.partial(attend_back_kernel, plan, count),
        grid_spec=pltpu.PrefetchScalarGridSpec(
            num_scalar_prefetch=1,
            grid=(lanes,),
            in_specs=[
                pl.BlockSpec(memory_space=pl.ANY),
                block,
                block,
                block,
                block,
                block,
                pl.BlockSpec((1, 8, total_rows), lambda p, *_: (p, 0, 0)),
                pl.BlockSpec(memory_space=pl.ANY),
                pl.BlockSpec(memory_space=pl.ANY),
                full(small_grad.shape),
            ],
            out_specs=[HELD for v in tokens + grads],
            scratch_shapes=[
                pltpu.VMEM((total_rows, 3 * width), BF),
                pltpu.VMEM((total_rows, width), F32),
                pltpu.VMEM((2, total_rows, total_rows), BF),
                pltpu.VMEM((2, total_rows, total_rows), BF),
                pltpu.VMEM(inward.shape, F32),
                pltpu.VMEM((width, total_rows), F32),
                pltpu.VMEM((8, LANE), F32),
                pltpu.VMEM(blocks, F32),
                pltpu.VMEM(lifted.shape, F32),
                pltpu.VMEM(inward.shape, BF),
                pltpu.SemaphoreType.DMA((3,)),
            ],
        ),
        out_shape=tokens + grads,
        compiler_params=params(40),
        cost_estimate=cost(14 * 10**9, 24 * 2**20, 6 * 10**6),
        name="attend_back",
    )(info, *stay([lifted, query, key, value, mixed, mixed_back, totals, inward, first_back]), small_grad)
    return values[:count], values[count:]


def pack_kernel(plan, count, share, rows_ref, table_ref, inward_ref, *refs):
    vectors, refs = refs[:VECTORS], refs[VECTORS:]
    outward_ref, expand_ref, contract_ref = refs[:3]
    pieces, early_ref, late_ref, copied = refs[3 : 3 + count], refs[3 + count], refs[4 + count], refs[5 + count]
    rank = lax.axis_index("seq")
    copies = [
        pltpu.make_async_copy(rows_ref.at[(rank ^ mask) // share], pieces[mask], copied.at[mask])
        for mask in range(count)
    ]
    for copy in copies:
        copy.start()
    at = 0
    for ref in (table_ref, inward_ref):
        for lane in range(ref.shape[1] // LANE):
            early_ref[0, at : at + TILE, :] = ref[:, lane * LANE : (lane + 1) * LANE]
            at += TILE
    rows = []
    for size, ref in zip(plan.owned, vectors):
        rows.append(jnp.concatenate([ref[...].astype(F32)] * (LANE // size), axis=1))
    rows.append(jnp.zeros((TILE - VECTORS, LANE), F32))
    early_ref[0, at : at + TILE, :] = jnp.concatenate(rows, axis=0).astype(BF)
    at = 0
    for ref in (outward_ref, expand_ref, contract_ref):
        rows = ref.shape[0]
        for lane in range(ref.shape[1] // LANE):
            late_ref[0, at : at + rows, :] = ref[:, lane * LANE : (lane + 1) * LANE]
            at += rows
    for copy in copies:
        copy.wait()


def pack(plan, count, share, rows, table, inward, vectors, outward, expand, contract):
    vectors = [v.reshape(1, -1) for v in vectors]
    outs = [pltpu.VMEM(rows.shape[1:], BF)] * count
    outs += [pltpu.VMEM((1, plan.early_rows, LANE), BF), pltpu.VMEM((1, plan.late_rows, LANE), BF)]
    values = pl.pallas_call(
        functools.partial(pack_kernel, plan, count, share),
        out_shape=outs,
        in_specs=[pl.BlockSpec(memory_space=pl.ANY)] + [HELD] * (5 + len(vectors)),
        out_specs=[HELD] * len(outs),
        scratch_shapes=[pltpu.SemaphoreType.DMA((count,))],
        cost_estimate=cost(0, 4 * 2**20),
        name="pack",
    )(rows, table, inward, *vectors, outward, expand, contract)
    return values[:count], values[count], values[count + 1]


def fold(terms, cuts):
    size = terms[0].shape[0] // cuts
    return [
        sum(term[index * size : (index + 1) * size].astype(F32) for term in terms).astype(BF)
        for index in range(cuts)
    ]


def finish_kernel(plan, info_ref, *refs):
    early, late, refs = refs[:4], refs[4:8], refs[8:]
    table_ref, inward_ref, outward_ref, expand_ref, contract_ref = refs[:5]
    vectors = refs[5:]
    early = sum(ref[0].astype(F32) for ref in early)
    late = sum(ref[...].astype(F32) for ref in late)
    for piece in range(plan.table_pieces):
        table_ref[:, piece * LANE : (piece + 1) * LANE] = early[piece * TILE : (piece + 1) * TILE]
    for piece in range(3 * plan.lanes):
        at = (plan.table_pieces + piece) * TILE
        inward_ref[:, piece * LANE : (piece + 1) * LANE] = early[at : at + TILE]
    at = 0
    for ref in (outward_ref, expand_ref, contract_ref):
        rows = ref.shape[0]
        for lane in range(ref.shape[1] // LANE):
            ref[:, lane * LANE : (lane + 1) * LANE] = late[at : at + rows]
            at += rows
    at = plan.early_pieces * TILE
    small = early[at : at + VECTORS]
    for vector, ref in enumerate(vectors):
        size = plan.owned[vector]
        slot = lax.rem(info_ref[1], LANE // size)
        row = pltpu.roll(small, LANE - slot * size, 1)
        ref[...] = row[vector : vector + 1, :size]


def finish(plan, info, early, late):
    own, width = plan.own_rows, plan.width
    outs = [
        like((own, plan.total_rows), F32),
        like((own, 3 * width), F32),
        like((own, width), F32),
        like((own, plan.hidden), F32),
        like((plan.hidden // plan.devices, width), F32),
    ] + [like((1, n), F32) for n in plan.owned]
    values = early + late
    return pl.pallas_call(
        functools.partial(finish_kernel, plan),
        grid_spec=pltpu.PrefetchScalarGridSpec(
            num_scalar_prefetch=1,
            grid=(1,),
            in_specs=[HELD for v in values],
            out_specs=[full(v.shape) for v in outs],
        ),
        out_shape=outs,
        name="finish",
    )(info, *hold(values))


def ordered(rank, pieces):
    for bit in (1, 2):
        flip = (rank & bit) > 0
        pieces = [jnp.where(flip, pieces[i ^ bit], pieces[i]) for i in range(4)]
    return jnp.stack(pieces)


def settle_kernel(count, share, info_ref, *refs):
    for mask in range(count):
        refs[count][pl.ds((info_ref[2] ^ mask) // share, 1), :, :] = refs[mask][...][None]


def settle_rows(info, micro_count, share, pieces):
    out = (micro_count,) + pieces[0].shape
    return pl.pallas_call(
        functools.partial(settle_kernel, len(pieces), share),
        grid_spec=pltpu.PrefetchScalarGridSpec(
            num_scalar_prefetch=1,
            grid=(1,),
            in_specs=[full(v.shape) for v in pieces],
            out_specs=full(out),
        ),
        out_shape=like(out, BF),
        cost_estimate=cost(0, 48 * 2**20),
        name="settle_rows",
    )(info, *pieces)


def cut_kernel(count, share, rows_ref, *refs):
    rank = lax.axis_index("seq")
    for mask in range(count):
        refs[mask][...] = rows_ref[pl.ds((rank ^ mask) // share, 1), :, :][0]


def cut_rows(rows, count, share):
    outs = [like(rows.shape[1:], BF)] * count
    return pl.pallas_call(
        functools.partial(cut_kernel, count, share),
        out_shape=outs,
        cost_estimate=cost(0, 4 * 2**20),
        name="cut_rows",
    )(rows)


def local(tokens, first_length, cotangent, positions, inward, intake, outward, outlet, steady, offset,
          expand, spread, contract, settle, temper, anchor):
    micro_count, pack_count, block_rows, width = tokens.shape
    assert pack_count == 1
    devices, count = lax.axis_size(AXES), lax.axis_size("seq")
    me, rank = lax.axis_index(AXES), lax.axis_index("seq")
    share = max(count // micro_count, 1)
    assert share * micro_count == count
    plan = Plan(devices, width, contract.shape[0] * devices, block_rows * count)
    micro = rank // share
    counted = (rank % share == 0).astype(jnp.int32)

    def info_of(lengths):
        first = jnp.sum(jnp.where(jnp.arange(micro_count) == micro, lengths[:, 0], 0))
        return jnp.stack([first, me, rank, counted]).astype(jnp.int32)

    vectors = (intake, outlet, steady, offset, spread, settle, temper, anchor)

    def swap(value, mask):
        return lax.ppermute(value, AXES, [(d, d ^ mask) for d in range(devices)]) if mask else value

    def exchange(pieces):
        return [swap(piece, mask) for mask, piece in enumerate(pieces)]

    def in_order(pieces):
        if count != 4 or share != 1:
            return settle_rows(info, micro_count, share, pieces)
        return ordered(rank, pieces)

    if plan.packed:
        rows_in, shard, late = pack(
            plan, count, share, tokens[:, 0], positions.T, inward, vectors, outward, expand, contract
        )
        rows_in = exchange(rows_in)
        shard, rows_in[1] = lax.optimization_barrier((shard, rows_in[1]))
        pieces = [swap(shard, mask) for mask in plan.z_order]
        pieces, rows_in, late, cotangent, first_length = lax.optimization_barrier(
            (pieces, rows_in, late, cotangent, first_length)
        )
        info = info_of(first_length)
        shard = jnp.concatenate(pieces, axis=0)
        pieces = [swap(shard, k << 1) for k in range(4)]
        late = [swap(late, mask) for mask in plan.z_order]
        upstreams = cut_rows(cotangent[:, 0], count, share)
        pieces, upstreams, late, info = lax.optimization_barrier((pieces, list(upstreams), late, info))
        late = jnp.concatenate(late, axis=0)
        late_x, late_y = swap(late, 2), swap(late, 4)
        shard = jnp.concatenate(pieces, axis=0)
        early = [shard, swap(shard, 1)]
        upstreams[1] = swap(upstreams[1], 1)
        late_core = swap(late, 1)
        early, late_core, late_x, late_y, upstreams = lax.optimization_barrier(
            (early, late_core, late_x, late_y, upstreams)
        )
        late_xy = swap(late_x, 4)
        upstreams[2:] = [swap(upstreams[mask], mask) for mask in (2, 3)]
        late_cores = [late_core, swap(late_x, 1), swap(late_y, 1)]
    else:
        info = info_of(first_length)
        rows_in = exchange(cut_rows(tokens[:, 0], count, share))
        upstreams = exchange(cut_rows(cotangent[:, 0], count, share))
        early, late = plain_weights(plan, positions, inward, vectors, outward, expand, contract)
    lifted, query, key, value, mixed, totals, inward_all, small = attend(plan, info, count, rows_in, early)
    if plan.packed:
        late_xy, late_cores, upstreams, mixed = lax.optimization_barrier(
            (late_xy, late_cores, upstreams, mixed)
        )
        late = [late, late_x, late_y, late_xy] + late_cores + [swap(late_xy, 1)]
    results, (mixed_back, first_back, small_grad), late_grads = feed(
        plan, info, count, lifted, mixed, upstreams, late, small
    )
    results = exchange(results)
    if plan.packed:
        stay_keep, go_keep, stay_send, go_send = late_grads
        cut = 8 * plan.late_cut
        go = [go_keep, swap(go_send, 1)]
        one_send, two_send = fold([v[:cut] for v in go], 1) + fold([v[cut:] for v in go], 1)
        stay_other = swap(stay_send, 1)
        one_send, two_send, mixed_back = lax.optimization_barrier((one_send, two_send, mixed_back))
        one_other, two_other = swap(one_send, 4), swap(two_send, 2)
    token_pieces, early_grads = attend_back(
        plan, info, count, lifted, (query, key, value, mixed, totals), mixed_back, inward_all,
        first_back, small_grad,
    )
    if plan.packed:
        one_other, two_other, stay_other, results, token_pieces, early_grads = lax.optimization_barrier(
            (one_other, two_other, stay_other, results, token_pieces, early_grads)
        )
        keep, send = early_grads
        send = swap(send, 1)
        one, one_send = fold([stay_keep[:cut], stay_other[:cut], one_other], 2)
        two, two_send = fold([stay_keep[cut:], stay_other[cut:], two_other], 2)
        one, one_send, two, two_send, keep = lax.optimization_barrier((one, one_send, two, two_send, keep))
        one_other, two_other = swap(one_send, 2), swap(two_send, 4)
        terms = fold([keep, send], 4)
        terms, results, token_pieces = lax.optimization_barrier((terms, results, token_pieces))
        terms = [swap(term, k << 1) for k, term in enumerate(terms)]
        output = settle_rows(info, micro_count, share, results)
        one_other, two_other, output = lax.optimization_barrier((one_other, two_other, output))
        ones, twos = fold([one, one_other], 4), fold([two, two_other], 4)
        late_terms = [jnp.concatenate(pair, axis=0) for pair in zip(ones, twos)]
        late_terms = [swap(term, mask) for term, mask in zip(late_terms, plan.z_order)]
        token_pieces = list(token_pieces)
        token_pieces[1] = swap(token_pieces[1], 1)
        terms, late_terms, output, token_pieces = lax.optimization_barrier(
            (terms, late_terms, output, token_pieces)
        )
        terms = fold(terms, 4)
        early_terms = [swap(term, mask) for term, mask in zip(terms, plan.z_order)]
        token_pieces[2:] = [swap(token_pieces[mask], mask) for mask in (2, 3)]
        early_terms, token_pieces = lax.optimization_barrier((early_terms, token_pieces))
        tokens_back = in_order(token_pieces)
        values = finish(plan, info, early_terms, late_terms)
        table_t, inward_own, outward_own, expand_own, contract_own = values[:5]
        own = [v.reshape(-1) for v in values[5:]]
        table_own = table_t.T
    else:
        output = in_order(results)
        tokens_back = in_order(exchange(token_pieces))
        table_own, inward_own, outward_own, expand_own, contract_own, own = plain_grads(
            plan, counted, early_grads, late_grads
        )
    return (output[:, None], tokens_back[:, None], table_own, inward_own, own[0], outward_own, own[1], own[2],
            own[3], expand_own, own[4], contract_own, own[5], own[6], own[7])


def plain_weights(plan, positions, inward, vectors, outward, expand, contract):
    lanes, width = plan.lanes, plan.width

    def gather(value, axis=0):
        return lax.all_gather(value, AXES, axis=axis, tiled=True)

    def in_pieces(value, size):
        return value.reshape(value.shape[0], -1, size).transpose(1, 0, 2)

    table = in_pieces(gather(positions, 1).T, LANE)
    small = jnp.concatenate([gather(v) for v in vectors]).astype(F32).reshape(-1, width)
    small = jnp.pad(small, ((0, plan.small_rows - small.shape[0]), (0, 0)))
    early = [table, in_pieces(gather(inward), LANE), small]
    return early, [gather(outward), in_pieces(gather(expand), width), gather(contract)]


def plain_grads(plan, counted, early_grads, late_grads):
    width = plan.width
    table, inward, small = early_grads
    outward, expand, contract = (jnp.where(counted > 0, g, BF(0)) for g in late_grads)

    def scatter(value, axis=0):
        return lax.psum_scatter(value, AXES, scatter_dimension=axis, tiled=True).astype(F32)

    def whole(value):
        return value.transpose(1, 0, 2).reshape(value.shape[1], -1)

    flat = small.reshape(-1)
    own = []
    for vector, length in enumerate(plan.lengths):
        start = plan.block_starts[vector] * LANE
        own.append(scatter(flat[start : start + length]))
    return (scatter(table.T, 1), scatter(whole(inward)), scatter(outward), scatter(whole(expand)),
            scatter(contract), own)


def solution(mesh):
    rows = P(None, "batch", "seq", None)
    table = P(None, AXES)
    matrix = P(AXES, None)
    vector = P(AXES)
    weights = (table, matrix, vector, matrix, vector, vector, vector, matrix, vector, matrix, vector,
               vector, vector)
    return jax.shard_map(
        local,
        mesh=mesh,
        in_specs=(rows, P(None, "batch"), rows) + weights,
        out_specs=(rows, rows) + weights,
        check_vma=False,
    )
```

```python
import functools

import jax
import jax.numpy as jnp
from jax import lax
from jax.experimental import pallas as pl
from jax.experimental.pallas import tpu as pltpu
from jax.sharding import PartitionSpec as P

AXES = ("batch", "seq")
LANE = 128
TILE = 16
FEED_ROWS = 512
STEP = 256
FAR = 1e30
BEND = 0.7978845608028654
BF = jnp.bfloat16
F32 = jnp.float32
VECTORS = 8


def times(left, right):
    return jnp.dot(left, right, preferred_element_type=F32)


def times_t(left, right):
    return lax.dot_general(left, right, (((1,), (1,)), ((), ())), preferred_element_type=F32)


def t_times(left, right):
    return lax.dot_general(left, right, (((0,), (0,)), ((), ())), preferred_element_type=F32)


def column_sum(values):
    return jnp.sum(values.astype(F32), axis=0, keepdims=True)


def aligned(index, size):
    return pl.ds(pl.multiple_of(index * size, size), size)


def like(shape, kind):
    return jax.ShapeDtypeStruct(shape, kind)


def full(shape):
    return pl.BlockSpec(shape, lambda *_: (0,) * len(shape), pipeline_mode=pl.Buffered(1))


HELD = pl.BlockSpec(memory_space=pltpu.VMEM)


def hold(values):
    return [pltpu.with_memory_space_constraint(v, pltpu.VMEM) for v in values]


def stay(values):
    return [pltpu.with_memory_space_constraint(v, pltpu.HBM) for v in values]


def params(megabytes):
    return pltpu.CompilerParams(vmem_limit_bytes=megabytes * 2**20)


def cost(flops, size, exps=0):
    return pl.CostEstimate(flops=flops, bytes_accessed=size, transcendentals=exps)


class Plan:
    def __init__(self, devices, width, hidden, total_rows):
        self.devices = devices
        self.width = width
        self.hidden = hidden
        self.total_rows = total_rows
        self.own_rows = width // devices
        self.packed = devices == 32 and self.own_rows % TILE == 0
        self.lanes = width // LANE
        self.parts = hidden // width
        self.table_pieces = total_rows // LANE
        self.early_pieces = self.table_pieces + 3 * self.lanes
        self.early_rows = (self.early_pieces + 1) * TILE
        self.late_rows = (self.lanes + hidden // LANE) * TILE + self.lanes * (hidden // devices)
        self.late_cut = (self.lanes + hidden // LANE) * TILE + hidden // devices
        lengths = [2 * width, width, width, width, hidden, width, width, width]
        self.lengths = lengths
        self.owned = [n // devices for n in lengths]
        self.small_rows = 16
        self.z_order = (0, 24, 8, 16)
        starts = [0]
        for n in lengths:
            starts.append(starts[-1] + n // LANE)
        self.block_starts = starts

    def place(self, mask):
        return ((mask >> 1) & 3) * 4 + self.z_order.index(mask & 24)

    def grad_piece(self, half, mask, at, rows):
        first = at < self.late_cut
        assert not first or at + rows <= self.late_cut
        swapped = mask if first else (mask & ~6) | ((mask >> 1) & 2) | ((mask & 2) << 1)
        place = self.place(swapped)
        last_rows = self.late_rows - self.late_cut
        if first:
            start = (place % 8) * self.late_cut + at
        else:
            start = 8 * self.late_cut + (place % 8) * last_rows + at - self.late_cut
        return half[place // 8].at[start : start + rows, :]


def fill_early(plan, me, halves, table_ref, inward_ref, small_ref, stage_ref):
    for mask in range(plan.devices):
        shard = halves[mask & 1].at[plan.place(mask)]
        owner = me ^ mask
        rows = aligned(owner, TILE)
        for piece in range(plan.table_pieces):
            table_ref[piece, rows, :] = shard[piece * TILE : (piece + 1) * TILE, :]
        for piece in range(3 * plan.lanes):
            at = plan.table_pieces + piece
            inward_ref[piece, rows, :] = shard[at * TILE : (at + 1) * TILE, :]
        at = plan.early_pieces * TILE
        stage_ref[pl.ds(owner, 1), :, :] = shard[at : at + TILE, :].astype(F32)[None]
    lane = lax.broadcasted_iota(jnp.int32, (1, LANE), 1)
    for vector, length in enumerate(plan.lengths):
        size = plan.owned[vector]
        group = LANE // size
        for block in range(length // LANE):
            row = jnp.zeros((1, LANE), F32)
            for index in range(group):
                own = stage_ref[block * group + index, vector : vector + 1, :]
                row = jnp.where(lane // size == index, own, row)
            at = plan.block_starts[vector] + block
            small_ref[at // plan.lanes : at // plan.lanes + 1, (at % plan.lanes) * LANE : (at % plan.lanes + 1) * LANE] = row


def own_lanes(value, head):
    lane = lax.broadcasted_iota(jnp.int32, value.shape, 1)
    return jnp.where((lane // (LANE // 2)) == head, value, jnp.zeros_like(value))


def causal():
    return lax.broadcasted_iota(jnp.int32, (STEP, STEP), 0) <= lax.broadcasted_iota(
        jnp.int32, (STEP, STEP), 1
    )


def attend_kernel(plan, count, info_ref, *refs):
    pieces, refs = refs[:count], refs[count:]
    if plan.packed:
        halves, refs = refs[:2], refs[2:]
    else:
        table_in, inward_in, small_in = refs[:3]
        refs = refs[3:]
    (lifted_ref, query_ref, key_ref, value_ref, mixed_ref, total_ref, inward_ref, small_ref) = refs[:8]
    low_ref, table_ref, place_ref, stage_ref = refs[8:]
    pair = pl.program_id(0)
    total_rows, width = plan.total_rows, plan.width
    half = total_rows // 2
    split = info_ref[0] < total_rows
    far = jnp.where(split, FAR, 0.0)

    @pl.when(pair == 0)
    def _():
        if plan.packed:
            fill_early(plan, info_ref[1], halves, table_ref, inward_ref, small_ref, stage_ref)
        else:
            table_ref[...] = table_in[...]
            inward_ref[...] = inward_in[...]
            small_ref[...] = small_in[...]
        eye = (
            lax.broadcasted_iota(jnp.int32, (half, half), 0)
            == lax.broadcasted_iota(jnp.int32, (half, half), 1)
        ).astype(BF)
        per_half = half // LANE
        for part in range(2):
            table = jnp.concatenate(
                [table_ref[part * per_half + i] for i in range(per_half)], axis=1
            )
            place_ref[part * half : (part + 1) * half, :] = times_t(eye, table)
        rows = total_rows // count
        for mask in range(count):
            start = (info_ref[2] ^ mask) * rows
            place = start - jnp.where(jnp.logical_and(split, start >= half), half, 0)
            lifted = pieces[mask][...].astype(F32) + place_ref[pl.ds(pl.multiple_of(place, rows), rows), :]
            spot = pl.ds(pl.multiple_of(start, rows), rows)
            lifted_ref[spot, :] = lifted
            low_ref[spot, :] = lifted.astype(BF)

    weights = jnp.concatenate([inward_ref[pair + i * plan.lanes] for i in range(3)], axis=1)
    lanes = aligned(pair, LANE)
    query_bias = small_ref[0:1, lanes]
    value_bias = small_ref[1:2, lanes]
    for block in range(total_rows // STEP):
        spot = slice(block * STEP, (block + 1) * STEP)
        joint = times(low_ref[spot, :], weights)
        query_ref[spot, :] = (joint[:, :LANE] + query_bias).astype(BF) * BF(0.125)
        key_ref[spot, :] = joint[:, LANE : 2 * LANE].astype(BF)
        value_ref[spot, :] = (joint[:, 2 * LANE :] + value_bias).astype(BF)

    keep = causal()
    lower = lax.broadcasted_iota(jnp.int32, (LANE, STEP), 0) < LANE // 2

    value_t = value_ref[...].T

    def logits_of(block, head):
        start = block * STEP
        other = half if start >= half else 0
        mine = own_lanes(query_ref[start : start + STEP, :], head)
        near = times_t(key_ref[start : start + STEP, :], mine)
        same = times_t(key_ref[other:start, :], mine) if start > other else None
        away = times_t(key_ref[:other, :], mine) if other else None
        return near, same, away

    def mixed_of(block, head, near, same, away):
        start = block * STEP
        other = half if start >= half else 0
        near = jnp.where(keep, near, -FAR)
        peak = jnp.max(near, axis=0, keepdims=True)
        if same is not None:
            peak = jnp.maximum(peak, jnp.max(same, axis=0, keepdims=True))
        if away is not None:
            peak = jnp.maximum(peak, jnp.max(away, axis=0, keepdims=True) - far)
        raised = [jnp.exp(piece - peak) for piece in (same, near) if piece is not None]
        total = sum(jnp.sum(piece, axis=0, keepdims=True) for piece in raised)
        low = jnp.concatenate([piece.astype(BF) for piece in raised], axis=0)
        mixed = times(value_t[:, other : start + STEP], low)
        if away is not None:
            away = jnp.exp(away - (peak + far))
            total = total + jnp.sum(away, axis=0, keepdims=True)
            mixed = mixed + times(value_t[:, :other], away.astype(BF))
        total_ref[0, head : head + 1, start : start + STEP] = peak + jnp.log(total)
        return mixed * (1.0 / total)

    tasks = [(block, head) for block in range(total_rows // STEP) for head in range(2)]
    ahead = logits_of(*tasks[0])
    parts = []
    for index, (block, head) in enumerate(tasks):
        logits, ahead = ahead, logits_of(*tasks[index + 1]) if index + 1 < len(tasks) else None
        parts.append(mixed_of(block, head, *logits))
        if head:
            mixed_ref[block * STEP : (block + 1) * STEP, :] = jnp.where(lower, *parts).T.astype(BF)
            parts = []


def attend(plan, info, count, pieces, weights):
    total_rows, width = plan.total_rows, plan.width
    block = pl.BlockSpec((total_rows, LANE), lambda p, *_: (0, p))
    low = pltpu.HBM((total_rows, width), BF)
    inward = (3 * plan.lanes, width, LANE)
    small = (plan.small_rows, width)
    return pl.pallas_call(
        functools.partial(attend_kernel, plan, count),
        grid_spec=pltpu.PrefetchScalarGridSpec(
            num_scalar_prefetch=1,
            grid=(plan.lanes,),
            in_specs=[HELD for v in pieces + weights],
            out_specs=[
                full((total_rows, width)),
                block,
                block,
                block,
                block,
                pl.BlockSpec((1, 8, total_rows), lambda p, *_: (p, 0, 0)),
                full(inward),
                full(small),
            ],
            scratch_shapes=[
                pltpu.VMEM((total_rows, width), BF),
                pltpu.VMEM((plan.table_pieces, width, LANE), BF),
                pltpu.VMEM((total_rows, width), F32),
                pltpu.VMEM((plan.devices, TILE, LANE), F32),
            ],
        ),
        out_shape=[
            pltpu.HBM((total_rows, width), F32),
            low,
            low,
            low,
            low,
            pltpu.HBM((plan.lanes, 8, total_rows), F32),
            pltpu.HBM(inward, BF),
            pltpu.HBM(small, F32),
        ],
        compiler_params=params(36),
        cost_estimate=cost(5 * 10**9, 14 * 2**20, 6 * 10**6),
        name="attend",
    )(info, *hold(pieces), *hold(weights))


def norm(rows):
    center = rows - jnp.mean(rows, axis=1, keepdims=True)
    root = lax.rsqrt(jnp.mean(center * center, axis=1, keepdims=True) + 1e-05)
    return center * root, root


def norm_back(upstream, gain, unit, root):
    scaled = upstream * gain
    mean = jnp.mean(scaled, axis=1, keepdims=True)
    slope = jnp.mean(scaled * unit, axis=1, keepdims=True)
    return (scaled - mean - unit * slope) * root


def feed_kernel(plan, count, info_ref, lifted_ref, mixed_ref, *refs):
    upstreams, refs = refs[:count], refs[count:]
    if plan.packed:
        late_quarters, small_ref = refs[:8], refs[8]
        refs = refs[9:]
    else:
        outward_in, expand_in, contract_in, small_ref = refs[:4]
        refs = refs[4:]
    results, refs = refs[:count], refs[count:]
    mixed_back_ref, first_back_ref, small_grad_ref = refs[:3]
    refs = refs[3:]
    if plan.packed:
        halves, refs = (refs[:2], refs[2:4]), refs[4:]
    else:
        outward_out, expand_out, contract_out = refs[:3]
        refs = refs[3:]
    (outward_ref, expand_ref, contract_ref, upstream_ref, result_ref, slope_ref, active_all, hidden_all, normed_all,
     lowered_all, branch_all, mixed_all, whole_ref, expand_sum, contract_sum) = refs
    step = pl.program_id(0)
    width, parts, lanes = plan.width, plan.parts, plan.lanes
    contract_own = plan.hidden // plan.devices
    contract_at = (lanes + parts * lanes) * TILE

    @pl.when(step == 0)
    def _():
        if plan.packed:
            for mask in range(plan.devices):
                at = plan.place(mask)
                shard = late_quarters[(mask & 1) * 4 + at // 4].at[at % 4]
                owner = info_ref[1] ^ mask
                rows, wide = aligned(owner, TILE), aligned(owner, contract_own)
                for lane in range(lanes):
                    cut = slice(lane * LANE, (lane + 1) * LANE)
                    outward_ref[rows, cut] = shard[lane * TILE : (lane + 1) * TILE, :]
                    for part in range(parts):
                        at = (lanes + part * lanes + lane) * TILE
                        expand_ref[part, rows, cut] = shard[at : at + TILE, :]
                    at = contract_at + lane * contract_own
                    contract_ref[wide, cut] = shard[at : at + contract_own, :]
        else:
            outward_ref[...] = outward_in[...]
            expand_ref[...] = expand_in[...]
            contract_ref[...] = contract_in[...]

    size = lifted_ref.shape[0]
    here = pl.ds(pl.multiple_of(step * size, size), size)
    rows = plan.total_rows // count
    group = size // rows

    def spot(mask):
        return pl.ds(pl.multiple_of(((info_ref[2] ^ mask) % group) * rows, rows), rows)

    for mask in range(count):
        @pl.when(step == mask // group)
        def _(mask=mask):
            upstream_ref[spot(mask), :] = upstreams[mask][...]

    outlet, steady, offset = (small_ref[i : i + 1, :] for i in (2, 3, 4))
    settle, temper, anchor = (small_ref[i + parts : i + parts + 1, :] for i in (5, 6, 7))
    mixed = mixed_ref[...]
    branch = times(mixed, outward_ref[...]) + outlet
    unit, root = norm(lifted_ref[...] + branch)
    normed = unit * steady + offset
    normed_low = normed.astype(BF)
    normed_all[here, :] = normed_low
    mixed_all[here, :] = mixed
    lowered = jnp.zeros_like(normed)
    for part in range(parts):
        cut = slice(part * width, (part + 1) * width)
        hidden = times(normed_low, expand_ref[part]) + small_ref[5 + part : 6 + part, :]
        square = hidden * hidden
        bend = jnp.tanh(hidden * (BEND + BEND * 0.044715 * square))
        half = 0.5 + 0.5 * bend
        active = (hidden * half).astype(BF)
        active_all[here, cut] = active
        slope_ref[:, cut] = half + (0.5 * hidden) * (1.0 - bend * bend) * (
            BEND + 3 * BEND * 0.044715 * square
        )
        lowered = lowered + times(active, contract_ref[cut, :])
    last_unit, last_root = norm(normed + (lowered + settle))
    result_ref[...] = (last_unit * temper + anchor).astype(BF)
    upstream = upstream_ref[...].astype(F32)
    temper_grad = column_sum(upstream * last_unit)
    anchor_grad = column_sum(upstream)
    second_back = norm_back(upstream, temper, last_unit, last_root)
    lowered_back = second_back.astype(BF)
    lowered_all[here, :] = lowered_back
    settle_grad = column_sum(lowered_back)
    normed_back = second_back
    spread_grads = []
    for part in range(parts):
        cut = slice(part * width, (part + 1) * width)
        active_back = times_t(lowered_back, contract_ref[cut, :])
        hidden_back = (active_back * slope_ref[:, cut]).astype(BF)
        spread_grads.append(column_sum(hidden_back))
        hidden_all[here, cut] = hidden_back
        normed_back = normed_back + times_t(hidden_back, expand_ref[part])
    first_back = norm_back(normed_back, steady, unit, root)
    first_back_ref[...] = first_back
    branch_back = first_back.astype(BF)
    mixed_back_ref[...] = times_t(branch_back, outward_ref[...]).astype(BF)
    branch_all[here, :] = branch_back
    zero = jnp.zeros_like(anchor_grad)
    grads = [zero, zero, column_sum(branch_back), column_sum(normed_back * unit)]
    grads += [column_sum(normed_back)] + spread_grads + [settle_grad, temper_grad, anchor_grad]
    grads += [zero] * (plan.small_rows - len(grads))
    small_term = jnp.concatenate(grads, axis=0)
    for mask in range(count):
        @pl.when(step == mask // group)
        def _(mask=mask):
            results[mask][...] = result_ref[spot(mask), :]

    @pl.when(step == 0)
    def _():
        small_grad_ref[...] = small_term

    @pl.when(step > 0)
    def _():
        small_grad_ref[...] += small_term

    @pl.when(step == pl.num_programs(0) - 1)
    def _():
        outward = t_times(mixed_all[...], branch_all[...])
        if plan.packed:
            me = info_ref[1]
            whole_ref[...] = outward
            for mask in range(plan.devices):
                half = halves[mask & 1]
                rows = aligned(me ^ mask, TILE)
                for lane in range(lanes):
                    cut = slice(lane * LANE, (lane + 1) * LANE)
                    plan.grad_piece(half, mask, lane * TILE, TILE)[...] = whole_ref[rows, cut].astype(BF)
        else:
            outward_out[...] = outward.astype(BF)
        per_part = plan.devices // parts
        for part in range(parts):
            cut = slice(part * width, (part + 1) * width)
            expand = t_times(normed_all[...], hidden_all[:, cut])
            if not plan.packed:
                expand_out[part] = expand.astype(BF)
                continue
            expand_sum[...] = expand
            for mask in range(plan.devices):
                rows = aligned(me ^ mask, TILE)
                for lane in range(lanes):
                    at = (lanes + part * lanes + lane) * TILE
                    plan.grad_piece(halves[mask & 1], mask, at, TILE)[...] = expand_sum[
                        rows, lane * LANE : (lane + 1) * LANE
                    ].astype(BF)
        for mask_part in range(parts):
            part = (me // per_part) ^ mask_part if plan.packed else mask_part
            cut = pl.ds(pl.multiple_of(part * width, width), width)
            contract = t_times(active_all[:, cut], lowered_all[...])
            if not plan.packed:
                contract_out[cut, :] = contract.astype(BF)
                continue
            contract_sum[...] = contract
            for index in range(per_part):
                mask = mask_part * per_part + index
                rows = aligned((me ^ mask) % per_part, contract_own)
                for lane in range(lanes):
                    at = contract_at + lane * contract_own
                    plan.grad_piece(halves[mask & 1], mask, at, contract_own)[...] = contract_sum[
                        rows, lane * LANE : (lane + 1) * LANE
                    ].astype(BF)


def feed(plan, info, count, lifted, mixed, upstreams, weights, small):
    total_rows, width, parts = plan.total_rows, plan.width, plan.parts
    piece = total_rows // count
    size = max(piece, FEED_ROWS)
    group = size // piece
    rows = pl.BlockSpec((size, width), lambda i, info: ((info[2] // group) ^ i, 0))
    outward, expand, contract = (width, width), (parts, width, width), (parts * width, width)
    if plan.packed:
        grads = [pltpu.VMEM((8 * plan.late_rows, LANE), BF)] * 4
    else:
        grads = [pltpu.VMEM(outward, BF), pltpu.VMEM(expand, BF), pltpu.VMEM(contract, BF)]
    ends = [pltpu.VMEM((piece, width), BF)] * count
    outs = [like((total_rows, width), BF), like((total_rows, width), F32), like(small.shape, F32)]
    values = pl.pallas_call(
        functools.partial(feed_kernel, plan, count),
        grid_spec=pltpu.PrefetchScalarGridSpec(
            num_scalar_prefetch=1,
            grid=(total_rows // size,),
            in_specs=[rows, rows]
            + [HELD for v in upstreams + weights]
            + [full(small.shape)],
            out_specs=[HELD for v in ends]
            + [rows, rows, full(small.shape)]
            + [HELD for v in grads],
            scratch_shapes=[
                pltpu.VMEM(outward, BF),
                pltpu.VMEM(expand, BF),
                pltpu.VMEM(contract, BF),
                pltpu.VMEM((size, width), BF),
                pltpu.VMEM((size, width), BF),
                pltpu.VMEM((size, parts * width), F32),
                pltpu.VMEM((total_rows, parts * width), BF),
                pltpu.VMEM((total_rows, parts * width), BF),
                pltpu.VMEM((total_rows, width), BF),
                pltpu.VMEM((total_rows, width), BF),
                pltpu.VMEM((total_rows, width), BF),
                pltpu.VMEM((total_rows, width), BF),
                pltpu.VMEM(outward, F32),
                pltpu.VMEM(outward, F32),
                pltpu.VMEM(outward, F32),
            ],
        ),
        out_shape=ends + outs + grads,
        compiler_params=params(50),
        cost_estimate=cost(15 * 10**9, 20 * 2**20, 2 * 10**6),
        name="feed",
    )(info, lifted, mixed, *hold(upstreams), *hold(weights), small)
    return values[:count], values[count : count + 3], values[count + 3 :]


def attend_back_kernel(
    plan, count, info_ref, lifted_ref, query_ref, key_ref, value_ref, mixed_ref, mixed_back_ref,
    total_ref, inward_ref, first_back_ref, small_grad_ref, *refs
):
    tokens, refs = refs[:count], refs[count:]
    if plan.packed:
        halves, refs = refs[:2], refs[2:]
    else:
        table_out, inward_out, small_out = refs[:3]
        refs = refs[3:]
    (joint_ref, sum_ref, share_ref, score_ref, grad_ref, table_ref, joint_sums, blocks_ref,
     lifted_here, inward_here, copied) = refs
    pair = pl.program_id(0)
    copies = [
        pltpu.make_async_copy(source, target, copied.at[index])
        for index, (source, target) in enumerate(
            ((lifted_ref, lifted_here), (inward_ref, inward_here), (first_back_ref, sum_ref))
        )
    ]

    @pl.when(pair == 0)
    def _():
        for copy in copies:
            copy.start()

    total_rows, lanes = plan.total_rows, plan.lanes
    half = total_rows // 2
    split = info_ref[0] < total_rows
    far = jnp.where(split, FAR, 0.0)
    blocks = total_rows // STEP

    keep = causal()
    lower = lax.broadcasted_iota(jnp.int32, (STEP, LANE), 1) < LANE // 2
    lower_t = lax.broadcasted_iota(jnp.int32, (LANE, STEP), 0) < LANE // 2
    product = (mixed_ref[...].astype(F32) * mixed_back_ref[...].astype(F32)).T
    scaled_key = (key_ref[...] * BF(0.125)).T
    betweens = [
        jnp.sum(product[head * LANE // 2 : (head + 1) * LANE // 2], axis=0, keepdims=True)
        for head in range(2)
    ]

    def logits_of(block, head):
        spot = slice(block * STEP, (block + 1) * STEP)
        keys = slice(0, (block + 1) * STEP)
        query = own_lanes(query_ref[spot, :], head)
        back = own_lanes(mixed_back_ref[spot, :], head)
        return times_t(key_ref[keys, :], query), times_t(value_ref[keys, :], back)

    def scores_of(block, head, logits, share_back):
        start = block * STEP
        spot = slice(start, start + STEP)
        total = total_ref[0, head : head + 1, spot]
        gap = betweens[head][:, spot]
        for under in range(block + 1):
            keys = slice(under * STEP, (under + 1) * STEP)
            away = start >= half and under * STEP < half
            share = jnp.exp(logits[keys] - (total + far if away else total))
            if under == block:
                share = jnp.where(keep, share, 0.0)
            score = share * (share_back[keys] - gap)
            share_ref[head, keys, spot] = share.astype(BF)
            score_ref[head, keys, spot] = score.astype(BF)

    def backs_of(block, head):
        start = block * STEP
        spot = slice(start, start + STEP)
        end = start + STEP
        query_back = times(scaled_key[:, :end], score_ref[head, :end, spot])
        key_back = times(score_ref[head, spot, start:], query_ref[start:, :])
        value_back = times(share_ref[head, spot, start:], mixed_back_ref[start:, :])
        return query_back, key_back, value_back

    tasks = [(block, head) for block in reversed(range(blocks)) for head in range(2)]
    ahead = logits_of(*tasks[0])
    parts = []
    for index, (block, head) in enumerate(tasks):
        logits, ahead = ahead, logits_of(*tasks[index + 1]) if index + 1 < len(tasks) else None
        scores_of(block, head, *logits)
        parts.append(backs_of(block, head))
        if head:
            spot = slice(block * STEP, (block + 1) * STEP)
            query_back = jnp.where(lower_t, parts[0][0], parts[1][0]).T
            key_back = jnp.where(lower, parts[0][1], parts[1][1])
            value_back = jnp.where(lower, parts[0][2], parts[1][2])
            for part, back in enumerate((query_back, key_back, value_back)):
                joint_ref[spot, aligned(pair + part * lanes, LANE)] = back.astype(BF)
            parts = []

    @pl.when(pair == lanes - 1)
    def _():
        for copy in copies:
            copy.wait()
        low = lifted_here[...].astype(BF).T
        weights = jnp.concatenate([inward_here[i] for i in range(3 * lanes)], axis=1)
        for block in range(blocks):
            spot = slice(block * STEP, (block + 1) * STEP)
            sum_ref[spot, :] += times_t(joint_ref[spot, :], weights)
        for part in range(3):
            joint = joint_ref[:, part * plan.width : (part + 1) * plan.width]
            grads = times(low, joint)
            for lane in range(lanes):
                grad_ref[part * lanes + lane] = grads[:, lane * LANE : (lane + 1) * LANE]
            if part != 1:
                sums = column_sum(joint)
                for lane in range(lanes):
                    at = lane if part == 0 else lane + lanes
                    joint_sums[at : at + 1, :] = sums[:, lane * LANE : (lane + 1) * LANE]
        rows = total_rows // count
        for mask in range(count):
            spot = pl.ds(pl.multiple_of((info_ref[2] ^ mask) * rows, rows), rows)
            tokens[mask][...] = sum_ref[spot, :].astype(BF)
        late = sum_ref[half:, :]
        early = sum_ref[:half, :] + jnp.where(split, late, 0.0)
        table_ref[:, :half] = early.T
        table_ref[:, half:] = jnp.where(split, 0.0, late).T
        counted = info_ref[3] > 0
        blocks_ref[: 2 * lanes, :] = joint_sums[: 2 * lanes, :]
        for row in range(2, plan.block_starts[-1] // lanes):
            for lane in range(lanes):
                blocks_ref[row * lanes + lane : row * lanes + lane + 1, :] = small_grad_ref[
                    row : row + 1, lane * LANE : (lane + 1) * LANE
                ]
        if plan.packed:
            for mask in range(plan.devices):
                shard = halves[mask & 1].at[plan.place(mask)]
                owner = info_ref[1] ^ mask
                own = aligned(owner, TILE)
                for piece in range(plan.table_pieces):
                    shard[piece * TILE : (piece + 1) * TILE, :] = table_ref[
                        own, piece * LANE : (piece + 1) * LANE
                    ].astype(BF)
                for piece in range(3 * lanes):
                    at = (plan.table_pieces + piece) * TILE
                    shard[at : at + TILE, :] = grad_ref[piece, own, :].astype(BF)
                rows = [
                    blocks_ref[pl.ds(plan.block_starts[v] + owner * plan.owned[v] // LANE, 1), :]
                    for v in range(VECTORS)
                ]
                rows.append(jnp.zeros((TILE - VECTORS, LANE), F32))
                at = plan.early_pieces * TILE
                shard[at : at + TILE, :] = jnp.concatenate(rows, axis=0).astype(BF)
        else:
            table_out[...] = jnp.where(counted, table_ref[...], 0.0).astype(BF)
            inward_out[...] = jnp.where(counted, grad_ref[...], 0.0).astype(BF)
            small_out[...] = jnp.where(counted, blocks_ref[...], 0.0)


def attend_back(plan, info, count, lifted, saved, mixed_back, inward, first_back, small_grad):
    query, key, value, mixed, totals = saved
    total_rows, width, lanes = plan.total_rows, plan.width, plan.lanes
    block = pl.BlockSpec((total_rows, LANE), lambda p, *_: (0, p))
    blocks = (plan.block_starts[-1], LANE)
    if plan.packed:
        grads = [pltpu.VMEM((plan.devices // 2, plan.early_rows, LANE), BF)] * 2
    else:
        grads = [pltpu.VMEM((width, total_rows), BF), pltpu.VMEM(inward.shape, BF), pltpu.VMEM(blocks, F32)]
    tokens = [pltpu.VMEM((total_rows // count, width), BF)] * count
    values = pl.pallas_call(
        functools.partial(attend_back_kernel, plan, count),
        grid_spec=pltpu.PrefetchScalarGridSpec(
            num_scalar_prefetch=1,
            grid=(lanes,),
            in_specs=[
                pl.BlockSpec(memory_space=pl.ANY),
                block,
                block,
                block,
                block,
                block,
                pl.BlockSpec((1, 8, total_rows), lambda p, *_: (p, 0, 0)),
                pl.BlockSpec(memory_space=pl.ANY),
                pl.BlockSpec(memory_space=pl.ANY),
                full(small_grad.shape),
            ],
            out_specs=[HELD for v in tokens + grads],
            scratch_shapes=[
                pltpu.VMEM((total_rows, 3 * width), BF),
                pltpu.VMEM((total_rows, width), F32),
                pltpu.VMEM((2, total_rows, total_rows), BF),
                pltpu.VMEM((2, total_rows, total_rows), BF),
                pltpu.VMEM(inward.shape, F32),
                pltpu.VMEM((width, total_rows), F32),
                pltpu.VMEM((8, LANE), F32),
                pltpu.VMEM(blocks, F32),
                pltpu.VMEM(lifted.shape, F32),
                pltpu.VMEM(inward.shape, BF),
                pltpu.SemaphoreType.DMA((3,)),
            ],
        ),
        out_shape=tokens + grads,
        compiler_params=params(40),
        cost_estimate=cost(14 * 10**9, 24 * 2**20, 6 * 10**6),
        name="attend_back",
    )(info, *stay([lifted, query, key, value, mixed, mixed_back, totals, inward, first_back]), small_grad)
    return values[:count], values[count:]


def pack_kernel(plan, count, share, rows_ref, table_ref, inward_ref, *refs):
    vectors, refs = refs[:VECTORS], refs[VECTORS:]
    outward_ref, expand_ref, contract_ref = refs[:3]
    pieces, early_ref, late_ref, copied = refs[3 : 3 + count], refs[3 + count], refs[4 + count], refs[5 + count]
    rank = lax.axis_index("seq")
    copies = [
        pltpu.make_async_copy(rows_ref.at[(rank ^ mask) // share], pieces[mask], copied.at[mask])
        for mask in range(count)
    ]
    for copy in copies:
        copy.start()
    at = 0
    for ref in (table_ref, inward_ref):
        for lane in range(ref.shape[1] // LANE):
            early_ref[0, at : at + TILE, :] = ref[:, lane * LANE : (lane + 1) * LANE]
            at += TILE
    rows = []
    for size, ref in zip(plan.owned, vectors):
        rows.append(jnp.concatenate([ref[...].astype(F32)] * (LANE // size), axis=1))
    rows.append(jnp.zeros((TILE - VECTORS, LANE), F32))
    early_ref[0, at : at + TILE, :] = jnp.concatenate(rows, axis=0).astype(BF)
    at = 0
    for ref in (outward_ref, expand_ref, contract_ref):
        rows = ref.shape[0]
        for lane in range(ref.shape[1] // LANE):
            late_ref[0, at : at + rows, :] = ref[:, lane * LANE : (lane + 1) * LANE]
            at += rows
    for copy in copies:
        copy.wait()


def pack(plan, count, share, rows, table, inward, vectors, outward, expand, contract):
    vectors = [v.reshape(1, -1) for v in vectors]
    outs = [pltpu.VMEM(rows.shape[1:], BF)] * count
    outs += [pltpu.VMEM((1, plan.early_rows, LANE), BF), pltpu.VMEM((1, plan.late_rows, LANE), BF)]
    values = pl.pallas_call(
        functools.partial(pack_kernel, plan, count, share),
        out_shape=outs,
        in_specs=[pl.BlockSpec(memory_space=pl.ANY)] + [HELD] * (5 + len(vectors)),
        out_specs=[HELD] * len(outs),
        scratch_shapes=[pltpu.SemaphoreType.DMA((count,))],
        cost_estimate=cost(0, 4 * 2**20),
        name="pack",
    )(rows, table, inward, *vectors, outward, expand, contract)
    return values[:count], values[count], values[count + 1]


def fold(terms, cuts):
    size = terms[0].shape[0] // cuts
    return [
        sum(term[index * size : (index + 1) * size].astype(F32) for term in terms).astype(BF)
        for index in range(cuts)
    ]


def finish_kernel(plan, info_ref, *refs):
    early, late, refs = refs[:4], refs[4:8], refs[8:]
    table_ref, inward_ref, outward_ref, expand_ref, contract_ref = refs[:5]
    vectors = refs[5:]
    early = sum(ref[0].astype(F32) for ref in early)
    late = sum(ref[...].astype(F32) for ref in late)
    for piece in range(plan.table_pieces):
        table_ref[:, piece * LANE : (piece + 1) * LANE] = early[piece * TILE : (piece + 1) * TILE]
    for piece in range(3 * plan.lanes):
        at = (plan.table_pieces + piece) * TILE
        inward_ref[:, piece * LANE : (piece + 1) * LANE] = early[at : at + TILE]
    at = 0
    for ref in (outward_ref, expand_ref, contract_ref):
        rows = ref.shape[0]
        for lane in range(ref.shape[1] // LANE):
            ref[:, lane * LANE : (lane + 1) * LANE] = late[at : at + rows]
            at += rows
    at = plan.early_pieces * TILE
    small = early[at : at + VECTORS]
    for vector, ref in enumerate(vectors):
        size = plan.owned[vector]
        slot = lax.rem(info_ref[1], LANE // size)
        row = pltpu.roll(small, LANE - slot * size, 1)
        ref[...] = row[vector : vector + 1, :size]


def finish(plan, info, early, late):
    own, width = plan.own_rows, plan.width
    outs = [
        like((own, plan.total_rows), F32),
        like((own, 3 * width), F32),
        like((own, width), F32),
        like((own, plan.hidden), F32),
        like((plan.hidden // plan.devices, width), F32),
    ] + [like((1, n), F32) for n in plan.owned]
    values = early + late
    return pl.pallas_call(
        functools.partial(finish_kernel, plan),
        grid_spec=pltpu.PrefetchScalarGridSpec(
            num_scalar_prefetch=1,
            grid=(1,),
            in_specs=[HELD for v in values],
            out_specs=[full(v.shape) for v in outs],
        ),
        out_shape=outs,
        name="finish",
    )(info, *hold(values))


def ordered(rank, pieces):
    for bit in (1, 2):
        flip = (rank & bit) > 0
        pieces = [jnp.where(flip, pieces[i ^ bit], pieces[i]) for i in range(4)]
    return jnp.stack(pieces)


def settle_kernel(count, share, info_ref, *refs):
    for mask in range(count):
        refs[count][pl.ds((info_ref[2] ^ mask) // share, 1), :, :] = refs[mask][...][None]


def settle_rows(info, micro_count, share, pieces):
    out = (micro_count,) + pieces[0].shape
    return pl.pallas_call(
        functools.partial(settle_kernel, len(pieces), share),
        grid_spec=pltpu.PrefetchScalarGridSpec(
            num_scalar_prefetch=1,
            grid=(1,),
            in_specs=[full(v.shape) for v in pieces],
            out_specs=full(out),
        ),
        out_shape=like(out, BF),
        cost_estimate=cost(0, 48 * 2**20),
        name="settle_rows",
    )(info, *pieces)


def cut_kernel(count, share, rows_ref, *refs):
    rank = lax.axis_index("seq")
    for mask in range(count):
        refs[mask][...] = rows_ref[pl.ds((rank ^ mask) // share, 1), :, :][0]


def cut_rows(rows, count, share):
    outs = [like(rows.shape[1:], BF)] * count
    return pl.pallas_call(
        functools.partial(cut_kernel, count, share),
        out_shape=outs,
        cost_estimate=cost(0, 4 * 2**20),
        name="cut_rows",
    )(rows)


def local(tokens, first_length, cotangent, positions, inward, intake, outward, outlet, steady, offset,
          expand, spread, contract, settle, temper, anchor):
    micro_count, pack_count, block_rows, width = tokens.shape
    assert pack_count == 1
    devices, count = lax.axis_size(AXES), lax.axis_size("seq")
    me, rank = lax.axis_index(AXES), lax.axis_index("seq")
    share = max(count // micro_count, 1)
    assert share * micro_count == count
    plan = Plan(devices, width, contract.shape[0] * devices, block_rows * count)
    micro = rank // share
    counted = (rank % share == 0).astype(jnp.int32)

    def info_of(lengths):
        first = jnp.sum(jnp.where(jnp.arange(micro_count) == micro, lengths[:, 0], 0))
        return jnp.stack([first, me, rank, counted]).astype(jnp.int32)

    vectors = (intake, outlet, steady, offset, spread, settle, temper, anchor)

    def swap(value, mask):
        return lax.ppermute(value, AXES, [(d, d ^ mask) for d in range(devices)]) if mask else value

    def exchange(pieces):
        return [swap(piece, mask) for mask, piece in enumerate(pieces)]

    def in_order(pieces):
        if count != 4 or share != 1:
            return settle_rows(info, micro_count, share, pieces)
        return ordered(rank, pieces)

    if plan.packed:
        rows_in, shard, late = pack(
            plan, count, share, tokens[:, 0], positions.T, inward, vectors, outward, expand, contract
        )
        rows_in = exchange(rows_in)
        shard, rows_in[1] = lax.optimization_barrier((shard, rows_in[1]))
        pieces = [swap(shard, mask) for mask in plan.z_order]
        pieces, rows_in, late, cotangent, first_length = lax.optimization_barrier(
            (pieces, rows_in, late, cotangent, first_length)
        )
        info = info_of(first_length)
        shard = jnp.concatenate(pieces, axis=0)
        pieces = [swap(shard, k << 1) for k in range(4)]
        late = [swap(late, mask) for mask in plan.z_order]
        upstreams = cut_rows(cotangent[:, 0], count, share)
        pieces, upstreams, late, info = lax.optimization_barrier((pieces, list(upstreams), late, info))
        late = jnp.concatenate(late, axis=0)
        late_x, late_y = swap(late, 2), swap(late, 4)
        shard = jnp.concatenate(pieces, axis=0)
        early = [shard, swap(shard, 1)]
        upstreams[1] = swap(upstreams[1], 1)
        late_core = swap(late, 1)
        early, late_core, late_x, late_y, upstreams = lax.optimization_barrier(
            (early, late_core, late_x, late_y, upstreams)
        )
        late_xy = swap(late_x, 4)
        upstreams[2:] = [swap(upstreams[mask], mask) for mask in (2, 3)]
        late_cores = [late_core, swap(late_x, 1), swap(late_y, 1)]
    else:
        info = info_of(first_length)
        rows_in = exchange(cut_rows(tokens[:, 0], count, share))
        upstreams = exchange(cut_rows(cotangent[:, 0], count, share))
        early, late = plain_weights(plan, positions, inward, vectors, outward, expand, contract)
    lifted, query, key, value, mixed, totals, inward_all, small = attend(plan, info, count, rows_in, early)
    if plan.packed:
        late_xy, late_cores, upstreams, mixed = lax.optimization_barrier(
            (late_xy, late_cores, upstreams, mixed)
        )
        late = [late, late_x, late_y, late_xy] + late_cores + [swap(late_xy, 1)]
    results, (mixed_back, first_back, small_grad), late_grads = feed(
        plan, info, count, lifted, mixed, upstreams, late, small
    )
    results = exchange(results)
    if plan.packed:
        stay_keep, go_keep, stay_send, go_send = late_grads
        cut = 8 * plan.late_cut
        go = [go_keep, swap(go_send, 1)]
        one_send, two_send = fold([v[:cut] for v in go], 1) + fold([v[cut:] for v in go], 1)
        stay_other = swap(stay_send, 1)
        one_send, two_send, mixed_back = lax.optimization_barrier((one_send, two_send, mixed_back))
        one_other, two_other = swap(one_send, 4), swap(two_send, 2)
    token_pieces, early_grads = attend_back(
        plan, info, count, lifted, (query, key, value, mixed, totals), mixed_back, inward_all,
        first_back, small_grad,
    )
    if plan.packed:
        one_other, two_other, stay_other, results, token_pieces, early_grads = lax.optimization_barrier(
            (one_other, two_other, stay_other, results, token_pieces, early_grads)
        )
        keep, send = early_grads
        send = swap(send, 1)
        one, one_send = fold([stay_keep[:cut], stay_other[:cut], one_other], 2)
        two, two_send = fold([stay_keep[cut:], stay_other[cut:], two_other], 2)
        one, one_send, two, two_send, keep = lax.optimization_barrier((one, one_send, two, two_send, keep))
        one_other, two_other = swap(one_send, 2), swap(two_send, 4)
        terms = fold([keep, send], 4)
        terms, results, token_pieces = lax.optimization_barrier((terms, results, token_pieces))
        terms = [swap(term, k << 1) for k, term in enumerate(terms)]
        output = settle_rows(info, micro_count, share, results)
        one_other, two_other, output = lax.optimization_barrier((one_other, two_other, output))
        ones, twos = fold([one, one_other], 4), fold([two, two_other], 4)
        late_terms = [jnp.concatenate(pair, axis=0) for pair in zip(ones, twos)]
        late_terms = [swap(term, mask) for term, mask in zip(late_terms, plan.z_order)]
        token_pieces = list(token_pieces)
        token_pieces[1] = swap(token_pieces[1], 1)
        terms, late_terms, output, token_pieces = lax.optimization_barrier(
            (terms, late_terms, output, token_pieces)
        )
        terms = fold(terms, 4)
        early_terms = [swap(term, mask) for term, mask in zip(terms, plan.z_order)]
        token_pieces[2:] = [swap(token_pieces[mask], mask) for mask in (2, 3)]
        early_terms, token_pieces = lax.optimization_barrier((early_terms, token_pieces))
        tokens_back = in_order(token_pieces)
        values = finish(plan, info, early_terms, late_terms)
        table_t, inward_own, outward_own, expand_own, contract_own = values[:5]
        own = [v.reshape(-1) for v in values[5:]]
        table_own = table_t.T
    else:
        output = in_order(results)
        tokens_back = in_order(exchange(token_pieces))
        table_own, inward_own, outward_own, expand_own, contract_own, own = plain_grads(
            plan, counted, early_grads, late_grads
        )
    return (output[:, None], tokens_back[:, None], table_own, inward_own, own[0], outward_own, own[1], own[2],
            own[3], expand_own, own[4], contract_own, own[5], own[6], own[7])


def plain_weights(plan, positions, inward, vectors, outward, expand, contract):
    lanes, width = plan.lanes, plan.width

    def gather(value, axis=0):
        return lax.all_gather(value, AXES, axis=axis, tiled=True)

    def in_pieces(value, size):
        return value.reshape(value.shape[0], -1, size).transpose(1, 0, 2)

    table = in_pieces(gather(positions, 1).T, LANE)
    small = jnp.concatenate([gather(v) for v in vectors]).astype(F32).reshape(-1, width)
    small = jnp.pad(small, ((0, plan.small_rows - small.shape[0]), (0, 0)))
    early = [table, in_pieces(gather(inward), LANE), small]
    return early, [gather(outward), in_pieces(gather(expand), width), gather(contract)]


def plain_grads(plan, counted, early_grads, late_grads):
    width = plan.width
    table, inward, small = early_grads
    outward, expand, contract = (jnp.where(counted > 0, g, BF(0)) for g in late_grads)

    def scatter(value, axis=0):
        return lax.psum_scatter(value, AXES, scatter_dimension=axis, tiled=True).astype(F32)

    def whole(value):
        return value.transpose(1, 0, 2).reshape(value.shape[1], -1)

    flat = small.reshape(-1)
    own = []
    for vector, length in enumerate(plan.lengths):
        start = plan.block_starts[vector] * LANE
        own.append(scatter(flat[start : start + length]))
    return (scatter(table.T, 1), scatter(whole(inward)), scatter(outward), scatter(whole(expand)),
            scatter(contract), own)


def solution(mesh):
    rows = P(None, "batch", "seq", None)
    table = P(None, AXES)
    matrix = P(AXES, None)
    vector = P(AXES)
    weights = (table, matrix, vector, matrix, vector, vector, vector, matrix, vector, matrix, vector,
               vector, vector)
    return jax.shard_map(
        local,
        mesh=mesh,
        in_specs=(rows, P(None, "batch"), rows) + weights,
        out_specs=(rows, rows) + weights,
        check_vma=False,
    )
```

```python
import functools

import jax
import jax.numpy as jnp
from jax import lax
from jax.experimental import pallas as pl
from jax.experimental.pallas import tpu as pltpu
from jax.sharding import PartitionSpec as P

AXES = ("batch", "seq")
LANE = 128
TILE = 16
FEED_ROWS = 512
STEP = 256
FAR = 1e30
BEND = 0.7978845608028654
BF = jnp.bfloat16
F32 = jnp.float32
VECTORS = 8


def times(left, right):
    return jnp.dot(left, right, preferred_element_type=F32)


def times_t(left, right):
    return lax.dot_general(left, right, (((1,), (1,)), ((), ())), preferred_element_type=F32)


def t_times(left, right):
    return lax.dot_general(left, right, (((0,), (0,)), ((), ())), preferred_element_type=F32)


def column_sum(values):
    return jnp.sum(values.astype(F32), axis=0, keepdims=True)


def aligned(index, size):
    return pl.ds(pl.multiple_of(index * size, size), size)


def like(shape, kind):
    return jax.ShapeDtypeStruct(shape, kind)


def full(shape):
    return pl.BlockSpec(shape, lambda *_: (0,) * len(shape), pipeline_mode=pl.Buffered(1))


HELD = pl.BlockSpec(memory_space=pltpu.VMEM)


def hold(values):
    return [pltpu.with_memory_space_constraint(v, pltpu.VMEM) for v in values]


def stay(values):
    return [pltpu.with_memory_space_constraint(v, pltpu.HBM) for v in values]


def params(megabytes):
    return pltpu.CompilerParams(vmem_limit_bytes=megabytes * 2**20)


def cost(flops, size, exps=0):
    return pl.CostEstimate(flops=flops, bytes_accessed=size, transcendentals=exps)


class Plan:
    def __init__(self, devices, width, hidden, total_rows):
        self.devices = devices
        self.width = width
        self.hidden = hidden
        self.total_rows = total_rows
        self.own_rows = width // devices
        self.packed = devices == 32 and self.own_rows % TILE == 0
        self.lanes = width // LANE
        self.parts = hidden // width
        self.table_pieces = total_rows // LANE
        self.early_pieces = self.table_pieces + 3 * self.lanes
        self.early_rows = (self.early_pieces + 1) * TILE
        self.late_rows = (self.lanes + hidden // LANE) * TILE + self.lanes * (hidden // devices)
        self.late_cut = (self.lanes + hidden // LANE) * TILE + hidden // devices
        lengths = [2 * width, width, width, width, hidden, width, width, width]
        self.lengths = lengths
        self.owned = [n // devices for n in lengths]
        self.small_rows = 16
        self.z_order = (0, 24, 8, 16)
        starts = [0]
        for n in lengths:
            starts.append(starts[-1] + n // LANE)
        self.block_starts = starts

    def place(self, mask):
        return ((mask >> 1) & 3) * 4 + self.z_order.index(mask & 24)

    def grad_piece(self, half, mask, at, rows):
        first = at < self.late_cut
        assert not first or at + rows <= self.late_cut
        swapped = mask if first else (mask & ~6) | ((mask >> 1) & 2) | ((mask & 2) << 1)
        place = self.place(swapped)
        last_rows = self.late_rows - self.late_cut
        if first:
            start = (place % 8) * self.late_cut + at
        else:
            start = 8 * self.late_cut + (place % 8) * last_rows + at - self.late_cut
        return half[place // 8].at[start : start + rows, :]


def fill_early(plan, me, halves, table_ref, inward_ref, small_ref, stage_ref):
    for mask in range(plan.devices):
        shard = halves[mask & 1].at[plan.place(mask)]
        owner = me ^ mask
        rows = aligned(owner, TILE)
        for piece in range(plan.table_pieces):
            table_ref[piece, rows, :] = shard[piece * TILE : (piece + 1) * TILE, :]
        for piece in range(3 * plan.lanes):
            at = plan.table_pieces + piece
            inward_ref[piece, rows, :] = shard[at * TILE : (at + 1) * TILE, :]
        at = plan.early_pieces * TILE
        stage_ref[pl.ds(owner, 1), :, :] = shard[at : at + TILE, :].astype(F32)[None]
    lane = lax.broadcasted_iota(jnp.int32, (1, LANE), 1)
    for vector, length in enumerate(plan.lengths):
        size = plan.owned[vector]
        group = LANE // size
        for block in range(length // LANE):
            row = jnp.zeros((1, LANE), F32)
            for index in range(group):
                own = stage_ref[block * group + index, vector : vector + 1, :]
                row = jnp.where(lane // size == index, own, row)
            at = plan.block_starts[vector] + block
            small_ref[at // plan.lanes : at // plan.lanes + 1, (at % plan.lanes) * LANE : (at % plan.lanes + 1) * LANE] = row


def own_lanes(value, head):
    lane = lax.broadcasted_iota(jnp.int32, value.shape, 1)
    return jnp.where((lane // (LANE // 2)) == head, value, jnp.zeros_like(value))


def causal():
    return lax.broadcasted_iota(jnp.int32, (STEP, STEP), 0) <= lax.broadcasted_iota(
        jnp.int32, (STEP, STEP), 1
    )


def attend_kernel(plan, count, info_ref, *refs):
    pieces, refs = refs[:count], refs[count:]
    if plan.packed:
        halves, refs = refs[:2], refs[2:]
    else:
        table_in, inward_in, small_in = refs[:3]
        refs = refs[3:]
    (lifted_ref, query_ref, key_ref, value_ref, mixed_ref, total_ref, inward_ref, small_ref) = refs[:8]
    low_ref, table_ref, place_ref, stage_ref = refs[8:]
    pair = pl.program_id(0)
    total_rows, width = plan.total_rows, plan.width
    half = total_rows // 2
    split = info_ref[0] < total_rows
    far = jnp.where(split, FAR, 0.0)

    @pl.when(pair == 0)
    def _():
        if plan.packed:
            fill_early(plan, info_ref[1], halves, table_ref, inward_ref, small_ref, stage_ref)
        else:
            table_ref[...] = table_in[...]
            inward_ref[...] = inward_in[...]
            small_ref[...] = small_in[...]
        eye = (
            lax.broadcasted_iota(jnp.int32, (half, half), 0)
            == lax.broadcasted_iota(jnp.int32, (half, half), 1)
        ).astype(BF)
        per_half = half // LANE
        for part in range(2):
            table = jnp.concatenate(
                [table_ref[part * per_half + i] for i in range(per_half)], axis=1
            )
            place_ref[part * half : (part + 1) * half, :] = times_t(eye, table)
        rows = total_rows // count
        for mask in range(count):
            start = (info_ref[2] ^ mask) * rows
            place = start - jnp.where(jnp.logical_and(split, start >= half), half, 0)
            lifted = pieces[mask][...].astype(F32) + place_ref[pl.ds(pl.multiple_of(place, rows), rows), :]
            spot = pl.ds(pl.multiple_of(start, rows), rows)
            lifted_ref[spot, :] = lifted
            low_ref[spot, :] = lifted.astype(BF)

    weights = jnp.concatenate([inward_ref[pair + i * plan.lanes] for i in range(3)], axis=1)
    lanes = aligned(pair, LANE)
    query_bias = small_ref[0:1, lanes]
    value_bias = small_ref[1:2, lanes]
    for block in range(total_rows // STEP):
        spot = slice(block * STEP, (block + 1) * STEP)
        joint = times(low_ref[spot, :], weights)
        query_ref[spot, :] = (joint[:, :LANE] + query_bias).astype(BF) * BF(0.125)
        key_ref[spot, :] = joint[:, LANE : 2 * LANE].astype(BF)
        value_ref[spot, :] = (joint[:, 2 * LANE :] + value_bias).astype(BF)

    keep = causal()
    lower = lax.broadcasted_iota(jnp.int32, (LANE, STEP), 0) < LANE // 2

    value_t = value_ref[...].T

    def logits_of(block, head):
        start = block * STEP
        other = half if start >= half else 0
        mine = own_lanes(query_ref[start : start + STEP, :], head)
        near = times_t(key_ref[start : start + STEP, :], mine)
        same = times_t(key_ref[other:start, :], mine) if start > other else None
        away = times_t(key_ref[:other, :], mine) if other else None
        return near, same, away

    def mixed_of(block, head, near, same, away):
        start = block * STEP
        other = half if start >= half else 0
        near = jnp.where(keep, near, -FAR)
        peak = jnp.max(near, axis=0, keepdims=True)
        if same is not None:
            peak = jnp.maximum(peak, jnp.max(same, axis=0, keepdims=True))
        if away is not None:
            peak = jnp.maximum(peak, jnp.max(away, axis=0, keepdims=True) - far)
        raised = [jnp.exp(piece - peak) for piece in (same, near) if piece is not None]
        total = sum(jnp.sum(piece, axis=0, keepdims=True) for piece in raised)
        low = jnp.concatenate([piece.astype(BF) for piece in raised], axis=0)
        mixed = times(value_t[:, other : start + STEP], low)
        if away is not None:
            away = jnp.exp(away - (peak + far))
            total = total + jnp.sum(away, axis=0, keepdims=True)
            mixed = mixed + times(value_t[:, :other], away.astype(BF))
        total_ref[0, head : head + 1, start : start + STEP] = peak + jnp.log(total)
        return mixed * (1.0 / total)

    tasks = [(block, head) for block in range(total_rows // STEP) for head in range(2)]
    ahead = logits_of(*tasks[0])
    parts = []
    for index, (block, head) in enumerate(tasks):
        logits, ahead = ahead, logits_of(*tasks[index + 1]) if index + 1 < len(tasks) else None
        parts.append(mixed_of(block, head, *logits))
        if head:
            mixed_ref[block * STEP : (block + 1) * STEP, :] = jnp.where(lower, *parts).T.astype(BF)
            parts = []


def attend(plan, info, count, pieces, weights):
    total_rows, width = plan.total_rows, plan.width
    block = pl.BlockSpec((total_rows, LANE), lambda p, *_: (0, p))
    low = pltpu.HBM((total_rows, width), BF)
    inward = (3 * plan.lanes, width, LANE)
    small = (plan.small_rows, width)
    return pl.pallas_call(
        functools.partial(attend_kernel, plan, count),
        grid_spec=pltpu.PrefetchScalarGridSpec(
            num_scalar_prefetch=1,
            grid=(plan.lanes,),
            in_specs=[HELD for v in pieces + weights],
            out_specs=[
                full((total_rows, width)),
                block,
                block,
                block,
                block,
                pl.BlockSpec((1, 8, total_rows), lambda p, *_: (p, 0, 0)),
                full(inward),
                full(small),
            ],
            scratch_shapes=[
                pltpu.VMEM((total_rows, width), BF),
                pltpu.VMEM((plan.table_pieces, width, LANE), BF),
                pltpu.VMEM((total_rows, width), F32),
                pltpu.VMEM((plan.devices, TILE, LANE), F32),
            ],
        ),
        out_shape=[
            pltpu.HBM((total_rows, width), F32),
            low,
            low,
            low,
            low,
            pltpu.HBM((plan.lanes, 8, total_rows), F32),
            pltpu.HBM(inward, BF),
            pltpu.HBM(small, F32),
        ],
        compiler_params=params(36),
        cost_estimate=cost(5 * 10**9, 14 * 2**20, 6 * 10**6),
        name="attend",
    )(info, *hold(pieces), *hold(weights))


def norm(rows):
    center = rows - jnp.mean(rows, axis=1, keepdims=True)
    root = lax.rsqrt(jnp.mean(center * center, axis=1, keepdims=True) + 1e-05)
    return center * root, root


def norm_back(upstream, gain, unit, root):
    scaled = upstream * gain
    mean = jnp.mean(scaled, axis=1, keepdims=True)
    slope = jnp.mean(scaled * unit, axis=1, keepdims=True)
    return (scaled - mean - unit * slope) * root


def feed_kernel(plan, count, info_ref, lifted_ref, mixed_ref, *refs):
    upstreams, refs = refs[:count], refs[count:]
    if plan.packed:
        late_quarters, small_ref = refs[:8], refs[8]
        refs = refs[9:]
    else:
        outward_in, expand_in, contract_in, small_ref = refs[:4]
        refs = refs[4:]
    results, refs = refs[:count], refs[count:]
    mixed_back_ref, first_back_ref, small_grad_ref = refs[:3]
    refs = refs[3:]
    if plan.packed:
        halves, refs = (refs[:2], refs[2:4]), refs[4:]
    else:
        outward_out, expand_out, contract_out = refs[:3]
        refs = refs[3:]
    (outward_ref, expand_ref, contract_ref, upstream_ref, result_ref, slope_ref, active_all, hidden_all, normed_all,
     lowered_all, branch_all, mixed_all, whole_ref, expand_sum, contract_sum) = refs
    step = pl.program_id(0)
    width, parts, lanes = plan.width, plan.parts, plan.lanes
    contract_own = plan.hidden // plan.devices
    contract_at = (lanes + parts * lanes) * TILE

    @pl.when(step == 0)
    def _():
        if plan.packed:
            for mask in range(plan.devices):
                at = plan.place(mask)
                shard = late_quarters[(mask & 1) * 4 + at // 4].at[at % 4]
                owner = info_ref[1] ^ mask
                rows, wide = aligned(owner, TILE), aligned(owner, contract_own)
                for lane in range(lanes):
                    cut = slice(lane * LANE, (lane + 1) * LANE)
                    outward_ref[rows, cut] = shard[lane * TILE : (lane + 1) * TILE, :]
                    for part in range(parts):
                        at = (lanes + part * lanes + lane) * TILE
                        expand_ref[part, rows, cut] = shard[at : at + TILE, :]
                    at = contract_at + lane * contract_own
                    contract_ref[wide, cut] = shard[at : at + contract_own, :]
        else:
            outward_ref[...] = outward_in[...]
            expand_ref[...] = expand_in[...]
            contract_ref[...] = contract_in[...]

    size = lifted_ref.shape[0]
    here = pl.ds(pl.multiple_of(step * size, size), size)
    rows = plan.total_rows // count
    group = size // rows

    def spot(mask):
        return pl.ds(pl.multiple_of(((info_ref[2] ^ mask) % group) * rows, rows), rows)

    for mask in range(count):
        @pl.when(step == mask // group)
        def _(mask=mask):
            upstream_ref[spot(mask), :] = upstreams[mask][...]

    outlet, steady, offset = (small_ref[i : i + 1, :] for i in (2, 3, 4))
    settle, temper, anchor = (small_ref[i + parts : i + parts + 1, :] for i in (5, 6, 7))
    mixed = mixed_ref[...]
    branch = times(mixed, outward_ref[...]) + outlet
    unit, root = norm(lifted_ref[...] + branch)
    normed = unit * steady + offset
    normed_low = normed.astype(BF)
    normed_all[here, :] = normed_low
    mixed_all[here, :] = mixed
    lowered = jnp.zeros_like(normed)
    for part in range(parts):
        cut = slice(part * width, (part + 1) * width)
        hidden = times(normed_low, expand_ref[part]) + small_ref[5 + part : 6 + part, :]
        square = hidden * hidden
        bend = jnp.tanh(hidden * (BEND + BEND * 0.044715 * square))
        half = 0.5 + 0.5 * bend
        active = (hidden * half).astype(BF)
        active_all[here, cut] = active
        slope_ref[:, cut] = half + (0.5 * hidden) * (1.0 - bend * bend) * (
            BEND + 3 * BEND * 0.044715 * square
        )
        lowered = lowered + times(active, contract_ref[cut, :])
    last_unit, last_root = norm(normed + (lowered + settle))
    result_ref[...] = (last_unit * temper + anchor).astype(BF)
    upstream = upstream_ref[...].astype(F32)
    temper_grad = column_sum(upstream * last_unit)
    anchor_grad = column_sum(upstream)
    second_back = norm_back(upstream, temper, last_unit, last_root)
    lowered_back = second_back.astype(BF)
    lowered_all[here, :] = lowered_back
    settle_grad = column_sum(lowered_back)
    normed_back = second_back
    spread_grads = []
    for part in range(parts):
        cut = slice(part * width, (part + 1) * width)
        active_back = times_t(lowered_back, contract_ref[cut, :])
        hidden_back = (active_back * slope_ref[:, cut]).astype(BF)
        spread_grads.append(column_sum(hidden_back))
        hidden_all[here, cut] = hidden_back
        normed_back = normed_back + times_t(hidden_back, expand_ref[part])
    first_back = norm_back(normed_back, steady, unit, root)
    first_back_ref[...] = first_back
    branch_back = first_back.astype(BF)
    mixed_back_ref[...] = times_t(branch_back, outward_ref[...]).astype(BF)
    branch_all[here, :] = branch_back
    zero = jnp.zeros_like(anchor_grad)
    grads = [zero, zero, column_sum(branch_back), column_sum(normed_back * unit)]
    grads += [column_sum(normed_back)] + spread_grads + [settle_grad, temper_grad, anchor_grad]
    grads += [zero] * (plan.small_rows - len(grads))
    small_term = jnp.concatenate(grads, axis=0)
    for mask in range(count):
        @pl.when(step == mask // group)
        def _(mask=mask):
            results[mask][...] = result_ref[spot(mask), :]

    @pl.when(step == 0)
    def _():
        small_grad_ref[...] = small_term

    @pl.when(step > 0)
    def _():
        small_grad_ref[...] += small_term

    @pl.when(step == pl.num_programs(0) - 1)
    def _():
        outward = t_times(mixed_all[...], branch_all[...])
        if plan.packed:
            me = info_ref[1]
            whole_ref[...] = outward
            for mask in range(plan.devices):
                half = halves[mask & 1]
                rows = aligned(me ^ mask, TILE)
                for lane in range(lanes):
                    cut = slice(lane * LANE, (lane + 1) * LANE)
                    plan.grad_piece(half, mask, lane * TILE, TILE)[...] = whole_ref[rows, cut].astype(BF)
        else:
            outward_out[...] = outward.astype(BF)
        per_part = plan.devices // parts
        for part in range(parts):
            cut = slice(part * width, (part + 1) * width)
            expand = t_times(normed_all[...], hidden_all[:, cut])
            if not plan.packed:
                expand_out[part] = expand.astype(BF)
                continue
            expand_sum[...] = expand
            for mask in range(plan.devices):
                rows = aligned(me ^ mask, TILE)
                for lane in range(lanes):
                    at = (lanes + part * lanes + lane) * TILE
                    plan.grad_piece(halves[mask & 1], mask, at, TILE)[...] = expand_sum[
                        rows, lane * LANE : (lane + 1) * LANE
                    ].astype(BF)
        for mask_part in range(parts):
            part = (me // per_part) ^ mask_part if plan.packed else mask_part
            cut = pl.ds(pl.multiple_of(part * width, width), width)
            contract = t_times(active_all[:, cut], lowered_all[...])
            if not plan.packed:
                contract_out[cut, :] = contract.astype(BF)
                continue
            contract_sum[...] = contract
            for index in range(per_part):
                mask = mask_part * per_part + index
                rows = aligned((me ^ mask) % per_part, contract_own)
                for lane in range(lanes):
                    at = contract_at + lane * contract_own
                    plan.grad_piece(halves[mask & 1], mask, at, contract_own)[...] = contract_sum[
                        rows, lane * LANE : (lane + 1) * LANE
                    ].astype(BF)


def feed(plan, info, count, lifted, mixed, upstreams, weights, small):
    total_rows, width, parts = plan.total_rows, plan.width, plan.parts
    piece = total_rows // count
    size = max(piece, FEED_ROWS)
    group = size // piece
    rows = pl.BlockSpec((size, width), lambda i, info: ((info[2] // group) ^ i, 0))
    outward, expand, contract = (width, width), (parts, width, width), (parts * width, width)
    if plan.packed:
        grads = [pltpu.VMEM((8 * plan.late_rows, LANE), BF)] * 4
    else:
        grads = [pltpu.VMEM(outward, BF), pltpu.VMEM(expand, BF), pltpu.VMEM(contract, BF)]
    ends = [pltpu.VMEM((piece, width), BF)] * count
    outs = [like((total_rows, width), BF), like((total_rows, width), F32), like(small.shape, F32)]
    values = pl.pallas_call(
        functools.partial(feed_kernel, plan, count),
        grid_spec=pltpu.PrefetchScalarGridSpec(
            num_scalar_prefetch=1,
            grid=(total_rows // size,),
            in_specs=[rows, rows]
            + [HELD for v in upstreams + weights]
            + [full(small.shape)],
            out_specs=[HELD for v in ends]
            + [rows, rows, full(small.shape)]
            + [HELD for v in grads],
            scratch_shapes=[
                pltpu.VMEM(outward, BF),
                pltpu.VMEM(expand, BF),
                pltpu.VMEM(contract, BF),
                pltpu.VMEM((size, width), BF),
                pltpu.VMEM((size, width), BF),
                pltpu.VMEM((size, parts * width), F32),
                pltpu.VMEM((total_rows, parts * width), BF),
                pltpu.VMEM((total_rows, parts * width), BF),
                pltpu.VMEM((total_rows, width), BF),
                pltpu.VMEM((total_rows, width), BF),
                pltpu.VMEM((total_rows, width), BF),
                pltpu.VMEM((total_rows, width), BF),
                pltpu.VMEM(outward, F32),
                pltpu.VMEM(outward, F32),
                pltpu.VMEM(outward, F32),
            ],
        ),
        out_shape=ends + outs + grads,
        compiler_params=params(50),
        cost_estimate=cost(15 * 10**9, 20 * 2**20, 2 * 10**6),
        name="feed",
    )(info, lifted, mixed, *hold(upstreams), *hold(weights), small)
    return values[:count], values[count : count + 3], values[count + 3 :]


def attend_back_kernel(
    plan, count, info_ref, lifted_ref, query_ref, key_ref, value_ref, mixed_ref, mixed_back_ref,
    total_ref, inward_ref, first_back_ref, small_grad_ref, *refs
):
    tokens, refs = refs[:count], refs[count:]
    if plan.packed:
        halves, refs = refs[:2], refs[2:]
    else:
        table_out, inward_out, small_out = refs[:3]
        refs = refs[3:]
    (joint_ref, sum_ref, share_ref, score_ref, grad_ref, table_ref, joint_sums, blocks_ref,
     lifted_here, inward_here, copied) = refs
    pair = pl.program_id(0)
    copies = [
        pltpu.make_async_copy(source, target, copied.at[index])
        for index, (source, target) in enumerate(
            ((lifted_ref, lifted_here), (inward_ref, inward_here), (first_back_ref, sum_ref))
        )
    ]

    @pl.when(pair == 0)
    def _():
        for copy in copies:
            copy.start()

    total_rows, lanes = plan.total_rows, plan.lanes
    half = total_rows // 2
    split = info_ref[0] < total_rows
    far = jnp.where(split, FAR, 0.0)
    blocks = total_rows // STEP

    keep = causal()
    lower = lax.broadcasted_iota(jnp.int32, (STEP, LANE), 1) < LANE // 2
    lower_t = lax.broadcasted_iota(jnp.int32, (LANE, STEP), 0) < LANE // 2
    product = (mixed_ref[...].astype(F32) * mixed_back_ref[...].astype(F32)).T
    scaled_key = (key_ref[...] * BF(0.125)).T
    betweens = [
        jnp.sum(product[head * LANE // 2 : (head + 1) * LANE // 2], axis=0, keepdims=True)
        for head in range(2)
    ]

    def logits_of(block, head):
        spot = slice(block * STEP, (block + 1) * STEP)
        keys = slice(0, (block + 1) * STEP)
        query = own_lanes(query_ref[spot, :], head)
        back = own_lanes(mixed_back_ref[spot, :], head)
        return times_t(key_ref[keys, :], query), times_t(value_ref[keys, :], back)

    def scores_of(block, head, logits, share_back):
        start = block * STEP
        spot = slice(start, start + STEP)
        total = total_ref[0, head : head + 1, spot]
        gap = betweens[head][:, spot]
        for under in range(block + 1):
            keys = slice(under * STEP, (under + 1) * STEP)
            away = start >= half and under * STEP < half
            share = jnp.exp(logits[keys] - (total + far if away else total))
            if under == block:
                share = jnp.where(keep, share, 0.0)
            score = share * (share_back[keys] - gap)
            share_ref[head, keys, spot] = share.astype(BF)
            score_ref[head, keys, spot] = score.astype(BF)

    def backs_of(block, head):
        start = block * STEP
        spot = slice(start, start + STEP)
        end = start + STEP
        query_back = times(scaled_key[:, :end], score_ref[head, :end, spot])
        key_back = times(score_ref[head, spot, start:], query_ref[start:, :])
        value_back = times(share_ref[head, spot, start:], mixed_back_ref[start:, :])
        return query_back, key_back, value_back

    tasks = [(block, head) for block in reversed(range(blocks)) for head in range(2)]
    ahead = logits_of(*tasks[0])
    parts = []
    for index, (block, head) in enumerate(tasks):
        logits, ahead = ahead, logits_of(*tasks[index + 1]) if index + 1 < len(tasks) else None
        scores_of(block, head, *logits)
        parts.append(backs_of(block, head))
        if head:
            spot = slice(block * STEP, (block + 1) * STEP)
            query_back = jnp.where(lower_t, parts[0][0], parts[1][0]).T
            key_back = jnp.where(lower, parts[0][1], parts[1][1])
            value_back = jnp.where(lower, parts[0][2], parts[1][2])
            for part, back in enumerate((query_back, key_back, value_back)):
                joint_ref[spot, aligned(pair + part * lanes, LANE)] = back.astype(BF)
            parts = []

    @pl.when(pair == lanes - 1)
    def _():
        for copy in copies:
            copy.wait()
        low = lifted_here[...].astype(BF).T
        weights = jnp.concatenate([inward_here[i] for i in range(3 * lanes)], axis=1)
        for block in range(blocks):
            spot = slice(block * STEP, (block + 1) * STEP)
            sum_ref[spot, :] += times_t(joint_ref[spot, :], weights)
        for part in range(3):
            joint = joint_ref[:, part * plan.width : (part + 1) * plan.width]
            grads = times(low, joint)
            for lane in range(lanes):
                grad_ref[part * lanes + lane] = grads[:, lane * LANE : (lane + 1) * LANE]
            if part != 1:
                sums = column_sum(joint)
                for lane in range(lanes):
                    at = lane if part == 0 else lane + lanes
                    joint_sums[at : at + 1, :] = sums[:, lane * LANE : (lane + 1) * LANE]
        rows = total_rows // count
        for mask in range(count):
            spot = pl.ds(pl.multiple_of((info_ref[2] ^ mask) * rows, rows), rows)
            tokens[mask][...] = sum_ref[spot, :].astype(BF)
        late = sum_ref[half:, :]
        early = sum_ref[:half, :] + jnp.where(split, late, 0.0)
        table_ref[:, :half] = early.T
        table_ref[:, half:] = jnp.where(split, 0.0, late).T
        counted = info_ref[3] > 0
        blocks_ref[: 2 * lanes, :] = joint_sums[: 2 * lanes, :]
        for row in range(2, plan.block_starts[-1] // lanes):
            for lane in range(lanes):
                blocks_ref[row * lanes + lane : row * lanes + lane + 1, :] = small_grad_ref[
                    row : row + 1, lane * LANE : (lane + 1) * LANE
                ]
        if plan.packed:
            for mask in range(plan.devices):
                shard = halves[mask & 1].at[plan.place(mask)]
                owner = info_ref[1] ^ mask
                own = aligned(owner, TILE)
                for piece in range(plan.table_pieces):
                    shard[piece * TILE : (piece + 1) * TILE, :] = table_ref[
                        own, piece * LANE : (piece + 1) * LANE
                    ].astype(BF)
                for piece in range(3 * lanes):
                    at = (plan.table_pieces + piece) * TILE
                    shard[at : at + TILE, :] = grad_ref[piece, own, :].astype(BF)
                rows = [
                    blocks_ref[pl.ds(plan.block_starts[v] + owner * plan.owned[v] // LANE, 1), :]
                    for v in range(VECTORS)
                ]
                rows.append(jnp.zeros((TILE - VECTORS, LANE), F32))
                at = plan.early_pieces * TILE
                shard[at : at + TILE, :] = jnp.concatenate(rows, axis=0).astype(BF)
        else:
            table_out[...] = jnp.where(counted, table_ref[...], 0.0).astype(BF)
            inward_out[...] = jnp.where(counted, grad_ref[...], 0.0).astype(BF)
            small_out[...] = jnp.where(counted, blocks_ref[...], 0.0)


def attend_back(plan, info, count, lifted, saved, mixed_back, inward, first_back, small_grad):
    query, key, value, mixed, totals = saved
    total_rows, width, lanes = plan.total_rows, plan.width, plan.lanes
    block = pl.BlockSpec((total_rows, LANE), lambda p, *_: (0, p))
    blocks = (plan.block_starts[-1], LANE)
    if plan.packed:
        grads = [pltpu.VMEM((plan.devices // 2, plan.early_rows, LANE), BF)] * 2
    else:
        grads = [pltpu.VMEM((width, total_rows), BF), pltpu.VMEM(inward.shape, BF), pltpu.VMEM(blocks, F32)]
    tokens = [pltpu.VMEM((total_rows // count, width), BF)] * count
    values = pl.pallas_call(
        functools.partial(attend_back_kernel, plan, count),
        grid_spec=pltpu.PrefetchScalarGridSpec(
            num_scalar_prefetch=1,
            grid=(lanes,),
            in_specs=[
                pl.BlockSpec(memory_space=pl.ANY),
                block,
                block,
                block,
                block,
                block,
                pl.BlockSpec((1, 8, total_rows), lambda p, *_: (p, 0, 0)),
                pl.BlockSpec(memory_space=pl.ANY),
                pl.BlockSpec(memory_space=pl.ANY),
                full(small_grad.shape),
            ],
            out_specs=[HELD for v in tokens + grads],
            scratch_shapes=[
                pltpu.VMEM((total_rows, 3 * width), BF),
                pltpu.VMEM((total_rows, width), F32),
                pltpu.VMEM((2, total_rows, total_rows), BF),
                pltpu.VMEM((2, total_rows, total_rows), BF),
                pltpu.VMEM(inward.shape, F32),
                pltpu.VMEM((width, total_rows), F32),
                pltpu.VMEM((8, LANE), F32),
                pltpu.VMEM(blocks, F32),
                pltpu.VMEM(lifted.shape, F32),
                pltpu.VMEM(inward.shape, BF),
                pltpu.SemaphoreType.DMA((3,)),
            ],
        ),
        out_shape=tokens + grads,
        compiler_params=params(40),
        cost_estimate=cost(14 * 10**9, 24 * 2**20, 6 * 10**6),
        name="attend_back",
    )(info, *stay([lifted, query, key, value, mixed, mixed_back, totals, inward, first_back]), small_grad)
    return values[:count], values[count:]


def pack_kernel(plan, count, share, rows_ref, table_ref, inward_ref, *refs):
    vectors, refs = refs[:VECTORS], refs[VECTORS:]
    outward_ref, expand_ref, contract_ref = refs[:3]
    pieces, early_ref, late_ref, copied = refs[3 : 3 + count], refs[3 + count], refs[4 + count], refs[5 + count]
    rank = lax.axis_index("seq")
    copies = [
        pltpu.make_async_copy(rows_ref.at[(rank ^ mask) // share], pieces[mask], copied.at[mask])
        for mask in range(count)
    ]
    for copy in copies:
        copy.start()
    at = 0
    for ref in (table_ref, inward_ref):
        for lane in range(ref.shape[1] // LANE):
            early_ref[0, at : at + TILE, :] = ref[:, lane * LANE : (lane + 1) * LANE]
            at += TILE
    rows = []
    for size, ref in zip(plan.owned, vectors):
        rows.append(jnp.concatenate([ref[...].astype(F32)] * (LANE // size), axis=1))
    rows.append(jnp.zeros((TILE - VECTORS, LANE), F32))
    early_ref[0, at : at + TILE, :] = jnp.concatenate(rows, axis=0).astype(BF)
    at = 0
    for ref in (outward_ref, expand_ref, contract_ref):
        rows = ref.shape[0]
        for lane in range(ref.shape[1] // LANE):
            late_ref[0, at : at + rows, :] = ref[:, lane * LANE : (lane + 1) * LANE]
            at += rows
    for copy in copies:
        copy.wait()


def pack(plan, count, share, rows, table, inward, vectors, outward, expand, contract):
    vectors = [v.reshape(1, -1) for v in vectors]
    outs = [pltpu.VMEM(rows.shape[1:], BF)] * count
    outs += [pltpu.VMEM((1, plan.early_rows, LANE), BF), pltpu.VMEM((1, plan.late_rows, LANE), BF)]
    values = pl.pallas_call(
        functools.partial(pack_kernel, plan, count, share),
        out_shape=outs,
        in_specs=[pl.BlockSpec(memory_space=pl.ANY)] + [HELD] * (5 + len(vectors)),
        out_specs=[HELD] * len(outs),
        scratch_shapes=[pltpu.SemaphoreType.DMA((count,))],
        cost_estimate=cost(0, 4 * 2**20),
        name="pack",
    )(rows, table, inward, *vectors, outward, expand, contract)
    return values[:count], values[count], values[count + 1]


def fold(terms, cuts):
    size = terms[0].shape[0] // cuts
    return [
        sum(term[index * size : (index + 1) * size].astype(F32) for term in terms).astype(BF)
        for index in range(cuts)
    ]


def finish_kernel(plan, info_ref, *refs):
    early, late, refs = refs[:4], refs[4:8], refs[8:]
    table_ref, inward_ref, outward_ref, expand_ref, contract_ref = refs[:5]
    vectors = refs[5:]
    early = sum(ref[0].astype(F32) for ref in early)
    late = sum(ref[...].astype(F32) for ref in late)
    for piece in range(plan.table_pieces):
        table_ref[:, piece * LANE : (piece + 1) * LANE] = early[piece * TILE : (piece + 1) * TILE]
    for piece in range(3 * plan.lanes):
        at = (plan.table_pieces + piece) * TILE
        inward_ref[:, piece * LANE : (piece + 1) * LANE] = early[at : at + TILE]
    at = 0
    for ref in (outward_ref, expand_ref, contract_ref):
        rows = ref.shape[0]
        for lane in range(ref.shape[1] // LANE):
            ref[:, lane * LANE : (lane + 1) * LANE] = late[at : at + rows]
            at += rows
    at = plan.early_pieces * TILE
    small = early[at : at + VECTORS]
    for vector, ref in enumerate(vectors):
        size = plan.owned[vector]
        slot = lax.rem(info_ref[1], LANE // size)
        row = pltpu.roll(small, lax.rem(LANE - slot * size, LANE), 1)
        ref[...] = row[vector : vector + 1, :size]


def finish(plan, info, early, late):
    own, width = plan.own_rows, plan.width
    outs = [
        like((own, plan.total_rows), F32),
        like((own, 3 * width), F32),
        like((own, width), F32),
        like((own, plan.hidden), F32),
        like((plan.hidden // plan.devices, width), F32),
    ] + [like((1, n), F32) for n in plan.owned]
    values = early + late
    return pl.pallas_call(
        functools.partial(finish_kernel, plan),
        grid_spec=pltpu.PrefetchScalarGridSpec(
            num_scalar_prefetch=1,
            grid=(1,),
            in_specs=[HELD for v in values],
            out_specs=[full(v.shape) for v in outs],
        ),
        out_shape=outs,
        name="finish",
    )(info, *hold(values))


def ordered(rank, pieces):
    for bit in (1, 2):
        flip = (rank & bit) > 0
        pieces = [jnp.where(flip, pieces[i ^ bit], pieces[i]) for i in range(4)]
    return jnp.stack(pieces)


def settle_kernel(count, share, info_ref, *refs):
    for mask in range(count):
        refs[count][pl.ds((info_ref[2] ^ mask) // share, 1), :, :] = refs[mask][...][None]


def settle_rows(info, micro_count, share, pieces):
    out = (micro_count,) + pieces[0].shape
    return pl.pallas_call(
        functools.partial(settle_kernel, len(pieces), share),
        grid_spec=pltpu.PrefetchScalarGridSpec(
            num_scalar_prefetch=1,
            grid=(1,),
            in_specs=[full(v.shape) for v in pieces],
            out_specs=full(out),
        ),
        out_shape=like(out, BF),
        cost_estimate=cost(0, 48 * 2**20),
        name="settle_rows",
    )(info, *pieces)


def cut_kernel(count, share, rows_ref, *refs):
    rank = lax.axis_index("seq")
    for mask in range(count):
        refs[mask][...] = rows_ref[pl.ds((rank ^ mask) // share, 1), :, :][0]


def cut_rows(rows, count, share):
    outs = [like(rows.shape[1:], BF)] * count
    return pl.pallas_call(
        functools.partial(cut_kernel, count, share),
        out_shape=outs,
        cost_estimate=cost(0, 4 * 2**20),
        name="cut_rows",
    )(rows)


def local(tokens, first_length, cotangent, positions, inward, intake, outward, outlet, steady, offset,
          expand, spread, contract, settle, temper, anchor):
    micro_count, pack_count, block_rows, width = tokens.shape
    assert pack_count == 1
    devices, count = lax.axis_size(AXES), lax.axis_size("seq")
    me, rank = lax.axis_index(AXES), lax.axis_index("seq")
    share = max(count // micro_count, 1)
    assert share * micro_count == count
    plan = Plan(devices, width, contract.shape[0] * devices, block_rows * count)
    micro = rank // share
    counted = (rank % share == 0).astype(jnp.int32)

    def info_of(lengths):
        first = jnp.sum(jnp.where(jnp.arange(micro_count) == micro, lengths[:, 0], 0))
        return jnp.stack([first, me, rank, counted]).astype(jnp.int32)

    vectors = (intake, outlet, steady, offset, spread, settle, temper, anchor)

    def swap(value, mask):
        return lax.ppermute(value, AXES, [(d, d ^ mask) for d in range(devices)]) if mask else value

    def exchange(pieces):
        return [swap(piece, mask) for mask, piece in enumerate(pieces)]

    def in_order(pieces):
        if count != 4 or share != 1:
            return settle_rows(info, micro_count, share, pieces)
        return ordered(rank, pieces)

    if plan.packed:
        rows_in, shard, late = pack(
            plan, count, share, tokens[:, 0], positions.T, inward, vectors, outward, expand, contract
        )
        rows_in = exchange(rows_in)
        shard, rows_in[1] = lax.optimization_barrier((shard, rows_in[1]))
        pieces = [swap(shard, mask) for mask in plan.z_order]
        pieces, rows_in, late, cotangent, first_length = lax.optimization_barrier(
            (pieces, rows_in, late, cotangent, first_length)
        )
        info = info_of(first_length)
        shard = jnp.concatenate(pieces, axis=0)
        pieces = [swap(shard, k << 1) for k in range(4)]
        late = [swap(late, mask) for mask in plan.z_order]
        upstreams = cut_rows(cotangent[:, 0], count, share)
        pieces, upstreams, late, info = lax.optimization_barrier((pieces, list(upstreams), late, info))
        late = jnp.concatenate(late, axis=0)
        late_x, late_y = swap(late, 2), swap(late, 4)
        shard = jnp.concatenate(pieces, axis=0)
        early = [shard, swap(shard, 1)]
        upstreams[1] = swap(upstreams[1], 1)
        late_core = swap(late, 1)
        early, late_core, late_x, late_y, upstreams = lax.optimization_barrier(
            (early, late_core, late_x, late_y, upstreams)
        )
        late_xy = swap(late_x, 4)
        upstreams[2:] = [swap(upstreams[mask], mask) for mask in (2, 3)]
        late_cores = [late_core, swap(late_x, 1), swap(late_y, 1)]
    else:
        info = info_of(first_length)
        rows_in = exchange(cut_rows(tokens[:, 0], count, share))
        upstreams = exchange(cut_rows(cotangent[:, 0], count, share))
        early, late = plain_weights(plan, positions, inward, vectors, outward, expand, contract)
    lifted, query, key, value, mixed, totals, inward_all, small = attend(plan, info, count, rows_in, early)
    if plan.packed:
        late_xy, late_cores, upstreams, mixed = lax.optimization_barrier(
            (late_xy, late_cores, upstreams, mixed)
        )
        late = [late, late_x, late_y, late_xy] + late_cores + [swap(late_xy, 1)]
    results, (mixed_back, first_back, small_grad), late_grads = feed(
        plan, info, count, lifted, mixed, upstreams, late, small
    )
    results = exchange(results)
    if plan.packed:
        stay_keep, go_keep, stay_send, go_send = late_grads
        cut = 8 * plan.late_cut
        go = [go_keep, swap(go_send, 1)]
        one_send, two_send = fold([v[:cut] for v in go], 1) + fold([v[cut:] for v in go], 1)
        stay_other = swap(stay_send, 1)
        one_send, two_send, mixed_back = lax.optimization_barrier((one_send, two_send, mixed_back))
        one_other, two_other = swap(one_send, 4), swap(two_send, 2)
    token_pieces, early_grads = attend_back(
        plan, info, count, lifted, (query, key, value, mixed, totals), mixed_back, inward_all,
        first_back, small_grad,
    )
    if plan.packed:
        one_other, two_other, stay_other, results, token_pieces, early_grads = lax.optimization_barrier(
            (one_other, two_other, stay_other, results, token_pieces, early_grads)
        )
        keep, send = early_grads
        send = swap(send, 1)
        one, one_send = fold([stay_keep[:cut], stay_other[:cut], one_other], 2)
        two, two_send = fold([stay_keep[cut:], stay_other[cut:], two_other], 2)
        one, one_send, two, two_send, keep = lax.optimization_barrier((one, one_send, two, two_send, keep))
        one_other, two_other = swap(one_send, 2), swap(two_send, 4)
        terms = fold([keep, send], 4)
        terms, results, token_pieces = lax.optimization_barrier((terms, results, token_pieces))
        terms = [swap(term, k << 1) for k, term in enumerate(terms)]
        output = settle_rows(info, micro_count, share, results)
        one_other, two_other, output = lax.optimization_barrier((one_other, two_other, output))
        ones, twos = fold([one, one_other], 4), fold([two, two_other], 4)
        late_terms = [jnp.concatenate(pair, axis=0) for pair in zip(ones, twos)]
        late_terms = [swap(term, mask) for term, mask in zip(late_terms, plan.z_order)]
        token_pieces = list(token_pieces)
        token_pieces[1] = swap(token_pieces[1], 1)
        terms, late_terms, output, token_pieces = lax.optimization_barrier(
            (terms, late_terms, output, token_pieces)
        )
        terms = fold(terms, 4)
        early_terms = [swap(term, mask) for term, mask in zip(terms, plan.z_order)]
        token_pieces[2:] = [swap(token_pieces[mask], mask) for mask in (2, 3)]
        early_terms, token_pieces = lax.optimization_barrier((early_terms, token_pieces))
        tokens_back = in_order(token_pieces)
        values = finish(plan, info, early_terms, late_terms)
        table_t, inward_own, outward_own, expand_own, contract_own = values[:5]
        own = [v.reshape(-1) for v in values[5:]]
        table_own = table_t.T
    else:
        output = in_order(results)
        tokens_back = in_order(exchange(token_pieces))
        table_own, inward_own, outward_own, expand_own, contract_own, own = plain_grads(
            plan, counted, early_grads, late_grads
        )
    return (output[:, None], tokens_back[:, None], table_own, inward_own, own[0], outward_own, own[1], own[2],
            own[3], expand_own, own[4], contract_own, own[5], own[6], own[7])


def plain_weights(plan, positions, inward, vectors, outward, expand, contract):
    lanes, width = plan.lanes, plan.width

    def gather(value, axis=0):
        return lax.all_gather(value, AXES, axis=axis, tiled=True)

    def in_pieces(value, size):
        return value.reshape(value.shape[0], -1, size).transpose(1, 0, 2)

    table = in_pieces(gather(positions, 1).T, LANE)
    small = jnp.concatenate([gather(v) for v in vectors]).astype(F32).reshape(-1, width)
    small = jnp.pad(small, ((0, plan.small_rows - small.shape[0]), (0, 0)))
    early = [table, in_pieces(gather(inward), LANE), small]
    return early, [gather(outward), in_pieces(gather(expand), width), gather(contract)]


def plain_grads(plan, counted, early_grads, late_grads):
    width = plan.width
    table, inward, small = early_grads
    outward, expand, contract = (jnp.where(counted > 0, g, BF(0)) for g in late_grads)

    def scatter(value, axis=0):
        return lax.psum_scatter(value, AXES, scatter_dimension=axis, tiled=True).astype(F32)

    def whole(value):
        return value.transpose(1, 0, 2).reshape(value.shape[1], -1)

    flat = small.reshape(-1)
    own = []
    for vector, length in enumerate(plan.lengths):
        start = plan.block_starts[vector] * LANE
        own.append(scatter(flat[start : start + length]))
    return (scatter(table.T, 1), scatter(whole(inward)), scatter(outward), scatter(whole(expand)),
            scatter(contract), own)


def solution(mesh):
    rows = P(None, "batch", "seq", None)
    table = P(None, AXES)
    matrix = P(AXES, None)
    vector = P(AXES)
    weights = (table, matrix, vector, matrix, vector, vector, vector, matrix, vector, matrix, vector,
               vector, vector)
    return jax.shard_map(
        local,
        mesh=mesh,
        in_specs=(rows, P(None, "batch"), rows) + weights,
        out_specs=(rows, rows) + weights,
        check_vma=False,
    )
```

```python
import functools

import jax
import jax.numpy as jnp
from jax import lax
from jax.experimental import pallas as pl
from jax.experimental.pallas import tpu as pltpu
from jax.sharding import PartitionSpec as P

AXES = ("batch", "seq")
LANE = 128
TILE = 16
FEED_ROWS = 512
STEP = 256
FAR = 1e30
BEND = 0.7978845608028654
BF = jnp.bfloat16
F32 = jnp.float32
VECTORS = 8


def times(left, right):
    return jnp.dot(left, right, preferred_element_type=F32)


def times_t(left, right):
    return lax.dot_general(left, right, (((1,), (1,)), ((), ())), preferred_element_type=F32)


def t_times(left, right):
    return lax.dot_general(left, right, (((0,), (0,)), ((), ())), preferred_element_type=F32)


def column_sum(values):
    return jnp.sum(values.astype(F32), axis=0, keepdims=True)


def aligned(index, size):
    return pl.ds(pl.multiple_of(index * size, size), size)


def like(shape, kind):
    return jax.ShapeDtypeStruct(shape, kind)


def full(shape):
    return pl.BlockSpec(shape, lambda *_: (0,) * len(shape), pipeline_mode=pl.Buffered(1))


HELD = pl.BlockSpec(memory_space=pltpu.VMEM)


def hold(values):
    return [pltpu.with_memory_space_constraint(v, pltpu.VMEM) for v in values]


def stay(values):
    return [pltpu.with_memory_space_constraint(v, pltpu.HBM) for v in values]


def params(megabytes):
    return pltpu.CompilerParams(vmem_limit_bytes=megabytes * 2**20)


def cost(flops, size, exps=0):
    return pl.CostEstimate(flops=flops, bytes_accessed=size, transcendentals=exps)


class Plan:
    def __init__(self, devices, width, hidden, total_rows):
        self.devices = devices
        self.width = width
        self.hidden = hidden
        self.total_rows = total_rows
        self.own_rows = width // devices
        self.packed = devices == 32 and self.own_rows % TILE == 0
        self.lanes = width // LANE
        self.parts = hidden // width
        self.table_pieces = total_rows // LANE
        self.early_pieces = self.table_pieces + 3 * self.lanes
        self.early_rows = (self.early_pieces + 1) * TILE
        self.late_rows = (self.lanes + hidden // LANE) * TILE + self.lanes * (hidden // devices)
        self.late_cut = (self.lanes + hidden // LANE) * TILE + hidden // devices
        lengths = [2 * width, width, width, width, hidden, width, width, width]
        self.lengths = lengths
        self.owned = [n // devices for n in lengths]
        self.small_rows = 16
        self.z_order = (0, 24, 8, 16)
        starts = [0]
        for n in lengths:
            starts.append(starts[-1] + n // LANE)
        self.block_starts = starts

    def place(self, mask):
        return ((mask >> 1) & 3) * 4 + self.z_order.index(mask & 24)

    def grad_piece(self, half, mask, at, rows):
        first = at < self.late_cut
        assert not first or at + rows <= self.late_cut
        swapped = mask if first else (mask & ~6) | ((mask >> 1) & 2) | ((mask & 2) << 1)
        place = self.place(swapped)
        last_rows = self.late_rows - self.late_cut
        if first:
            start = (place % 8) * self.late_cut + at
        else:
            start = 8 * self.late_cut + (place % 8) * last_rows + at - self.late_cut
        return half[place // 8].at[start : start + rows, :]


def fill_early(plan, me, halves, table_ref, inward_ref, small_ref, stage_ref):
    for mask in range(plan.devices):
        shard = halves[mask & 1].at[plan.place(mask)]
        owner = me ^ mask
        rows = aligned(owner, TILE)
        for piece in range(plan.table_pieces):
            table_ref[piece, rows, :] = shard[piece * TILE : (piece + 1) * TILE, :]
        for piece in range(3 * plan.lanes):
            at = plan.table_pieces + piece
            inward_ref[piece, rows, :] = shard[at * TILE : (at + 1) * TILE, :]
        at = plan.early_pieces * TILE
        stage_ref[pl.ds(owner, 1), :, :] = shard[at : at + TILE, :].astype(F32)[None]
    lane = lax.broadcasted_iota(jnp.int32, (1, LANE), 1)
    for vector, length in enumerate(plan.lengths):
        size = plan.owned[vector]
        group = LANE // size
        for block in range(length // LANE):
            row = jnp.zeros((1, LANE), F32)
            for index in range(group):
                own = stage_ref[block * group + index, vector : vector + 1, :]
                row = jnp.where(lane // size == index, own, row)
            at = plan.block_starts[vector] + block
            small_ref[at // plan.lanes : at // plan.lanes + 1, (at % plan.lanes) * LANE : (at % plan.lanes + 1) * LANE] = row


def own_lanes(value, head):
    lane = lax.broadcasted_iota(jnp.int32, value.shape, 1)
    return jnp.where((lane // (LANE // 2)) == head, value, jnp.zeros_like(value))


def causal():
    return lax.broadcasted_iota(jnp.int32, (STEP, STEP), 0) <= lax.broadcasted_iota(
        jnp.int32, (STEP, STEP), 1
    )


def attend_kernel(plan, count, info_ref, *refs):
    pieces, refs = refs[:count], refs[count:]
    if plan.packed:
        halves, refs = refs[:2], refs[2:]
    else:
        table_in, inward_in, small_in = refs[:3]
        refs = refs[3:]
    (lifted_ref, query_ref, key_ref, value_ref, mixed_ref, total_ref, inward_ref, small_ref) = refs[:8]
    low_ref, table_ref, place_ref, stage_ref = refs[8:]
    pair = pl.program_id(0)
    total_rows, width = plan.total_rows, plan.width
    half = total_rows // 2
    split = info_ref[0] < total_rows
    far = jnp.where(split, FAR, 0.0)

    @pl.when(pair == 0)
    def _():
        if plan.packed:
            fill_early(plan, info_ref[1], halves, table_ref, inward_ref, small_ref, stage_ref)
        else:
            table_ref[...] = table_in[...]
            inward_ref[...] = inward_in[...]
            small_ref[...] = small_in[...]
        eye = (
            lax.broadcasted_iota(jnp.int32, (half, half), 0)
            == lax.broadcasted_iota(jnp.int32, (half, half), 1)
        ).astype(BF)
        per_half = half // LANE
        for part in range(2):
            table = jnp.concatenate(
                [table_ref[part * per_half + i] for i in range(per_half)], axis=1
            )
            place_ref[part * half : (part + 1) * half, :] = times_t(eye, table)
        rows = total_rows // count
        for mask in range(count):
            start = (info_ref[2] ^ mask) * rows
            place = start - jnp.where(jnp.logical_and(split, start >= half), half, 0)
            lifted = pieces[mask][...].astype(F32) + place_ref[pl.ds(pl.multiple_of(place, rows), rows), :]
            spot = pl.ds(pl.multiple_of(start, rows), rows)
            lifted_ref[spot, :] = lifted
            low_ref[spot, :] = lifted.astype(BF)

    weights = jnp.concatenate([inward_ref[pair + i * plan.lanes] for i in range(3)], axis=1)
    lanes = aligned(pair, LANE)
    query_bias = small_ref[0:1, lanes]
    value_bias = small_ref[1:2, lanes]
    for block in range(total_rows // STEP):
        spot = slice(block * STEP, (block + 1) * STEP)
        joint = times(low_ref[spot, :], weights)
        query_ref[spot, :] = (joint[:, :LANE] + query_bias).astype(BF) * BF(0.125)
        key_ref[spot, :] = joint[:, LANE : 2 * LANE].astype(BF)
        value_ref[spot, :] = (joint[:, 2 * LANE :] + value_bias).astype(BF)

    keep = causal()
    lower = lax.broadcasted_iota(jnp.int32, (LANE, STEP), 0) < LANE // 2

    value_t = value_ref[...].T

    def logits_of(block, head):
        start = block * STEP
        other = half if start >= half else 0
        mine = own_lanes(query_ref[start : start + STEP, :], head)
        near = times_t(key_ref[start : start + STEP, :], mine)
        same = times_t(key_ref[other:start, :], mine) if start > other else None
        away = times_t(key_ref[:other, :], mine) if other else None
        return near, same, away

    def mixed_of(block, head, near, same, away):
        start = block * STEP
        other = half if start >= half else 0
        near = jnp.where(keep, near, -FAR)
        peak = jnp.max(near, axis=0, keepdims=True)
        if same is not None:
            peak = jnp.maximum(peak, jnp.max(same, axis=0, keepdims=True))
        if away is not None:
            peak = jnp.maximum(peak, jnp.max(away, axis=0, keepdims=True) - far)
        raised = [jnp.exp(piece - peak) for piece in (same, near) if piece is not None]
        total = sum(jnp.sum(piece, axis=0, keepdims=True) for piece in raised)
        low = jnp.concatenate([piece.astype(BF) for piece in raised], axis=0)
        mixed = times(value_t[:, other : start + STEP], low)
        if away is not None:
            away = jnp.exp(away - (peak + far))
            total = total + jnp.sum(away, axis=0, keepdims=True)
            mixed = mixed + times(value_t[:, :other], away.astype(BF))
        total_ref[0, head : head + 1, start : start + STEP] = peak + jnp.log(total)
        return mixed * (1.0 / total)

    tasks = [(block, head) for block in range(total_rows // STEP) for head in range(2)]
    ahead = logits_of(*tasks[0])
    parts = []
    for index, (block, head) in enumerate(tasks):
        logits, ahead = ahead, logits_of(*tasks[index + 1]) if index + 1 < len(tasks) else None
        parts.append(mixed_of(block, head, *logits))
        if head:
            mixed_ref[block * STEP : (block + 1) * STEP, :] = jnp.where(lower, *parts).T.astype(BF)
            parts = []


def attend(plan, info, count, pieces, weights):
    total_rows, width = plan.total_rows, plan.width
    block = pl.BlockSpec((total_rows, LANE), lambda p, *_: (0, p))
    low = pltpu.HBM((total_rows, width), BF)
    inward = (3 * plan.lanes, width, LANE)
    small = (plan.small_rows, width)
    return pl.pallas_call(
        functools.partial(attend_kernel, plan, count),
        grid_spec=pltpu.PrefetchScalarGridSpec(
            num_scalar_prefetch=1,
            grid=(plan.lanes,),
            in_specs=[HELD for v in pieces + weights],
            out_specs=[
                full((total_rows, width)),
                block,
                block,
                block,
                block,
                pl.BlockSpec((1, 8, total_rows), lambda p, *_: (p, 0, 0)),
                full(inward),
                full(small),
            ],
            scratch_shapes=[
                pltpu.VMEM((total_rows, width), BF),
                pltpu.VMEM((plan.table_pieces, width, LANE), BF),
                pltpu.VMEM((total_rows, width), F32),
                pltpu.VMEM((plan.devices, TILE, LANE), F32),
            ],
        ),
        out_shape=[
            pltpu.HBM((total_rows, width), F32),
            low,
            low,
            low,
            low,
            pltpu.HBM((plan.lanes, 8, total_rows), F32),
            pltpu.HBM(inward, BF),
            pltpu.HBM(small, F32),
        ],
        compiler_params=params(36),
        cost_estimate=cost(5 * 10**9, 14 * 2**20, 6 * 10**6),
        name="attend",
    )(info, *hold(pieces), *hold(weights))


def norm(rows):
    center = rows - jnp.mean(rows, axis=1, keepdims=True)
    root = lax.rsqrt(jnp.mean(center * center, axis=1, keepdims=True) + 1e-05)
    return center * root, root


def norm_back(upstream, gain, unit, root):
    scaled = upstream * gain
    mean = jnp.mean(scaled, axis=1, keepdims=True)
    slope = jnp.mean(scaled * unit, axis=1, keepdims=True)
    return (scaled - mean - unit * slope) * root


def feed_kernel(plan, count, info_ref, lifted_ref, mixed_ref, *refs):
    upstreams, refs = refs[:count], refs[count:]
    if plan.packed:
        late_quarters, small_ref = refs[:8], refs[8]
        refs = refs[9:]
    else:
        outward_in, expand_in, contract_in, small_ref = refs[:4]
        refs = refs[4:]
    results, refs = refs[:count], refs[count:]
    mixed_back_ref, first_back_ref, small_grad_ref = refs[:3]
    refs = refs[3:]
    if plan.packed:
        halves, refs = (refs[:2], refs[2:4]), refs[4:]
    else:
        outward_out, expand_out, contract_out = refs[:3]
        refs = refs[3:]
    (outward_ref, expand_ref, contract_ref, upstream_ref, result_ref, slope_ref, active_all, hidden_all, normed_all,
     lowered_all, branch_all, mixed_all, whole_ref, expand_sum, contract_sum) = refs
    step = pl.program_id(0)
    width, parts, lanes = plan.width, plan.parts, plan.lanes
    contract_own = plan.hidden // plan.devices
    contract_at = (lanes + parts * lanes) * TILE

    @pl.when(step == 0)
    def _():
        if plan.packed:
            for mask in range(plan.devices):
                at = plan.place(mask)
                shard = late_quarters[(mask & 1) * 4 + at // 4].at[at % 4]
                owner = info_ref[1] ^ mask
                rows, wide = aligned(owner, TILE), aligned(owner, contract_own)
                for lane in range(lanes):
                    cut = slice(lane * LANE, (lane + 1) * LANE)
                    outward_ref[rows, cut] = shard[lane * TILE : (lane + 1) * TILE, :]
                    for part in range(parts):
                        at = (lanes + part * lanes + lane) * TILE
                        expand_ref[part, rows, cut] = shard[at : at + TILE, :]
                    at = contract_at + lane * contract_own
                    contract_ref[wide, cut] = shard[at : at + contract_own, :]
        else:
            outward_ref[...] = outward_in[...]
            expand_ref[...] = expand_in[...]
            contract_ref[...] = contract_in[...]

    size = lifted_ref.shape[0]
    here = pl.ds(pl.multiple_of(step * size, size), size)
    rows = plan.total_rows // count
    group = size // rows

    def spot(mask):
        return pl.ds(pl.multiple_of(((info_ref[2] ^ mask) % group) * rows, rows), rows)

    for mask in range(count):
        @pl.when(step == mask // group)
        def _(mask=mask):
            upstream_ref[spot(mask), :] = upstreams[mask][...]

    outlet, steady, offset = (small_ref[i : i + 1, :] for i in (2, 3, 4))
    settle, temper, anchor = (small_ref[i + parts : i + parts + 1, :] for i in (5, 6, 7))
    mixed = mixed_ref[...]
    branch = times(mixed, outward_ref[...]) + outlet
    unit, root = norm(lifted_ref[...] + branch)
    normed = unit * steady + offset
    normed_low = normed.astype(BF)
    normed_all[here, :] = normed_low
    mixed_all[here, :] = mixed
    lowered = jnp.zeros_like(normed)
    for part in range(parts):
        cut = slice(part * width, (part + 1) * width)
        hidden = times(normed_low, expand_ref[part]) + small_ref[5 + part : 6 + part, :]
        square = hidden * hidden
        bend = jnp.tanh(hidden * (BEND + BEND * 0.044715 * square))
        half = 0.5 + 0.5 * bend
        active = (hidden * half).astype(BF)
        active_all[here, cut] = active
        slope_ref[:, cut] = half + (0.5 * hidden) * (1.0 - bend * bend) * (
            BEND + 3 * BEND * 0.044715 * square
        )
        lowered = lowered + times(active, contract_ref[cut, :])
    last_unit, last_root = norm(normed + (lowered + settle))
    result_ref[...] = (last_unit * temper + anchor).astype(BF)
    upstream = upstream_ref[...].astype(F32)
    temper_grad = column_sum(upstream * last_unit)
    anchor_grad = column_sum(upstream)
    second_back = norm_back(upstream, temper, last_unit, last_root)
    lowered_back = second_back.astype(BF)
    lowered_all[here, :] = lowered_back
    settle_grad = column_sum(lowered_back)
    normed_back = second_back
    spread_grads = []
    for part in range(parts):
        cut = slice(part * width, (part + 1) * width)
        active_back = times_t(lowered_back, contract_ref[cut, :])
        hidden_back = (active_back * slope_ref[:, cut]).astype(BF)
        spread_grads.append(column_sum(hidden_back))
        hidden_all[here, cut] = hidden_back
        normed_back = normed_back + times_t(hidden_back, expand_ref[part])
    first_back = norm_back(normed_back, steady, unit, root)
    first_back_ref[...] = first_back
    branch_back = first_back.astype(BF)
    mixed_back_ref[...] = times_t(branch_back, outward_ref[...]).astype(BF)
    branch_all[here, :] = branch_back
    zero = jnp.zeros_like(anchor_grad)
    grads = [zero, zero, column_sum(branch_back), column_sum(normed_back * unit)]
    grads += [column_sum(normed_back)] + spread_grads + [settle_grad, temper_grad, anchor_grad]
    grads += [zero] * (plan.small_rows - len(grads))
    small_term = jnp.concatenate(grads, axis=0)
    for mask in range(count):
        @pl.when(step == mask // group)
        def _(mask=mask):
            results[mask][...] = result_ref[spot(mask), :]

    @pl.when(step == 0)
    def _():
        small_grad_ref[...] = small_term

    @pl.when(step > 0)
    def _():
        small_grad_ref[...] += small_term

    @pl.when(step == pl.num_programs(0) - 1)
    def _():
        outward = t_times(mixed_all[...], branch_all[...])
        if plan.packed:
            me = info_ref[1]
            whole_ref[...] = outward
            for mask in range(plan.devices):
                half = halves[mask & 1]
                rows = aligned(me ^ mask, TILE)
                for lane in range(lanes):
                    cut = slice(lane * LANE, (lane + 1) * LANE)
                    plan.grad_piece(half, mask, lane * TILE, TILE)[...] = whole_ref[rows, cut].astype(BF)
        else:
            outward_out[...] = outward.astype(BF)
        per_part = plan.devices // parts
        for part in range(parts):
            cut = slice(part * width, (part + 1) * width)
            expand = t_times(normed_all[...], hidden_all[:, cut])
            if not plan.packed:
                expand_out[part] = expand.astype(BF)
                continue
            expand_sum[...] = expand
            for mask in range(plan.devices):
                rows = aligned(me ^ mask, TILE)
                for lane in range(lanes):
                    at = (lanes + part * lanes + lane) * TILE
                    plan.grad_piece(halves[mask & 1], mask, at, TILE)[...] = expand_sum[
                        rows, lane * LANE : (lane + 1) * LANE
                    ].astype(BF)
        for mask_part in range(parts):
            part = (me // per_part) ^ mask_part if plan.packed else mask_part
            cut = pl.ds(pl.multiple_of(part * width, width), width)
            contract = t_times(active_all[:, cut], lowered_all[...])
            if not plan.packed:
                contract_out[cut, :] = contract.astype(BF)
                continue
            contract_sum[...] = contract
            for index in range(per_part):
                mask = mask_part * per_part + index
                rows = aligned((me ^ mask) % per_part, contract_own)
                for lane in range(lanes):
                    at = contract_at + lane * contract_own
                    plan.grad_piece(halves[mask & 1], mask, at, contract_own)[...] = contract_sum[
                        rows, lane * LANE : (lane + 1) * LANE
                    ].astype(BF)


def feed(plan, info, count, lifted, mixed, upstreams, weights, small):
    total_rows, width, parts = plan.total_rows, plan.width, plan.parts
    piece = total_rows // count
    size = max(piece, FEED_ROWS)
    group = size // piece
    rows = pl.BlockSpec((size, width), lambda i, info: ((info[2] // group) ^ i, 0))
    outward, expand, contract = (width, width), (parts, width, width), (parts * width, width)
    if plan.packed:
        grads = [pltpu.VMEM((8 * plan.late_rows, LANE), BF)] * 4
    else:
        grads = [pltpu.VMEM(outward, BF), pltpu.VMEM(expand, BF), pltpu.VMEM(contract, BF)]
    ends = [pltpu.VMEM((piece, width), BF)] * count
    outs = [like((total_rows, width), BF), like((total_rows, width), F32), like(small.shape, F32)]
    values = pl.pallas_call(
        functools.partial(feed_kernel, plan, count),
        grid_spec=pltpu.PrefetchScalarGridSpec(
            num_scalar_prefetch=1,
            grid=(total_rows // size,),
            in_specs=[rows, rows]
            + [HELD for v in upstreams + weights]
            + [full(small.shape)],
            out_specs=[HELD for v in ends]
            + [rows, rows, full(small.shape)]
            + [HELD for v in grads],
            scratch_shapes=[
                pltpu.VMEM(outward, BF),
                pltpu.VMEM(expand, BF),
                pltpu.VMEM(contract, BF),
                pltpu.VMEM((size, width), BF),
                pltpu.VMEM((size, width), BF),
                pltpu.VMEM((size, parts * width), F32),
                pltpu.VMEM((total_rows, parts * width), BF),
                pltpu.VMEM((total_rows, parts * width), BF),
                pltpu.VMEM((total_rows, width), BF),
                pltpu.VMEM((total_rows, width), BF),
                pltpu.VMEM((total_rows, width), BF),
                pltpu.VMEM((total_rows, width), BF),
                pltpu.VMEM(outward, F32),
                pltpu.VMEM(outward, F32),
                pltpu.VMEM(outward, F32),
            ],
        ),
        out_shape=ends + outs + grads,
        compiler_params=params(50),
        cost_estimate=cost(15 * 10**9, 20 * 2**20, 2 * 10**6),
        name="feed",
    )(info, lifted, mixed, *hold(upstreams), *hold(weights), small)
    return values[:count], values[count : count + 3], values[count + 3 :]


def attend_back_kernel(
    plan, count, info_ref, lifted_ref, query_ref, key_ref, value_ref, mixed_ref, mixed_back_ref,
    total_ref, inward_ref, first_back_ref, small_grad_ref, *refs
):
    tokens, refs = refs[:count], refs[count:]
    if plan.packed:
        halves, refs = refs[:2], refs[2:]
    else:
        table_out, inward_out, small_out = refs[:3]
        refs = refs[3:]
    (joint_ref, sum_ref, share_ref, score_ref, grad_ref, table_ref, joint_sums, blocks_ref,
     lifted_here, inward_here, copied) = refs
    pair = pl.program_id(0)
    copies = [
        pltpu.make_async_copy(source, target, copied.at[index])
        for index, (source, target) in enumerate(
            ((lifted_ref, lifted_here), (inward_ref, inward_here), (first_back_ref, sum_ref))
        )
    ]

    @pl.when(pair == 0)
    def _():
        for copy in copies:
            copy.start()

    total_rows, lanes = plan.total_rows, plan.lanes
    half = total_rows // 2
    split = info_ref[0] < total_rows
    far = jnp.where(split, FAR, 0.0)
    blocks = total_rows // STEP

    keep = causal()
    lower = lax.broadcasted_iota(jnp.int32, (STEP, LANE), 1) < LANE // 2
    lower_t = lax.broadcasted_iota(jnp.int32, (LANE, STEP), 0) < LANE // 2
    product = (mixed_ref[...].astype(F32) * mixed_back_ref[...].astype(F32)).T
    scaled_key = (key_ref[...] * BF(0.125)).T
    betweens = [
        jnp.sum(product[head * LANE // 2 : (head + 1) * LANE // 2], axis=0, keepdims=True)
        for head in range(2)
    ]

    def logits_of(block, head):
        spot = slice(block * STEP, (block + 1) * STEP)
        keys = slice(0, (block + 1) * STEP)
        query = own_lanes(query_ref[spot, :], head)
        back = own_lanes(mixed_back_ref[spot, :], head)
        return times_t(key_ref[keys, :], query), times_t(value_ref[keys, :], back)

    def scores_of(block, head, logits, share_back):
        start = block * STEP
        spot = slice(start, start + STEP)
        total = total_ref[0, head : head + 1, spot]
        gap = betweens[head][:, spot]
        for under in range(block + 1):
            keys = slice(under * STEP, (under + 1) * STEP)
            away = start >= half and under * STEP < half
            share = jnp.exp(logits[keys] - (total + far if away else total))
            if under == block:
                share = jnp.where(keep, share, 0.0)
            score = share * (share_back[keys] - gap)
            share_ref[head, keys, spot] = share.astype(BF)
            score_ref[head, keys, spot] = score.astype(BF)

    def backs_of(block, head):
        start = block * STEP
        spot = slice(start, start + STEP)
        end = start + STEP
        query_back = times(scaled_key[:, :end], score_ref[head, :end, spot])
        key_back = times(score_ref[head, spot, start:], query_ref[start:, :])
        value_back = times(share_ref[head, spot, start:], mixed_back_ref[start:, :])
        return query_back, key_back, value_back

    tasks = [(block, head) for block in reversed(range(blocks)) for head in range(2)]
    ahead = logits_of(*tasks[0])
    parts = []
    for index, (block, head) in enumerate(tasks):
        logits, ahead = ahead, logits_of(*tasks[index + 1]) if index + 1 < len(tasks) else None
        scores_of(block, head, *logits)
        parts.append(backs_of(block, head))
        if head:
            spot = slice(block * STEP, (block + 1) * STEP)
            query_back = jnp.where(lower_t, parts[0][0], parts[1][0]).T
            key_back = jnp.where(lower, parts[0][1], parts[1][1])
            value_back = jnp.where(lower, parts[0][2], parts[1][2])
            for part, back in enumerate((query_back, key_back, value_back)):
                joint_ref[spot, aligned(pair + part * lanes, LANE)] = back.astype(BF)
            parts = []

    @pl.when(pair == lanes - 1)
    def _():
        for copy in copies:
            copy.wait()
        low = lifted_here[...].astype(BF).T
        weights = jnp.concatenate([inward_here[i] for i in range(3 * lanes)], axis=1)
        for block in range(blocks):
            spot = slice(block * STEP, (block + 1) * STEP)
            sum_ref[spot, :] += times_t(joint_ref[spot, :], weights)
        for part in range(3):
            joint = joint_ref[:, part * plan.width : (part + 1) * plan.width]
            grads = times(low, joint)
            for lane in range(lanes):
                grad_ref[part * lanes + lane] = grads[:, lane * LANE : (lane + 1) * LANE]
            if part != 1:
                sums = column_sum(joint)
                for lane in range(lanes):
                    at = lane if part == 0 else lane + lanes
                    joint_sums[at : at + 1, :] = sums[:, lane * LANE : (lane + 1) * LANE]
        rows = total_rows // count
        for mask in range(count):
            spot = pl.ds(pl.multiple_of((info_ref[2] ^ mask) * rows, rows), rows)
            tokens[mask][...] = sum_ref[spot, :].astype(BF)
        late = sum_ref[half:, :]
        early = sum_ref[:half, :] + jnp.where(split, late, 0.0)
        table_ref[:, :half] = early.T
        table_ref[:, half:] = jnp.where(split, 0.0, late).T
        counted = info_ref[3] > 0
        blocks_ref[: 2 * lanes, :] = joint_sums[: 2 * lanes, :]
        for row in range(2, plan.block_starts[-1] // lanes):
            for lane in range(lanes):
                blocks_ref[row * lanes + lane : row * lanes + lane + 1, :] = small_grad_ref[
                    row : row + 1, lane * LANE : (lane + 1) * LANE
                ]
        if plan.packed:
            for mask in range(plan.devices):
                shard = halves[mask & 1].at[plan.place(mask)]
                owner = info_ref[1] ^ mask
                own = aligned(owner, TILE)
                for piece in range(plan.table_pieces):
                    shard[piece * TILE : (piece + 1) * TILE, :] = table_ref[
                        own, piece * LANE : (piece + 1) * LANE
                    ].astype(BF)
                for piece in range(3 * lanes):
                    at = (plan.table_pieces + piece) * TILE
                    shard[at : at + TILE, :] = grad_ref[piece, own, :].astype(BF)
                rows = [
                    blocks_ref[pl.ds(plan.block_starts[v] + owner * plan.owned[v] // LANE, 1), :]
                    for v in range(VECTORS)
                ]
                rows.append(jnp.zeros((TILE - VECTORS, LANE), F32))
                at = plan.early_pieces * TILE
                shard[at : at + TILE, :] = jnp.concatenate(rows, axis=0).astype(BF)
        else:
            table_out[...] = jnp.where(counted, table_ref[...], 0.0).astype(BF)
            inward_out[...] = jnp.where(counted, grad_ref[...], 0.0).astype(BF)
            small_out[...] = jnp.where(counted, blocks_ref[...], 0.0)


def attend_back(plan, info, count, lifted, saved, mixed_back, inward, first_back, small_grad):
    query, key, value, mixed, totals = saved
    total_rows, width, lanes = plan.total_rows, plan.width, plan.lanes
    block = pl.BlockSpec((total_rows, LANE), lambda p, *_: (0, p))
    blocks = (plan.block_starts[-1], LANE)
    if plan.packed:
        grads = [pltpu.VMEM((plan.devices // 2, plan.early_rows, LANE), BF)] * 2
    else:
        grads = [pltpu.VMEM((width, total_rows), BF), pltpu.VMEM(inward.shape, BF), pltpu.VMEM(blocks, F32)]
    tokens = [pltpu.VMEM((total_rows // count, width), BF)] * count
    values = pl.pallas_call(
        functools.partial(attend_back_kernel, plan, count),
        grid_spec=pltpu.PrefetchScalarGridSpec(
            num_scalar_prefetch=1,
            grid=(lanes,),
            in_specs=[
                pl.BlockSpec(memory_space=pl.ANY),
                block,
                block,
                block,
                block,
                block,
                pl.BlockSpec((1, 8, total_rows), lambda p, *_: (p, 0, 0)),
                pl.BlockSpec(memory_space=pl.ANY),
                pl.BlockSpec(memory_space=pl.ANY),
                full(small_grad.shape),
            ],
            out_specs=[HELD for v in tokens + grads],
            scratch_shapes=[
                pltpu.VMEM((total_rows, 3 * width), BF),
                pltpu.VMEM((total_rows, width), F32),
                pltpu.VMEM((2, total_rows, total_rows), BF),
                pltpu.VMEM((2, total_rows, total_rows), BF),
                pltpu.VMEM(inward.shape, F32),
                pltpu.VMEM((width, total_rows), F32),
                pltpu.VMEM((8, LANE), F32),
                pltpu.VMEM(blocks, F32),
                pltpu.VMEM(lifted.shape, F32),
                pltpu.VMEM(inward.shape, BF),
                pltpu.SemaphoreType.DMA((3,)),
            ],
        ),
        out_shape=tokens + grads,
        compiler_params=params(40),
        cost_estimate=cost(14 * 10**9, 24 * 2**20, 6 * 10**6),
        name="attend_back",
    )(info, *stay([lifted, query, key, value, mixed, mixed_back, totals, inward, first_back]), small_grad)
    return values[:count], values[count:]


def pack_kernel(plan, count, share, rows_ref, table_ref, inward_ref, *refs):
    vectors, refs = refs[:VECTORS], refs[VECTORS:]
    outward_ref, expand_ref, contract_ref = refs[:3]
    pieces, early_ref, late_ref, copied = refs[3 : 3 + count], refs[3 + count], refs[4 + count], refs[5 + count]
    rank = lax.axis_index("seq")
    copies = [
        pltpu.make_async_copy(rows_ref.at[(rank ^ mask) // share], pieces[mask], copied.at[mask])
        for mask in range(count)
    ]
    for copy in copies:
        copy.start()
    at = 0
    for ref in (table_ref, inward_ref):
        for lane in range(ref.shape[1] // LANE):
            early_ref[0, at : at + TILE, :] = ref[:, lane * LANE : (lane + 1) * LANE]
            at += TILE
    rows = []
    for size, ref in zip(plan.owned, vectors):
        rows.append(jnp.concatenate([ref[...].astype(F32)] * (LANE // size), axis=1))
    rows.append(jnp.zeros((TILE - VECTORS, LANE), F32))
    early_ref[0, at : at + TILE, :] = jnp.concatenate(rows, axis=0).astype(BF)
    at = 0
    for ref in (outward_ref, expand_ref, contract_ref):
        rows = ref.shape[0]
        for lane in range(ref.shape[1] // LANE):
            late_ref[0, at : at + rows, :] = ref[:, lane * LANE : (lane + 1) * LANE]
            at += rows
    for copy in copies:
        copy.wait()


def pack(plan, count, share, rows, table, inward, vectors, outward, expand, contract):
    vectors = [v.reshape(1, -1) for v in vectors]
    outs = [pltpu.VMEM(rows.shape[1:], BF)] * count
    outs += [pltpu.VMEM((1, plan.early_rows, LANE), BF), pltpu.VMEM((1, plan.late_rows, LANE), BF)]
    values = pl.pallas_call(
        functools.partial(pack_kernel, plan, count, share),
        out_shape=outs,
        in_specs=[pl.BlockSpec(memory_space=pl.ANY)] + [HELD] * (5 + len(vectors)),
        out_specs=[HELD] * len(outs),
        scratch_shapes=[pltpu.SemaphoreType.DMA((count,))],
        cost_estimate=cost(0, 4 * 2**20),
        name="pack",
    )(rows, table, inward, *vectors, outward, expand, contract)
    return values[:count], values[count], values[count + 1]


def fold(terms, cuts):
    size = terms[0].shape[0] // cuts
    return [
        sum(term[index * size : (index + 1) * size].astype(F32) for term in terms).astype(BF)
        for index in range(cuts)
    ]


def finish_kernel(plan, info_ref, *refs):
    early, late, refs = refs[:4], refs[4:8], refs[8:]
    table_ref, inward_ref, outward_ref, expand_ref, contract_ref = refs[:5]
    vectors = refs[5:]
    early = sum(ref[0].astype(F32) for ref in early)
    late = sum(ref[...].astype(F32) for ref in late)
    for piece in range(plan.table_pieces):
        table_ref[:, piece * LANE : (piece + 1) * LANE] = early[piece * TILE : (piece + 1) * TILE]
    for piece in range(3 * plan.lanes):
        at = (plan.table_pieces + piece) * TILE
        inward_ref[:, piece * LANE : (piece + 1) * LANE] = early[at : at + TILE]
    at = 0
    for ref in (outward_ref, expand_ref, contract_ref):
        rows = ref.shape[0]
        for lane in range(ref.shape[1] // LANE):
            ref[:, lane * LANE : (lane + 1) * LANE] = late[at : at + rows]
            at += rows
    at = plan.early_pieces * TILE
    small = early[at : at + VECTORS]
    for vector, ref in enumerate(vectors):
        size = plan.owned[vector]
        slot = lax.rem(info_ref[1], LANE // size)
        row = pltpu.roll(small, lax.rem(LANE - slot * size, LANE), 1)
        ref[...] = row[vector : vector + 1, :size]


def finish(plan, info, early, late):
    own, width = plan.own_rows, plan.width
    outs = [
        like((own, plan.total_rows), F32),
        like((own, 3 * width), F32),
        like((own, width), F32),
        like((own, plan.hidden), F32),
        like((plan.hidden // plan.devices, width), F32),
    ] + [like((1, n), F32) for n in plan.owned]
    values = early + late
    return pl.pallas_call(
        functools.partial(finish_kernel, plan),
        grid_spec=pltpu.PrefetchScalarGridSpec(
            num_scalar_prefetch=1,
            grid=(1,),
            in_specs=[HELD for v in values],
            out_specs=[full(v.shape) for v in outs],
        ),
        out_shape=outs,
        name="finish",
    )(info, *hold(values))


def ordered(rank, pieces):
    for bit in (1, 2):
        flip = (rank & bit) > 0
        pieces = [jnp.where(flip, pieces[i ^ bit], pieces[i]) for i in range(4)]
    return jnp.stack(pieces)


def settle_kernel(count, share, info_ref, *refs):
    for mask in range(count):
        refs[count][pl.ds((info_ref[2] ^ mask) // share, 1), :, :] = refs[mask][...][None]


def settle_rows(info, micro_count, share, pieces):
    out = (micro_count,) + pieces[0].shape
    return pl.pallas_call(
        functools.partial(settle_kernel, len(pieces), share),
        grid_spec=pltpu.PrefetchScalarGridSpec(
            num_scalar_prefetch=1,
            grid=(1,),
            in_specs=[full(v.shape) for v in pieces],
            out_specs=full(out),
        ),
        out_shape=like(out, BF),
        cost_estimate=cost(0, 48 * 2**20),
        name="settle_rows",
    )(info, *pieces)


def cut_kernel(count, share, rows_ref, *refs):
    rank = lax.axis_index("seq")
    for mask in range(count):
        refs[mask][...] = rows_ref[pl.ds((rank ^ mask) // share, 1), :, :][0]


def cut_rows(rows, count, share):
    outs = [like(rows.shape[1:], BF)] * count
    return pl.pallas_call(
        functools.partial(cut_kernel, count, share),
        out_shape=outs,
        cost_estimate=cost(0, 4 * 2**20),
        name="cut_rows",
    )(rows)


def local(tokens, first_length, cotangent, positions, inward, intake, outward, outlet, steady, offset,
          expand, spread, contract, settle, temper, anchor):
    micro_count, pack_count, block_rows, width = tokens.shape
    assert pack_count == 1
    devices, count = lax.axis_size(AXES), lax.axis_size("seq")
    me, rank = lax.axis_index(AXES), lax.axis_index("seq")
    share = max(count // micro_count, 1)
    assert share * micro_count == count
    plan = Plan(devices, width, contract.shape[0] * devices, block_rows * count)
    micro = rank // share
    counted = (rank % share == 0).astype(jnp.int32)

    def info_of(lengths):
        first = jnp.sum(jnp.where(jnp.arange(micro_count) == micro, lengths[:, 0], 0))
        return jnp.stack([first, me, rank, counted]).astype(jnp.int32)

    vectors = (intake, outlet, steady, offset, spread, settle, temper, anchor)

    def swap(value, mask):
        return lax.ppermute(value, AXES, [(d, d ^ mask) for d in range(devices)]) if mask else value

    def exchange(pieces):
        moved = list(pieces)
        for mask in reversed(range(1, count)):
            moved[mask] = swap(pieces[mask], mask)
        return moved

    def in_order(pieces):
        if count != 4 or share != 1:
            return settle_rows(info, micro_count, share, pieces)
        return ordered(rank, pieces)

    if plan.packed:
        rows_in, shard, late = pack(
            plan, count, share, tokens[:, 0], positions.T, inward, vectors, outward, expand, contract
        )
        rows_in = exchange(rows_in)
        shard, rows_in[1] = lax.optimization_barrier((shard, rows_in[1]))
        pieces = [swap(shard, mask) for mask in plan.z_order]
        pieces, rows_in, late, cotangent, first_length = lax.optimization_barrier(
            (pieces, rows_in, late, cotangent, first_length)
        )
        info = info_of(first_length)
        shard = jnp.concatenate(pieces, axis=0)
        pieces = [swap(shard, k << 1) for k in range(4)]
        late = [swap(late, mask) for mask in plan.z_order]
        upstreams = cut_rows(cotangent[:, 0], count, share)
        pieces, upstreams, late, info = lax.optimization_barrier((pieces, list(upstreams), late, info))
        late = jnp.concatenate(late, axis=0)
        late_x, late_y = swap(late, 2), swap(late, 4)
        shard = jnp.concatenate(pieces, axis=0)
        early = [shard, swap(shard, 1)]
        upstreams[1] = swap(upstreams[1], 1)
        late_core = swap(late, 1)
        early, late_core, late_x, late_y, upstreams = lax.optimization_barrier(
            (early, late_core, late_x, late_y, upstreams)
        )
        late_xy = swap(late_x, 4)
        upstreams[2:] = [swap(upstreams[mask], mask) for mask in (2, 3)]
        late_cores = [late_core, swap(late_x, 1), swap(late_y, 1)]
    else:
        info = info_of(first_length)
        rows_in = exchange(cut_rows(tokens[:, 0], count, share))
        upstreams = exchange(cut_rows(cotangent[:, 0], count, share))
        early, late = plain_weights(plan, positions, inward, vectors, outward, expand, contract)
    lifted, query, key, value, mixed, totals, inward_all, small = attend(plan, info, count, rows_in, early)
    if plan.packed:
        late_xy, late_cores, upstreams, mixed = lax.optimization_barrier(
            (late_xy, late_cores, upstreams, mixed)
        )
        late = [late, late_x, late_y, late_xy] + late_cores + [swap(late_xy, 1)]
    results, (mixed_back, first_back, small_grad), late_grads = feed(
        plan, info, count, lifted, mixed, upstreams, late, small
    )
    results = exchange(results)
    if plan.packed:
        stay_keep, go_keep, stay_send, go_send = late_grads
        cut = 8 * plan.late_cut
        go = [go_keep, swap(go_send, 1)]
        one_send, two_send = fold([v[:cut] for v in go], 1) + fold([v[cut:] for v in go], 1)
        stay_other = swap(stay_send, 1)
        one_send, two_send, mixed_back = lax.optimization_barrier((one_send, two_send, mixed_back))
        one_other, two_other = swap(one_send, 4), swap(two_send, 2)
    token_pieces, early_grads = attend_back(
        plan, info, count, lifted, (query, key, value, mixed, totals), mixed_back, inward_all,
        first_back, small_grad,
    )
    if plan.packed:
        one_other, two_other, stay_other, results, token_pieces, early_grads = lax.optimization_barrier(
            (one_other, two_other, stay_other, results, token_pieces, early_grads)
        )
        keep, send = early_grads
        send = swap(send, 1)
        one, one_send = fold([stay_keep[:cut], stay_other[:cut], one_other], 2)
        two, two_send = fold([stay_keep[cut:], stay_other[cut:], two_other], 2)
        one, one_send, two, two_send, keep = lax.optimization_barrier((one, one_send, two, two_send, keep))
        one_other, two_other = swap(one_send, 2), swap(two_send, 4)
        terms = fold([keep, send], 4)
        terms, results, token_pieces = lax.optimization_barrier((terms, results, token_pieces))
        terms = [swap(term, k << 1) for k, term in enumerate(terms)]
        output = settle_rows(info, micro_count, share, results)
        one_other, two_other, output = lax.optimization_barrier((one_other, two_other, output))
        ones, twos = fold([one, one_other], 4), fold([two, two_other], 4)
        late_terms = [jnp.concatenate(pair, axis=0) for pair in zip(ones, twos)]
        late_terms = [swap(term, mask) for term, mask in zip(late_terms, plan.z_order)]
        token_pieces = list(token_pieces)
        token_pieces[1] = swap(token_pieces[1], 1)
        terms, late_terms, output, token_pieces = lax.optimization_barrier(
            (terms, late_terms, output, token_pieces)
        )
        terms = fold(terms, 4)
        early_terms = [swap(term, mask) for term, mask in zip(terms, plan.z_order)]
        for mask in (3, 2):
            token_pieces[mask] = swap(token_pieces[mask], mask)
        early_terms, token_pieces = lax.optimization_barrier((early_terms, token_pieces))
        tokens_back = in_order(token_pieces)
        values = finish(plan, info, early_terms, late_terms)
        table_t, inward_own, outward_own, expand_own, contract_own = values[:5]
        own = [v.reshape(-1) for v in values[5:]]
        table_own = table_t.T
    else:
        output = in_order(results)
        tokens_back = in_order(exchange(token_pieces))
        table_own, inward_own, outward_own, expand_own, contract_own, own = plain_grads(
            plan, counted, early_grads, late_grads
        )
    return (output[:, None], tokens_back[:, None], table_own, inward_own, own[0], outward_own, own[1], own[2],
            own[3], expand_own, own[4], contract_own, own[5], own[6], own[7])


def plain_weights(plan, positions, inward, vectors, outward, expand, contract):
    lanes, width = plan.lanes, plan.width

    def gather(value, axis=0):
        return lax.all_gather(value, AXES, axis=axis, tiled=True)

    def in_pieces(value, size):
        return value.reshape(value.shape[0], -1, size).transpose(1, 0, 2)

    table = in_pieces(gather(positions, 1).T, LANE)
    small = jnp.concatenate([gather(v) for v in vectors]).astype(F32).reshape(-1, width)
    small = jnp.pad(small, ((0, plan.small_rows - small.shape[0]), (0, 0)))
    early = [table, in_pieces(gather(inward), LANE), small]
    return early, [gather(outward), in_pieces(gather(expand), width), gather(contract)]


def plain_grads(plan, counted, early_grads, late_grads):
    width = plan.width
    table, inward, small = early_grads
    outward, expand, contract = (jnp.where(counted > 0, g, BF(0)) for g in late_grads)

    def scatter(value, axis=0):
        return lax.psum_scatter(value, AXES, scatter_dimension=axis, tiled=True).astype(F32)

    def whole(value):
        return value.transpose(1, 0, 2).reshape(value.shape[1], -1)

    flat = small.reshape(-1)
    own = []
    for vector, length in enumerate(plan.lengths):
        start = plan.block_starts[vector] * LANE
        own.append(scatter(flat[start : start + length]))
    return (scatter(table.T, 1), scatter(whole(inward)), scatter(outward), scatter(whole(expand)),
            scatter(contract), own)


def solution(mesh):
    rows = P(None, "batch", "seq", None)
    table = P(None, AXES)
    matrix = P(AXES, None)
    vector = P(AXES)
    weights = (table, matrix, vector, matrix, vector, vector, vector, matrix, vector, matrix, vector,
               vector, vector)
    return jax.shard_map(
        local,
        mesh=mesh,
        in_specs=(rows, P(None, "batch"), rows) + weights,
        out_specs=(rows, rows) + weights,
        check_vma=False,
    )
```
